32 devices in a mesh: section: 2 (over core), dp: 16 (over z, y, x).
Axes of the slice: x: 2, y: 2, z: 4, core: 2. Of those that a mesh axis runs over, the one named last changes fastest.
Arguments:
- features: float32 [2, 19200, 512], P('section', 'dp'), may hold values from -6 to 6
- out_grad: float32 [2, 19200, 512], P('section', 'dp'), may hold values from -6 to 6
- lengths: int32 [2, 16, 3], P('section', 'dp'), may hold values from 100 to 400, as said below
- join_pick: int32 [16, 3], P('dp'), may hold values from 0 to 2, each once within a row
- dw_weight: float32 [2, 5, 5, 512], P('section'), may hold values from -2.5 to 2.5
- pw_weight: float32 [2, 5, 512, 512], P('section'), may hold values from -0.25 to 0.25
- bn_gain: float32 [2, 6, 512], P('section'), may hold values from 0.5 to 1.5
- bn_bias: float32 [2, 6, 512], P('section'), may hold values from -2 to 2
- res_weight: float32 [2, 512, 512], P('section'), may hold values from -0.25 to 0.25
- se_down: float32 [2, 512, 64], P('section'), may hold values from -0.5 to 0.5
- se_down_bias: float32 [2, 64], P('section'), may hold values from -2.5 to 2.5
- se_up: float32 [2, 64, 512], P('section'), may hold values from -1.5 to 1.5
- se_up_bias: float32 [2, 512], P('section'), may hold values from -2.5 to 2.5
Outputs:
- block_out: float32 [2, 19200, 512], P('section', 'dp')
- features_grad: float32 [2, 19200, 512], P('section', 'dp')
- dw_weight_grad: float32 [2, 5, 5, 512], P('section')
- pw_weight_grad: float32 [2, 5, 512, 512], P('section')
- bn_gain_grad: float32 [2, 6, 512], P('section')
- bn_bias_grad: float32 [2, 6, 512], P('section')
- res_weight_grad: float32 [2, 512, 512], P('section')
- se_down_grad: float32 [2, 512, 64], P('section')
- se_down_bias_grad: float32 [2, 64], P('section')
- se_up_grad: float32 [2, 64, 512], P('section')
- se_up_bias_grad: float32 [2, 512], P('section')
The draws below stay inside these ranges and needn't reach their ends.
Inputs may be any that keep to these rules, and one draw needn't show every extreme that they name: `lengths`: row 0 lies between 200 and 400, row 1 between 100 and 200; each of these four ends is taken by some entry. `join_pick`: each row is a permutation of the 3 slots.
All inputs are finite; a program needn't handle non-finite values.
Results may differ from the reference program's by a relative error of at most 0.0003.
Values sent between devices are 32-bit elements; how exact they have to be, the bound alone decides.
No kernel may reach another device: no remote copies, remote signals or barrier semaphores. Data moves between devices by JAX's collectives and lax.ppermute only.
A program may use at most 320 MiB of HBM per device.

```python
import jax
import jax.numpy as jnp
from jax import lax

C = 512
SE_WIDTH = 64
KERNEL = 5
LMAX = 400
MB = 3
HALF = 200
FRAMES = 19200
N_DP = 16


def draw_lengths(key, part):
    key = jax.random.fold_in(key, 11)
    keys = jax.random.split(key, 3)
    long_rows = jax.random.randint(keys[0], (N_DP, MB), LMAX // 2, LMAX + 1)
    short_rows = jax.random.randint(keys[1], (N_DP, MB), LMAX // 4, LMAX // 2 + 1)
    order = jax.random.permutation(keys[2], N_DP * MB)
    flat_pos = jnp.arange(N_DP * MB).reshape(N_DP, MB)
    long_rows = jnp.where(flat_pos == order[0], LMAX, long_rows)
    long_rows = jnp.where(flat_pos == order[1], LMAX // 2, long_rows)
    short_rows = jnp.where(flat_pos == order[0], LMAX // 4, short_rows)
    short_rows = jnp.where(flat_pos == order[1], LMAX // 2, short_rows)
    return jnp.stack([long_rows, short_rows]).astype(jnp.int32)


def steps_of(stream_key, shape, cuts, smallest, largest):
    factor_of, own = 1.0, jax.random.fold_in(stream_key, 6)
    for dim, shards_of in cuts:
        heights = jnp.exp(jax.random.uniform(jax.random.fold_in(own, dim), (shards_of,), jnp.float32, smallest / len(cuts), largest / len(cuts)))
        factor_of = factor_of * jnp.repeat(heights, shape[dim] // shards_of).reshape([-1 if axis == dim else 1 for axis in range(len(shape))])
    return factor_of


def scatter_about(stream_key, extent, scale, most, cuts=(), held_as=jnp.bfloat16):
    factor_of = steps_of(stream_key, extent, cuts, -0.22, 0.18) if cuts else 1.0
    entries = jax.random.normal(stream_key, extent, jnp.float32) * scale * factor_of
    return jnp.minimum(jnp.maximum(entries, -most), most).astype(held_as)


def setup_inputs(seed: int = 0) -> dict:
    splits = jax.random.split(jax.random.key(seed), 14)
    features = scatter_about(splits[0], (2, FRAMES, C), 1.0, 6.0, ((0, 2), (1, 16)), jnp.float32)
    out_grad = scatter_about(splits[1], (2, FRAMES, C), 1.0, 6.0, ((0, 2), (1, 16)), jnp.float32)
    lengths = draw_lengths(jax.random.fold_in(splits[13], 71), 0)
    join_pick = jax.vmap(lambda own: jax.random.permutation(own, MB))(jax.random.split(splits[3], N_DP)).reshape((N_DP, MB)).astype(jnp.int32)
    dw_weight = scatter_about(splits[4], (2, 5, KERNEL, C), KERNEL ** -0.5, 2.5, ((0, 2),), jnp.float32)
    pw_weight = scatter_about(splits[5], (2, 5, C, C), C ** -0.5, 0.25, ((0, 2),), jnp.float32)
    bn_gain = jnp.clip(1.0 + 0.1 * jax.random.normal(splits[6], (2, 6, C), jnp.float32), 0.5, 1.5)
    bn_bias = scatter_about(splits[7], (2, 6, C), 0.4, 2.0, ((0, 2),), jnp.float32)
    res_weight = scatter_about(splits[8], (2, C, C), C ** -0.5, 0.25, ((0, 2),), jnp.float32)
    se_down = scatter_about(splits[9], (2, C, SE_WIDTH), (C // 4) ** -0.5, 0.5, ((0, 2),), jnp.float32)
    se_down_bias = scatter_about(splits[10], (2, SE_WIDTH), 0.5, 2.5, ((0, 2),), jnp.float32)
    se_up = scatter_about(splits[11], (2, SE_WIDTH, C), (SE_WIDTH // 4) ** -0.5, 1.5, ((0, 2),), jnp.float32)
    se_up_bias = scatter_about(splits[12], (2, C), 0.5, 2.5, ((0, 2),), jnp.float32)
    return {"features": features, "out_grad": out_grad, "lengths": lengths, "join_pick": join_pick, "dw_weight": dw_weight, "pw_weight": pw_weight, "bn_gain": bn_gain, "bn_bias": bn_bias, "res_weight": res_weight, "se_down": se_down, "se_down_bias": se_down_bias, "se_up": se_up, "se_up_bias": se_up_bias}


EPSILON = 1e-05
PRECISE = lax.Precision.HIGHEST

def rows_shift(values, offset):
    if offset > 0:
        return jnp.concatenate([values[..., offset:, :], jnp.zeros_like(values[..., :offset, :])], axis=-2)
    if offset < 0:
        return jnp.concatenate([jnp.zeros_like(values[..., offset:, :]), values[..., :offset, :]], axis=-2)
    return values

def label_shift(labels, offset):
    if offset > 0:
        filler = jnp.full(labels.shape[:-1] + (offset,), -7, jnp.int32)
        return jnp.concatenate([labels[..., offset:], filler], axis=-1)
    if offset < 0:
        filler = jnp.full(labels.shape[:-1] + (-offset,), -7, jnp.int32)
        return jnp.concatenate([filler, labels[..., :offset]], axis=-1)
    return labels

def depthwise(values, labels, kernel):
    taps_all = kernel.shape[0]
    total = jnp.zeros_like(values)
    for tap_no in range(taps_all):
        offset = tap_no - taps_all // 2
        same_label = (label_shift(labels, offset) == labels).astype(jnp.float32)
        total = total + kernel[tap_no] * rows_shift(values, offset) * same_label[..., None]
    return total

def decimate(values):
    frames = values.shape[-2] // 2
    kept_rows = values.reshape(values.shape[:-2] + (frames, 2, values.shape[-1]))[..., 0, :]
    return jnp.concatenate([kept_rows, jnp.zeros_like(kept_rows)], axis=-2)

def conv_pre(values, kernel, matrix, labels, strided, last):
    mixed = depthwise(values, labels, kernel)
    if last:
        mixed = jnp.where(strided, decimate(mixed), mixed)
    return jnp.einsum('...tc,ce->...te', mixed, matrix, precision=PRECISE)

def residual_pre(values, matrix, strided):
    picked = jnp.where(strided, decimate(values), values)
    return jnp.einsum('...tc,ce->...te', picked, matrix, precision=PRECISE)

def excite_tail(active, res_norm, down_w, down_bias, up_w, up_bias, labels):
    member = (labels[..., None] == jnp.arange(2, dtype=jnp.int32)).astype(jnp.float32)
    counts = lax.optimization_barrier(jnp.sum(member, axis=-2))
    seg_means = jnp.einsum('...tk,...tc->...kc', member, active, precision=PRECISE) / jnp.maximum(counts, 1.0)[..., None]
    hidden = jax.nn.silu(jnp.einsum('...kc,ce->...ke', seg_means, down_w, precision=PRECISE) + down_bias)
    gate_rows = jax.nn.sigmoid(jnp.einsum('...ke,ec->...kc', hidden, up_w, precision=PRECISE) + up_bias)
    scaled = active * jnp.einsum('...tk,...kc->...tc', member, gate_rows, precision=PRECISE)
    valid_rows = (labels >= 0).astype(jnp.float32)[..., None]
    return jax.nn.silu(scaled + res_norm) * valid_rows

def batch_norm(pre_norm, valid_rows, gain_row, bias_row):
    total_rows = jnp.sum(valid_rows)
    leading = tuple(range(pre_norm.ndim - 1))
    center = lax.optimization_barrier(jnp.sum(pre_norm * valid_rows, axis=leading)) / total_rows
    spread = lax.rsqrt(lax.optimization_barrier(jnp.sum(pre_norm * pre_norm * valid_rows, axis=leading)) / total_rows - center * center + EPSILON)
    return gain_row * (pre_norm - center) * spread + bias_row

def block(source, labels_in, labels_out, strided, params):
    kernels, matrices, gains, biases, res_matrix, down_w, down_bias, up_w, up_bias = params
    valid_in = (labels_in >= 0).astype(jnp.float32)[..., None]
    valid_out = (labels_out >= 0).astype(jnp.float32)[..., None]
    values = source
    for layer_no in range(5):
        last = layer_no == 4
        pre_norm = conv_pre(values, kernels[layer_no], matrices[layer_no], labels_in, strided, last)
        valid_rows = valid_out if last else valid_in
        values = jax.nn.silu(batch_norm(pre_norm, valid_rows, gains[layer_no], biases[layer_no])) * valid_rows
    res_norm = batch_norm(residual_pre(source, res_matrix, strided), valid_out, gains[5], biases[5])
    return excite_tail(values, res_norm, down_w, down_bias, up_w, up_bias, labels_out)

def forward(feature_in, weight_in, lengths, join_pick):
    channels = feature_in.shape[-1]
    first_inputs = feature_in[0].reshape(N_DP, MB, LMAX, channels)
    join_inputs = feature_in[1].reshape(N_DP, MB, LMAX, channels)
    first_params = tuple((entry[0] for entry in weight_in))
    second_params = tuple((entry[1] for entry in weight_in))
    position = jnp.arange(LMAX, dtype=jnp.int32)[None, :]
    slot_ids = jnp.arange(MB, dtype=jnp.int32)[None, :]
    run_block = jax.checkpoint(block, static_argnums=(3,))
    first_outs = []
    second_outs = []
    for micro_no in range(MB):
        first_len = lengths[0][:, micro_no][:, None]
        half_len = (first_len + 1) // 2
        labels_in = jnp.where(position < first_len, 0, -1).astype(jnp.int32)
        labels_out = jnp.where(position < half_len, 0, -1).astype(jnp.int32)
        first_out = run_block(first_inputs[:, micro_no], labels_in, labels_out, True, first_params)
        choose = join_pick[:, micro_no][:, None] == slot_ids
        joined = jnp.einsum('dm,dmtc->dtc', choose.astype(jnp.float32), join_inputs, precision=PRECISE)
        joined_len = lax.optimization_barrier(jnp.sum(jnp.where(choose, lengths[1], 0), axis=1))[:, None]
        source = jnp.concatenate([first_out[:, :HALF], joined[:, HALF:]], axis=1)
        inside = (position >= HALF) & (position < HALF + joined_len)
        labels_two = jnp.where(position < half_len, 0, jnp.where(inside, 1, -1)).astype(jnp.int32)
        second_out = run_block(source, labels_two, labels_two, False, second_params)
        first_outs.append(first_out)
        second_outs.append(second_out)
    first_all = jnp.stack(first_outs, axis=1).reshape(N_DP * MB * LMAX, channels)
    second_all = jnp.stack(second_outs, axis=1).reshape(N_DP * MB * LMAX, channels)
    return jnp.stack([first_all, second_all])

def reference(features, out_grad, lengths, join_pick, dw_weight, pw_weight, bn_gain, bn_bias, res_weight, se_down, se_down_bias, se_up, se_up_bias):
    params = (dw_weight, pw_weight, bn_gain, bn_bias, res_weight, se_down, se_down_bias, se_up, se_up_bias)
    outputs, pullback = jax.vjp(lambda feature_in, weight_in: forward(feature_in, weight_in, lengths, join_pick), features, params)
    feat_grad, weight_grads = pullback(out_grad)
    return (outputs, feat_grad, weight_grads[0], weight_grads[1], weight_grads[2], weight_grads[3], weight_grads[4], weight_grads[5], weight_grads[6], weight_grads[7], weight_grads[8])
```

```python
import jax
import jax.numpy as jnp
from jax import lax
from jax.sharding import PartitionSpec as P

EPSILON = 1e-05
PRECISE = lax.Precision.HIGHEST
TAPS = 5


def swapped(block, axis, mask):
    size = lax.axis_size(axis)
    return lax.ppermute(block, axis, [(i, i ^ mask) for i in range(size)])


def total_over(block, form):
    size = lax.axis_size("dp")
    if size & (size - 1):
        return lax.psum(block, "dp")
    if form == "pairs":
        step = 1
        while step < size:
            block = block + swapped(block, "dp", step)
            step *= 2
        return block
    if form == "fours":
        step = 1
        while step < size:
            if step * 4 <= size:
                one = swapped(block, "dp", step)
                two = swapped(block, "dp", 2 * step)
                three = swapped(block, "dp", 3 * step)
                block = (block + one) + (two + three)
                step *= 4
            else:
                block = block + swapped(block, "dp", step)
                step *= 2
        return block
    if form == "gather":
        return jnp.sum(lax.all_gather(block, "dp"), axis=0)
    spread = jnp.broadcast_to(block, (size,) + block.shape)
    return jnp.sum(lax.all_to_all(spread, "dp", 0, 0), axis=0)


def dot(a, b):
    return jnp.dot(a, b, precision=PRECISE, preferred_element_type=jnp.float32)


def shifted(values, offset):
    rows = values.shape[-2]
    if offset == 0:
        return values
    pad = [(0, 0)] * values.ndim
    pad[-2] = (max(-offset, 0), max(offset, 0))
    return jnp.pad(values, pad)[..., max(offset, 0) : max(offset, 0) + rows, :]


def conv(values, kernel):
    return sum(kernel[k] * shifted(values, k - TAPS // 2) for k in range(TAPS))


def conv_back(grad, kernel):
    return sum(kernel[k] * shifted(grad, TAPS // 2 - k) for k in range(TAPS))


def conv_weight(grad, values):
    axes = tuple(range(grad.ndim - 1))
    return jnp.stack([jnp.sum(grad * shifted(values, k - TAPS // 2), axis=axes) for k in range(TAPS)])


def sums_of(first, second):
    return jnp.stack([jnp.sum(first, axis=1), jnp.sum(second, axis=1)], axis=1)


def center_spread(sums, rows):
    center = sums[:, 0] / rows
    spread = lax.rsqrt(sums[:, 1] / rows - center * center + EPSILON)
    return center[:, None], spread[:, None]


def swish_grad(u):
    s = jax.nn.sigmoid(u)
    return s * (1.0 + u * (1.0 - s))


def split(values, parts):
    mb, rows, channels = values.shape
    return values.reshape(mb * parts, rows // parts, channels)


class Block:
    def __init__(self, weights, valid_in, valid_out, parts, strided, member_counts):
        (self.dw, self.pw, self.gain, self.bias, self.res_w, self.down, self.down_b, self.up, self.up_b) = weights
        self.valid_in, self.valid_out = valid_in, valid_out
        self.parts, self.strided = parts, strided
        self.counts = member_counts

    def conv(self, h, i):
        y = conv(split(h, self.parts), self.dw[i]).reshape(h.shape)
        return y[:, ::2] if self.strided and i == 4 else y

    def forward(self, x, form):
        self.x = x
        picked = x[:, ::2] if self.strided else x
        self.picked = picked
        self.r = dot(picked, self.res_w)
        h = x
        self.z, self.h, self.y, self.stats = [], [], [], []
        for i in range(5):
            valid = self.valid_out if i == 4 else self.valid_in
            self.h.append(h)
            y = self.conv(h, i)
            z = dot(y, self.pw[i])
            zv = z * valid
            sums = sums_of(zv, zv * z)
            if i == 0:
                rv = self.r * self.valid_out
                rows = jnp.stack([jnp.sum(self.valid_in, axis=1), jnp.sum(self.valid_out, axis=1)], axis=1)
                rows = jnp.broadcast_to(rows, rows.shape[:2] + (z.shape[-1],))
                total = total_over(jnp.concatenate([sums, sums_of(rv, rv * self.r), rows], axis=1), form)
                self.rows_in, self.rows_out = total[:, 4], total[:, 5]
                self.res_stats = center_spread(total[:, 2:4], self.rows_out)
                total = total[:, :2]
            else:
                total = total_over(sums, form)
            rows = self.rows_out if i == 4 else self.rows_in
            center, spread = center_spread(total, rows)
            self.z.append(z)
            self.y.append(y)
            self.stats.append((center, spread))
            u = self.gain[i] * ((z - center) * spread) + self.bias[i]
            h = jax.nn.silu(u) * valid
        self.h4 = h
        mb, rows, channels = h.shape
        parts = self.parts
        means = jnp.sum(split(h, parts), axis=1) / jnp.maximum(self.counts, 1.0)[:, None]
        self.means = means
        self.p = dot(means, self.down) + self.down_b
        self.hidden = jax.nn.silu(self.p)
        self.gate = jax.nn.sigmoid(dot(self.hidden, self.up) + self.up_b)
        a = (split(h, parts) * self.gate[:, None]).reshape(h.shape)
        self.rh = (self.r - self.res_stats[0]) * self.res_stats[1]
        rn = self.gain[5] * self.rh + self.bias[5]
        self.t = a + rn
        return jax.nn.silu(self.t) * self.valid_out

    def dz(self, du, zh, i, total, rows, spread, valid):
        rows = rows[:, None]
        bias_sum, gain_sum = total[:, :1], total[:, 1:2]
        return self.gain[i] * spread * (du - bias_sum / rows - zh * gain_sum / rows) * valid

    def backward(self, grad_out, form):
        parts = self.parts
        dt = grad_out * self.valid_out * swish_grad(self.t)
        shape = dt.shape
        de = jnp.sum(split(dt * self.h4, parts), axis=1)
        dq = de * self.gate * (1.0 - self.gate)
        up_grad = dot(self.hidden.T, dq)
        up_b_grad = jnp.sum(dq, axis=0)
        dp = dot(dq, self.up.T) * swish_grad(self.p)
        down_grad = dot(self.means.T, dp)
        down_b_grad = jnp.sum(dp, axis=0)
        dm = dot(dp, self.down.T) / jnp.maximum(self.counts, 1.0)[:, None]
        dh = (split(dt, parts) * self.gate[:, None] + dm[:, None]).reshape(shape)
        gains, biases, dws, pws = [None] * 6, [None] * 6, [None] * 5, [None] * 5
        for i in reversed(range(5)):
            last = i == 4
            valid = self.valid_out if last else self.valid_in
            rows = self.rows_out if last else self.rows_in
            center, spread = self.stats[i]
            zh = (self.z[i] - center) * spread
            du = dh * valid * swish_grad(self.gain[i] * zh + self.bias[i])
            sums = sums_of(du, du * zh)
            if last:
                total = total_over(jnp.concatenate([sums, sums_of(dt, dt * self.rh)], axis=1), form)
                biases[5], gains[5] = jnp.sum(total[:, 2], axis=0), jnp.sum(total[:, 3], axis=0)
                dr = self.dz(dt, self.rh, 5, total[:, 2:4], self.rows_out, self.res_stats[1], self.valid_out)
                res_grad = dot(self.picked.reshape(-1, shape[-1]).T, dr.reshape(-1, shape[-1]))
                dx_res = dot(dr, self.res_w.T)
            else:
                total = total_over(sums, form)
            biases[i], gains[i] = jnp.sum(total[:, 0], axis=0), jnp.sum(total[:, 1], axis=0)
            dz = self.dz(du, zh, i, total, rows, spread, valid)
            pws[i] = dot(self.y[i].reshape(-1, shape[-1]).T, dz.reshape(-1, shape[-1]))
            dy = dot(dz, self.pw[i].T)
            if last and self.strided:
                dy = jnp.stack([dy, jnp.zeros_like(dy)], axis=2).reshape(self.x.shape)
            dws[i] = conv_weight(split(dy, parts), split(self.h[i], parts))
            dh = conv_back(split(dy, parts), self.dw[i]).reshape(self.x.shape)
        if self.strided:
            dx_res = jnp.stack([dx_res, jnp.zeros_like(dx_res)], axis=2).reshape(self.x.shape)
        dx = dh * self.valid_in + dx_res
        grads = (jnp.stack(dws), jnp.stack(pws), res_grad, down_grad, down_b_grad, up_grad, up_b_grad)
        return dx, jnp.stack(gains), jnp.stack(biases), grads


def per_device(features, out_grad, lengths, join_pick, *weights):
    first = lax.axis_index("section") == 0
    mb = join_pick.shape[1]
    channels = features.shape[-1]
    slot = features.shape[1] // mb
    half = slot // 2
    inputs = features[0].reshape(mb, slot, channels)
    cotangent = out_grad[0].reshape(mb, slot, channels)
    own = lengths[0, 0]
    picks = join_pick[0]
    weights = tuple(w[0] for w in weights)
    place = jnp.arange(slot, dtype=jnp.int32)[None, :]

    def mask(rows, length):
        return (place[:, :rows] < length[:, None]).astype(jnp.float32)[..., None]

    half_len = (own + 1) // 2
    half_far = lax.ppermute(half_len.astype(jnp.float32), "section", [(0, 1)])
    valid_in, valid_out = mask(slot, own), mask(half, half_len)
    c14 = Block(weights, valid_in, valid_out, 1, True, half_len.astype(jnp.float32)[:, None][:, 0])
    first_out = c14.forward(inputs * valid_in, "pairs")
    arrived = lax.ppermute(first_out, "section", [(0, 1)])

    join_len = own[picks]
    joined = inputs[:, half:][picks]
    half_far = half_far.astype(jnp.int32)
    valid = jnp.concatenate([mask(half, half_far), mask(half, join_len)], axis=1)
    counts = jnp.stack([half_far, join_len], axis=1).reshape(-1).astype(jnp.float32)
    c15 = Block(weights, valid, valid, 2, False, counts)
    second_out = c15.forward(jnp.concatenate([arrived, joined], axis=1) * valid, "swap")
    dx2, gain2, bias2, grads2 = c15.backward(cotangent, "gather")
    back = lax.ppermute(dx2[:, :half], "section", [(1, 0)])
    grads2 = lax.psum(grads2, "dp")
    dx1, gain1, bias1, grads1 = c14.backward(cotangent[:, :half] + back, "fours")
    grads1 = lax.psum(grads1, "dp")

    pad = jnp.zeros((mb, half, channels), jnp.float32)
    block_out = jnp.where(first, jnp.concatenate([first_out, pad], axis=1), second_out)
    hit = (picks[None, :] == jnp.arange(mb)[:, None]).astype(jnp.float32)
    placed = sum(hit[:, m, None, None] * dx2[m, half:][None] for m in range(mb))
    dx = jnp.where(first, dx1, jnp.concatenate([pad, placed], axis=1))
    grads = [jnp.where(first, a, b)[None] for a, b in zip(grads1, grads2)]
    gain = jnp.where(first, gain1, gain2)[None]
    bias = jnp.where(first, bias1, bias2)[None]
    block_out = block_out.reshape(features.shape)
    return (block_out, dx.reshape(features.shape), grads[0], grads[1], gain, bias, *grads[2:])


def solution(mesh):
    rows = P("section", "dp", None)
    own = lambda dims: P("section", *([None] * dims))
    weights = (own(3), own(3), own(2), own(2), own(2), own(2), own(1), own(2), own(1))
    in_specs = (rows, rows, rows, P("dp", None), *weights)
    out_specs = (rows, rows, *weights)
    return jax.shard_map(per_device, mesh=mesh, in_specs=in_specs, out_specs=out_specs, check_vma=False)
```

```python
import functools

import jax
import jax.numpy as jnp
from jax import lax
from jax.experimental import pallas as pl
from jax.experimental.pallas import tpu as pltpu
from jax.sharding import PartitionSpec as P

EPSILON = 1e-05
EXACT = lax.Precision.HIGHEST
TAPS = 5
MB = 3
OWN = 2
SLOT = 400
HALF = 200
KEPT = 208
C = 512
LANES = 128
CHUNKS = [slice(c, c + LANES) for c in range(0, C, LANES)]
SE = 64
BF16, F32 = jnp.bfloat16, jnp.float32
VMEM_BYTES = 60 << 20


def radices(size, most):
    stages, left = [], size
    while left > 1:
        radix = min(most, left)
        while left % radix:
            radix -= 1
        stages.append(radix)
        left //= radix
    return stages


def exchange(block, radix, stride):
    size = lax.axis_size("dp")
    if radix == size:
        return lax.all_to_all(block, "dp", 0, 0)
    groups = []
    for base in range(size):
        if (base // stride) % radix == 0:
            groups.append([base + j * stride for j in range(radix)])
    return lax.all_to_all(block, "dp", 0, 0, axis_index_groups=groups)


def shared(block, stages):
    stride = 1
    for no, radix in enumerate(stages):
        if no:
            block = jnp.broadcast_to(jnp.sum(block, axis=0), (radix,) + block.shape[1:])
        block = exchange(block, radix, stride)
        stride *= radix
    return block


def halves(x):
    high = x.astype(BF16)
    return high, (x - high.astype(F32)).astype(BF16)


def sigmoid(x):
    return 0.5 * jnp.tanh(0.5 * x) + 0.5


def exact_dot(a, b, dims=((1,), (0,))):
    return lax.dot_general(a, b, (dims, ((), ())), precision=EXACT, preferred_element_type=F32)


def fast_dot(a, b, dims=((1,), (0,))):
    return lax.dot_general(a, b, (dims, ((), ())), preferred_element_type=F32)


def three_dots(high, low, w_ref, dims=((1,), (0,))):
    w_high, w_low = w_ref[0, 0], w_ref[0, 1]
    return fast_dot(high, w_high, dims) + (fast_dot(low, w_high, dims) + fast_dot(high, w_low, dims))


def column_sum(x):
    return jnp.sum(x, axis=0, keepdims=True)


class Rows:
    def __init__(self, meta, m, two, rows, which=0):
        place = lax.broadcasted_iota(jnp.int32, (rows, LANES), 0)
        if two:
            later = place >= HALF
            limit = jnp.where(later, HALF + meta[OWN + m], meta[m])
            self.mask = place < limit
        else:
            self.mask = place < meta[which * OWN + m]

    def keep(self, x):
        return jnp.where(self.mask, x, 0.0)


class Padded:
    def __init__(self, ref, two):
        self.ref = ref
        self.pieces = [(8, 0, HALF), (16 + HALF, HALF, HALF)] if two else [(8, 0, SLOT)]

    def put(self, x):
        zeros = jnp.zeros((8, LANES), F32)
        for at, start, rows in self.pieces:
            self.ref[at - 8 : at, :] = zeros
            self.ref[at : at + rows, :] = x[start : start + rows]
        self.ref[at + rows : at + rows + 8, :] = zeros

    def get(self, offset):
        parts = [self.ref[at + offset : at + offset + rows, :] for at, _, rows in self.pieces]
        return parts[0] if len(parts) == 1 else jnp.concatenate(parts, axis=0)

    def conv(self, kernel):
        total = kernel[0:1] * self.get(-2)
        for k in range(1, TAPS):
            total = total + kernel[k : k + 1] * self.get(k - 2)
        return total

    def conv_back(self, kernel):
        total = kernel[0:1] * self.get(2)
        for k in range(1, TAPS):
            total = total + kernel[k : k + 1] * self.get(2 - k)
        return total


def every_other(ref, x):
    ref[0:SLOT, :] = x
    ref[SLOT : 2 * KEPT, :] = jnp.zeros((2 * KEPT - SLOT, LANES), F32)
    return ref[pl.ds(0, KEPT, stride=2), :]


def spread_out(ref, x):
    ref[...] = jnp.zeros_like(ref)
    ref[pl.ds(0, KEPT, stride=2), :] = x
    return ref[0:SLOT, :]


def center_spread(sums, rows):
    center = sums[0:1] / rows
    return center, lax.rsqrt(sums[1:2] / rows - center * center + EPSILON)


def added(ref):
    return jnp.sum(ref[:, 0], axis=0)


def send(ref, rows):
    for copy in range(ref.shape[0]):
        for row, x in enumerate(rows):
            ref[copy, 0, row : row + 1, 0 : x.shape[1]] = x


def pad_scratch():
    return pltpu.VMEM((len(CHUNKS), SLOT + 24, LANES), F32)


def stride_scratch():
    return pltpu.VMEM((len(CHUNKS), 2 * KEPT, LANES), F32)


def slots(rows, cols=C):
    return pl.BlockSpec((1, rows, cols), lambda m, *_: (m, 0, 0))


def copies(count, rows, cols=C):
    return pl.BlockSpec((count, 1, rows, cols), lambda m, *_: (0, m, 0, 0))


def whole(*shape):
    return pl.BlockSpec(shape, lambda m, *_: (0,) * len(shape))


def layer(i, *shape):
    return pl.BlockSpec((1,) + shape, lambda m, *_: (i,) + (0,) * len(shape))


def f32(*shape):
    return jax.ShapeDtypeStruct(shape, F32)


def bf16(*shape):
    return jax.ShapeDtypeStruct(shape, BF16)


def call(body, meta, args, outs, scratch=(), name=None, flops=0, steps=OWN, after=(), into=None):
    arrays, in_specs = [a for a, _ in args], [s for _, s in args]
    shapes, out_specs = [a for a, _ in outs], [s for _, s in outs]
    size = sum(a.size * a.dtype.itemsize for a in arrays + shapes)
    extra = list(after) + ([] if into is None else [into])
    count = len(arrays)

    def inner(meta, *refs):
        body(meta, *refs[:count], *refs[count + len(extra) :])

    return pl.pallas_call(
        inner,
        out_shape=shapes,
        grid_spec=pltpu.PrefetchScalarGridSpec(
            num_scalar_prefetch=1,
            grid=(steps,),
            in_specs=in_specs + [pl.BlockSpec(memory_space=pl.ANY)] * len(extra),
            out_specs=out_specs,
            scratch_shapes=list(scratch),
        ),
        input_output_aliases={} if into is None else {count + len(extra): 0},
        compiler_params=pltpu.CompilerParams(vmem_limit_bytes=VMEM_BYTES),
        cost_estimate=pl.CostEstimate(flops=flops, bytes_accessed=size, transcendentals=0),
        name=name,
    )(meta, *arrays, *extra)


def prepare(meta, own, far, block, name):
    count = own[0].shape[0] + len(own) - 1

    def body(meta, *refs):
        out = refs[-1]
        sides = []
        for side in (refs[: len(own)], refs[len(own) : -1]):
            w = side[0][0]
            if len(own) > 1:
                w = jnp.where(pl.program_id(0) < count - 1, w, side[1][...])
            sides.append(w)
        w = jnp.where(meta[2 * OWN] == 1 - block, sides[0], sides[1])
        out[0, 0], out[0, 1] = halves(w)

    stacked = pl.BlockSpec((1, C, C), lambda j, *_: (jnp.minimum(j, own[0].shape[0] - 1), 0, 0))
    specs = [stacked, whole(C, C)][: len(own)]
    out = pl.BlockSpec((1, 2, C, C), lambda j, *_: (j, 0, 0, 0))
    args = list(zip(own, specs)) + list(zip(far, specs))
    return call(body, meta, args, [(bf16(count, 2, C, C), out)], name=name, steps=count)[0]


class Block:
    def __init__(self, two, meta, weights, ready, stages):
        self.two, self.meta, self.stages = two, meta, stages
        self.dw, self.gain, self.bias, self.down, self.down_b, self.up, self.up_b = weights
        self.ready = ready
        self.tail_rows = SLOT if two else KEPT
        self.first, self.last = stages[0], stages[-1]
        self.tag = "c15" if two else "c14"

    def rows_of(self, i):
        return self.tail_rows if i == 4 else SLOT

    def valid(self, meta, m, i):
        last = i == 4 and not self.two
        return Rows(meta, m, self.two, self.rows_of(i), which=1 if last else 0)

    def matrix(self, i):
        first, rest = self.ready
        return (first, layer(0, 2, C, C)) if i == 0 else (rest, layer(i, 2, C, C))

    def source_args(self):
        if not self.two:
            return [(self.x, slots(SLOT)), (self.x_far, whole(SLOT, C))]
        far = pl.BlockSpec((HALF, C), lambda m, *_: (m, 0))
        near = pl.BlockSpec((1, 1, HALF, C), lambda m, meta: (meta[2 * OWN + 1], 1, 0, 0))
        return [(self.arrived, slots(HALF)), (self.joined_far, far), (self.joined, near)]

    def source(self, meta, refs, cs):
        lower = meta[2 * OWN] == 1
        if not self.two:
            return jnp.where(lower, refs[0][0, :, cs], refs[1][:, cs])
        joined = jnp.where(lower, refs[1][:, cs], refs[2][0, 0, :, cs])
        return jnp.concatenate([refs[0][0, :, cs], joined], axis=0)

    def before_args(self, i):
        if i == 0:
            return self.source_args()
        return [(self.z[i - 1], slots(SLOT)), (self.stats[i - 1], slots(2))]


    def forward_layer(self, i, after=()):
        two, count = self.two, self.first
        strided = i == 4 and not two
        rows = self.rows_of(i)
        n_src = len(self.source_args())
        width = C + LANES if i == 0 else C
        sent = 4 if i == 1 else 2

        def body(meta, *refs):
            refs = list(refs)
            take = lambda n: [refs.pop(0) for _ in range(n)]
            m = pl.program_id(0)
            if i == 0:
                src = take(n_src)
            else:
                z_ref, got_ref = take(2)
                n_ref, = take(1) if i > 1 else (None,)
                gain_ref, bias_ref = take(2)
                res_sum, = take(1) if i == 1 else (None,)
            dw_ref, w_ref, z_out, pay = take(4)
            if i:
                stat_out, = take(1)
            if i == 1:
                n_out, = take(1)
            pad, y_ref = take(2)
            alt, = take(1) if strided else (None,)
            valid_in = self.valid(meta, m, 0)
            if i:
                sums = added(got_ref)
                if i == 1:
                    count_in = jnp.maximum(jnp.concatenate([sums[0:1, C:]] * len(CHUNKS), axis=1), 1.0)
                    count_out = jnp.maximum(jnp.concatenate([sums[1:2, C:]] * len(CHUNKS), axis=1), 1.0)
                    n_out[0, 0:1, :] = count_in
                    n_out[0, 1:2, :] = count_out
                else:
                    count_in = n_ref[0, 0:1, :]
                center, spread = center_spread(sums[:, :C], count_in)
                stat_out[0, 0:1, :] = center
                stat_out[0, 1:2, :] = spread
                scale = gain_ref[i - 1 : i] * spread
                shift = bias_ref[i - 1 : i] - center * scale
            for c, cs in enumerate(CHUNKS):
                if i == 0:
                    h = valid_in.keep(self.source(meta, src, cs))
                else:
                    u = z_ref[0, :, cs] * scale[:, cs] + shift[:, cs]
                    h = valid_in.keep(u * sigmoid(u))
                padded = Padded(pad.at[c], two)
                padded.put(h)
                y = padded.conv(dw_ref[0, :, cs])
                if strided:
                    y = every_other(alt.at[c], y)
                high, low = halves(y)
                y_ref[:, cs] = high
                y_ref[:, C + cs.start : C + cs.stop] = low
            z = three_dots(y_ref[:, 0:C], y_ref[:, C : 2 * C], w_ref)
            z_out[0] = z
            valid = self.valid(meta, m, i)
            one, square = [], []
            for cs in CHUNKS:
                kept = valid.keep(z[:, cs])
                one.append(column_sum(kept))
                square.append(column_sum(kept * kept))
            if i == 0:
                if two:
                    number = (meta[m] + meta[OWN + m]).astype(F32)
                    numbers = number, number
                else:
                    numbers = meta[m].astype(F32), meta[OWN + m].astype(F32)
                one.append(jnp.full((1, LANES), numbers[0], F32))
                square.append(jnp.full((1, LANES), numbers[1], F32))
            out = [jnp.concatenate(one, axis=1), jnp.concatenate(square, axis=1)]
            if i == 1:
                out += [res_sum[0, 0:1, :], res_sum[0, 1:2, :]]
            send(pay, out)

        if i == 0:
            args = list(self.source_args())
        else:
            got = 4 if i == 2 else 2
            args = [(self.z[i - 1], slots(SLOT)), (self.got[i - 1], copies(self.last, got, C + LANES if i == 1 else C))]
            if i > 1:
                args.append((self.number, slots(2)))
            args += [(self.gain, whole(6, C)), (self.bias, whole(6, C))]
            if i == 1:
                args.append((self.res_sum, slots(2)))
        args += [(self.dw, layer(i, TAPS, C)), self.matrix(i)]
        outs = [(f32(OWN, rows, C), slots(rows)), (f32(count, OWN, sent, width), copies(count, sent, width))]
        if i:
            outs.append((f32(OWN, 2, C), slots(2)))
        if i == 1:
            outs.append((f32(OWN, 2, C), slots(2)))
        scratch = [pad_scratch(), pltpu.VMEM((rows, 2 * C), BF16)]
        if strided:
            scratch.append(stride_scratch())
        result = call(body, self.meta, args, outs, scratch, f"{self.tag}_forward_{i}", 6 * OWN * rows * C * C, after=after)
        self.z.append(result[0])
        if i:
            self.stats.append(result[2])
        if i == 1:
            self.number = result[3]
        self.got.append(shared(result[1], self.stages))

    def residual(self):
        two, rows = self.two, self.tail_rows

        def body(meta, *refs):
            refs = list(refs)
            src = [refs.pop(0) for _ in self.source_args()]
            w_ref, r_out, x_out, sum_out = refs[:4]
            alt = refs[4] if not two else None
            m = pl.program_id(0)
            valid_in = self.valid(meta, m, 0)
            for c, cs in enumerate(CHUNKS):
                x = valid_in.keep(self.source(meta, src, cs))
                if not two:
                    x = every_other(alt.at[c], x)
                high, low = halves(x)
                x_out[0, :, cs] = high
                x_out[0, :, C + cs.start : C + cs.stop] = low
            r = three_dots(x_out[0, :, 0:C], x_out[0, :, C : 2 * C], w_ref)
            r_out[0] = r
            valid = self.valid(meta, m, 4)
            for cs in CHUNKS:
                kept = valid.keep(r[:, cs])
                sum_out[0, 0:1, cs] = column_sum(kept)
                sum_out[0, 1:2, cs] = column_sum(kept * kept)

        args = self.source_args() + [self.matrix(5)]
        outs = [
            (f32(OWN, rows, C), slots(rows)),
            (bf16(OWN, rows, 2 * C), slots(rows, 2 * C)),
            (f32(OWN, 2, C), slots(2)),
        ]
        scratch = [] if two else [stride_scratch()]
        self.r, self.picked, self.res_sum = call(
            body, self.meta, args, outs, scratch, f"{self.tag}_residual", 6 * OWN * rows * C * C
        )

    def forward(self, after=()):
        self.z, self.got, self.stats = [], [], []
        self.forward_layer(0)
        self.residual()
        for i in range(1, 5):
            self.forward_layer(i, after if i == 2 else ())


    def segments(self):
        return [(0, HALF), (HALF, HALF)] if self.two else [(0, self.tail_rows)]

    def lengths(self, meta, m):
        if self.two:
            return [meta[m], meta[OWN + m]]
        return [meta[OWN + m]]

    def squeeze(self, sums, counts, se_refs):
        down, down_b, up, up_b = se_refs
        means = [s / jnp.maximum(jnp.full((1, C), n.astype(F32)), 1.0) for s, n in zip(sums, counts)]
        means = jnp.concatenate(means + [jnp.zeros((8 - len(means), C), F32)], axis=0)
        p = exact_dot(means, down[...]) + down_b[...]
        hidden = p * sigmoid(p)
        gate = sigmoid(exact_dot(hidden, up[...]) + up_b[...])
        return means, p, gate

    def se_args(self):
        return [(self.down, whole(C, SE)), (self.down_b, whole(1, SE)), (self.up, whole(SE, C)), (self.up_b, whole(1, C))]

    def by_segment(self, rows, cs):
        parts = [jnp.broadcast_to(rows[j : j + 1, cs], (n, LANES)) for j, (_, n) in enumerate(self.segments())]
        return parts[0] if len(parts) == 1 else jnp.concatenate(parts, axis=0)

    def seg_sums(self, x):
        return [column_sum(x[at : at + n]) for at, n in self.segments()]

    def tail(self, cotangent=None, far=None):
        two, rows, count = self.two, self.tail_rows, self.first
        back = cotangent is not None

        def body(meta, *refs):
            refs = list(refs)
            take = lambda n: [refs.pop(0) for _ in range(n)]
            m = pl.program_id(0)
            z_ref, got4, r_ref, got1, n_ref, gain, bias = take(7)
            se_refs = take(4)
            if back:
                cot_ref, far_ref = take(2)
            out, stat_out, rstat_out, means_out, p_out, gate_out = take(6)
            if back:
                du_out, dt_out, pay, dq_out, dp_out = take(5)
            h_ref, = take(1)
            valid = self.valid(meta, m, 4)
            number = n_ref[0, 1:2, :]
            center, spread = center_spread(added(got4), number)
            rcenter, rspread = center_spread(added(got1)[2:4], number)
            stat_out[0, 0:1, :] = center
            stat_out[0, 1:2, :] = spread
            rstat_out[0, 0:1, :] = rcenter
            rstat_out[0, 1:2, :] = rspread
            scale = gain[4:5] * spread
            shift = bias[4:5] - center * scale
            rscale = gain[5:6] * rspread
            rshift = bias[5:6] - rcenter * rscale
            sums = []
            for cs in CHUNKS:
                u = z_ref[0, :, cs] * scale[:, cs] + shift[:, cs]
                h = valid.keep(u * sigmoid(u))
                h_ref[:, cs] = h
                sums.append(self.seg_sums(h))
            sums = [jnp.concatenate([s[j] for s in sums], axis=1) for j in range(len(self.segments()))]
            means, p, gate = self.squeeze(sums, self.lengths(meta, m), se_refs)
            means_out[0] = means
            p_out[0] = p
            gate_out[0] = gate
            for cs in CHUNKS:
                t = h_ref[:, cs] * self.by_segment(gate, cs) + r_ref[0, :, cs] * rscale[:, cs] + rshift[:, cs]
                result = valid.keep(t * sigmoid(t))
                out[0, 0:rows, cs] = result
                if rows < SLOT:
                    out[0, rows:SLOT, cs] = jnp.zeros((SLOT - rows, LANES), F32)
            if back:
                state = (z_ref, r_ref, gain, bias, center, spread, rcenter, rspread)
                cot = lambda cs: jnp.where(meta[2 * OWN] == 1, far_ref[0, :, cs], cot_ref[0, :, cs])
                self.tail_back(valid, meta, m, state, cot, (means, p, gate), se_refs, du_out, dt_out, pay, dq_out, dp_out)

        args = [
            (self.z[4], slots(rows)), (self.got[4], copies(self.last, 2)), (self.r, slots(rows)),
            (self.got[1], copies(self.last, 4)), (self.number, slots(2)),
            (self.gain, whole(6, C)), (self.bias, whole(6, C)),
        ] + self.se_args()
        outs = [
            (f32(OWN, SLOT, C), slots(SLOT)), (f32(OWN, 2, C), slots(2)), (f32(OWN, 2, C), slots(2)),
            (f32(OWN, 8, C), slots(8)), (f32(OWN, 8, SE), slots(8, SE)), (f32(OWN, 8, C), slots(8)),
        ]
        if back:
            last = pl.BlockSpec((1, SLOT, C), lambda m, *_: (MB - 1, 0, 0))
            args += [(cotangent, last), (far, slots(SLOT))]
            outs += self.tail_outs()
        result = call(body, self.meta, args, outs, [pltpu.VMEM((rows, C), F32)], f"{self.tag}_tail")
        self.stats.append(result[1])
        self.rstat, self.se_state = result[2], result[3:6]
        if back:
            self.tail_results(result[6:])
        return result[0]

    def tail_outs(self):
        rows, count = self.tail_rows, self.first
        return [
            (f32(OWN, rows, C), slots(rows)), (f32(OWN, rows, C), slots(rows)),
            (f32(count, OWN, 4, C), copies(count, 4)), (f32(OWN, 8, C), slots(8)), (f32(OWN, 8, SE), slots(8, SE)),
        ]

    def tail_results(self, result):
        self.du, self.dt, pay, self.dq, self.dp = result
        self.locals = [jnp.sum(pay[0], axis=0)]
        self.back_got = shared(pay, self.stages)

    def tail_back(self, valid, meta, m, state, cot, se, se_refs, du_out, dt_out, pay, dq_out, dp_out):
        z_ref, r_ref, gain, bias, center, spread, rcenter, rspread = state
        means, p, gate = se
        down, down_b, up, up_b = se_refs
        scale = gain[4:5] * spread
        shift = bias[4:5] - center * scale
        res_gain, res_bias, gate_grad = [], [], []
        for cs in CHUNKS:
            u = z_ref[0, :, cs] * scale[:, cs] + shift[:, cs]
            h = valid.keep(u * sigmoid(u))
            rh = (r_ref[0, :, cs] - rcenter[:, cs]) * rspread[:, cs]
            t = h * self.by_segment(gate, cs) + gain[5:6, cs] * rh + bias[5:6, cs]
            s = sigmoid(t)
            dt = valid.keep(cot(cs) * (s * (1.0 + t * (1.0 - s))))
            dt_out[0, :, cs] = dt
            res_bias.append(column_sum(dt))
            res_gain.append(column_sum(dt * rh))
            gate_grad.append(self.seg_sums(dt * h))
        segs = len(self.segments())
        de = [jnp.concatenate([g[j] for g in gate_grad], axis=1) for j in range(segs)]
        de = jnp.concatenate(de + [jnp.zeros((8 - segs, C), F32)], axis=0)
        dq = de * gate * (1.0 - gate)
        s = sigmoid(p)
        dp = exact_dot(dq, up[...], ((1,), (1,))) * (s * (1.0 + p * (1.0 - s)))
        dm = exact_dot(dp, down[...], ((1,), (1,)))
        dq_out[0] = dq
        dp_out[0] = dp
        dm = [
            dm[j : j + 1] / jnp.maximum(jnp.full((1, C), n.astype(F32)), 1.0)
            for j, n in enumerate(self.lengths(meta, m))
        ]
        dm = jnp.concatenate(dm, axis=0) if segs > 1 else dm[0]
        bias_sum, gain_sum = [], []
        for cs in CHUNKS:
            z = z_ref[0, :, cs]
            u = z * scale[:, cs] + shift[:, cs]
            s = sigmoid(u)
            dh = dt_out[0, :, cs] * self.by_segment(gate, cs) + self.by_segment(dm, cs)
            du = valid.keep(dh * (s * (1.0 + u * (1.0 - s))))
            du_out[0, :, cs] = du
            bias_sum.append(column_sum(du))
            gain_sum.append(column_sum(du * ((z - center[:, cs]) * spread[:, cs])))
        rows = [jnp.concatenate(x, axis=1) for x in (bias_sum, gain_sum, res_bias, res_gain)]
        send(pay, rows)

    def tail_backward(self, cotangent, far, back):
        rows = self.tail_rows

        def body(meta, z_ref, r_ref, stat, rstat, gain, bias, means, p, gate, down, down_b, up, up_b, cot_ref, far_ref, back_ref, *outs):
            m = pl.program_id(0)
            valid = self.valid(meta, m, 4)
            state = (z_ref, r_ref, gain, bias, stat[0, 0:1], stat[0, 1:2], rstat[0, 0:1], rstat[0, 1:2])
            zeros = jnp.zeros((rows - HALF, LANES), F32)

            def cot(cs):
                here = jnp.where(meta[2 * OWN] == 1, cot_ref[0, 0:HALF, cs], far_ref[:, cs])
                return jnp.concatenate([here + back_ref[0, :, cs], zeros], axis=0)

            self.tail_back(valid, meta, m, state, cot, (means[0], p[0], gate[0]), (down, down_b, up, up_b), *outs)

        args = [
            (self.z[4], slots(rows)), (self.r, slots(rows)), (self.stats[4], slots(2)), (self.rstat, slots(2)),
            (self.gain, whole(6, C)), (self.bias, whole(6, C)),
            (self.se_state[0], slots(8)), (self.se_state[1], slots(8, SE)), (self.se_state[2], slots(8)),
        ] + self.se_args() + [(cotangent, slots(SLOT)), (far, whole(HALF, C)), (back, slots(HALF))]
        self.tail_results(call(body, self.meta, args, self.tail_outs(), (), f"{self.tag}_tail_back"))


    def norm_grad(self, du, zh, scale, sums, number, cs):
        return scale[:, cs] * (du - sums[0:1, cs] / number[:, cs] - zh * (sums[1:2, cs] / number[:, cs]))

    def backward_layer(self, i):
        two, count = self.two, self.first
        strided = i == 4 and not two
        rows = self.rows_of(i)

        def body(meta, *refs):
            refs = list(refs)
            take = lambda n: [refs.pop(0) for _ in range(n)]
            m = pl.program_id(0)
            got, n_ref, du_ref, z_ref, stat, gain, bias, dw_ref, w_ref = take(9)
            if i:
                zp_ref, statp = take(2)
            else:
                dxr_ref, = take(1)
            dz_out, dy_out = take(2)
            if i:
                du_out, pay = take(2)
            elif two:
                back_out, dx_out = take(2)
            else:
                dx_out, = take(1)
            pad, = take(1)
            alt, = take(1) if refs else (None,)
            sums = added(got)
            last = i == 4
            number = n_ref[0, 1:2, :] if last else n_ref[0, 0:1, :]
            center, spread = stat[0, 0:1], stat[0, 1:2]
            scale = gain[i : i + 1] * spread
            valid = self.valid(meta, m, i)
            for cs in CHUNKS:
                zh = (z_ref[0, :, cs] - center[:, cs]) * spread[:, cs]
                dz = valid.keep(self.norm_grad(du_ref[0, :, cs], zh, scale, sums, number, cs))
                high, low = halves(dz)
                dz_out[0, :, cs] = high
                dz_out[0, :, C + cs.start : C + cs.stop] = low
            dy = three_dots(dz_out[0, :, 0:C], dz_out[0, :, C : 2 * C], w_ref, ((1,), (1,)))
            dy_out[0] = dy
            valid_in = self.valid(meta, m, 0)
            if i:
                pcenter, pspread = statp[0, 0:1], statp[0, 1:2]
                pscale = gain[i - 1 : i] * pspread
                pshift = bias[i - 1 : i] - pcenter * pscale
            bias_sum, gain_sum = [], []
            for c, cs in enumerate(CHUNKS):
                grad = dy[:, cs]
                if strided:
                    grad = spread_out(alt.at[c], grad)
                padded = Padded(pad.at[c], two)
                padded.put(grad)
                dh = padded.conv_back(dw_ref[0, :, cs])
                if i:
                    z = zp_ref[0, :, cs]
                    u = z * pscale[:, cs] + pshift[:, cs]
                    s = sigmoid(u)
                    du = valid_in.keep(dh * (s * (1.0 + u * (1.0 - s))))
                    du_out[0, :, cs] = du
                    bias_sum.append(column_sum(du))
                    gain_sum.append(column_sum(du * ((z - pcenter[:, cs]) * pspread[:, cs])))
                    continue
                dxr = dxr_ref[0, :, cs]
                if not two:
                    dxr = spread_out(alt.at[c], dxr)
                dx = valid_in.keep(dh) + dxr
                if two:
                    back_out[0, :, cs] = dx[:HALF]
                    dx_out[0, :, cs] = dx[HALF:]
                else:
                    dx_out[0, :, cs] = dx
            if i:
                send(pay, [jnp.concatenate(bias_sum, axis=1), jnp.concatenate(gain_sum, axis=1)])

        sent = 4 if i == 4 else 2
        args = [
            (self.back_got, copies(self.last, sent)), (self.number, slots(2)), (self.du, slots(rows)),
            (self.z[i], slots(rows)), (self.stats[i], slots(2)), (self.gain, whole(6, C)), (self.bias, whole(6, C)),
            (self.dw, layer(i, TAPS, C)), self.matrix(i),
        ]
        if i:
            args += self.before_args(i)
        else:
            args.append((self.dxr, slots(self.tail_rows)))
        outs = [
            (bf16(OWN, rows, 2 * C), slots(rows, 2 * C)), (f32(OWN, rows, C), slots(rows)),
        ]
        if i:
            outs += [(f32(OWN, SLOT, C), slots(SLOT)), (f32(count, OWN, 2, C), copies(count, 2))]
        elif two:
            outs += [(f32(OWN, HALF, C), slots(HALF)), (f32(OWN, HALF, C), slots(HALF))]
        else:
            outs += [(f32(OWN, SLOT, C), slots(SLOT))]
        scratch = [pad_scratch()]
        if strided or (i == 0 and not two):
            scratch.append(stride_scratch())
        result = call(
            body, self.meta, args, outs, scratch, f"{self.tag}_backward_{i}", 6 * OWN * rows * C * C, after=self.done
        )
        dz, dy = result[:2]
        got = self.back_got
        if i:
            self.du = result[2]
            self.locals.append(jnp.sum(result[3][0], axis=0))
            self.back_got = shared(result[3], self.stages)
        self.weight_grad(i, dz, dy)
        if i == 4:
            self.residual_back(got)
        return result[2:]

    def residual_back(self, got):
        rows = self.tail_rows

        def body(meta, got, n_ref, dt_ref, r_ref, rstat, gain, w_ref, x_ref, dw_out, dxr_out, dr):
            m = pl.program_id(0)
            sums = added(got)[2:4]
            number = n_ref[0, 1:2, :]
            center, spread = rstat[0, 0:1], rstat[0, 1:2]
            scale = gain[5:6] * spread
            valid = self.valid(meta, m, 4)
            for cs in CHUNKS:
                rh = (r_ref[0, :, cs] - center[:, cs]) * spread[:, cs]
                high, low = halves(valid.keep(self.norm_grad(dt_ref[0, :, cs], rh, scale, sums, number, cs)))
                dr[:, cs] = high
                dr[:, C + cs.start : C + cs.stop] = low
            high, low = dr[:, 0:C], dr[:, C : 2 * C]
            dxr_out[0] = three_dots(high, low, w_ref, ((1,), (1,)))
            grad = self.outer(x_ref[0, :, 0:C], x_ref[0, :, C : 2 * C], high, low)

            @pl.when(m == 0)
            def _():
                dw_out[...] = grad

            @pl.when(m > 0)
            def _():
                dw_out[...] += grad

        args = [
            (got, copies(self.last, 4)), (self.number, slots(2)), (self.dt, slots(rows)), (self.r, slots(rows)),
            (self.rstat, slots(2)), (self.gain, whole(6, C)), self.matrix(5), (self.picked, slots(rows, 2 * C)),
        ]
        outs = [self.piece_out(5), (f32(OWN, rows, C), slots(rows))]
        self.pieces[0], self.dxr = call(
            body, self.meta, args, outs, [pltpu.VMEM((rows, 2 * C), BF16)], f"{self.tag}_residual_back",
            12 * OWN * rows * C * C, into=self.pieces[0],
        )

    def piece_out(self, i):
        place = PLACES[i][1]
        return (f32(PIECE_ROWS[PLACES[i][0]], C), pl.BlockSpec((C, C), lambda m, *_: (place, 0)))

    def outer(self, ah, al, bh, bl):
        dims = ((0,), (0,))
        return fast_dot(ah, bh, dims) + (fast_dot(al, bh, dims) + fast_dot(ah, bl, dims))

    def weight_grad(self, i, dz, dy):
        two = self.two
        strided = i == 4 and not two
        rows = self.rows_of(i)
        n_src = len(self.source_args())

        def body(meta, *refs):
            refs = list(refs)
            take = lambda n: [refs.pop(0) for _ in range(n)]
            m = pl.program_id(0)
            dz_ref, dy_ref, dw_ref = take(3)
            if i:
                zp_ref, statp, gain, bias = take(4)
                center, spread = statp[0, 0:1], statp[0, 1:2]
                scale = gain[i - 1 : i] * spread
                shift = bias[i - 1 : i] - center * scale
            else:
                src = take(n_src)
            pw_out, taps_out, pad, yh, yl = take(5)
            alts = take(2) if strided else None
            valid_in = self.valid(meta, m, 0)
            taps = [[] for _ in range(TAPS)]
            for c, cs in enumerate(CHUNKS):
                if i:
                    u = zp_ref[0, :, cs] * scale[:, cs] + shift[:, cs]
                    h = valid_in.keep(u * sigmoid(u))
                else:
                    h = valid_in.keep(self.source(meta, src, cs))
                padded = Padded(pad.at[c], two)
                padded.put(h)
                grad = dy_ref[0, :, cs]
                if strided:
                    grad = spread_out(alts[0].at[c], grad)
                y = None
                for k in range(TAPS):
                    moved = padded.get(k - 2)
                    taps[k].append(column_sum(grad * moved))
                    term = dw_ref[0, k : k + 1, cs] * moved
                    y = term if y is None else y + term
                if strided:
                    y = every_other(alts[1].at[c], y)
                yh[:, cs], yl[:, cs] = halves(y)
            grad = self.outer(yh[...], yl[...], dz_ref[0, :, 0:C], dz_ref[0, :, C : 2 * C])
            taps = [jnp.concatenate(t, axis=1) for t in taps]

            @pl.when(m == 0)
            def _():
                pw_out[...] = grad
                for k in range(TAPS):
                    taps_out[k : k + 1, :] = taps[k]

            @pl.when(m > 0)
            def _():
                pw_out[...] += grad
                for k in range(TAPS):
                    taps_out[k : k + 1, :] += taps[k]

        args = [(dz, slots(rows, 2 * C)), (dy, slots(rows)), (self.dw, layer(i, TAPS, C))] + self.before_args(i)
        if i:
            args += [(self.gain, whole(6, C)), (self.bias, whole(6, C))]
        outs = [self.piece_out(i), (f32(TAPS, C), whole(TAPS, C))]
        scratch = [pad_scratch(), pltpu.VMEM((rows, C), BF16), pltpu.VMEM((rows, C), BF16)]
        if strided:
            scratch += [stride_scratch(), stride_scratch()]
        which = PLACES[i][0]
        self.pieces[which], self.dw_grad[i] = call(
            body, self.meta, args, outs, scratch, f"{self.tag}_weights_{i}", 6 * OWN * rows * C * C, into=self.pieces[which]
        )
        self.done = (self.dw_grad[i],)

    def backward(self, send, waits=None):
        self.pieces, self.dw_grad, self.done = [None, None], [None] * 5, ()
        for i in reversed(range(5)):
            if waits and i in waits:
                self.done += (waits[i],)
            result = self.backward_layer(i)
            if i == 3:
                send(self, 0)
        send(self, 1)
        return result

    def small_grads(self):
        means, p, _ = self.se_state
        flat = lambda x: x.reshape(-1, x.shape[-1])
        means, p, dq, dp = flat(means), flat(p), flat(self.dq), flat(self.dp)
        hidden = p * jax.nn.sigmoid(p)
        dims = ((0,), (0,))
        norms = [n[:2] for n in reversed(self.locals)] + [self.locals[0][2:]]
        down_b = jnp.pad(jnp.sum(dp, axis=0, keepdims=True), ((0, 0), (0, C - SE)))
        rows = self.dw_grad + norms + [exact_dot(hidden, dq, dims), exact_dot(dp, means, dims)]
        rows += [jnp.sum(dq, axis=0, keepdims=True), down_b]
        rows = jnp.concatenate(rows, axis=0)
        return jnp.pad(rows, ((0, SMALL - rows.shape[0]), (0, 0)))


PLACES = {4: (0, 0), 3: (0, 1), 5: (0, 2), 2: (1, 0), 1: (1, 1), 0: (1, 2)}
SMALL = 176
PIECE_ROWS = (3 * C, 3 * C + SMALL)


def swap(x):
    return lax.ppermute(x, "section", [(0, 1), (1, 0)])


def chip_half(piece, first):
    half = piece.shape[0] // 2
    away = lax.dynamic_slice_in_dim(piece, jnp.where(first, half, 0), half)
    kept = lax.dynamic_slice_in_dim(piece, jnp.where(first, 0, half), half)
    return kept + swap(away)


def per_device(features, out_grad, lengths, join_pick, dw, pw, gain, bias, res_w, down, down_b, up, up_b):
    first = lax.axis_index("section") == 0
    size = lax.axis_size("dp")
    inputs = features.reshape(MB, SLOT, C)
    cotangent = out_grad.reshape(MB, SLOT, C)
    own, picks = lengths[0, 0], join_pick[0]

    far_len = swap(own)
    joining = jnp.concatenate([lax.dynamic_index_in_dim(inputs, picks[m], 0, False)[HALF:] for m in range(OWN)], axis=0)
    far_rows = swap(jnp.where(first, inputs[MB - 1], joining))
    far_w0 = swap(pw[0, 0:1])
    taps = jnp.concatenate([dw[0].reshape(5 * TAPS, C), gain[0], bias[0]], axis=0)
    far_taps = swap(taps)
    far_pw, far_res = swap(pw[0]), swap(res_w[0])
    wide = jnp.pad(down_b, ((0, 0), (0, C - SE)))
    squeeze = jnp.concatenate([down[0].T, up[0], up_b, wide], axis=0)
    far_squeeze = swap(squeeze)
    far_cot = lax.ppermute(cotangent[:OWN], "section", [(1, 0)])
    far_cot0 = lax.ppermute(cotangent[MB - 1, :HALF], "section", [(0, 1)])

    flag = first.astype(jnp.int32)[None]
    mine = lambda v: jnp.where(first, v[:OWN], jnp.concatenate([v[OWN:], jnp.zeros((1,), v.dtype)]))
    length = mine(jnp.where(first, own, far_len))
    half_len = (length + 1) // 2
    join_len = mine(jnp.where(first, far_len, own)[picks])
    meta1 = jnp.concatenate([length, half_len, flag])
    meta2 = jnp.concatenate([half_len, join_len, flag, picks[MB - 1 :]])

    def small(block):
        t = jnp.where(first == (block == 0), taps, far_taps)
        q = jnp.where(first == (block == 0), squeeze, far_squeeze)
        return (
            t[: 5 * TAPS].reshape(5, TAPS, C), t[5 * TAPS : 5 * TAPS + 6], t[5 * TAPS + 6 :],
            q[:SE].T, q[2 * SE + 1 :, :SE], q[SE : 2 * SE], q[2 * SE : 2 * SE + 1],
        )

    w0 = prepare(meta1, [pw[0, 0:1]], [far_w0], 0, "prepare_first")
    ready = [prepare(meta1, [pw[0], res_w[0]], [far_pw, far_res], block, f"prepare_{block}") for block in range(2)]

    stages = radices(size, 16)
    c14 = Block(False, meta1, small(0), (w0, ready[0]), stages)
    c14.x, c14.x_far = inputs, far_rows
    c14.forward((ready[1],))
    out0 = c14.tail()
    c15 = Block(True, meta2, small(1), (ready[1], ready[1]), stages)
    c15.arrived, c15.joined_far, c15.joined = out0, far_rows, features.reshape(MB, 2, HALF, C)
    c15.forward()
    out1 = c15.tail(cotangent, far_cot)

    sums, totals = {}, []

    def send(block, no):
        piece = block.pieces[no]
        if no:
            piece = lax.dynamic_update_slice_in_dim(piece, block.small_grads(), 3 * C, 0)
        half = chip_half(piece, first)
        if totals:
            half, _ = lax.optimization_barrier((half, totals[-1]))
        total = lax.psum(half, "dp")
        totals.append(total)
        sums[block.tag, no] = total

    back, dx1 = c15.backward(send)
    c14.tail_backward(cotangent, far_cot0, back)
    dx0, = c14.backward(send, {3: totals[0], 0: totals[1]})

    full = []
    for no in range(2):
        a, b = sums["c14", no], sums["c15", no]
        came = swap(jnp.where(first, b, a))
        full.append(jnp.where(first, jnp.concatenate([a, came], axis=0), jnp.concatenate([came, b], axis=0)))
    matrix = lambda i: full[PLACES[i][0]][PLACES[i][1] * C : (PLACES[i][1] + 1) * C]
    pw_grad = jnp.stack([matrix(i) for i in range(5)])[None]
    rows = full[1][3 * C :]
    dw_grad = rows[: 5 * TAPS].reshape(1, 5, TAPS, C)
    norms = rows[5 * TAPS : 5 * TAPS + 12].reshape(6, 2, C)
    rest = rows[5 * TAPS + 12 :]
    up_grad, down_grad = rest[:SE], rest[SE : 2 * SE].T
    up_b_grad, down_b_grad = rest[2 * SE : 2 * SE + 1], rest[2 * SE + 1 : 2 * SE + 2, :SE]

    to_upper = lambda x: lax.ppermute(x, "section", [(0, 1)])
    to_lower = lambda x: lax.ppermute(x, "section", [(1, 0)])
    pad = jnp.zeros((1, HALF, C), F32)
    lower = jnp.concatenate([out0, jnp.concatenate([to_lower(out0[0:1, :HALF]), pad], axis=1)], axis=0)
    upper = jnp.concatenate([to_upper(out1), out1[0:1]], axis=0)
    block_out = jnp.where(first, lower, upper)
    lower = jnp.concatenate([dx0, to_lower(dx0[0:1])], axis=0)
    joins = jnp.concatenate([to_upper(dx1), dx1[0:1]], axis=0)
    joins = jnp.stack([lax.dynamic_index_in_dim(joins, jnp.argmax(picks == s), 0, False) for s in range(MB)])
    upper = jnp.concatenate([jnp.zeros_like(joins), joins], axis=1)
    dx = jnp.where(first, lower, upper)
    return (
        block_out.reshape(features.shape), dx.reshape(features.shape), dw_grad, pw_grad,
        norms[None, :, 1], norms[None, :, 0], matrix(5)[None], down_grad[None], down_b_grad, up_grad[None], up_b_grad,
    )


def solution(mesh):
    rows = P("section", "dp", None)
    own = lambda dims: P("section", *([None] * dims))
    weights = (own(3), own(3), own(2), own(2), own(2), own(2), own(1), own(2), own(1))
    in_specs = (rows, rows, rows, P("dp", None), *weights)
    out_specs = (rows, rows, *weights)
    return jax.shard_map(per_device, mesh=mesh, in_specs=in_specs, out_specs=out_specs, check_vma=False)
```

```python
import copy

import jax
import jax.numpy as jnp
from jax import lax
from jax.experimental import pallas as pl
from jax.experimental.pallas import tpu as pltpu
from jax.sharding import PartitionSpec as P

EPSILON = 1e-05
EXACT = lax.Precision.HIGHEST
TAPS = 5
MB = 3
OWN = 2
SLOT = 400
HALF = 200
KEPT = 208
C = 512
LANES = 128
CHUNKS = [slice(c, c + LANES) for c in range(0, C, LANES)]
SE = 64
BF16, F32 = jnp.bfloat16, jnp.float32
VMEM_BYTES = 24 << 20


def radices(size, most):
    stages, left = [], size
    while left > 1:
        radix = min(most, left)
        while left % radix:
            radix -= 1
        stages.append(radix)
        left //= radix
    return stages


def exchange(block, radix, stride):
    size = lax.axis_size("dp")
    if radix == size:
        return lax.all_to_all(block, "dp", 0, 0)
    groups = []
    for base in range(size):
        if (base // stride) % radix == 0:
            groups.append([base + j * stride for j in range(radix)])
    return lax.all_to_all(block, "dp", 0, 0, axis_index_groups=groups)


def shared(block, stages):
    stride = 1
    for no, radix in enumerate(stages):
        if no:
            block = jnp.broadcast_to(jnp.sum(block, axis=0), (radix,) + block.shape[1:])
        block = exchange(block, radix, stride)
        stride *= radix
    return block


def halves(x):
    high = x.astype(BF16)
    return high, (x - high.astype(F32)).astype(BF16)


def sigmoid(x):
    return 0.5 * jnp.tanh(0.5 * x) + 0.5


def exact_dot(a, b, dims=((1,), (0,))):
    return lax.dot_general(a, b, (dims, ((), ())), precision=EXACT, preferred_element_type=F32)


def fast_dot(a, b, dims=((1,), (0,))):
    return lax.dot_general(a, b, (dims, ((), ())), preferred_element_type=F32)


def stacked_dot(high, low, w_ref, back=False):
    w_high, w_low = w_ref[0, 0], w_ref[0, 1]
    w = jnp.concatenate([w_high, w_high, w_low], axis=1 if back else 0)
    x = jnp.concatenate([high, low, high], axis=1)
    return fast_dot(x, w, ((1,), (1 if back else 0,)))


def stacked_outer(a_high, a_low, b_high, b_low):
    a = jnp.concatenate([a_high, a_low, a_high], axis=0)
    b = jnp.concatenate([b_high, b_high, b_low], axis=0)
    return fast_dot(a, b, ((0,), (0,)))


def column_sum(x):
    return jnp.sum(x, axis=0, keepdims=True)


class Rows:
    def __init__(self, meta, m, two, rows, which=0):
        place = lax.broadcasted_iota(jnp.int32, (rows, LANES), 0)
        if two:
            later = place >= HALF
            limit = jnp.where(later, HALF + meta[OWN + m], meta[m])
            self.mask = place < limit
        else:
            self.mask = place < meta[which * OWN + m]

    def keep(self, x):
        return jnp.where(self.mask, x, 0.0)


class Padded:
    def __init__(self, ref, two):
        self.ref = ref
        self.pieces = [(8, 0, HALF), (16 + HALF, HALF, HALF)] if two else [(8, 0, SLOT)]

    def put(self, x):
        zeros = jnp.zeros((8, LANES), F32)
        for at, start, rows in self.pieces:
            self.ref[at - 8 : at, :] = zeros
            self.ref[at : at + rows, :] = x[start : start + rows]
        self.ref[at + rows : at + rows + 8, :] = zeros

    def get(self, offset):
        parts = [self.ref[at + offset : at + offset + rows, :] for at, _, rows in self.pieces]
        return parts[0] if len(parts) == 1 else jnp.concatenate(parts, axis=0)

    def conv(self, kernel):
        total = kernel[0:1] * self.get(-2)
        for k in range(1, TAPS):
            total = total + kernel[k : k + 1] * self.get(k - 2)
        return total

    def conv_back(self, kernel):
        total = kernel[0:1] * self.get(2)
        for k in range(1, TAPS):
            total = total + kernel[k : k + 1] * self.get(2 - k)
        return total


def every_other(ref, x):
    ref[0:SLOT, :] = x
    ref[SLOT : 2 * KEPT, :] = jnp.zeros((2 * KEPT - SLOT, LANES), F32)
    return ref[pl.ds(0, KEPT, stride=2), :]


def spread_out(ref, x):
    ref[...] = jnp.zeros_like(ref)
    ref[pl.ds(0, KEPT, stride=2), :] = x
    return ref[0:SLOT, :]


def center_spread(sums, rows):
    center = sums[0:1] / rows
    return center, lax.rsqrt(sums[1:2] / rows - center * center + EPSILON)


def added(ref):
    return jnp.sum(ref[:, 0], axis=0)


def send(ref, rows):
    for copy in range(ref.shape[0]):
        for row, x in enumerate(rows):
            ref[copy, 0, row : row + 1, 0 : x.shape[1]] = x


def pad_scratch():
    return pltpu.VMEM((len(CHUNKS), SLOT + 24, LANES), F32)


def stride_scratch():
    return pltpu.VMEM((len(CHUNKS), 2 * KEPT, LANES), F32)


def slots(rows, cols=C):
    return pl.BlockSpec((1, rows, cols), lambda m, *_: (m, 0, 0))


def copies(count, rows, cols=C):
    return pl.BlockSpec((count, 1, rows, cols), lambda m, *_: (0, m, 0, 0))


def whole(*shape):
    return pl.BlockSpec(shape, lambda m, *_: (0,) * len(shape))


def layer(i, *shape):
    return pl.BlockSpec((1,) + shape, lambda m, *_: (i,) + (0,) * len(shape))


def f32(*shape):
    return jax.ShapeDtypeStruct(shape, F32)


def bf16(*shape):
    return jax.ShapeDtypeStruct(shape, BF16)


def call(body, meta, args, outs, scratch=(), name=None, flops=0, steps=OWN, after=(), into=None):
    arrays, in_specs = [a for a, _ in args], [s for _, s in args]
    shapes, out_specs = [a for a, _ in outs], [s for _, s in outs]
    size = sum(a.size * a.dtype.itemsize for a in arrays + shapes)
    extra = list(after) + ([] if into is None else [into])
    count = len(arrays)

    def inner(meta, *refs):
        body(meta, *refs[:count], *refs[count + len(extra) :])

    return pl.pallas_call(
        inner,
        out_shape=shapes,
        grid_spec=pltpu.PrefetchScalarGridSpec(
            num_scalar_prefetch=1,
            grid=(steps,),
            in_specs=in_specs + [pl.BlockSpec(memory_space=pl.ANY)] * len(extra),
            out_specs=out_specs,
            scratch_shapes=list(scratch),
        ),
        input_output_aliases={} if into is None else {count + len(extra): 0},
        compiler_params=pltpu.CompilerParams(vmem_limit_bytes=VMEM_BYTES),
        cost_estimate=pl.CostEstimate(flops=flops, bytes_accessed=size, transcendentals=0),
        name=name,
    )(meta, *arrays, *extra)


def choose(meta, block, own, far):
    return jnp.where(meta[2 * OWN] == 1 - block, own, far)


def prepare(meta, own, far, block, start, stop):
    def body(meta, *refs):
        pair = [ref[0] for ref in refs[:2]]
        if stop == 6:
            last = pl.program_id(0) == 5 - start
            pair = [jnp.where(last, ref[...], w) for ref, w in zip(refs[2:4], pair)]
        out = refs[-1]
        out[0, 0], out[0, 1] = halves(choose(meta, block, *pair))

    matrix = pl.BlockSpec((1, C, C), lambda j, *_: (jnp.minimum(j + start, 4), 0, 0))
    args = [(own[0], matrix), (far[0], matrix)]
    if stop == 6:
        args += [(own[1], whole(C, C)), (far[1], whole(C, C))]
    out = pl.BlockSpec((1, 2, C, C), lambda j, *_: (j, 0, 0, 0))
    name = f"prepare_{block}_{start}"
    return call(body, meta, args, [(bf16(stop - start, 2, C, C), out)], name=name, steps=stop - start)[0]


class Block:
    def __init__(self, two, meta, weights, ready, stages):
        self.two, self.meta, self.stages = two, meta, stages
        self.dw, self.gain, self.bias, self.down, self.down_b, self.up, self.up_b = weights
        self.ready = ready
        self.tail_rows = SLOT if two else KEPT
        self.first, self.last = stages[0], stages[-1]
        self.tag = "c15" if two else "c14"

    def rows_of(self, i):
        return self.tail_rows if i == 4 else SLOT

    def valid(self, meta, m, i):
        last = i == 4 and not self.two
        return Rows(meta, m, self.two, self.rows_of(i), which=1 if last else 0)

    def matrix(self, i):
        array, at = self.ready[i]
        return (array, layer(at, 2, C, C))

    def source_args(self):
        if not self.two:
            return [(self.x, slots(SLOT)), (self.x_far, whole(SLOT, C))]
        far = pl.BlockSpec((HALF, C), lambda m, *_: (m, 0))
        near = pl.BlockSpec((1, 1, HALF, C), lambda m, meta: (meta[2 * OWN + 1], 1, 0, 0))
        return [(self.arrived, slots(HALF)), (self.joined_far, far), (self.joined, near)]

    def source(self, meta, refs, cs):
        lower = meta[2 * OWN] == 1
        if not self.two:
            return jnp.where(lower, refs[0][0, :, cs], refs[1][:, cs])
        joined = jnp.where(lower, refs[1][:, cs], refs[2][0, 0, :, cs])
        return jnp.concatenate([refs[0][0, :, cs], joined], axis=0)

    def before_args(self, i):
        if i == 0:
            return self.source_args()
        return [(self.z[i - 1], slots(SLOT)), (self.stats[i - 1], slots(2))]


    def forward_layer(self, i, after=()):
        two, count = self.two, self.first
        strided = i == 4 and not two
        rows = self.rows_of(i)
        n_src = len(self.source_args())
        width = C + LANES if i == 0 else C
        sent = 4 if i == 3 else 2
        makes = i == 0 and not two

        def body(meta, *refs):
            refs = list(refs)
            take = lambda n: [refs.pop(0) for _ in range(n)]
            m = pl.program_id(0)
            if i == 0:
                src = take(n_src)
            else:
                z_ref, got_ref = take(2)
                n_ref, = take(1) if i > 1 else (None,)
                gain_ref, bias_ref = take(2)
                res_sum, = take(1) if i == 3 else (None,)
            dw_ref, = take(1)
            if makes:
                own_ref, far_ref, z_out, pay, w_ref = take(5)

                @pl.when(m == 0)
                def _():
                    w_ref[0, 0], w_ref[0, 1] = halves(choose(meta, 0, own_ref[0], far_ref[0]))

            else:
                w_ref, z_out, pay = take(3)
            if i:
                stat_out, = take(1)
            if i == 1:
                n_out, = take(1)
            pad, y_ref = take(2)
            alt, = take(1) if strided else (None,)
            valid_in = self.valid(meta, m, 0)
            if i:
                sums = added(got_ref)
                if i == 1:
                    count_in = jnp.maximum(jnp.concatenate([sums[0:1, C:]] * len(CHUNKS), axis=1), 1.0)
                    count_out = jnp.maximum(jnp.concatenate([sums[1:2, C:]] * len(CHUNKS), axis=1), 1.0)
                    n_out[0, 0:1, :] = count_in
                    n_out[0, 1:2, :] = count_out
                else:
                    count_in = n_ref[0, 0:1, :]
                center, spread = center_spread(sums[:, :C], count_in)
                stat_out[0, 0:1, :] = center
                stat_out[0, 1:2, :] = spread
                scale = gain_ref[i - 1 : i] * spread
                shift = bias_ref[i - 1 : i] - center * scale
            for c, cs in enumerate(CHUNKS):
                if i == 0:
                    h = valid_in.keep(self.source(meta, src, cs))
                else:
                    u = z_ref[0, :, cs] * scale[:, cs] + shift[:, cs]
                    h = valid_in.keep(u * sigmoid(u))
                padded = Padded(pad.at[c], two)
                padded.put(h)
                y = padded.conv(dw_ref[0, :, cs])
                if strided:
                    y = every_other(alt.at[c], y)
                high, low = halves(y)
                y_ref[:, cs] = high
                y_ref[:, C + cs.start : C + cs.stop] = low
            z = stacked_dot(y_ref[:, 0:C], y_ref[:, C : 2 * C], w_ref)
            z_out[0] = z
            valid = self.valid(meta, m, i)
            one, square = [], []
            for cs in CHUNKS:
                kept = valid.keep(z[:, cs])
                one.append(column_sum(kept))
                square.append(column_sum(kept * kept))
            if i == 0:
                if two:
                    number = (meta[m] + meta[OWN + m]).astype(F32)
                    numbers = number, number
                else:
                    numbers = meta[m].astype(F32), meta[OWN + m].astype(F32)
                one.append(jnp.full((1, LANES), numbers[0], F32))
                square.append(jnp.full((1, LANES), numbers[1], F32))
            out = [jnp.concatenate(one, axis=1), jnp.concatenate(square, axis=1)]
            if i == 3:
                out += [res_sum[0, 0:1, :], res_sum[0, 1:2, :]]
            send(pay, out)

        if i == 0:
            args = list(self.source_args())
        else:
            got = 4 if i == 4 else 2
            args = [(self.z[i - 1], slots(SLOT)), (self.got[i - 1], copies(self.last, got, C + LANES if i == 1 else C))]
            if i > 1:
                args.append((self.number, slots(2)))
            args += [(self.gain, whole(6, C)), (self.bias, whole(6, C))]
            if i == 3:
                args.append((self.res_sum, slots(2)))
        args.append((self.dw, layer(i, TAPS, C)))
        args += [(w, layer(0, C, C)) for w in self.first_matrix] if makes else [self.matrix(i)]
        outs = [(f32(OWN, rows, C), slots(rows)), (f32(count, OWN, sent, width), copies(count, sent, width))]
        if i:
            outs.append((f32(OWN, 2, C), slots(2)))
        if i == 1:
            outs.append((f32(OWN, 2, C), slots(2)))
        if makes:
            outs.append((bf16(1, 2, C, C), layer(0, 2, C, C)))
        scratch = [pad_scratch(), pltpu.VMEM((rows, 2 * C), BF16)]
        if strided:
            scratch.append(stride_scratch())
        result = call(body, self.meta, args, outs, scratch, f"{self.tag}_forward_{i}", 6 * OWN * rows * C * C, after=after)
        self.z.append(result[0])
        if makes:
            self.ready[0] = (result[2], 0)
        if i:
            self.stats.append(result[2])
        if i == 1:
            self.number = result[3]
        self.got.append(shared(result[1], self.stages))

    def residual(self):
        two, rows = self.two, self.tail_rows

        def body(meta, *refs):
            refs = list(refs)
            src = [refs.pop(0) for _ in self.source_args()]
            w_ref, r_out, x_out, sum_out = refs[:4]
            alt = refs[4] if not two else None
            m = pl.program_id(0)
            valid_in = self.valid(meta, m, 0)
            for c, cs in enumerate(CHUNKS):
                x = valid_in.keep(self.source(meta, src, cs))
                if not two:
                    x = every_other(alt.at[c], x)
                high, low = halves(x)
                x_out[0, :, cs] = high
                x_out[0, :, C + cs.start : C + cs.stop] = low
            r = stacked_dot(x_out[0, :, 0:C], x_out[0, :, C : 2 * C], w_ref)
            r_out[0] = r
            valid = self.valid(meta, m, 4)
            for cs in CHUNKS:
                kept = valid.keep(r[:, cs])
                sum_out[0, 0:1, cs] = column_sum(kept)
                sum_out[0, 1:2, cs] = column_sum(kept * kept)

        args = self.source_args() + [self.matrix(5)]
        outs = [
            (f32(OWN, rows, C), slots(rows)),
            (bf16(OWN, rows, 2 * C), slots(rows, 2 * C)),
            (f32(OWN, 2, C), slots(2)),
        ]
        scratch = [] if two else [stride_scratch()]
        self.r, self.picked, self.res_sum = call(
            body, self.meta, args, outs, scratch, f"{self.tag}_residual", 6 * OWN * rows * C * C
        )

    def forward(self, after=None):
        self.z, self.got, self.stats = [], [], []
        for i in range(5):
            if i == 2:
                self.residual()
            self.forward_layer(i, (after or {}).get(i, ()))


    def segments(self):
        return [(0, HALF), (HALF, HALF)] if self.two else [(0, self.tail_rows)]

    def lengths(self, meta, m):
        if self.two:
            return [meta[m], meta[OWN + m]]
        return [meta[OWN + m]]

    def squeeze(self, sums, counts, se_refs):
        down_t, down_b, up, up_b = se_refs
        means = [s / jnp.maximum(jnp.full((1, C), n.astype(F32)), 1.0) for s, n in zip(sums, counts)]
        ps = [jnp.sum(down_t[...] * mean, axis=1, keepdims=True) + down_b[...] for mean in means]
        gates = [sigmoid(column_sum(up[...] * (p * sigmoid(p))) + up_b[...]) for p in ps]
        return means, ps, gates

    def squeeze_back(self, des, ps, gates, counts, se_refs):
        down_t, down_b, up, up_b = se_refs
        dqs, dps, shares = [], [], []
        for de, p, gate, n in zip(des, ps, gates, counts):
            dq = de * gate * (1.0 - gate)
            s = sigmoid(p)
            dp = jnp.sum(up[...] * dq, axis=1, keepdims=True) * (s * (1.0 + p * (1.0 - s)))
            dm = column_sum(down_t[...] * dp)
            dqs.append(dq)
            dps.append(dp)
            shares.append(dm / jnp.maximum(jnp.full((1, C), n.astype(F32)), 1.0))
        return dqs, dps, shares

    def se_args(self):
        return [(self.down, whole(SE, C)), (self.down_b, whole(SE, 1)), (self.up, whole(SE, C)), (self.up_b, whole(1, C))]

    def store_rows(self, ref, rows):
        ref[0] = jnp.concatenate(rows + [jnp.zeros((8 - len(rows), C), F32)], axis=0)

    def store_columns(self, ref, columns):
        ref[0] = jnp.zeros((SE, 8), F32)
        for j, column in enumerate(columns):
            ref[0, :, j : j + 1] = column

    def by_segment(self, rows, cs):
        parts = [jnp.broadcast_to(row[:, cs], (n, LANES)) for row, (_, n) in zip(rows, self.segments())]
        return parts[0] if len(parts) == 1 else jnp.concatenate(parts, axis=0)

    def seg_sums(self, x):
        return [column_sum(x[at : at + n]) for at, n in self.segments()]

    def tail(self, cotangent=None, far=None, after=()):
        two, rows = self.two, self.tail_rows
        back = cotangent is not None

        def body(meta, *refs):
            refs = list(refs)
            take = lambda n: [refs.pop(0) for _ in range(n)]
            m = pl.program_id(0)
            z_ref, got4, r_ref, got3, n_ref, gain, bias = take(7)
            se_refs = take(4)
            if back:
                cot_ref, far_ref = take(2)
            out, stat_out, rstat_out, means_out, p_out, gate_out = take(6)
            if back:
                du_out, dt_out, pay, dq_out, dp_out = take(5)
            h_ref, = take(1)
            if back:
                slope_ref, = take(1)
            valid = self.valid(meta, m, 4)
            number = n_ref[0, 1:2, :]
            center, spread = center_spread(added(got4), number)
            rcenter, rspread = center_spread(added(got3)[2:4], number)
            stat_out[0, 0:1, :] = center
            stat_out[0, 1:2, :] = spread
            rstat_out[0, 0:1, :] = rcenter
            rstat_out[0, 1:2, :] = rspread
            scale = gain[4:5] * spread
            shift = bias[4:5] - center * scale
            sums = []
            for cs in CHUNKS:
                u = z_ref[0, :, cs] * scale[:, cs] + shift[:, cs]
                s = sigmoid(u)
                h = valid.keep(u * s)
                h_ref[:, cs] = h
                if back:
                    slope_ref[:, cs] = valid.keep(s * (1.0 + u * (1.0 - s)))
                sums.append(self.seg_sums(h))
            sums = [jnp.concatenate([s[j] for s in sums], axis=1) for j in range(len(self.segments()))]
            counts = self.lengths(meta, m)
            means, ps, gates = self.squeeze(sums, counts, se_refs)
            self.store_rows(means_out, means)
            self.store_columns(p_out, ps)
            self.store_rows(gate_out, gates)
            res_gain, res_bias, gate_grad = [], [], []
            for cs in CHUNKS:
                h = h_ref[:, cs]
                rh = (r_ref[0, :, cs] - rcenter[:, cs]) * rspread[:, cs]
                t = h * self.by_segment(gates, cs) + gain[5:6, cs] * rh + bias[5:6, cs]
                s = sigmoid(t)
                out[0, 0:rows, cs] = valid.keep(t * s)
                if rows < SLOT:
                    out[0, rows:SLOT, cs] = jnp.zeros((SLOT - rows, LANES), F32)
                if back:
                    cot = jnp.where(meta[2 * OWN] == 1, far_ref[0, :, cs], cot_ref[0, :, cs])
                    dt = valid.keep(cot * (s * (1.0 + t * (1.0 - s))))
                    dt_out[0, :, cs] = dt
                    res_bias.append(column_sum(dt))
                    res_gain.append(column_sum(dt * rh))
                    gate_grad.append(self.seg_sums(dt * h))
            if not back:
                return
            des = [jnp.concatenate([g[j] for g in gate_grad], axis=1) for j in range(len(counts))]
            dqs, dps, shares = self.squeeze_back(des, ps, gates, counts, se_refs)
            self.store_rows(dq_out, dqs)
            self.store_columns(dp_out, dps)
            bias_sum, gain_sum = [], []
            for cs in CHUNKS:
                dh = dt_out[0, :, cs] * self.by_segment(gates, cs) + self.by_segment(shares, cs)
                du = dh * slope_ref[:, cs]
                du_out[0, :, cs] = du
                bias_sum.append(column_sum(du))
                gain_sum.append(column_sum(du * ((z_ref[0, :, cs] - center[:, cs]) * spread[:, cs])))
            send(pay, [jnp.concatenate(x, axis=1) for x in (bias_sum, gain_sum, res_bias, res_gain)])

        args = [
            (self.z[4], slots(rows)), (self.got[4], copies(self.last, 2)), (self.r, slots(rows)),
            (self.got[3], copies(self.last, 4)), (self.number, slots(2)),
            (self.gain, whole(6, C)), (self.bias, whole(6, C)),
        ] + self.se_args()
        outs = [
            (f32(OWN, SLOT, C), slots(SLOT)), (f32(OWN, 2, C), slots(2)), (f32(OWN, 2, C), slots(2)),
            (f32(OWN, 8, C), slots(8)), (f32(OWN, SE, 8), slots(SE, 8)), (f32(OWN, 8, C), slots(8)),
        ]
        scratch = [pltpu.VMEM((rows, C), F32)]
        if back:
            last = pl.BlockSpec((1, SLOT, C), lambda m, *_: (MB - 1, 0, 0))
            args += [(cotangent, last), (far, slots(SLOT))]
            outs += self.tail_outs()
            scratch.append(pltpu.VMEM((rows, C), F32))
        result = call(body, self.meta, args, outs, scratch, f"{self.tag}_tail", after=after)
        self.stats.append(result[1])
        self.rstat, self.se_state = result[2], result[3:6]
        if back:
            self.tail_results(result[6:])
        return result[0]

    def tail_outs(self):
        rows, count = self.tail_rows, self.first
        return [
            (f32(OWN, rows, C), slots(rows)), (f32(OWN, rows, C), slots(rows)),
            (f32(count, OWN, 4, C), copies(count, 4)), (f32(OWN, 8, C), slots(8)), (f32(OWN, SE, 8), slots(SE, 8)),
        ]

    def tail_results(self, result):
        self.du, self.dt, pay, self.dq, self.dp = result
        self.locals = [jnp.sum(pay[0], axis=0)]
        self.back_got = shared(pay, self.stages)

    def tail_backward(self, cotangent, far, back):
        rows = self.tail_rows

        def body(meta, z_ref, r_ref, stat, rstat, gain, bias, p_ref, gate_ref, down, down_b, up, up_b, cot_ref, far_ref, back_ref,
                 du_out, dt_out, pay, dq_out, dp_out, slope_ref):
            m = pl.program_id(0)
            valid = self.valid(meta, m, 4)
            center, spread, rcenter, rspread = stat[0, 0:1], stat[0, 1:2], rstat[0, 0:1], rstat[0, 1:2]
            scale = gain[4:5] * spread
            shift = bias[4:5] - center * scale
            zeros = jnp.zeros((rows - HALF, LANES), F32)
            counts = self.lengths(meta, m)
            ps = [p_ref[0, :, j : j + 1] for j in range(len(counts))]
            gates = [gate_ref[0, j : j + 1, :] for j in range(len(counts))]
            res_gain, res_bias, gate_grad = [], [], []
            for cs in CHUNKS:
                u = z_ref[0, :, cs] * scale[:, cs] + shift[:, cs]
                s = sigmoid(u)
                h = valid.keep(u * s)
                slope_ref[:, cs] = valid.keep(s * (1.0 + u * (1.0 - s)))
                rh = (r_ref[0, :, cs] - rcenter[:, cs]) * rspread[:, cs]
                t = h * self.by_segment(gates, cs) + gain[5:6, cs] * rh + bias[5:6, cs]
                s = sigmoid(t)
                here = jnp.where(meta[2 * OWN] == 1, cot_ref[0, 0:HALF, cs], far_ref[:, cs])
                cot = jnp.concatenate([here + back_ref[0, :, cs], zeros], axis=0)
                dt = valid.keep(cot * (s * (1.0 + t * (1.0 - s))))
                dt_out[0, :, cs] = dt
                res_bias.append(column_sum(dt))
                res_gain.append(column_sum(dt * rh))
                gate_grad.append(self.seg_sums(dt * h))
            des = [jnp.concatenate([g[j] for g in gate_grad], axis=1) for j in range(len(counts))]
            dqs, dps, shares = self.squeeze_back(des, ps, gates, counts, (down, down_b, up, up_b))
            self.store_rows(dq_out, dqs)
            self.store_columns(dp_out, dps)
            bias_sum, gain_sum = [], []
            for cs in CHUNKS:
                dh = dt_out[0, :, cs] * self.by_segment(gates, cs) + self.by_segment(shares, cs)
                du = dh * slope_ref[:, cs]
                du_out[0, :, cs] = du
                bias_sum.append(column_sum(du))
                gain_sum.append(column_sum(du * ((z_ref[0, :, cs] - center[:, cs]) * spread[:, cs])))
            send(pay, [jnp.concatenate(x, axis=1) for x in (bias_sum, gain_sum, res_bias, res_gain)])

        args = [
            (self.z[4], slots(rows)), (self.r, slots(rows)), (self.stats[4], slots(2)), (self.rstat, slots(2)),
            (self.gain, whole(6, C)), (self.bias, whole(6, C)),
            (self.se_state[1], slots(SE, 8)), (self.se_state[2], slots(8)),
        ] + self.se_args() + [(cotangent, slots(SLOT)), (far, whole(HALF, C)), (back, slots(HALF))]
        scratch = [pltpu.VMEM((rows, C), F32)]
        self.tail_results(call(body, self.meta, args, self.tail_outs(), scratch, f"{self.tag}_tail_back"))


    def norm_grad(self, du, zh, scale, sums, number, cs):
        return scale[:, cs] * (du - sums[0:1, cs] / number[:, cs] - zh * (sums[1:2, cs] / number[:, cs]))

    def backward_layer(self, i):
        two, count = self.two, self.first
        strided = i == 4 and not two
        rows = self.rows_of(i)

        def body(meta, *refs):
            refs = list(refs)
            take = lambda n: [refs.pop(0) for _ in range(n)]
            m = pl.program_id(0)
            got, n_ref, du_ref, z_ref, stat, gain, bias, dw_ref, w_ref = take(9)
            if i:
                zp_ref, statp = take(2)
            else:
                dxr_ref, = take(1)
            dz_out, dy_out = take(2)
            if i:
                du_out, pay = take(2)
            elif two:
                back_out, dx_out = take(2)
            else:
                dx_out, = take(1)
            pad, = take(1)
            alt, = take(1) if refs else (None,)
            sums = added(got)
            last = i == 4
            number = n_ref[0, 1:2, :] if last else n_ref[0, 0:1, :]
            center, spread = stat[0, 0:1], stat[0, 1:2]
            scale = gain[i : i + 1] * spread
            valid = self.valid(meta, m, i)
            for cs in CHUNKS:
                zh = (z_ref[0, :, cs] - center[:, cs]) * spread[:, cs]
                dz = valid.keep(self.norm_grad(du_ref[0, :, cs], zh, scale, sums, number, cs))
                high, low = halves(dz)
                dz_out[0, :, cs] = high
                dz_out[0, :, C + cs.start : C + cs.stop] = low
            dy = stacked_dot(dz_out[0, :, 0:C], dz_out[0, :, C : 2 * C], w_ref, True)
            dy_out[0] = dy
            valid_in = self.valid(meta, m, 0)
            if i:
                pcenter, pspread = statp[0, 0:1], statp[0, 1:2]
                pscale = gain[i - 1 : i] * pspread
                pshift = bias[i - 1 : i] - pcenter * pscale
            bias_sum, gain_sum = [], []
            for c, cs in enumerate(CHUNKS):
                grad = dy[:, cs]
                if strided:
                    grad = spread_out(alt.at[c], grad)
                padded = Padded(pad.at[c], two)
                padded.put(grad)
                dh = padded.conv_back(dw_ref[0, :, cs])
                if i:
                    z = zp_ref[0, :, cs]
                    u = z * pscale[:, cs] + pshift[:, cs]
                    s = sigmoid(u)
                    du = valid_in.keep(dh * (s * (1.0 + u * (1.0 - s))))
                    du_out[0, :, cs] = du
                    bias_sum.append(column_sum(du))
                    gain_sum.append(column_sum(du * ((z - pcenter[:, cs]) * pspread[:, cs])))
                    continue
                dxr = dxr_ref[0, :, cs]
                if not two:
                    dxr = spread_out(alt.at[c], dxr)
                dx = valid_in.keep(dh) + dxr
                if two:
                    back_out[0, :, cs] = dx[:HALF]
                    dx_out[0, :, cs] = dx[HALF:]
                else:
                    dx_out[0, :, cs] = dx
            if i:
                send(pay, [jnp.concatenate(bias_sum, axis=1), jnp.concatenate(gain_sum, axis=1)])

        sent = 4 if i == 4 else 2
        args = [
            (self.back_got, copies(self.last, sent)), (self.number, slots(2)), (self.du, slots(rows)),
            (self.z[i], slots(rows)), (self.stats[i], slots(2)), (self.gain, whole(6, C)), (self.bias, whole(6, C)),
            (self.dw, layer(i, TAPS, C)), self.matrix(i),
        ]
        if i:
            args += self.before_args(i)
        else:
            args.append((self.dxr, slots(self.tail_rows)))
        outs = [
            (bf16(OWN, rows, 2 * C), slots(rows, 2 * C)), (f32(OWN, rows, C), slots(rows)),
        ]
        if i:
            outs += [(f32(OWN, SLOT, C), slots(SLOT)), (f32(count, OWN, 2, C), copies(count, 2))]
        elif two:
            outs += [(f32(OWN, HALF, C), slots(HALF)), (f32(OWN, HALF, C), slots(HALF))]
        else:
            outs += [(f32(OWN, SLOT, C), slots(SLOT))]
        scratch = [pad_scratch()]
        if strided or (i == 0 and not two):
            scratch.append(stride_scratch())
        result = call(
            body, self.meta, args, outs, scratch, f"{self.tag}_backward_{i}", 6 * OWN * rows * C * C, after=self.done
        )
        dz, dy = result[:2]
        got = self.back_got
        if i:
            self.du = result[2]
            self.locals.append(jnp.sum(result[3][0], axis=0))
            self.back_got = shared(result[3], self.stages)
        self.weight_grad(i, dz, dy)
        if i == 4:
            self.residual_back(got)
        return result[2:]

    def residual_back(self, got):
        rows = self.tail_rows

        def body(meta, got, n_ref, dt_ref, r_ref, rstat, gain, w_ref, x_ref, dw_out, dxr_out, dr):
            m = pl.program_id(0)
            sums = added(got)[2:4]
            number = n_ref[0, 1:2, :]
            center, spread = rstat[0, 0:1], rstat[0, 1:2]
            scale = gain[5:6] * spread
            valid = self.valid(meta, m, 4)
            for cs in CHUNKS:
                rh = (r_ref[0, :, cs] - center[:, cs]) * spread[:, cs]
                high, low = halves(valid.keep(self.norm_grad(dt_ref[0, :, cs], rh, scale, sums, number, cs)))
                dr[:, cs] = high
                dr[:, C + cs.start : C + cs.stop] = low
            high, low = dr[:, 0:C], dr[:, C : 2 * C]
            dxr_out[0] = stacked_dot(high, low, w_ref, True)
            grad = stacked_outer(x_ref[0, :, 0:C], x_ref[0, :, C : 2 * C], high, low)

            @pl.when(m == 0)
            def _():
                dw_out[...] = grad

            @pl.when(m > 0)
            def _():
                dw_out[...] += grad

        args = [
            (got, copies(self.last, 4)), (self.number, slots(2)), (self.dt, slots(rows)), (self.r, slots(rows)),
            (self.rstat, slots(2)), (self.gain, whole(6, C)), self.matrix(5), (self.picked, slots(rows, 2 * C)),
        ]
        outs = [self.piece_out(5), (f32(OWN, rows, C), slots(rows))]
        which = PLACES[self.tag][5][0]
        self.pieces[which], self.dxr = call(
            body, self.meta, args, outs, [pltpu.VMEM((rows, 2 * C), BF16)], f"{self.tag}_residual_back",
            12 * OWN * rows * C * C, into=self.pieces[which],
        )

    def piece_out(self, i):
        which, place = PLACES[self.tag][i]
        rows = PIECE_ROWS[self.tag][which]
        return (f32(rows, C), pl.BlockSpec((C, C), lambda m, *_: (place, 0)))

    def weight_grad(self, i, dz, dy):
        two = self.two
        strided = i == 4 and not two
        rows = self.rows_of(i)
        n_src = len(self.source_args())

        def body(meta, *refs):
            refs = list(refs)
            take = lambda n: [refs.pop(0) for _ in range(n)]
            m = pl.program_id(0)
            dz_ref, dy_ref, dw_ref = take(3)
            if i:
                zp_ref, statp, gain, bias = take(4)
                center, spread = statp[0, 0:1], statp[0, 1:2]
                scale = gain[i - 1 : i] * spread
                shift = bias[i - 1 : i] - center * scale
            else:
                src = take(n_src)
            pw_out, taps_out, pad, yh, yl = take(5)
            alts = take(2) if strided else None
            valid_in = self.valid(meta, m, 0)
            taps = [[] for _ in range(TAPS)]
            for c, cs in enumerate(CHUNKS):
                if i:
                    u = zp_ref[0, :, cs] * scale[:, cs] + shift[:, cs]
                    h = valid_in.keep(u * sigmoid(u))
                else:
                    h = valid_in.keep(self.source(meta, src, cs))
                padded = Padded(pad.at[c], two)
                padded.put(h)
                grad = dy_ref[0, :, cs]
                if strided:
                    grad = spread_out(alts[0].at[c], grad)
                y = None
                for k in range(TAPS):
                    moved = padded.get(k - 2)
                    taps[k].append(column_sum(grad * moved))
                    term = dw_ref[0, k : k + 1, cs] * moved
                    y = term if y is None else y + term
                if strided:
                    y = every_other(alts[1].at[c], y)
                yh[:, cs], yl[:, cs] = halves(y)
            grad = stacked_outer(yh[...], yl[...], dz_ref[0, :, 0:C], dz_ref[0, :, C : 2 * C])
            taps = [jnp.concatenate(t, axis=1) for t in taps]

            @pl.when(m == 0)
            def _():
                pw_out[...] = grad
                for k in range(TAPS):
                    taps_out[k : k + 1, :] = taps[k]

            @pl.when(m > 0)
            def _():
                pw_out[...] += grad
                for k in range(TAPS):
                    taps_out[k : k + 1, :] += taps[k]

        args = [(dz, slots(rows, 2 * C)), (dy, slots(rows)), (self.dw, layer(i, TAPS, C))] + self.before_args(i)
        if i:
            args += [(self.gain, whole(6, C)), (self.bias, whole(6, C))]
        outs = [self.piece_out(i), (f32(TAPS, C), whole(TAPS, C))]
        scratch = [pad_scratch(), pltpu.VMEM((rows, C), BF16), pltpu.VMEM((rows, C), BF16)]
        if strided:
            scratch += [stride_scratch(), stride_scratch()]
        which = PLACES[self.tag][i][0]
        self.pieces[which], self.dw_grad[i] = call(
            body, self.meta, args, outs, scratch, f"{self.tag}_weights_{i}", 6 * OWN * rows * C * C, into=self.pieces[which]
        )
        self.done = (self.dw_grad[i],)

    def backward(self, before=None, after=None):
        self.pieces, self.dw_grad, self.done = [None, None], [None] * 5, ()
        for i in reversed(range(5)):
            if before and i in before:
                self.done += tuple(before[i]())
            result = self.backward_layer(i)
            if after and i in after:
                after[i]()
        return result

    def small_grads(self, rows):
        means, p, _ = self.se_state
        flat = lambda x: x.reshape(-1, x.shape[-1])
        columns = lambda x: jnp.swapaxes(x, 0, 1).reshape(SE, -1)
        means, p, dq, dp = flat(means), columns(p), flat(self.dq), columns(self.dp)
        hidden = p * jax.nn.sigmoid(p)
        norms = [n[:2] for n in reversed(self.locals)] + [self.locals[0][2:]]
        down_b = jnp.pad(jnp.sum(dp, axis=1)[None], ((0, 0), (0, C - SE)))
        out = self.dw_grad + norms + [exact_dot(hidden, dq), exact_dot(dp, means)]
        out += [jnp.sum(dq, axis=0, keepdims=True), down_b]
        out = jnp.concatenate(out, axis=0)
        return jnp.pad(out, ((0, rows - out.shape[0]), (0, 0)))


PLACES = {
    "c15": {0: (0, 0), 1: (0, 1), 2: (0, 2), 3: (0, 3), 4: (0, 4), 5: (0, 5)},
    "c14": {3: (0, 0), 4: (0, 1), 5: (0, 2), 0: (1, 0), 1: (1, 1), 2: (1, 2)},
}
SMALL = 256
PIECE_ROWS = {"c15": (6 * C + SMALL,), "c14": (3 * C, 3 * C + SMALL)}


def swap(x):
    return lax.ppermute(x, "section", [(0, 1), (1, 0)])


def chip_half(piece, first):
    half = piece.shape[0] // 2
    away = lax.dynamic_slice_in_dim(piece, jnp.where(first, half, 0), half)
    kept = lax.dynamic_slice_in_dim(piece, jnp.where(first, 0, half), half)
    return kept + swap(away)


class Reduction:
    def __init__(self, x, stages):
        self.x = x
        self.todo = []
        stride = 1
        for radix in stages:
            self.todo.append((True, radix, stride))
            stride *= radix
        self.todo += [(False, radix, stride) for _, radix, stride in reversed(self.todo)]

    def step(self):
        scatter, radix, stride = self.todo.pop(0)
        rows = self.x.shape[0]
        if scatter:
            parts = exchange(self.x.reshape(radix, rows // radix, C), radix, stride)
            self.x = jnp.sum(parts, axis=0)
        else:
            parts = exchange(jnp.broadcast_to(self.x, (radix,) + self.x.shape), radix, stride)
            self.x = parts.reshape(radix * rows, C)
        return (self.x,)

    def finish(self):
        while self.todo:
            self.step()
        return self.x


def per_device(features, out_grad, lengths, join_pick, dw, pw, gain, bias, res_w, down, down_b, up, up_b):
    first = lax.axis_index("section") == 0
    size = lax.axis_size("dp")
    inputs = features.reshape(MB, SLOT, C)
    cotangent = out_grad.reshape(MB, SLOT, C)
    own, picks = lengths[0, 0], join_pick[0]
    to_upper = lambda x: lax.ppermute(x, "section", [(0, 1)])
    to_lower = lambda x: lax.ppermute(x, "section", [(1, 0)])

    far_len = swap(own)
    joining = jnp.concatenate([lax.dynamic_index_in_dim(inputs, picks[m], 0, False)[HALF:] for m in range(OWN)], axis=0)
    far_rows = swap(jnp.where(first, inputs[MB - 1], joining))
    far_w0 = swap(pw[0, 0:1])
    taps = jnp.concatenate([dw[0].reshape(5 * TAPS, C), gain[0], bias[0]], axis=0)
    far_taps = swap(taps)
    far_pw, far_res = swap(pw[0]), swap(res_w[0])
    wide = jnp.pad(down_b, ((0, 0), (0, C - SE)))
    squeeze = jnp.concatenate([down[0].T, up[0], up_b, wide], axis=0)
    far_squeeze = swap(squeeze)
    far_cot = to_lower(cotangent[:OWN])
    far_cot0 = to_upper(cotangent[MB - 1, :HALF])

    flag = first.astype(jnp.int32)[None]
    mine = lambda v: jnp.where(first, v[:OWN], jnp.concatenate([v[OWN:], jnp.zeros((1,), v.dtype)]))
    length = mine(jnp.where(first, own, far_len))
    half_len = (length + 1) // 2
    join_len = mine(jnp.where(first, far_len, own)[picks])
    meta1 = jnp.concatenate([length, half_len, flag])
    meta2 = jnp.concatenate([half_len, join_len, flag, picks[MB - 1 :]])

    def small(block):
        t = jnp.where(first == (block == 0), taps, far_taps)
        q = jnp.where(first == (block == 0), squeeze, far_squeeze)
        return (
            t[: 5 * TAPS].reshape(5, TAPS, C), t[5 * TAPS : 5 * TAPS + 6], t[5 * TAPS + 6 :],
            q[:SE], q[2 * SE + 1, :SE][:, None], q[SE : 2 * SE], q[2 * SE : 2 * SE + 1],
        )

    def prepared(block, start, stop):
        array = prepare(meta1, (pw[0], res_w[0]), (far_pw, far_res), block, start, stop)
        return array, {i: (array, i - start) for i in range(start, stop)}

    parts0 = [prepared(0, 1, 3), prepared(0, 3, 6)]
    parts1 = [prepared(1, 0, 3), prepared(1, 3, 6)]

    stages, deep = radices(size, 16), radices(size, 4)
    c14 = Block(False, meta1, small(0), {**parts0[0][1], **parts0[1][1]}, stages)
    c14.x, c14.x_far, c14.first_matrix = inputs, far_rows, (pw[0], far_w0)
    c14.forward({2: (parts0[1][0],), 4: (parts1[0][0],)})
    out0 = c14.tail(after=(parts1[1][0],))
    c15 = Block(True, meta2, small(1), {**parts1[0][1], **parts1[1][1]}, stages)
    c15.arrived, c15.joined_far, c15.joined = out0, far_rows, features.reshape(MB, 2, HALF, C)
    c15.forward()
    out1 = c15.tail(cotangent, far_cot)
    back, dx1 = c15.backward()

    def ready(block, no):
        piece = block.pieces[no]
        if no == len(PIECE_ROWS[block.tag]) - 1:
            piece = lax.dynamic_update_slice_in_dim(piece, block.small_grads(SMALL), piece.shape[0] - SMALL, 0)
        return chip_half(piece, first)

    c14.tail_backward(cotangent, far_cot0, back)
    half15 = ready(c15, 0)
    sum15 = lax.psum(half15, "dp")

    def last_pass(half15):
        early, last = [], copy.copy(c14)
        last.locals = list(c14.locals)
        dx0, = last.backward(
            before={4: lambda: (half15,), 1: lambda: early[0].step(), 0: lambda: early[0].step()},
            after={3: lambda: early.append(Reduction(ready(last, 0), deep))},
        )
        part14 = early[0].finish()
        return dx0, part14, Reduction(ready(last, 1), deep).finish()

    shapes = jax.eval_shape(last_pass, half15)
    nothing = lambda x: jax.tree.map(lambda y: jnp.zeros(y.shape, y.dtype), shapes)
    dx0, part14, last14 = lax.cond(own[0] > 0, last_pass, nothing, half15)
    sum15, last14 = lax.optimization_barrier((sum15, last14))
    came15 = to_upper(sum15)
    came14, came_last = to_lower(part14), to_lower(last14)

    full15 = jnp.concatenate([came15, sum15], axis=0)
    start14 = jnp.concatenate([part14, came14], axis=0)
    end14 = jnp.concatenate([last14, came_last], axis=0)
    pw_grad = jnp.where(first, jnp.concatenate([end14[: 3 * C], start14[: 2 * C]], axis=0), full15[: 5 * C])
    res_grad = jnp.where(first, start14[2 * C :], full15[5 * C : 6 * C])
    rows = jnp.where(first, end14[3 * C :], full15[6 * C :])
    dw_grad = rows[: 5 * TAPS].reshape(1, 5, TAPS, C)
    norms = rows[5 * TAPS : 5 * TAPS + 12].reshape(6, 2, C)
    rest = rows[5 * TAPS + 12 :]
    up_grad, down_grad = rest[:SE], rest[SE : 2 * SE].T
    up_b_grad, down_b_grad = rest[2 * SE : 2 * SE + 1], rest[2 * SE + 1 : 2 * SE + 2, :SE]

    pad = jnp.zeros((1, HALF, C), F32)
    lower = jnp.concatenate([out0, jnp.concatenate([to_lower(out0[0:1, :HALF]), pad], axis=1)], axis=0)
    upper = jnp.concatenate([to_upper(out1), out1[0:1]], axis=0)
    block_out = jnp.where(first, lower, upper)
    lower = jnp.concatenate([dx0, to_lower(dx0[0:1])], axis=0)
    joins = jnp.concatenate([to_upper(dx1), dx1[0:1]], axis=0)
    joins = jnp.stack([lax.dynamic_index_in_dim(joins, jnp.argmax(picks == s), 0, False) for s in range(MB)])
    upper = jnp.concatenate([jnp.zeros_like(joins), joins], axis=1)
    dx = jnp.where(first, lower, upper)
    return (
        block_out.reshape(features.shape), dx.reshape(features.shape), dw_grad, pw_grad.reshape(1, 5, C, C),
        norms[None, :, 1], norms[None, :, 0], res_grad[None], down_grad[None], down_b_grad, up_grad[None], up_b_grad,
    )


def solution(mesh):
    rows = P("section", "dp", None)
    own = lambda dims: P("section", *([None] * dims))
    weights = (own(3), own(3), own(2), own(2), own(2), own(2), own(1), own(2), own(1))
    in_specs = (rows, rows, rows, P("dp", None), *weights)
    out_specs = (rows, rows, *weights)
    return jax.shard_map(per_device, mesh=mesh, in_specs=in_specs, out_specs=out_specs, check_vma=False)
```

```python
import copy

import jax
import jax.numpy as jnp
from jax import lax
from jax.experimental import pallas as pl
from jax.experimental.pallas import tpu as pltpu
from jax.sharding import PartitionSpec as P

EPSILON = 1e-05
EXACT = lax.Precision.HIGHEST
TAPS = 5
MB = 3
OWN = 2
SLOT = 400
HALF = 200
KEPT = 208
C = 512
LANES = 128
CHUNKS = [slice(c, c + LANES) for c in range(0, C, LANES)]
SE = 64
BF16, F32 = jnp.bfloat16, jnp.float32
VMEM_BYTES = 60 << 20


def radices(size, most):
    stages, left = [], size
    while left > 1:
        radix = min(most, left)
        while left % radix:
            radix -= 1
        stages.append(radix)
        left //= radix
    return stages


def exchange(block, radix, stride):
    size = lax.axis_size("dp")
    if radix == size:
        return lax.all_to_all(block, "dp", 0, 0)
    groups = []
    for base in range(size):
        if (base // stride) % radix == 0:
            groups.append([base + j * stride for j in range(radix)])
    return lax.all_to_all(block, "dp", 0, 0, axis_index_groups=groups)


def shared(block, stages):
    stride = 1
    for no, radix in enumerate(stages):
        if no:
            block = jnp.broadcast_to(jnp.sum(block, axis=0), (radix,) + block.shape[1:])
        block = exchange(block, radix, stride)
        stride *= radix
    return block


def halves(x):
    high = x.astype(BF16)
    return high, (x - high.astype(F32)).astype(BF16)


def sigmoid(x):
    return 0.5 * jnp.tanh(0.5 * x) + 0.5


def exact_dot(a, b, dims=((1,), (0,))):
    return lax.dot_general(a, b, (dims, ((), ())), precision=EXACT, preferred_element_type=F32)


def fast_dot(a, b, dims=((1,), (0,))):
    return lax.dot_general(a, b, (dims, ((), ())), preferred_element_type=F32)


def stacked_dot(high, low, w_ref, back=False):
    w_high, w_low = w_ref[0, 0], w_ref[0, 1]
    w = jnp.concatenate([w_high, w_high, w_low], axis=1 if back else 0)
    x = jnp.concatenate([high, low, high], axis=1)
    return fast_dot(x, w, ((1,), (1 if back else 0,)))


def stacked_outer(a_high, a_low, b_high, b_low):
    a = jnp.concatenate([a_high, a_low, a_high], axis=0)
    b = jnp.concatenate([b_high, b_high, b_low], axis=0)
    return fast_dot(a, b, ((0,), (0,)))


def column_sum(x):
    return jnp.sum(x, axis=0, keepdims=True)


class Rows:
    def __init__(self, meta, m, two, rows, which=0):
        place = lax.broadcasted_iota(jnp.int32, (rows, LANES), 0)
        if two:
            later = place >= HALF
            limit = jnp.where(later, HALF + meta[OWN + m], meta[m])
            self.mask = place < limit
        else:
            self.mask = place < meta[which * OWN + m]

    def keep(self, x):
        return jnp.where(self.mask, x, 0.0)


class Padded:
    def __init__(self, ref, two):
        self.ref = ref
        self.pieces = [(8, 0, HALF), (16 + HALF, HALF, HALF)] if two else [(8, 0, SLOT)]

    def put(self, x):
        zeros = jnp.zeros((8, LANES), F32)
        for at, start, rows in self.pieces:
            self.ref[at - 8 : at, :] = zeros
            self.ref[at : at + rows, :] = x[start : start + rows]
        self.ref[at + rows : at + rows + 8, :] = zeros

    def get(self, offset):
        parts = [self.ref[at + offset : at + offset + rows, :] for at, _, rows in self.pieces]
        return parts[0] if len(parts) == 1 else jnp.concatenate(parts, axis=0)

    def conv(self, kernel):
        total = kernel[0:1] * self.get(-2)
        for k in range(1, TAPS):
            total = total + kernel[k : k + 1] * self.get(k - 2)
        return total

    def conv_back(self, kernel):
        total = kernel[0:1] * self.get(2)
        for k in range(1, TAPS):
            total = total + kernel[k : k + 1] * self.get(2 - k)
        return total


def every_other(ref, x):
    ref[0:SLOT, :] = x
    ref[SLOT : 2 * KEPT, :] = jnp.zeros((2 * KEPT - SLOT, LANES), F32)
    return ref[pl.ds(0, KEPT, stride=2), :]


def spread_out(ref, x):
    ref[...] = jnp.zeros_like(ref)
    ref[pl.ds(0, KEPT, stride=2), :] = x
    return ref[0:SLOT, :]


def center_spread(sums, rows):
    center = sums[0:1] / rows
    return center, lax.rsqrt(sums[1:2] / rows - center * center + EPSILON)


def added(ref):
    return jnp.sum(ref[:, 0], axis=0)


def send(ref, rows):
    for copy in range(ref.shape[0]):
        for row, x in enumerate(rows):
            ref[copy, 0, row : row + 1, 0 : x.shape[1]] = x


def pad_scratch():
    return pltpu.VMEM((len(CHUNKS), SLOT + 24, LANES), F32)


def stride_scratch():
    return pltpu.VMEM((len(CHUNKS), 2 * KEPT, LANES), F32)


def slots(rows, cols=C):
    return pl.BlockSpec((1, rows, cols), lambda m, *_: (m, 0, 0))


def copies(count, rows, cols=C):
    return pl.BlockSpec((count, 1, rows, cols), lambda m, *_: (0, m, 0, 0))


def whole(*shape):
    return pl.BlockSpec(shape, lambda m, *_: (0,) * len(shape))


def layer(i, *shape):
    return pl.BlockSpec((1,) + shape, lambda m, *_: (i,) + (0,) * len(shape))


def f32(*shape):
    return jax.ShapeDtypeStruct(shape, F32)


def bf16(*shape):
    return jax.ShapeDtypeStruct(shape, BF16)


def call(body, meta, args, outs, scratch=(), name=None, flops=0, steps=OWN, after=(), into=()):
    arrays, in_specs = [a for a, _ in args], [s for _, s in args]
    shapes, out_specs = [a for a, _ in outs], [s for _, s in outs]
    size = sum(a.size * a.dtype.itemsize for a in arrays + shapes)
    extra = list(after) + list(into)
    count = len(arrays)

    def inner(meta, *refs):
        body(meta, *refs[:count], *refs[count + len(extra) :])

    return pl.pallas_call(
        inner,
        out_shape=shapes,
        grid_spec=pltpu.PrefetchScalarGridSpec(
            num_scalar_prefetch=1,
            grid=(steps,),
            in_specs=in_specs + [pl.BlockSpec(memory_space=pl.ANY)] * len(extra),
            out_specs=out_specs,
            scratch_shapes=list(scratch),
        ),
        input_output_aliases={1 + count + len(after) + j: j for j in range(len(into))},
        compiler_params=pltpu.CompilerParams(vmem_limit_bytes=VMEM_BYTES),
        cost_estimate=pl.CostEstimate(flops=flops, bytes_accessed=size, transcendentals=0),
        name=name,
    )(meta, *arrays, *extra)


def choose(meta, block, own, far):
    return jnp.where(meta[2 * OWN] == 1 - block, own, far)


def prepare(meta, own, far, block, start, stop):
    def body(meta, *refs):
        pair = [ref[0] for ref in refs[:2]]
        if stop == 6:
            last = pl.program_id(0) == 5 - start
            pair = [jnp.where(last, ref[...], w) for ref, w in zip(refs[2:4], pair)]
        out = refs[-1]
        out[0, 0], out[0, 1] = halves(choose(meta, block, *pair))

    matrix = pl.BlockSpec((1, C, C), lambda j, *_: (jnp.minimum(j + start, 4), 0, 0))
    args = [(own[0], matrix), (far[0], matrix)]
    if stop == 6:
        args += [(own[1], whole(C, C)), (far[1], whole(C, C))]
    out = pl.BlockSpec((1, 2, C, C), lambda j, *_: (j, 0, 0, 0))
    name = f"prepare_{block}_{start}"
    return call(body, meta, args, [(bf16(stop - start, 2, C, C), out)], name=name, steps=stop - start)[0]


class Block:
    def __init__(self, two, meta, weights, ready, stages):
        self.two, self.meta, self.stages = two, meta, stages
        self.dw, self.gain, self.bias, self.down, self.down_b, self.up, self.up_b = weights
        self.ready = ready
        self.tail_rows = SLOT if two else KEPT
        self.first, self.last = stages[0], stages[-1]
        self.tag = "c15" if two else "c14"

    def rows_of(self, i):
        return self.tail_rows if i == 4 else SLOT

    def valid(self, meta, m, i):
        last = i == 4 and not self.two
        return Rows(meta, m, self.two, self.rows_of(i), which=1 if last else 0)

    def matrix(self, i):
        array, at = self.ready[i]
        return (array, layer(at, 2, C, C))

    def source_args(self):
        if not self.two:
            return [(self.x, slots(SLOT)), (self.x_far, whole(SLOT, C))]
        far = pl.BlockSpec((HALF, C), lambda m, *_: (m, 0))
        near = pl.BlockSpec((1, 1, HALF, C), lambda m, meta: (meta[2 * OWN + 1], 1, 0, 0))
        return [(self.arrived, slots(HALF)), (self.joined_far, far), (self.joined, near)]

    def source(self, meta, refs, cs):
        lower = meta[2 * OWN] == 1
        if not self.two:
            return jnp.where(lower, refs[0][0, :, cs], refs[1][:, cs])
        joined = jnp.where(lower, refs[1][:, cs], refs[2][0, 0, :, cs])
        return jnp.concatenate([refs[0][0, :, cs], joined], axis=0)

    def before_args(self, i):
        if i == 0:
            return self.source_args()
        return [(self.z[i - 1], slots(SLOT)), (self.stats[i - 1], slots(2))]


    def forward_layer(self, i, after=()):
        two, count = self.two, self.first
        strided = i == 4 and not two
        rows = self.rows_of(i)
        n_src = len(self.source_args())
        width = C + LANES if i == 0 else C
        sent = 4 if i == 3 else 2
        makes = i == 0 and not two

        def body(meta, *refs):
            refs = list(refs)
            take = lambda n: [refs.pop(0) for _ in range(n)]
            m = pl.program_id(0)
            if i == 0:
                src = take(n_src)
            else:
                z_ref, got_ref = take(2)
                n_ref, = take(1) if i > 1 else (None,)
                gain_ref, bias_ref = take(2)
                res_sum, = take(1) if i == 3 else (None,)
            dw_ref, = take(1)
            if makes:
                own_ref, far_ref, z_out, pay, w_ref = take(5)

                @pl.when(m == 0)
                def _():
                    w_ref[0, 0], w_ref[0, 1] = halves(choose(meta, 0, own_ref[0], far_ref[0]))

            else:
                w_ref, z_out, pay = take(3)
            if i:
                stat_out, = take(1)
            if i == 1:
                n_out, = take(1)
            pad, y_ref = take(2)
            alt, = take(1) if strided else (None,)
            valid_in = self.valid(meta, m, 0)
            if i:
                sums = added(got_ref)
                if i == 1:
                    count_in = jnp.maximum(jnp.concatenate([sums[0:1, C:]] * len(CHUNKS), axis=1), 1.0)
                    count_out = jnp.maximum(jnp.concatenate([sums[1:2, C:]] * len(CHUNKS), axis=1), 1.0)
                    n_out[0, 0:1, :] = count_in
                    n_out[0, 1:2, :] = count_out
                else:
                    count_in = n_ref[0, 0:1, :]
                center, spread = center_spread(sums[:, :C], count_in)
                stat_out[0, 0:1, :] = center
                stat_out[0, 1:2, :] = spread
                scale = gain_ref[i - 1 : i] * spread
                shift = bias_ref[i - 1 : i] - center * scale
            for c, cs in enumerate(CHUNKS):
                if i == 0:
                    h = valid_in.keep(self.source(meta, src, cs))
                else:
                    u = z_ref[0, :, cs] * scale[:, cs] + shift[:, cs]
                    h = valid_in.keep(u * sigmoid(u))
                padded = Padded(pad.at[c], two)
                padded.put(h)
                y = padded.conv(dw_ref[0, :, cs])
                if strided:
                    y = every_other(alt.at[c], y)
                high, low = halves(y)
                y_ref[:, cs] = high
                y_ref[:, C + cs.start : C + cs.stop] = low
            z = stacked_dot(y_ref[:, 0:C], y_ref[:, C : 2 * C], w_ref)
            z_out[0] = z
            valid = self.valid(meta, m, i)
            one, square = [], []
            for cs in CHUNKS:
                kept = valid.keep(z[:, cs])
                one.append(column_sum(kept))
                square.append(column_sum(kept * kept))
            if i == 0:
                if two:
                    number = (meta[m] + meta[OWN + m]).astype(F32)
                    numbers = number, number
                else:
                    numbers = meta[m].astype(F32), meta[OWN + m].astype(F32)
                one.append(jnp.full((1, LANES), numbers[0], F32))
                square.append(jnp.full((1, LANES), numbers[1], F32))
            out = [jnp.concatenate(one, axis=1), jnp.concatenate(square, axis=1)]
            if i == 3:
                out += [res_sum[0, 0:1, :], res_sum[0, 1:2, :]]
            send(pay, out)

        if i == 0:
            args = list(self.source_args())
        else:
            got = 4 if i == 4 else 2
            args = [(self.z[i - 1], slots(SLOT)), (self.got[i - 1], copies(self.last, got, C + LANES if i == 1 else C))]
            if i > 1:
                args.append((self.number, slots(2)))
            args += [(self.gain, whole(6, C)), (self.bias, whole(6, C))]
            if i == 3:
                args.append((self.res_sum, slots(2)))
        args.append((self.dw, layer(i, TAPS, C)))
        args += [(w, layer(0, C, C)) for w in self.first_matrix] if makes else [self.matrix(i)]
        outs = [(f32(OWN, rows, C), slots(rows)), (f32(count, OWN, sent, width), copies(count, sent, width))]
        if i:
            outs.append((f32(OWN, 2, C), slots(2)))
        if i == 1:
            outs.append((f32(OWN, 2, C), slots(2)))
        if makes:
            outs.append((bf16(1, 2, C, C), layer(0, 2, C, C)))
        scratch = [pad_scratch(), pltpu.VMEM((rows, 2 * C), BF16)]
        if strided:
            scratch.append(stride_scratch())
        result = call(body, self.meta, args, outs, scratch, f"{self.tag}_forward_{i}", 6 * OWN * rows * C * C, after=after)
        self.z.append(result[0])
        if makes:
            self.ready[0] = (result[2], 0)
        if i:
            self.stats.append(result[2])
        if i == 1:
            self.number = result[3]
        self.got.append(shared(result[1], self.stages))

    def residual(self):
        two, rows = self.two, self.tail_rows

        def body(meta, *refs):
            refs = list(refs)
            src = [refs.pop(0) for _ in self.source_args()]
            w_ref, r_out, x_out, sum_out = refs[:4]
            alt = refs[4] if not two else None
            m = pl.program_id(0)
            valid_in = self.valid(meta, m, 0)
            for c, cs in enumerate(CHUNKS):
                x = valid_in.keep(self.source(meta, src, cs))
                if not two:
                    x = every_other(alt.at[c], x)
                high, low = halves(x)
                x_out[0, :, cs] = high
                x_out[0, :, C + cs.start : C + cs.stop] = low
            r = stacked_dot(x_out[0, :, 0:C], x_out[0, :, C : 2 * C], w_ref)
            r_out[0] = r
            valid = self.valid(meta, m, 4)
            for cs in CHUNKS:
                kept = valid.keep(r[:, cs])
                sum_out[0, 0:1, cs] = column_sum(kept)
                sum_out[0, 1:2, cs] = column_sum(kept * kept)

        args = self.source_args() + [self.matrix(5)]
        outs = [
            (f32(OWN, rows, C), slots(rows)),
            (bf16(OWN, rows, 2 * C), slots(rows, 2 * C)),
            (f32(OWN, 2, C), slots(2)),
        ]
        scratch = [] if two else [stride_scratch()]
        self.r, self.picked, self.res_sum = call(
            body, self.meta, args, outs, scratch, f"{self.tag}_residual", 6 * OWN * rows * C * C
        )

    def forward(self, after=None):
        self.z, self.got, self.stats = [], [], []
        for i in range(5):
            if i == 2:
                self.residual()
            self.forward_layer(i, (after or {}).get(i, ()))


    def segments(self):
        return [(0, HALF), (HALF, HALF)] if self.two else [(0, self.tail_rows)]

    def lengths(self, meta, m):
        if self.two:
            return [meta[m], meta[OWN + m]]
        return [meta[OWN + m]]

    def squeeze(self, sums, counts, se_refs):
        down_t, down_b, up, up_b = se_refs
        means = [s / jnp.maximum(jnp.full((1, C), n.astype(F32)), 1.0) for s, n in zip(sums, counts)]
        ps = [jnp.sum(down_t[...] * mean, axis=1, keepdims=True) + down_b[...] for mean in means]
        gates = [sigmoid(column_sum(up[...] * (p * sigmoid(p))) + up_b[...]) for p in ps]
        return means, ps, gates

    def squeeze_back(self, des, ps, gates, counts, se_refs):
        down_t, down_b, up, up_b = se_refs
        dqs, dps, shares = [], [], []
        for de, p, gate, n in zip(des, ps, gates, counts):
            dq = de * gate * (1.0 - gate)
            s = sigmoid(p)
            dp = jnp.sum(up[...] * dq, axis=1, keepdims=True) * (s * (1.0 + p * (1.0 - s)))
            dm = column_sum(down_t[...] * dp)
            dqs.append(dq)
            dps.append(dp)
            shares.append(dm / jnp.maximum(jnp.full((1, C), n.astype(F32)), 1.0))
        return dqs, dps, shares

    def se_args(self):
        return [(self.down, whole(SE, C)), (self.down_b, whole(SE, 1)), (self.up, whole(SE, C)), (self.up_b, whole(1, C))]

    def store_rows(self, ref, rows):
        ref[0] = jnp.concatenate(rows + [jnp.zeros((8 - len(rows), C), F32)], axis=0)

    def store_columns(self, ref, columns):
        ref[0] = jnp.zeros((SE, 8), F32)
        for j, column in enumerate(columns):
            ref[0, :, j : j + 1] = column

    def by_segment(self, rows, cs):
        parts = [jnp.broadcast_to(row[:, cs], (n, LANES)) for row, (_, n) in zip(rows, self.segments())]
        return parts[0] if len(parts) == 1 else jnp.concatenate(parts, axis=0)

    def seg_sums(self, x):
        return [column_sum(x[at : at + n]) for at, n in self.segments()]

    def tail(self, cotangent=None, far=None, after=()):
        two, rows = self.two, self.tail_rows
        back = cotangent is not None

        def body(meta, *refs):
            refs = list(refs)
            take = lambda n: [refs.pop(0) for _ in range(n)]
            m = pl.program_id(0)
            z_ref, got4, r_ref, got3, n_ref, gain, bias = take(7)
            se_refs = take(4)
            if back:
                cot_ref, far_ref = take(2)
            out, stat_out, rstat_out, means_out, p_out, gate_out = take(6)
            if back:
                du_out, dt_out, pay, dq_out, dp_out = take(5)
            h_ref, = take(1)
            if back:
                slope_ref, = take(1)
            valid = self.valid(meta, m, 4)
            number = n_ref[0, 1:2, :]
            center, spread = center_spread(added(got4), number)
            rcenter, rspread = center_spread(added(got3)[2:4], number)
            stat_out[0, 0:1, :] = center
            stat_out[0, 1:2, :] = spread
            rstat_out[0, 0:1, :] = rcenter
            rstat_out[0, 1:2, :] = rspread
            scale = gain[4:5] * spread
            shift = bias[4:5] - center * scale
            sums = []
            for cs in CHUNKS:
                u = z_ref[0, :, cs] * scale[:, cs] + shift[:, cs]
                s = sigmoid(u)
                h = valid.keep(u * s)
                h_ref[:, cs] = h
                if back:
                    slope_ref[:, cs] = valid.keep(s * (1.0 + u * (1.0 - s)))
                sums.append(self.seg_sums(h))
            sums = [jnp.concatenate([s[j] for s in sums], axis=1) for j in range(len(self.segments()))]
            counts = self.lengths(meta, m)
            means, ps, gates = self.squeeze(sums, counts, se_refs)
            self.store_rows(means_out, means)
            self.store_columns(p_out, ps)
            self.store_rows(gate_out, gates)
            res_gain, res_bias, gate_grad = [], [], []
            for cs in CHUNKS:
                h = h_ref[:, cs]
                rh = (r_ref[0, :, cs] - rcenter[:, cs]) * rspread[:, cs]
                t = h * self.by_segment(gates, cs) + gain[5:6, cs] * rh + bias[5:6, cs]
                s = sigmoid(t)
                out[0, 0:rows, cs] = valid.keep(t * s)
                if rows < SLOT:
                    out[0, rows:SLOT, cs] = jnp.zeros((SLOT - rows, LANES), F32)
                if back:
                    cot = jnp.where(meta[2 * OWN] == 1, far_ref[0, :, cs], cot_ref[0, :, cs])
                    dt = valid.keep(cot * (s * (1.0 + t * (1.0 - s))))
                    dt_out[0, :, cs] = dt
                    res_bias.append(column_sum(dt))
                    res_gain.append(column_sum(dt * rh))
                    gate_grad.append(self.seg_sums(dt * h))
            if not back:
                return
            des = [jnp.concatenate([g[j] for g in gate_grad], axis=1) for j in range(len(counts))]
            dqs, dps, shares = self.squeeze_back(des, ps, gates, counts, se_refs)
            self.store_rows(dq_out, dqs)
            self.store_columns(dp_out, dps)
            bias_sum, gain_sum = [], []
            for cs in CHUNKS:
                dh = dt_out[0, :, cs] * self.by_segment(gates, cs) + self.by_segment(shares, cs)
                du = dh * slope_ref[:, cs]
                du_out[0, :, cs] = du
                bias_sum.append(column_sum(du))
                gain_sum.append(column_sum(du * ((z_ref[0, :, cs] - center[:, cs]) * spread[:, cs])))
            send(pay, [jnp.concatenate(x, axis=1) for x in (bias_sum, gain_sum, res_bias, res_gain)])

        args = [
            (self.z[4], slots(rows)), (self.got[4], copies(self.last, 2)), (self.r, slots(rows)),
            (self.got[3], copies(self.last, 4)), (self.number, slots(2)),
            (self.gain, whole(6, C)), (self.bias, whole(6, C)),
        ] + self.se_args()
        outs = [
            (f32(OWN, SLOT, C), slots(SLOT)), (f32(OWN, 2, C), slots(2)), (f32(OWN, 2, C), slots(2)),
            (f32(OWN, 8, C), slots(8)), (f32(OWN, SE, 8), slots(SE, 8)), (f32(OWN, 8, C), slots(8)),
        ]
        scratch = [pltpu.VMEM((rows, C), F32)]
        if back:
            last = pl.BlockSpec((1, SLOT, C), lambda m, *_: (MB - 1, 0, 0))
            args += [(cotangent, last), (far, slots(SLOT))]
            outs += self.tail_outs()
            scratch.append(pltpu.VMEM((rows, C), F32))
        result = call(body, self.meta, args, outs, scratch, f"{self.tag}_tail", after=after)
        self.stats.append(result[1])
        self.rstat, self.se_state = result[2], result[3:6]
        if back:
            self.tail_results(result[6:])
        return result[0]

    def tail_outs(self):
        rows, count = self.tail_rows, self.first
        return [
            (f32(OWN, rows, C), slots(rows)), (f32(OWN, rows, C), slots(rows)),
            (f32(count, OWN, 4, C), copies(count, 4)), (f32(OWN, 8, C), slots(8)), (f32(OWN, SE, 8), slots(SE, 8)),
        ]

    def tail_results(self, result):
        self.du, self.dt, pay, self.dq, self.dp = result
        self.locals = [jnp.sum(pay[0], axis=0)]
        self.back_got = shared(pay, self.stages)

    def tail_backward(self, cotangent, far, back):
        rows = self.tail_rows

        def body(meta, z_ref, r_ref, stat, rstat, gain, bias, p_ref, gate_ref, down, down_b, up, up_b, cot_ref, far_ref, back_ref,
                 du_out, dt_out, pay, dq_out, dp_out, slope_ref):
            m = pl.program_id(0)
            valid = self.valid(meta, m, 4)
            center, spread, rcenter, rspread = stat[0, 0:1], stat[0, 1:2], rstat[0, 0:1], rstat[0, 1:2]
            scale = gain[4:5] * spread
            shift = bias[4:5] - center * scale
            zeros = jnp.zeros((rows - HALF, LANES), F32)
            counts = self.lengths(meta, m)
            ps = [p_ref[0, :, j : j + 1] for j in range(len(counts))]
            gates = [gate_ref[0, j : j + 1, :] for j in range(len(counts))]
            res_gain, res_bias, gate_grad = [], [], []
            for cs in CHUNKS:
                u = z_ref[0, :, cs] * scale[:, cs] + shift[:, cs]
                s = sigmoid(u)
                h = valid.keep(u * s)
                slope_ref[:, cs] = valid.keep(s * (1.0 + u * (1.0 - s)))
                rh = (r_ref[0, :, cs] - rcenter[:, cs]) * rspread[:, cs]
                t = h * self.by_segment(gates, cs) + gain[5:6, cs] * rh + bias[5:6, cs]
                s = sigmoid(t)
                here = jnp.where(meta[2 * OWN] == 1, cot_ref[0, 0:HALF, cs], far_ref[:, cs])
                cot = jnp.concatenate([here + back_ref[0, :, cs], zeros], axis=0)
                dt = valid.keep(cot * (s * (1.0 + t * (1.0 - s))))
                dt_out[0, :, cs] = dt
                res_bias.append(column_sum(dt))
                res_gain.append(column_sum(dt * rh))
                gate_grad.append(self.seg_sums(dt * h))
            des = [jnp.concatenate([g[j] for g in gate_grad], axis=1) for j in range(len(counts))]
            dqs, dps, shares = self.squeeze_back(des, ps, gates, counts, (down, down_b, up, up_b))
            self.store_rows(dq_out, dqs)
            self.store_columns(dp_out, dps)
            bias_sum, gain_sum = [], []
            for cs in CHUNKS:
                dh = dt_out[0, :, cs] * self.by_segment(gates, cs) + self.by_segment(shares, cs)
                du = dh * slope_ref[:, cs]
                du_out[0, :, cs] = du
                bias_sum.append(column_sum(du))
                gain_sum.append(column_sum(du * ((z_ref[0, :, cs] - center[:, cs]) * spread[:, cs])))
            send(pay, [jnp.concatenate(x, axis=1) for x in (bias_sum, gain_sum, res_bias, res_gain)])

        args = [
            (self.z[4], slots(rows)), (self.r, slots(rows)), (self.stats[4], slots(2)), (self.rstat, slots(2)),
            (self.gain, whole(6, C)), (self.bias, whole(6, C)),
            (self.se_state[1], slots(SE, 8)), (self.se_state[2], slots(8)),
        ] + self.se_args() + [(cotangent, slots(SLOT)), (far, whole(HALF, C)), (back, slots(HALF))]
        scratch = [pltpu.VMEM((rows, C), F32)]
        self.tail_results(call(body, self.meta, args, self.tail_outs(), scratch, f"{self.tag}_tail_back"))


    def norm_grad(self, du, zh, scale, sums, number, cs):
        return scale[:, cs] * (du - sums[0:1, cs] / number[:, cs] - zh * (sums[1:2, cs] / number[:, cs]))

    def backward_layer(self, i):
        two, count = self.two, self.first
        strided = i == 4 and not two
        rows = self.rows_of(i)

        def body(meta, *refs):
            refs = list(refs)
            take = lambda n: [refs.pop(0) for _ in range(n)]
            m = pl.program_id(0)
            got, n_ref, du_ref, z_ref, stat, gain, bias, dw_ref, w_ref = take(9)
            if i:
                zp_ref, statp = take(2)
            else:
                dxr_ref, = take(1)
            dz_out, dy_out = take(2)
            if i:
                du_out, pay = take(2)
            elif two:
                back_out, dx_out = take(2)
            else:
                dx_out, = take(1)
            pad, = take(1)
            alt, = take(1) if refs else (None,)
            sums = added(got)
            last = i == 4
            number = n_ref[0, 1:2, :] if last else n_ref[0, 0:1, :]
            center, spread = stat[0, 0:1], stat[0, 1:2]
            scale = gain[i : i + 1] * spread
            valid = self.valid(meta, m, i)
            for cs in CHUNKS:
                zh = (z_ref[0, :, cs] - center[:, cs]) * spread[:, cs]
                dz = valid.keep(self.norm_grad(du_ref[0, :, cs], zh, scale, sums, number, cs))
                high, low = halves(dz)
                dz_out[0, :, cs] = high
                dz_out[0, :, C + cs.start : C + cs.stop] = low
            dy = stacked_dot(dz_out[0, :, 0:C], dz_out[0, :, C : 2 * C], w_ref, True)
            dy_out[0] = dy
            valid_in = self.valid(meta, m, 0)
            if i:
                pcenter, pspread = statp[0, 0:1], statp[0, 1:2]
                pscale = gain[i - 1 : i] * pspread
                pshift = bias[i - 1 : i] - pcenter * pscale
            bias_sum, gain_sum = [], []
            for c, cs in enumerate(CHUNKS):
                grad = dy[:, cs]
                if strided:
                    grad = spread_out(alt.at[c], grad)
                padded = Padded(pad.at[c], two)
                padded.put(grad)
                dh = padded.conv_back(dw_ref[0, :, cs])
                if i:
                    z = zp_ref[0, :, cs]
                    u = z * pscale[:, cs] + pshift[:, cs]
                    s = sigmoid(u)
                    du = valid_in.keep(dh * (s * (1.0 + u * (1.0 - s))))
                    du_out[0, :, cs] = du
                    bias_sum.append(column_sum(du))
                    gain_sum.append(column_sum(du * ((z - pcenter[:, cs]) * pspread[:, cs])))
                    continue
                dxr = dxr_ref[0, :, cs]
                if not two:
                    dxr = spread_out(alt.at[c], dxr)
                dx = valid_in.keep(dh) + dxr
                if two:
                    back_out[0, :, cs] = dx[:HALF]
                    dx_out[0, :, cs] = dx[HALF:]
                else:
                    dx_out[0, :, cs] = dx
            if i:
                send(pay, [jnp.concatenate(bias_sum, axis=1), jnp.concatenate(gain_sum, axis=1)])

        sent = 4 if i == 4 else 2
        args = [
            (self.back_got, copies(self.last, sent)), (self.number, slots(2)), (self.du, slots(rows)),
            (self.z[i], slots(rows)), (self.stats[i], slots(2)), (self.gain, whole(6, C)), (self.bias, whole(6, C)),
            (self.dw, layer(i, TAPS, C)), self.matrix(i),
        ]
        if i:
            args += self.before_args(i)
        else:
            args.append((self.dxr, slots(self.tail_rows)))
        outs = [
            (bf16(OWN, rows, 2 * C), slots(rows, 2 * C)), (f32(OWN, rows, C), slots(rows)),
        ]
        if i:
            outs += [(f32(OWN, SLOT, C), slots(SLOT)), (f32(count, OWN, 2, C), copies(count, 2))]
        elif two:
            outs += [(f32(OWN, HALF, C), slots(HALF)), (f32(OWN, HALF, C), slots(HALF))]
        else:
            outs += [(f32(OWN, SLOT, C), slots(SLOT))]
        scratch = [pad_scratch()]
        if strided or (i == 0 and not two):
            scratch.append(stride_scratch())
        result = call(
            body, self.meta, args, outs, scratch, f"{self.tag}_backward_{i}", 6 * OWN * rows * C * C, after=self.done
        )
        dz, dy = result[:2]
        got = self.back_got
        if i:
            self.du = result[2]
            self.locals.append(jnp.sum(result[3][0], axis=0))
            self.back_got = shared(result[3], self.stages)
        self.weight_grad(i, dz, dy)
        if i == 4:
            self.residual_back(got)
        return result[2:]

    def residual_back(self, got):
        rows = self.tail_rows

        def body(meta, got, n_ref, dt_ref, r_ref, rstat, gain, w_ref, x_ref, kept_out, away_out, dxr_out, dr, total):
            m = pl.program_id(0)
            sums = added(got)[2:4]
            number = n_ref[0, 1:2, :]
            center, spread = rstat[0, 0:1], rstat[0, 1:2]
            scale = gain[5:6] * spread
            valid = self.valid(meta, m, 4)
            for cs in CHUNKS:
                rh = (r_ref[0, :, cs] - center[:, cs]) * spread[:, cs]
                high, low = halves(valid.keep(self.norm_grad(dt_ref[0, :, cs], rh, scale, sums, number, cs)))
                dr[:, cs] = high
                dr[:, C + cs.start : C + cs.stop] = low
            high, low = dr[:, 0:C], dr[:, C : 2 * C]
            dxr_out[0] = stacked_dot(high, low, w_ref, True)
            grad = stacked_outer(x_ref[0, :, 0:C], x_ref[0, :, C : 2 * C], high, low)
            self.add_halves(meta, m, grad, total, kept_out, away_out)

        args = [
            (got, copies(self.last, 4)), (self.number, slots(2)), (self.dt, slots(rows)), (self.r, slots(rows)),
            (self.rstat, slots(2)), (self.gain, whole(6, C)), self.matrix(5), (self.picked, slots(rows, 2 * C)),
        ]
        outs = self.piece_out(5) + [(f32(OWN, rows, C), slots(rows))]
        which = PLACES[self.tag][5][0]
        *self.pieces[which], self.dxr = call(
            body, self.meta, args, outs, [pltpu.VMEM((rows, 2 * C), BF16), pltpu.VMEM((C, C), F32)],
            f"{self.tag}_residual_back", 12 * OWN * rows * C * C, into=self.pieces[which],
        )

    def piece_out(self, i):
        which, place = PLACES[self.tag][i]
        rows = PIECE_ROWS[self.tag][which]
        return [(f32(rows, C), pl.BlockSpec((C // 2, C), lambda m, *_: (place, 0)))] * 2

    def add_halves(self, meta, m, grad, total, kept_out, away_out):
        @pl.when(m == 0)
        def _():
            total[...] = grad

        @pl.when(m > 0)
        def _():
            top, bottom = total[0 : C // 2] + grad[0 : C // 2], total[C // 2 : C] + grad[C // 2 : C]
            lower = meta[2 * OWN] == 1
            kept_out[...] = jnp.where(lower, top, bottom)
            away_out[...] = jnp.where(lower, bottom, top)

    def weight_grad(self, i, dz, dy):
        two = self.two
        strided = i == 4 and not two
        rows = self.rows_of(i)
        n_src = len(self.source_args())

        def body(meta, *refs):
            refs = list(refs)
            take = lambda n: [refs.pop(0) for _ in range(n)]
            m = pl.program_id(0)
            dz_ref, dy_ref, dw_ref = take(3)
            if i:
                zp_ref, statp, gain, bias = take(4)
                center, spread = statp[0, 0:1], statp[0, 1:2]
                scale = gain[i - 1 : i] * spread
                shift = bias[i - 1 : i] - center * scale
            else:
                src = take(n_src)
            kept_out, away_out, taps_out, pad, yh, yl, total = take(7)
            alts = take(2) if strided else None
            valid_in = self.valid(meta, m, 0)
            taps = [[] for _ in range(TAPS)]
            for c, cs in enumerate(CHUNKS):
                if i:
                    u = zp_ref[0, :, cs] * scale[:, cs] + shift[:, cs]
                    h = valid_in.keep(u * sigmoid(u))
                else:
                    h = valid_in.keep(self.source(meta, src, cs))
                padded = Padded(pad.at[c], two)
                padded.put(h)
                grad = dy_ref[0, :, cs]
                if strided:
                    grad = spread_out(alts[0].at[c], grad)
                y = None
                for k in range(TAPS):
                    moved = padded.get(k - 2)
                    taps[k].append(column_sum(grad * moved))
                    term = dw_ref[0, k : k + 1, cs] * moved
                    y = term if y is None else y + term
                if strided:
                    y = every_other(alts[1].at[c], y)
                yh[:, cs], yl[:, cs] = halves(y)
            grad = stacked_outer(yh[...], yl[...], dz_ref[0, :, 0:C], dz_ref[0, :, C : 2 * C])
            taps = [jnp.concatenate(t, axis=1) for t in taps]

            self.add_halves(meta, m, grad, total, kept_out, away_out)

            @pl.when(m == 0)
            def _():
                for k in range(TAPS):
                    taps_out[k : k + 1, :] = taps[k]

            @pl.when(m > 0)
            def _():
                for k in range(TAPS):
                    taps_out[k : k + 1, :] += taps[k]

        args = [(dz, slots(rows, 2 * C)), (dy, slots(rows)), (self.dw, layer(i, TAPS, C))] + self.before_args(i)
        if i:
            args += [(self.gain, whole(6, C)), (self.bias, whole(6, C))]
        outs = self.piece_out(i) + [(f32(TAPS, C), whole(TAPS, C))]
        scratch = [pad_scratch(), pltpu.VMEM((rows, C), BF16), pltpu.VMEM((rows, C), BF16), pltpu.VMEM((C, C), F32)]
        if strided:
            scratch += [stride_scratch(), stride_scratch()]
        which = PLACES[self.tag][i][0]
        *self.pieces[which], self.dw_grad[i] = call(
            body, self.meta, args, outs, scratch, f"{self.tag}_weights_{i}", 6 * OWN * rows * C * C, into=self.pieces[which]
        )
        self.done = (self.dw_grad[i],)

    def backward(self, layers):
        if layers[0] == 4:
            self.pieces, self.dw_grad, self.done = [[], []], [None] * 5, ()
        for i in layers:
            result = self.backward_layer(i)
        return result

    def fork(self, state=None):
        other = copy.copy(self)
        other.__dict__.update(state or {})
        for name in ("pieces", "dw_grad", "locals"):
            if name in other.__dict__:
                setattr(other, name, list(getattr(other, name)))
        return other

    def state(self):
        names = ("du", "dt", "dq", "dp", "dxr", "back_got", "pieces", "dw_grad", "locals")
        return {name: getattr(self, name) for name in names}

    def half(self, no, small, first):
        kept, away = self.pieces[no]
        if small is not None:
            parts = small[: SMALL // 2], small[SMALL // 2 :]
            at = kept.shape[0] - SMALL // 2
            kept = lax.dynamic_update_slice_in_dim(kept, jnp.where(first, *parts), at, 0)
            away = lax.dynamic_update_slice_in_dim(away, jnp.where(first, *parts[::-1]), at, 0)
        return kept + swap(away)

    def small_grads(self, rows):
        means, p, _ = self.se_state
        flat = lambda x: x.reshape(-1, x.shape[-1])
        columns = lambda x: jnp.swapaxes(x, 0, 1).reshape(SE, -1)
        means, p, dq, dp = flat(means), columns(p), flat(self.dq), columns(self.dp)
        hidden = p * jax.nn.sigmoid(p)
        norms = [n[:2] for n in reversed(self.locals)] + [self.locals[0][2:]]
        down_b = jnp.pad(jnp.sum(dp, axis=1)[None], ((0, 0), (0, C - SE)))
        out = self.dw_grad + norms + [exact_dot(hidden, dq), exact_dot(dp, means)]
        out += [jnp.sum(dq, axis=0, keepdims=True), down_b]
        out = jnp.concatenate(out, axis=0)
        return jnp.pad(out, ((0, rows - out.shape[0]), (0, 0)))


PLACES = {
    "c15": {2: (0, 0), 3: (0, 1), 4: (0, 2), 5: (0, 3), 0: (1, 0), 1: (1, 1)},
    "c14": {3: (0, 0), 4: (0, 1), 5: (0, 2), 0: (1, 0), 1: (1, 1), 2: (1, 2)},
}
SMALL = 256
PIECE_ROWS = {"c15": (2 * C, C + SMALL // 2), "c14": (3 * C // 2, 3 * C // 2 + SMALL // 2)}


def swap(x):
    return lax.ppermute(x, "section", [(0, 1), (1, 0)])


def fenced(always, work, x):
    shapes = jax.eval_shape(work, x)
    return lax.cond(always, work, lambda x: jax.tree.map(lambda y: jnp.zeros(y.shape, y.dtype), shapes), x)


class Reduction:
    def __init__(self, x, stages):
        self.x = x
        self.todo = []
        stride = 1
        for radix in stages:
            self.todo.append((True, radix, stride))
            stride *= radix
        self.todo += [(False, radix, stride) for _, radix, stride in reversed(self.todo)]

    def step(self):
        scatter, radix, stride = self.todo.pop(0)
        rows = self.x.shape[0]
        if scatter:
            parts = exchange(self.x.reshape(radix, rows // radix, C), radix, stride)
            self.x = jnp.sum(parts, axis=0)
        else:
            parts = exchange(jnp.broadcast_to(self.x, (radix,) + self.x.shape), radix, stride)
            self.x = parts.reshape(radix * rows, C)
        return (self.x,)

    def finish(self):
        while self.todo:
            self.step()
        return self.x


def per_device(features, out_grad, lengths, join_pick, dw, pw, gain, bias, res_w, down, down_b, up, up_b):
    first = lax.axis_index("section") == 0
    size = lax.axis_size("dp")
    inputs = features.reshape(MB, SLOT, C)
    cotangent = out_grad.reshape(MB, SLOT, C)
    own, picks = lengths[0, 0], join_pick[0]
    to_upper = lambda x: lax.ppermute(x, "section", [(0, 1)])
    to_lower = lambda x: lax.ppermute(x, "section", [(1, 0)])

    far_len = swap(own)
    joining = jnp.concatenate([lax.dynamic_index_in_dim(inputs, picks[m], 0, False)[HALF:] for m in range(OWN)], axis=0)
    far_rows = swap(jnp.where(first, inputs[MB - 1], joining))
    far_w0 = swap(pw[0, 0:1])
    taps = jnp.concatenate([dw[0].reshape(5 * TAPS, C), gain[0], bias[0]], axis=0)
    far_taps = swap(taps)
    far_pw, far_res = swap(pw[0]), swap(res_w[0])
    wide = jnp.pad(down_b, ((0, 0), (0, C - SE)))
    squeeze = jnp.concatenate([down[0].T, up[0], up_b, wide], axis=0)
    far_squeeze = swap(squeeze)
    far_cot = to_lower(cotangent[:OWN])
    far_cot0 = to_upper(cotangent[MB - 1, :HALF])

    flag = first.astype(jnp.int32)[None]
    mine = lambda v: jnp.where(first, v[:OWN], jnp.concatenate([v[OWN:], jnp.zeros((1,), v.dtype)]))
    length = mine(jnp.where(first, own, far_len))
    half_len = (length + 1) // 2
    join_len = mine(jnp.where(first, far_len, own)[picks])
    meta1 = jnp.concatenate([length, half_len, flag])
    meta2 = jnp.concatenate([half_len, join_len, flag, picks[MB - 1 :]])

    def small(block):
        t = jnp.where(first == (block == 0), taps, far_taps)
        q = jnp.where(first == (block == 0), squeeze, far_squeeze)
        return (
            t[: 5 * TAPS].reshape(5, TAPS, C), t[5 * TAPS : 5 * TAPS + 6], t[5 * TAPS + 6 :],
            q[:SE], q[2 * SE + 1, :SE][:, None], q[SE : 2 * SE], q[2 * SE : 2 * SE + 1],
        )

    def prepared(block, start, stop):
        array = prepare(meta1, (pw[0], res_w[0]), (far_pw, far_res), block, start, stop)
        return array, {i: (array, i - start) for i in range(start, stop)}

    parts0 = [prepared(0, 1, 3), prepared(0, 3, 6)]
    parts1 = [prepared(1, 0, 3), prepared(1, 3, 6)]

    stages, deep = radices(size, 16), radices(size, 4)
    c14 = Block(False, meta1, small(0), {**parts0[0][1], **parts0[1][1]}, stages)
    c14.x, c14.x_far, c14.first_matrix = inputs, far_rows, (pw[0], far_w0)
    c14.forward({2: (parts0[1][0],), 4: (parts1[0][0],)})
    out0 = c14.tail(after=(parts1[1][0],))
    c15 = Block(True, meta2, small(1), {**parts1[0][1], **parts1[1][1]}, stages)
    c15.arrived, c15.joined_far, c15.joined = out0, far_rows, features.reshape(MB, 2, HALF, C)
    c15.forward()
    out1 = c15.tail(cotangent, far_cot)
    c15.backward((4, 3, 2))
    always = own[0] > 0

    half0 = c15.half(0, None, first)
    sum0 = lax.psum(half0, "dp")

    def middle(half0):
        upper, lower = c15.fork({"done": c15.done + (half0,)}), c14.fork()
        back, dx1 = upper.backward((1, 0))
        half1 = upper.half(1, upper.small_grads(SMALL), first)
        lower.tail_backward(cotangent, far_cot0, back)
        lower.backward((4, 3, 2))
        return dx1, half1, lower.half(0, None, first), lower.state()

    dx1, half1, half2, state = fenced(always, middle, half0)
    sum0, half2 = lax.optimization_barrier((sum0, half2))
    sum1, sum2 = lax.psum((half1, half2), "dp")
    came0 = to_upper(sum0)

    def ending(half2):
        last = c14.fork({**state, "done": (half2,)})
        dx0, = last.backward((1, 0))
        reduction = Reduction(last.half(1, last.small_grads(SMALL), first), deep)
        reduction.step()
        pad = jnp.zeros((1, HALF, C), F32)
        lower = jnp.concatenate([out0, jnp.concatenate([to_lower(out0[0:1, :HALF]), pad], axis=1)], axis=0)
        upper = jnp.concatenate([to_upper(out1), out1[0:1]], axis=0)
        block_out = jnp.where(first, lower, upper)
        lower = jnp.concatenate([dx0, to_lower(dx0[0:1])], axis=0)
        joins = jnp.concatenate([to_upper(dx1), dx1[0:1]], axis=0)
        joins = jnp.stack([lax.dynamic_index_in_dim(joins, jnp.argmax(picks == s), 0, False) for s in range(MB)])
        upper = jnp.concatenate([jnp.zeros_like(joins), joins], axis=1)
        dx = jnp.where(first, lower, upper)
        reduction.x, block_out, dx = lax.optimization_barrier((reduction.x, block_out, dx))
        sum3 = reduction.finish()
        return block_out, dx, sum3, to_lower(sum3)

    block_out, dx, sum3, came3 = fenced(always, ending, half2)
    sum1, sum2, sum3 = lax.optimization_barrier((sum1, sum2, sum3))
    came1, came2 = to_upper(sum1), to_lower(sum2)

    size3, size1 = 3 * C // 2, C
    mats14 = lambda a, b: jnp.concatenate([b[:size3], a[:C], a[C:size3]], axis=0)
    mats15 = lambda a, b: jnp.concatenate([b[:size1], a], axis=0)
    near = jnp.where(first, mats14(sum2, sum3), mats15(sum0, sum1)).reshape(6, 1, C // 2, C)
    far = jnp.where(first, mats14(came2, came3), mats15(came0, came1)).reshape(6, 1, C // 2, C)
    matrices = jnp.where(first, jnp.concatenate([near, far], axis=1), jnp.concatenate([far, near], axis=1))
    pw_grad, res_grad = matrices[:5].reshape(1, 5, C, C), matrices[5].reshape(1, C, C)
    near, far = jnp.where(first, sum3[size3:], sum1[size1:]), jnp.where(first, came3[size3:], came1[size1:])
    rows = jnp.where(first, jnp.concatenate([near, far], axis=0), jnp.concatenate([far, near], axis=0))
    dw_grad = rows[: 5 * TAPS].reshape(1, 5, TAPS, C)
    norms = rows[5 * TAPS : 5 * TAPS + 12].reshape(6, 2, C)
    rest = rows[5 * TAPS + 12 :]
    up_grad, down_grad = rest[:SE], rest[SE : 2 * SE].T
    up_b_grad, down_b_grad = rest[2 * SE : 2 * SE + 1], rest[2 * SE + 1 : 2 * SE + 2, :SE]
    return (
        block_out.reshape(features.shape), dx.reshape(features.shape), dw_grad, pw_grad,
        norms[None, :, 1], norms[None, :, 0], res_grad, down_grad[None], down_b_grad, up_grad[None], up_b_grad,
    )


def solution(mesh):
    rows = P("section", "dp", None)
    own = lambda dims: P("section", *([None] * dims))
    weights = (own(3), own(3), own(2), own(2), own(2), own(2), own(1), own(2), own(1))
    in_specs = (rows, rows, rows, P("dp", None), *weights)
    out_specs = (rows, rows, *weights)
    return jax.shard_map(per_device, mesh=mesh, in_specs=in_specs, out_specs=out_specs, check_vma=False)
```

```python
import copy

import jax
import jax.numpy as jnp
from jax import lax
from jax.experimental import pallas as pl
from jax.experimental.pallas import tpu as pltpu
from jax.sharding import PartitionSpec as P

EPSILON = 1e-05
EXACT = lax.Precision.HIGHEST
TAPS = 5
MB = 3
OWN = 2
SLOT = 400
HALF = 200
KEPT = 208
C = 512
LANES = 128
CHUNKS = [slice(c, c + LANES) for c in range(0, C, LANES)]
SE = 64
BF16, F32 = jnp.bfloat16, jnp.float32
VMEM_BYTES = 60 << 20
TAIL_ROWS = 2 * SE + 8
SMALL = 256


def radices(size, most):
    stages, left = [], size
    while left > 1:
        radix = min(most, left)
        while left % radix:
            radix -= 1
        stages.append(radix)
        left //= radix
    return stages


def exchange(block, radix, stride):
    size = lax.axis_size("dp")
    if radix == size:
        return lax.all_to_all(block, "dp", 0, 0)
    groups = []
    for base in range(size):
        if (base // stride) % radix == 0:
            groups.append([base + j * stride for j in range(radix)])
    return lax.all_to_all(block, "dp", 0, 0, axis_index_groups=groups)


def shared(block, stages):
    stride = 1
    for no, radix in enumerate(stages):
        if no:
            block = jnp.broadcast_to(jnp.sum(block, axis=0), (radix,) + block.shape[1:])
        block = exchange(block, radix, stride)
        stride *= radix
    return block


def halves(x):
    high = x.astype(BF16)
    return high, (x - high.astype(F32)).astype(BF16)


def sigmoid(x):
    return 0.5 * jnp.tanh(0.5 * x) + 0.5


def exact_dot(a, b, dims=((1,), (0,))):
    return lax.dot_general(a, b, (dims, ((), ())), precision=EXACT, preferred_element_type=F32)


def fast_dot(a, b, dims=((1,), (0,))):
    return lax.dot_general(a, b, (dims, ((), ())), preferred_element_type=F32)


def stacked_dot(high, low, w, back=False):
    w_high, w_low = w[0], w[1]
    w = jnp.concatenate([w_high, w_high, w_low], axis=1 if back else 0)
    x = jnp.concatenate([high, low, high], axis=1)
    return fast_dot(x, w, ((1,), (1 if back else 0,)))


def stacked_outer(a_high, a_low, b_high, b_low):
    a = jnp.concatenate([a_high, a_low, a_high], axis=0)
    b = jnp.concatenate([b_high, b_high, b_low], axis=0)
    return fast_dot(a, b, ((0,), (0,)))


def column_sum(x):
    return jnp.sum(x, axis=0, keepdims=True)


class Rows:
    def __init__(self, meta, m, two, rows, which=0):
        place = lax.broadcasted_iota(jnp.int32, (rows, LANES), 0)
        if two:
            later = place >= HALF
            limit = jnp.where(later, HALF + meta[OWN + m], meta[m])
            self.mask = place < limit
        else:
            self.mask = place < meta[which * OWN + m]

    def keep(self, x):
        return jnp.where(self.mask, x, 0.0)


class Padded:
    def __init__(self, ref, two):
        self.ref = ref
        self.pieces = [(8, 0, HALF), (16 + HALF, HALF, HALF)] if two else [(8, 0, SLOT)]

    def put(self, x):
        zeros = jnp.zeros((8, LANES), F32)
        for at, start, rows in self.pieces:
            self.ref[at - 8 : at, :] = zeros
            self.ref[at : at + rows, :] = x[start : start + rows]
        self.ref[at + rows : at + rows + 8, :] = zeros

    def get(self, offset):
        parts = [self.ref[at + offset : at + offset + rows, :] for at, _, rows in self.pieces]
        return parts[0] if len(parts) == 1 else jnp.concatenate(parts, axis=0)

    def conv(self, kernel):
        total = kernel[0:1] * self.get(-2)
        for k in range(1, TAPS):
            total = total + kernel[k : k + 1] * self.get(k - 2)
        return total

    def conv_back(self, kernel):
        total = kernel[0:1] * self.get(2)
        for k in range(1, TAPS):
            total = total + kernel[k : k + 1] * self.get(2 - k)
        return total


def every_other(ref, x):
    ref[0:SLOT, :] = x
    ref[SLOT : 2 * KEPT, :] = jnp.zeros((2 * KEPT - SLOT, LANES), F32)
    return ref[pl.ds(0, KEPT, stride=2), :]


def spread_out(ref, x):
    ref[...] = jnp.zeros_like(ref)
    ref[pl.ds(0, KEPT, stride=2), :] = x
    return ref[0:SLOT, :]


def center_spread(sums, rows):
    center = sums[0:1] / rows
    return center, lax.rsqrt(sums[1:2] / rows - center * center + EPSILON)


def added(ref):
    return jnp.sum(ref[:, 0], axis=0)


def accumulate(ref, m, at, value):
    rows = slice(at, at + value.shape[0])
    ref[rows, :] = jnp.where(m == 0, value, ref[rows, :] + value)


def send(ref, rows):
    for copy in range(ref.shape[0]):
        for row, x in enumerate(rows):
            ref[copy, 0, row : row + 1, 0 : x.shape[1]] = x


def pad_scratch():
    return pltpu.VMEM((len(CHUNKS), SLOT + 24, LANES), F32)


def stride_scratch():
    return pltpu.VMEM((len(CHUNKS), 2 * KEPT, LANES), F32)


def slots(rows, cols=C):
    return pl.BlockSpec((1, rows, cols), lambda m, *_: (m, 0, 0))


def copies(count, rows, cols=C):
    return pl.BlockSpec((count, 1, rows, cols), lambda m, *_: (0, m, 0, 0))


def whole(*shape):
    return pl.BlockSpec(shape, lambda m, *_: (0,) * len(shape))


def layer(i, *shape):
    return pl.BlockSpec((1,) + shape, lambda m, *_: (i,) + (0,) * len(shape))


def f32(*shape):
    return jax.ShapeDtypeStruct(shape, F32)


def bf16(*shape):
    return jax.ShapeDtypeStruct(shape, BF16)


class Streamed:
    def __init__(self, parts=2):
        self.parts = parts


class Fixed:
    def __init__(self, at):
        self.at = at


class Stream:
    def __init__(self, ref, buf, sem, parts):
        self.ref, self.buf, self.sem, self.parts = ref, buf, sem, parts
        self.width = buf.shape[2] // parts
        self.waited = set()

    def copy(self, m, part, out=False):
        cols = slice(part * self.width, (part + 1) * self.width)
        pair = [self.ref.at[m, :, cols], self.buf.at[m, :, cols]]
        return pltpu.make_async_copy(*(pair[::-1] if out else pair), self.sem.at[m, part])

    def ready(self, m, cs):
        part = cs.start // self.width
        if part not in self.waited:
            self.waited.add(part)
            self.copy(m, part).wait()

    def chunk(self, m, cs):
        self.ready(m, cs)
        return self.buf[m, :, cs]

    def sent(self, m, cs):
        if cs.stop % self.width == 0:
            self.copy(m, cs.stop // self.width - 1, out=True).start()


class Entry:
    def __init__(self, ref, buf, sem, at):
        self.buf = buf
        self.copy = pltpu.make_async_copy(ref.at[at], buf, sem.at[0])

    def load(self, m):
        pl.when(m == 0)(self.copy.wait)
        return self.buf


def call(body, meta, args, outs, scratch=(), name=None, flops=0, steps=OWN, after=(), into=()):
    arrays, in_specs = [a for a, _ in args], [s for _, s in args]
    shapes, out_specs = [a for a, _ in outs], [s for _, s in outs]
    size = sum(a.size * a.dtype.itemsize for a in arrays + shapes)
    extra = list(after) + list(into)
    count, skip = len(arrays), len(arrays) + len(extra)
    scratch, auto = list(scratch), []
    for a, spec in zip(arrays + shapes, in_specs + out_specs):
        if isinstance(spec, Streamed):
            auto += [pltpu.VMEM(a.shape, a.dtype), pltpu.SemaphoreType.DMA((a.shape[0], spec.parts))]
        elif isinstance(spec, Fixed):
            auto += [pltpu.VMEM(a.shape[1:], a.dtype), pltpu.SemaphoreType.DMA((1,))]
    anywhere = pl.BlockSpec(memory_space=pl.ANY)
    plain = lambda spec: anywhere if isinstance(spec, (Streamed, Fixed)) else spec

    def inner(meta, *refs):
        held = list(refs[len(refs) - len(auto) :])

        def wrap(ref, spec):
            if isinstance(spec, Streamed):
                return Stream(ref, held.pop(0), held.pop(0), spec.parts)
            if isinstance(spec, Fixed):
                return Entry(ref, held.pop(0), held.pop(0), spec.at)
            return ref

        ins = [wrap(r, s) for r, s in zip(refs[:count], in_specs)]
        results = [wrap(r, s) for r, s in zip(refs[skip : skip + len(shapes)], out_specs)]
        m = pl.program_id(0)

        @pl.when(m == 0)
        def _():
            for slot in range(OWN):
                for ref in ins:
                    if isinstance(ref, Stream):
                        for part in range(ref.parts):
                            ref.copy(slot, part).start()
                    elif isinstance(ref, Entry) and slot == 0:
                        ref.copy.start()

        body(meta, *ins, *results, *refs[skip + len(shapes) : len(refs) - len(auto)])

        @pl.when(m == steps - 1)
        def _():
            for ref in results:
                if isinstance(ref, Stream):
                    for slot in range(OWN):
                        for part in range(ref.parts):
                            ref.copy(slot, part, out=True).wait()

    return pl.pallas_call(
        inner,
        out_shape=shapes,
        grid_spec=pltpu.PrefetchScalarGridSpec(
            num_scalar_prefetch=1,
            grid=(steps,),
            in_specs=[plain(spec) for spec in in_specs] + [anywhere] * len(extra),
            out_specs=[plain(spec) for spec in out_specs],
            scratch_shapes=scratch + auto,
        ),
        input_output_aliases={1 + count + len(after) + j: j for j in range(len(into))},
        compiler_params=pltpu.CompilerParams(vmem_limit_bytes=VMEM_BYTES),
        cost_estimate=pl.CostEstimate(flops=flops, bytes_accessed=size, transcendentals=0),
        name=name,
    )(meta, *arrays, *extra)


def choose(meta, block, own, far):
    return jnp.where(meta[2 * OWN] == 1 - block, own, far)


def prepare(meta, own, far, block, start, stop):
    def body(meta, *refs):
        pair = [ref[0] for ref in refs[:2]]
        if stop == 6:
            last = pl.program_id(0) == 5 - start
            pair = [jnp.where(last, ref[...], w) for ref, w in zip(refs[2:4], pair)]
        out = refs[-1]
        out[0, 0], out[0, 1] = halves(choose(meta, block, *pair))

    matrix = pl.BlockSpec((1, C, C), lambda j, *_: (jnp.minimum(j + start, 4), 0, 0))
    args = [(own[0], matrix), (far[0], matrix)]
    if stop == 6:
        args += [(own[1], whole(C, C)), (far[1], whole(C, C))]
    out = pl.BlockSpec((1, 2, C, C), lambda j, *_: (j, 0, 0, 0))
    name = f"prepare_{block}_{start}"
    return call(body, meta, args, [(bf16(stop - start, 2, C, C), out)], name=name, steps=stop - start)[0]


class Block:
    def __init__(self, two, meta, weights, ready, stages):
        self.done, self.stop_sum = (), None
        self.two, self.meta, self.stages = two, meta, stages
        self.dw, self.gain, self.bias, self.down, self.down_b, self.up, self.up_b = weights
        self.ready = ready
        self.tail_rows = SLOT if two else KEPT
        self.first, self.last = stages[0], stages[-1]
        self.tag = "c15" if two else "c14"

    def rows_of(self, i):
        return self.tail_rows if i == 4 else SLOT

    def valid(self, meta, m, i):
        last = i == 4 and not self.two
        return Rows(meta, m, self.two, self.rows_of(i), which=1 if last else 0)

    def matrix(self, i):
        array, at = self.ready[i]
        return (array, Fixed(at))

    def source_args(self):
        if not self.two:
            return [(self.x, slots(SLOT)), (self.x_far, whole(SLOT, C))]
        far = pl.BlockSpec((HALF, C), lambda m, *_: (m, 0))
        near = pl.BlockSpec((1, 1, HALF, C), lambda m, meta: (meta[2 * OWN + 1], 1, 0, 0))
        return [(self.arrived, slots(HALF)), (self.joined_far, far), (self.joined, near)]

    def source(self, meta, refs, cs):
        lower = meta[2 * OWN] == 1
        if not self.two:
            return jnp.where(lower, refs[0][0, :, cs], refs[1][:, cs])
        joined = jnp.where(lower, refs[1][:, cs], refs[2][0, 0, :, cs])
        return jnp.concatenate([refs[0][0, :, cs], joined], axis=0)

    def before_args(self, i):
        if i == 0:
            return self.source_args()
        return [(self.z[i - 1], Streamed()), (self.stats[i - 1], slots(2))]


    def forward_layer(self, i, after=()):
        two, count = self.two, self.first
        strided = i == 4 and not two
        rows = self.rows_of(i)
        n_src = len(self.source_args())
        width = C + LANES if i == 0 else C
        sent = 4 if i == 3 else 2
        makes = i == 0 and not two

        def body(meta, *refs):
            refs = list(refs)
            take = lambda n: [refs.pop(0) for _ in range(n)]
            m = pl.program_id(0)
            if i == 0:
                src = take(n_src)
            else:
                z_ref, got_ref = take(2)
                n_ref, = take(1) if i > 1 else (None,)
                gain_ref, bias_ref = take(2)
                res_sum, = take(1) if i == 3 else (None,)
            dw_ref, = take(1)
            if makes:
                own_ref, far_ref, z_out, pay, w_ref = take(5)

                @pl.when(m == 0)
                def _():
                    w_ref[0, 0], w_ref[0, 1] = halves(choose(meta, 0, own_ref[0], far_ref[0]))

            else:
                w_ref, z_out, pay = take(3)
            if i:
                stat_out, = take(1)
            if i == 1:
                n_out, = take(1)
            pad, y_ref = take(2)
            alt, = take(1) if strided else (None,)
            valid_in = self.valid(meta, m, 0)
            if i:
                sums = added(got_ref)
                if i == 1:
                    count_in = jnp.maximum(jnp.concatenate([sums[0:1, C:]] * len(CHUNKS), axis=1), 1.0)
                    count_out = jnp.maximum(jnp.concatenate([sums[1:2, C:]] * len(CHUNKS), axis=1), 1.0)
                    n_out[0, 0:1, :] = count_in
                    n_out[0, 1:2, :] = count_out
                else:
                    count_in = n_ref[0, 0:1, :]
                center, spread = center_spread(sums[:, :C], count_in)
                stat_out[0, 0:1, :] = center
                stat_out[0, 1:2, :] = spread
                scale = gain_ref[i - 1 : i] * spread
                shift = bias_ref[i - 1 : i] - center * scale
            for c, cs in enumerate(CHUNKS):
                if i == 0:
                    h = valid_in.keep(self.source(meta, src, cs))
                else:
                    u = z_ref.chunk(m, cs) * scale[:, cs] + shift[:, cs]
                    h = valid_in.keep(u * sigmoid(u))
                padded = Padded(pad.at[c], two)
                padded.put(h)
                y = padded.conv(dw_ref[0, :, cs])
                if strided:
                    y = every_other(alt.at[c], y)
                high, low = halves(y)
                y_ref[:, cs] = high
                y_ref[:, C + cs.start : C + cs.stop] = low
            w = w_ref.at[0] if makes else w_ref.load(m)
            z = stacked_dot(y_ref[:, 0:C], y_ref[:, C : 2 * C], w)
            z_out.buf[m] = z
            z_out.sent(m, slice(0, C))
            valid = self.valid(meta, m, i)
            one, square = [], []
            for cs in CHUNKS:
                kept = valid.keep(z[:, cs])
                one.append(column_sum(kept))
                square.append(column_sum(kept * kept))
            if i == 0:
                if two:
                    number = (meta[m] + meta[OWN + m]).astype(F32)
                    numbers = number, number
                else:
                    numbers = meta[m].astype(F32), meta[OWN + m].astype(F32)
                one.append(jnp.full((1, LANES), numbers[0], F32))
                square.append(jnp.full((1, LANES), numbers[1], F32))
            out = [jnp.concatenate(one, axis=1), jnp.concatenate(square, axis=1)]
            if i == 3:
                out += [res_sum[0, 0:1, :], res_sum[0, 1:2, :]]
            send(pay, out)

        if i == 0:
            args = list(self.source_args())
        else:
            got = 4 if i == 4 else 2
            args = [(self.z[i - 1], Streamed()), (self.got[i - 1], copies(self.last, got, C + LANES if i == 1 else C))]
            if i > 1:
                args.append((self.number, slots(2)))
            args += [(self.gain, whole(6, C)), (self.bias, whole(6, C))]
            if i == 3:
                args.append((self.res_sum, slots(2)))
        args.append((self.dw, layer(i, TAPS, C)))
        args += [(w, layer(0, C, C)) for w in self.first_matrix] if makes else [self.matrix(i)]
        outs = [(f32(OWN, rows, C), Streamed(1)), (f32(count, OWN, sent, width), copies(count, sent, width))]
        if i:
            outs.append((f32(OWN, 2, C), slots(2)))
        if i == 1:
            outs.append((f32(OWN, 2, C), slots(2)))
        if makes:
            outs.append((bf16(1, 2, C, C), layer(0, 2, C, C)))
        scratch = [pad_scratch(), pltpu.VMEM((rows, 2 * C), BF16)]
        if strided:
            scratch.append(stride_scratch())
        result = call(body, self.meta, args, outs, scratch, f"{self.tag}_forward_{i}", 6 * OWN * rows * C * C, after=after)
        self.z.append(result[0])
        if makes:
            self.ready[0] = (result[2], 0)
        if i:
            self.stats.append(result[2])
        if i == 1:
            self.number = result[3]
        self.got.append(shared(result[1], self.stages))

    def residual(self):
        two, rows = self.two, self.tail_rows

        def body(meta, *refs):
            refs = list(refs)
            src = [refs.pop(0) for _ in self.source_args()]
            w_ref, r_out, x_out, sum_out = refs[:4]
            alt = refs[4] if not two else None
            m = pl.program_id(0)
            valid_in = self.valid(meta, m, 0)
            for c, cs in enumerate(CHUNKS):
                x = valid_in.keep(self.source(meta, src, cs))
                if not two:
                    x = every_other(alt.at[c], x)
                high, low = halves(x)
                x_out[0, :, cs] = high
                x_out[0, :, C + cs.start : C + cs.stop] = low
            r = stacked_dot(x_out[0, :, 0:C], x_out[0, :, C : 2 * C], w_ref.load(m))
            r_out[0] = r
            valid = self.valid(meta, m, 4)
            for cs in CHUNKS:
                kept = valid.keep(r[:, cs])
                sum_out[0, 0:1, cs] = column_sum(kept)
                sum_out[0, 1:2, cs] = column_sum(kept * kept)

        args = self.source_args() + [self.matrix(5)]
        outs = [
            (f32(OWN, rows, C), slots(rows)),
            (bf16(OWN, rows, 2 * C), slots(rows, 2 * C)),
            (f32(OWN, 2, C), slots(2)),
        ]
        scratch = [] if two else [stride_scratch()]
        self.r, self.picked, self.res_sum = call(
            body, self.meta, args, outs, scratch, f"{self.tag}_residual", 6 * OWN * rows * C * C
        )

    def forward(self, after=None):
        self.z, self.got, self.stats = [], [], []
        for i in range(5):
            if i == 2:
                self.residual()
            self.forward_layer(i, (after or {}).get(i, ()))


    def segments(self):
        return [(0, HALF), (HALF, HALF)] if self.two else [(0, self.tail_rows)]

    def lengths(self, meta, m):
        if self.two:
            return [meta[m], meta[OWN + m]]
        return [meta[OWN + m]]

    def squeeze(self, sums, counts, se_refs):
        down_t, down_b, up, up_b = se_refs
        means = [s / jnp.maximum(jnp.full((1, C), n.astype(F32)), 1.0) for s, n in zip(sums, counts)]
        ps = [jnp.sum(down_t[...] * mean, axis=1, keepdims=True) + down_b[...] for mean in means]
        gates = [sigmoid(column_sum(up[...] * (p * sigmoid(p))) + up_b[...]) for p in ps]
        return means, ps, gates

    def squeeze_back(self, des, ps, gates, counts, se_refs, means, small, m):
        down_t, down_b, up, up_b = se_refs
        shares, up_grad, down_grad, dq_sum, dp_sum = [], 0.0, 0.0, 0.0, 0.0
        for de, p, gate, n, mean in zip(des, ps, gates, counts, means):
            dq = de * gate * (1.0 - gate)
            s = sigmoid(p)
            dp = jnp.sum(up[...] * dq, axis=1, keepdims=True) * (s * (1.0 + p * (1.0 - s)))
            shares.append(column_sum(down_t[...] * dp) / jnp.maximum(jnp.full((1, C), n.astype(F32)), 1.0))
            up_grad, down_grad = up_grad + (p * s) * dq, down_grad + dp * mean
            dq_sum, dp_sum = dq_sum + dq, dp_sum + dp
        row, col = (lax.broadcasted_iota(jnp.int32, (SE, C), axis) for axis in (0, 1))
        dp_row = column_sum(jnp.where(row == col, dp_sum, 0.0))
        accumulate(small, m, 0, up_grad)
        accumulate(small, m, SE, down_grad)
        accumulate(small, m, 2 * SE, dq_sum)
        accumulate(small, m, 2 * SE + 1, dp_row)
        return shares

    def last_norm(self, m, dt_out, du_out, z_ref, slope_ref, gates, shares, center, spread, res_bias, res_gain, pay, small):
        bias_sum, gain_sum = [], []
        for cs in CHUNKS:
            dh = dt_out.buf[m, :, cs] * self.by_segment(gates, cs) + self.by_segment(shares, cs)
            du = dh * slope_ref[:, cs]
            du_out.buf[m, :, cs] = du
            du_out.sent(m, cs)
            bias_sum.append(column_sum(du))
            gain_sum.append(column_sum(du * ((z_ref.chunk(m, cs) - center[:, cs]) * spread[:, cs])))
        rows = [jnp.concatenate(x, axis=1) for x in (bias_sum, gain_sum, res_bias, res_gain)]
        send(pay, rows)
        for j, row in enumerate(rows):
            accumulate(small, m, 2 * SE + 2 + j, row)

    def se_args(self):
        return [(self.down, whole(SE, C)), (self.down_b, whole(SE, 1)), (self.up, whole(SE, C)), (self.up_b, whole(1, C))]

    def store_rows(self, ref, rows):
        ref[0] = jnp.concatenate(rows + [jnp.zeros((8 - len(rows), C), F32)], axis=0)

    def store_columns(self, ref, columns):
        ref[0] = jnp.zeros((SE, 8), F32)
        for j, column in enumerate(columns):
            ref[0, :, j : j + 1] = column

    def by_segment(self, rows, cs):
        parts = [jnp.broadcast_to(row[:, cs], (n, LANES)) for row, (_, n) in zip(rows, self.segments())]
        return parts[0] if len(parts) == 1 else jnp.concatenate(parts, axis=0)

    def seg_sums(self, x):
        return [column_sum(x[at : at + n]) for at, n in self.segments()]

    def tail(self, cotangent=None, far=None, after=()):
        two, rows = self.two, self.tail_rows
        back = cotangent is not None

        def body(meta, *refs):
            refs = list(refs)
            take = lambda n: [refs.pop(0) for _ in range(n)]
            m = pl.program_id(0)
            z_ref, got4, r_ref, got3, n_ref, gain, bias = take(7)
            se_refs = take(4)
            if back:
                cot_ref, far_ref = take(2)
            out, stat_out, rstat_out, means_out, p_out, gate_out = take(6)
            if back:
                small, du_out, dt_out, pay = take(4)
            h_ref, = take(1)
            if back:
                slope_ref, = take(1)
            valid = self.valid(meta, m, 4)
            number = n_ref[0, 1:2, :]
            center, spread = center_spread(added(got4), number)
            rcenter, rspread = center_spread(added(got3)[2:4], number)
            stat_out[0, 0:1, :] = center
            stat_out[0, 1:2, :] = spread
            rstat_out[0, 0:1, :] = rcenter
            rstat_out[0, 1:2, :] = rspread
            scale = gain[4:5] * spread
            shift = bias[4:5] - center * scale
            sums = []
            for cs in CHUNKS:
                u = z_ref.chunk(m, cs) * scale[:, cs] + shift[:, cs]
                s = sigmoid(u)
                h = valid.keep(u * s)
                h_ref[:, cs] = h
                if back:
                    slope_ref[:, cs] = valid.keep(s * (1.0 + u * (1.0 - s)))
                sums.append(self.seg_sums(h))
            sums = [jnp.concatenate([s[j] for s in sums], axis=1) for j in range(len(self.segments()))]
            counts = self.lengths(meta, m)
            means, ps, gates = self.squeeze(sums, counts, se_refs)
            self.store_rows(means_out, means)
            self.store_columns(p_out, ps)
            self.store_rows(gate_out, gates)
            res_gain, res_bias, gate_grad = [], [], []
            for cs in CHUNKS:
                h = h_ref[:, cs]
                rh = (r_ref.chunk(m, cs) - rcenter[:, cs]) * rspread[:, cs]
                t = h * self.by_segment(gates, cs) + gain[5:6, cs] * rh + bias[5:6, cs]
                s = sigmoid(t)
                out.buf[m, 0:rows, cs] = valid.keep(t * s)
                if rows < SLOT:
                    out.buf[m, rows:SLOT, cs] = jnp.zeros((SLOT - rows, LANES), F32)
                out.sent(m, cs)
                if back:
                    own_cot = cot_ref.load(m) if cs.start == 0 else cot_ref.buf
                    cot = jnp.where(meta[2 * OWN] == 1, far_ref.chunk(m, cs), own_cot[:, cs])
                    dt = valid.keep(cot * (s * (1.0 + t * (1.0 - s))))
                    dt_out.buf[m, :, cs] = dt
                    dt_out.sent(m, cs)
                    res_bias.append(column_sum(dt))
                    res_gain.append(column_sum(dt * rh))
                    gate_grad.append(self.seg_sums(dt * h))
            if not back:
                return
            des = [jnp.concatenate([g[j] for g in gate_grad], axis=1) for j in range(len(counts))]
            shares = self.squeeze_back(des, ps, gates, counts, se_refs, means, small, m)
            self.last_norm(m, dt_out, du_out, z_ref, slope_ref, gates, shares, center, spread, res_bias, res_gain, pay, small)

        args = [
            (self.z[4], Streamed()), (self.got[4], copies(self.last, 2)), (self.r, Streamed()),
            (self.got[3], copies(self.last, 4)), (self.number, slots(2)),
            (self.gain, whole(6, C)), (self.bias, whole(6, C)),
        ] + self.se_args()
        outs = [
            (f32(OWN, SLOT, C), Streamed()), (f32(OWN, 2, C), slots(2)), (f32(OWN, 2, C), slots(2)),
            (f32(OWN, 8, C), slots(8)), (f32(OWN, SE, 8), slots(SE, 8)), (f32(OWN, 8, C), slots(8)),
        ]
        scratch = [pltpu.VMEM((rows, C), F32)]
        if back:
            args += [(cotangent, Fixed(MB - 1)), (far, Streamed())]
            outs += self.tail_outs()
            scratch.append(pltpu.VMEM((rows, C), F32))
        result = call(body, self.meta, args, outs, scratch, f"{self.tag}_tail", after=after)
        self.stats.append(result[1])
        self.rstat, self.se_state = result[2], result[3:6]
        if back:
            self.tail_results(result[6:])
        return result[0]

    def tail_outs(self):
        rows, count = self.tail_rows, self.first
        return [
            (f32(SMALL, C), whole(TAIL_ROWS, C)), (f32(OWN, rows, C), Streamed()), (f32(OWN, rows, C), Streamed()),
            (f32(count, OWN, 4, C), copies(count, 4)),
        ]

    def tail_results(self, result):
        self.small, self.du, self.dt, pay = result
        self.back_got = shared(pay, self.stages)

    def tail_backward(self, cotangent, far, back):
        rows = self.tail_rows

        def body(meta, z_ref, r_ref, stat, rstat, gain, bias, means_ref, p_ref, gate_ref, down, down_b, up, up_b, cot_ref, far_ref, back_ref,
                 small, du_out, dt_out, pay, slope_ref):
            m = pl.program_id(0)
            valid = self.valid(meta, m, 4)
            center, spread, rcenter, rspread = stat[0, 0:1], stat[0, 1:2], rstat[0, 0:1], rstat[0, 1:2]
            scale = gain[4:5] * spread
            shift = bias[4:5] - center * scale
            zeros = jnp.zeros((rows - HALF, LANES), F32)
            counts = self.lengths(meta, m)
            ps = [p_ref[0, :, j : j + 1] for j in range(len(counts))]
            gates = [gate_ref[0, j : j + 1, :] for j in range(len(counts))]
            means = [means_ref[0, j : j + 1, :] for j in range(len(counts))]
            res_gain, res_bias, gate_grad = [], [], []
            for cs in CHUNKS:
                u = z_ref.chunk(m, cs) * scale[:, cs] + shift[:, cs]
                s = sigmoid(u)
                h = valid.keep(u * s)
                slope_ref[:, cs] = valid.keep(s * (1.0 + u * (1.0 - s)))
                rh = (r_ref.chunk(m, cs) - rcenter[:, cs]) * rspread[:, cs]
                t = h * self.by_segment(gates, cs) + gain[5:6, cs] * rh + bias[5:6, cs]
                s = sigmoid(t)
                here = jnp.where(meta[2 * OWN] == 1, cot_ref[0, 0:HALF, cs], far_ref[:, cs])
                cot = jnp.concatenate([here + back_ref[0, :, cs], zeros], axis=0)
                dt = valid.keep(cot * (s * (1.0 + t * (1.0 - s))))
                dt_out.buf[m, :, cs] = dt
                dt_out.sent(m, cs)
                res_bias.append(column_sum(dt))
                res_gain.append(column_sum(dt * rh))
                gate_grad.append(self.seg_sums(dt * h))
            des = [jnp.concatenate([g[j] for g in gate_grad], axis=1) for j in range(len(counts))]
            shares = self.squeeze_back(des, ps, gates, counts, (down, down_b, up, up_b), means, small, m)
            self.last_norm(m, dt_out, du_out, z_ref, slope_ref, gates, shares, center, spread, res_bias, res_gain, pay, small)

        args = [
            (self.z[4], Streamed()), (self.r, Streamed()), (self.stats[4], slots(2)), (self.rstat, slots(2)),
            (self.gain, whole(6, C)), (self.bias, whole(6, C)),
            (self.se_state[0], slots(8)), (self.se_state[1], slots(SE, 8)), (self.se_state[2], slots(8)),
        ] + self.se_args() + [(cotangent, slots(SLOT)), (far, whole(HALF, C)), (back, slots(HALF))]
        scratch = [pltpu.VMEM((rows, C), F32)]
        self.tail_results(call(body, self.meta, args, self.tail_outs(), scratch, f"{self.tag}_tail_back"))


    def norm_grad(self, du, zh, scale, sums, number, cs):
        return scale[:, cs] * (du - sums[0:1, cs] / number[:, cs] - zh * (sums[1:2, cs] / number[:, cs]))

    def backward_layer(self, i):
        two, count = self.two, self.first
        strided = i == 4 and not two
        rows = self.rows_of(i)
        n_src = len(self.source_args())

        def body(meta, *refs):
            refs = list(refs)
            take = lambda n: [refs.pop(0) for _ in range(n)]
            m = pl.program_id(0)
            du_ref, z_ref, w_ref, got, n_ref, stat, gain, bias, dw_ref = take(9)
            if i:
                zp_ref, statp = take(2)
            else:
                dxr_ref, = take(1)
                src = take(n_src)
            small, dz_out = take(2)
            if i:
                du_out, pay = take(2)
            elif two:
                back_out, dx_out = take(2)
            else:
                dx_out, = take(1)
            pad, = take(1)
            alt, = take(1) if refs else (None,)
            sums = added(got)
            number = n_ref[0, 1:2, :] if i == 4 else n_ref[0, 0:1, :]
            center, spread = stat[0, 0:1], stat[0, 1:2]
            scale = gain[i : i + 1] * spread
            valid = self.valid(meta, m, i)
            for cs in CHUNKS:
                zh = (z_ref.chunk(m, cs) - center[:, cs]) * spread[:, cs]
                dz = valid.keep(self.norm_grad(du_ref.chunk(m, cs), zh, scale, sums, number, cs))
                high, low = halves(dz)
                dz_out.buf[m, :, cs] = high
                dz_out.buf[m, :, C + cs.start : C + cs.stop] = low
            dz_out.sent(m, slice(0, 2 * C))
            dy = stacked_dot(dz_out.buf[m, :, 0:C], dz_out.buf[m, :, C : 2 * C], w_ref.load(m), True)
            valid_in = self.valid(meta, m, 0)
            if i:
                pcenter, pspread = statp[0, 0:1], statp[0, 1:2]
                pscale = gain[i - 1 : i] * pspread
                pshift = bias[i - 1 : i] - pcenter * pscale
            taps, bias_sum, gain_sum = [[] for _ in range(TAPS)], [], []
            for c, cs in enumerate(CHUNKS):
                grad = dy[:, cs]
                if strided:
                    grad = spread_out(alt.at[c], grad)
                padded = Padded(pad.at[c], two)
                padded.put(grad)
                if i:
                    z = zp_ref.chunk(m, cs)
                    u = z * pscale[:, cs] + pshift[:, cs]
                    s = sigmoid(u)
                    h = valid_in.keep(u * s)
                else:
                    h = valid_in.keep(self.source(meta, src, cs))
                dh = None
                for k in range(TAPS):
                    moved = padded.get(2 - k)
                    taps[k].append(column_sum(h * moved))
                    term = dw_ref[0, k : k + 1, cs] * moved
                    dh = term if dh is None else dh + term
                if i:
                    du = valid_in.keep(dh * (s * (1.0 + u * (1.0 - s))))
                    du_out.buf[m, :, cs] = du
                    du_out.sent(m, cs)
                    bias_sum.append(column_sum(du))
                    gain_sum.append(column_sum(du * ((z - pcenter[:, cs]) * pspread[:, cs])))
                    continue
                dxr = dxr_ref.chunk(m, cs)
                if not two:
                    dxr = spread_out(alt.at[c], dxr)
                dx = valid_in.keep(dh) + dxr
                if two:
                    back_out.buf[m, :, cs] = dx[:HALF]
                    back_out.sent(m, cs)
                    dx = dx[HALF:]
                dx_out.buf[m, :, cs] = dx
                dx_out.sent(m, cs)
            rows = taps + [bias_sum, gain_sum] if i else taps
            rows = [jnp.concatenate(x, axis=1) for x in rows]
            for j, row in enumerate(rows):
                accumulate(small, m, j, row)
            if i:
                send(pay, rows[TAPS:])

        sent = 4 if i == 4 else 2
        args = [
            (self.du, Streamed()), (self.z[i], Streamed()), self.matrix(i), (self.back_got, copies(self.last, sent)),
            (self.number, slots(2)), (self.stats[i], slots(2)), (self.gain, whole(6, C)), (self.bias, whole(6, C)),
            (self.dw, layer(i, TAPS, C)),
        ]
        if not i:
            args.append((self.dxr, Streamed()))
        args += self.before_args(i)
        place = TAIL_ROWS // 8 + i
        outs = [(f32(SMALL, C), pl.BlockSpec((8, C), lambda m, *_: (place, 0))), (bf16(OWN, rows, 2 * C), Streamed(1))]
        if i:
            outs += [(f32(OWN, SLOT, C), Streamed()), (f32(count, OWN, 2, C), copies(count, 2))]
        elif two:
            outs += [(f32(OWN, HALF, C), Streamed()), (f32(OWN, HALF, C), Streamed())]
        else:
            outs += [(f32(OWN, SLOT, C), Streamed())]
        scratch = [pad_scratch()]
        if strided or (i == 0 and not two):
            scratch.append(stride_scratch())
        self.small, dz, *result = call(
            body, self.meta, args, outs, scratch, f"{self.tag}_backward_{i}", 6 * OWN * rows * C * C,
            after=self.done, into=(self.small,),
        )
        got = self.back_got
        if i:
            self.du = result[0]
            if self.stop_sum == i:
                self.pending = i, dz, result[1]
                return result
            self.back_got = shared(result[1], self.stages)
        self.weight_grad(i, dz)
        if i == 4:
            self.residual_back(got)
        return result

    def residual_back(self, got):
        rows = self.tail_rows

        def body(meta, got, n_ref, dt_ref, r_ref, rstat, gain, w_ref, x_ref, kept_out, away_out, dxr_out, dr, total):
            m = pl.program_id(0)
            sums = added(got)[2:4]
            number = n_ref[0, 1:2, :]
            center, spread = rstat[0, 0:1], rstat[0, 1:2]
            scale = gain[5:6] * spread
            valid = self.valid(meta, m, 4)
            for cs in CHUNKS:
                rh = (r_ref[0, :, cs] - center[:, cs]) * spread[:, cs]
                high, low = halves(valid.keep(self.norm_grad(dt_ref[0, :, cs], rh, scale, sums, number, cs)))
                dr[:, cs] = high
                dr[:, C + cs.start : C + cs.stop] = low
            high, low = dr[:, 0:C], dr[:, C : 2 * C]
            dxr_out[0] = stacked_dot(high, low, w_ref.load(m), True)
            grad = stacked_outer(x_ref[0, :, 0:C], x_ref[0, :, C : 2 * C], high, low)
            self.add_halves(meta, m, grad, total, kept_out, away_out)

        args = [
            (got, copies(self.last, 4)), (self.number, slots(2)), (self.dt, slots(rows)), (self.r, slots(rows)),
            (self.rstat, slots(2)), (self.gain, whole(6, C)), self.matrix(5), (self.picked, slots(rows, 2 * C)),
        ]
        outs = self.piece_out(5) + [(f32(OWN, rows, C), slots(rows))]
        which = PLACES[5][0]
        *self.pieces[which], self.dxr = call(
            body, self.meta, args, outs, [pltpu.VMEM((rows, 2 * C), BF16), pltpu.VMEM((C, C), F32)],
            f"{self.tag}_residual_back", 12 * OWN * rows * C * C, into=self.pieces[which],
        )

    def piece_out(self, i):
        which, place = PLACES[i]
        rows = PIECE_ROWS[which]
        return [(f32(rows, C), pl.BlockSpec((C // 2, C), lambda m, *_: (place, 0)))] * 2

    def add_halves(self, meta, m, grad, total, kept_out, away_out):
        @pl.when(m == 0)
        def _():
            total[...] = grad

        @pl.when(m > 0)
        def _():
            top, bottom = total[0 : C // 2] + grad[0 : C // 2], total[C // 2 : C] + grad[C // 2 : C]
            lower = meta[2 * OWN] == 1
            kept_out[...] = jnp.where(lower, top, bottom)
            away_out[...] = jnp.where(lower, bottom, top)

    def weight_grad(self, i, dz):
        two = self.two
        strided = i == 4 and not two
        rows = self.rows_of(i)
        n_src = len(self.source_args())

        def body(meta, *refs):
            refs = list(refs)
            take = lambda n: [refs.pop(0) for _ in range(n)]
            m = pl.program_id(0)
            if i:
                zp_ref, statp, gain, bias = take(4)
                center, spread = statp[0, 0:1], statp[0, 1:2]
                scale = gain[i - 1 : i] * spread
                shift = bias[i - 1 : i] - center * scale
            else:
                src = take(n_src)
            dz_ref, dw_ref, kept_out, away_out, pad, yh, yl, total = take(8)
            alt, = take(1) if strided else (None,)
            valid_in = self.valid(meta, m, 0)
            for c, cs in enumerate(CHUNKS):
                if i:
                    u = zp_ref.chunk(m, cs) * scale[:, cs] + shift[:, cs]
                    h = valid_in.keep(u * sigmoid(u))
                else:
                    h = valid_in.keep(self.source(meta, src, cs))
                padded = Padded(pad.at[c], two)
                padded.put(h)
                y = padded.conv(dw_ref[0, :, cs])
                if strided:
                    y = every_other(alt.at[c], y)
                yh[:, cs], yl[:, cs] = halves(y)
            dz_ref.ready(m, slice(0, C))
            grad = stacked_outer(yh[...], yl[...], dz_ref.buf[m, :, 0:C], dz_ref.buf[m, :, C : 2 * C])
            self.add_halves(meta, m, grad, total, kept_out, away_out)

        args = self.before_args(i)
        if i:
            args += [(self.gain, whole(6, C)), (self.bias, whole(6, C))]
        args += [(dz, Streamed(1)), (self.dw, layer(i, TAPS, C))]
        scratch = [pad_scratch(), pltpu.VMEM((rows, C), BF16), pltpu.VMEM((rows, C), BF16), pltpu.VMEM((C, C), F32)]
        if strided:
            scratch.append(stride_scratch())
        which = PLACES[i][0]
        self.pieces[which] = call(
            body, self.meta, args, self.piece_out(i), scratch, f"{self.tag}_weights_{i}", 6 * OWN * rows * C * C,
            into=self.pieces[which],
        )
        self.done = (self.pieces[which][0],)

    def backward(self, layers):
        if layers[0] == 4:
            self.pieces = [[], []]
        for i in layers:
            result = self.backward_layer(i)
        return result

    def resume(self):
        i, dz, payload = self.pending
        self.back_got = shared(payload, self.stages)
        self.weight_grad(i, dz)

    def fork(self, state=None):
        other = copy.copy(self)
        other.__dict__.update(state or {})
        if "pieces" in other.__dict__:
            other.pieces = list(other.pieces)
        return other

    def state(self):
        return {name: getattr(self, name) for name in ("du", "dxr", "back_got", "pieces", "small")}

    def half(self, no, first):
        kept, away = self.pieces[no]
        if no:
            parts = self.small[: SMALL // 2], self.small[SMALL // 2 :]
            at = kept.shape[0] - SMALL // 2
            kept = lax.dynamic_update_slice_in_dim(kept, jnp.where(first, *parts), at, 0)
            away = lax.dynamic_update_slice_in_dim(away, jnp.where(first, *parts[::-1]), at, 0)
        return kept + swap(away)


PLACES = {3: (0, 0), 4: (0, 1), 5: (0, 2), 0: (1, 0), 1: (1, 1), 2: (1, 2)}
PIECE_ROWS = (3 * C // 2, 3 * C // 2 + SMALL // 2)


def swap(x):
    return lax.ppermute(x, "section", [(0, 1), (1, 0)])


def fenced(always, work, x):
    shapes = jax.eval_shape(work, x)
    return lax.cond(always, work, lambda x: jax.tree.map(lambda y: jnp.zeros(y.shape, y.dtype), shapes), x)


class Reduction:
    def __init__(self, x, stages):
        self.x = x
        self.todo = []
        stride = 1
        for radix in stages:
            self.todo.append((True, radix, stride))
            stride *= radix
        self.todo += [(False, radix, stride) for _, radix, stride in reversed(self.todo)]

    def step(self):
        scatter, radix, stride = self.todo.pop(0)
        rows = self.x.shape[0]
        if scatter:
            parts = exchange(self.x.reshape(radix, rows // radix, C), radix, stride)
            self.x = jnp.sum(parts, axis=0)
        else:
            parts = exchange(jnp.broadcast_to(self.x, (radix,) + self.x.shape), radix, stride)
            self.x = parts.reshape(radix * rows, C)
        return (self.x,)

    def finish(self):
        while self.todo:
            self.step()
        return self.x


def per_device(features, out_grad, lengths, join_pick, dw, pw, gain, bias, res_w, down, down_b, up, up_b):
    first = lax.axis_index("section") == 0
    size = lax.axis_size("dp")
    inputs = features.reshape(MB, SLOT, C)
    cotangent = out_grad.reshape(MB, SLOT, C)
    own, picks = lengths[0, 0], join_pick[0]
    to_upper = lambda x: lax.ppermute(x, "section", [(0, 1)])
    to_lower = lambda x: lax.ppermute(x, "section", [(1, 0)])

    far_len = swap(own)
    joining = jnp.concatenate([lax.dynamic_index_in_dim(inputs, picks[m], 0, False)[HALF:] for m in range(OWN)], axis=0)
    far_rows = swap(jnp.where(first, inputs[MB - 1], joining))
    far_w0 = swap(pw[0, 0:1])
    taps = jnp.concatenate([dw[0].reshape(5 * TAPS, C), gain[0], bias[0]], axis=0)
    far_taps = swap(taps)
    far_pw, far_res = swap(pw[0]), swap(res_w[0])
    wide = jnp.pad(down_b, ((0, 0), (0, C - SE)))
    squeeze = jnp.concatenate([down[0].T, up[0], up_b, wide], axis=0)
    far_squeeze = swap(squeeze)
    far_cot = to_lower(cotangent[:OWN])
    far_cot0 = to_upper(cotangent[MB - 1, :HALF])

    flag = first.astype(jnp.int32)[None]
    mine = lambda v: jnp.where(first, v[:OWN], jnp.concatenate([v[OWN:], jnp.zeros((1,), v.dtype)]))
    length = mine(jnp.where(first, own, far_len))
    half_len = (length + 1) // 2
    join_len = mine(jnp.where(first, far_len, own)[picks])
    meta1 = jnp.concatenate([length, half_len, flag])
    meta2 = jnp.concatenate([half_len, join_len, flag, picks[MB - 1 :]])

    def small(block):
        t = jnp.where(first == (block == 0), taps, far_taps)
        q = jnp.where(first == (block == 0), squeeze, far_squeeze)
        return (
            t[: 5 * TAPS].reshape(5, TAPS, C), t[5 * TAPS : 5 * TAPS + 6], t[5 * TAPS + 6 :],
            q[:SE], q[2 * SE + 1, :SE][:, None], q[SE : 2 * SE], q[2 * SE : 2 * SE + 1],
        )

    def prepared(block, start, stop):
        array = prepare(meta1, (pw[0], res_w[0]), (far_pw, far_res), block, start, stop)
        return array, {i: (array, i - start) for i in range(start, stop)}

    parts0 = [prepared(0, 1, 3), prepared(0, 3, 6)]
    parts1 = [prepared(1, 0, 3), prepared(1, 3, 6)]

    stages, deep = radices(size, 16), radices(size, 4)
    c14 = Block(False, meta1, small(0), {**parts0[0][1], **parts0[1][1]}, stages)
    c14.x, c14.x_far, c14.first_matrix = inputs, far_rows, (pw[0], far_w0)
    c14.forward({2: (parts0[1][0],), 4: (parts1[0][0],)})
    out0 = c14.tail(after=(parts1[1][0],))
    c15 = Block(True, meta2, small(1), {**parts1[0][1], **parts1[1][1]}, stages)
    c15.arrived, c15.joined_far, c15.joined = out0, far_rows, features.reshape(MB, 2, HALF, C)
    c15.forward()
    out1 = c15.tail(cotangent, far_cot)
    c15.stop_sum = 2
    c15.backward((4, 3, 2))
    always = own[0] > 0

    half0 = c15.half(0, first)
    sum0 = lax.psum(half0, "dp")

    def middle(half0):
        upper, lower = c15.fork({"done": (half0,)}), c14.fork()
        upper.resume()
        back, dx1 = upper.backward((1, 0))
        lower.tail_backward(cotangent, far_cot0, back)
        lower.done = upper.done
        half1 = upper.half(1, first)
        lower.backward((4, 3, 2))
        return dx1, half1, lower.half(0, first), lower.state()

    dx1, half1, half2, state = fenced(always, middle, half0)
    sum0, half2 = lax.optimization_barrier((sum0, half2))
    sum1, sum2 = lax.psum((half1, half2), "dp")
    came0 = to_upper(sum0)

    def ending(half2):
        last = c14.fork({**state, "done": (half2,)})
        dx0, = last.backward((1, 0))
        reduction = Reduction(last.half(1, first), deep)
        reduction.step()
        pad = jnp.zeros((1, HALF, C), F32)
        lower = jnp.concatenate([out0, jnp.concatenate([to_lower(out0[0:1, :HALF]), pad], axis=1)], axis=0)
        upper = jnp.concatenate([to_upper(out1), out1[0:1]], axis=0)
        block_out = jnp.where(first, lower, upper)
        lower = jnp.concatenate([dx0, to_lower(dx0[0:1])], axis=0)
        joins = jnp.concatenate([to_upper(dx1), dx1[0:1]], axis=0)
        joins = jnp.stack([lax.dynamic_index_in_dim(joins, jnp.argmax(picks == s), 0, False) for s in range(MB)])
        upper = jnp.concatenate([jnp.zeros_like(joins), joins], axis=1)
        dx = jnp.where(first, lower, upper)
        reduction.x, block_out, dx = lax.optimization_barrier((reduction.x, block_out, dx))
        sum3 = reduction.finish()
        return block_out, dx, sum3

    block_out, dx, sum3 = fenced(always, ending, half2)
    sum1, sum2, sum3 = lax.optimization_barrier((sum1, sum2, sum3))
    came1, came2, came3 = to_upper(sum1), to_lower(sum2), to_lower(sum3)
    pw_grad, res_grad, rows = unpack(meta1, (sum2, sum3, came2, came3), (sum0, sum1, came0, came1))
    dw_grad = rows[TAIL_ROWS : TAIL_ROWS + 40].reshape(1, 5, 8, C)
    norms = jnp.concatenate([dw_grad[0, 1:, TAPS : TAPS + 2], rows[None, 2 * SE + 2 : 2 * SE + 4], rows[None, 2 * SE + 4 : 2 * SE + 6]], axis=0)
    return (
        block_out.reshape(features.shape), dx.reshape(features.shape), dw_grad[:, :, :TAPS], pw_grad[None],
        norms[None, :, 1], norms[None, :, 0], res_grad, rows[SE : 2 * SE].T[None], rows[2 * SE + 1 : 2 * SE + 2, :SE],
        rows[:SE][None], rows[2 * SE : 2 * SE + 1],
    )


def unpack(meta, c14, c15):
    half = C // 2

    def body(meta, *refs):
        sources, (pw, res, rows), sem = refs[:8], refs[8:11], refs[11]

        def copies_of(parts, lower):
            near, far = parts[:2], parts[2:]
            top, bottom = (near, far) if lower else (far, near)
            out = []
            for i, (which, place) in PLACES.items():
                for side, pair in enumerate((top, bottom)):
                    source = pair[which].at[place * half : (place + 1) * half, :]
                    matrix = res.at[0] if i == 5 else pw.at[i]
                    out.append((source, matrix.at[side * half : (side + 1) * half, :]))
            for side, pair in enumerate((top, bottom)):
                source = pair[1].at[3 * half : 3 * half + SMALL // 2, :]
                out.append((source, rows.at[side * SMALL // 2 : (side + 1) * SMALL // 2, :]))
            return [pltpu.make_async_copy(a, b, sem.at[j]) for j, (a, b) in enumerate(out)]

        def run(parts, lower):
            def go():
                moves = copies_of(parts, lower)
                for move in moves:
                    move.start()
                for move in moves:
                    move.wait()

            return go

        pl.when(meta[2 * OWN] == 1)(run(sources[:4], True))
        pl.when(meta[2 * OWN] != 1)(run(sources[4:], False))

    anywhere = pl.BlockSpec(memory_space=pl.ANY)
    args = [(x, anywhere) for x in c14 + c15]
    outs = [(f32(5, C, C), anywhere), (f32(1, C, C), anywhere), (f32(SMALL, C), anywhere)]
    return call(body, meta, args, outs, [pltpu.SemaphoreType.DMA((14,))], "unpack", steps=1)


def solution(mesh):
    rows = P("section", "dp", None)
    own = lambda dims: P("section", *([None] * dims))
    weights = (own(3), own(3), own(2), own(2), own(2), own(2), own(1), own(2), own(1))
    in_specs = (rows, rows, rows, P("dp", None), *weights)
    out_specs = (rows, rows, *weights)
    return jax.shard_map(per_device, mesh=mesh, in_specs=in_specs, out_specs=out_specs, check_vma=False)
```

```python
import copy

import jax
import jax.numpy as jnp
from jax import lax
from jax.experimental import pallas as pl
from jax.experimental.pallas import tpu as pltpu
from jax.sharding import PartitionSpec as P

EPSILON = 1e-05
EXACT = lax.Precision.HIGHEST
TAPS = 5
MB = 3
OWN = 2
SLOT = 400
HALF = 200
KEPT = 208
C = 512
LANES = 128
CHUNKS = [slice(c, c + LANES) for c in range(0, C, LANES)]
SE = 64
BF16, F32 = jnp.bfloat16, jnp.float32
VMEM_BYTES = 60 << 20
TAIL_ROWS = 2 * SE + 8
SMALL = 256


def radices(size, most):
    stages, left = [], size
    while left > 1:
        radix = min(most, left)
        while left % radix:
            radix -= 1
        stages.append(radix)
        left //= radix
    return stages


def exchange(block, radix, stride):
    size = lax.axis_size("dp")
    if radix == size:
        return lax.all_to_all(block, "dp", 0, 0)
    groups = []
    for base in range(size):
        if (base // stride) % radix == 0:
            groups.append([base + j * stride for j in range(radix)])
    return lax.all_to_all(block, "dp", 0, 0, axis_index_groups=groups)


def shared(block, stages):
    stride = 1
    for no, radix in enumerate(stages):
        if no:
            block = jnp.broadcast_to(jnp.sum(block, axis=0), (radix,) + block.shape[1:])
        block = exchange(block, radix, stride)
        stride *= radix
    return block


def halves(x):
    high = x.astype(BF16)
    return high, (x - high.astype(F32)).astype(BF16)


def sigmoid(x):
    return 0.5 * jnp.tanh(0.5 * x) + 0.5


def exact_dot(a, b, dims=((1,), (0,))):
    return lax.dot_general(a, b, (dims, ((), ())), precision=EXACT, preferred_element_type=F32)


def fast_dot(a, b, dims=((1,), (0,))):
    return lax.dot_general(a, b, (dims, ((), ())), preferred_element_type=F32)


def stacked_dot(high, low, w, back=False):
    w_high, w_low = w[0], w[1]
    w = jnp.concatenate([w_high, w_high, w_low], axis=1 if back else 0)
    x = jnp.concatenate([high, low, high], axis=1)
    return fast_dot(x, w, ((1,), (1 if back else 0,)))


def stacked_outer(a_high, a_low, b_high, b_low):
    a = jnp.concatenate([a_high, a_low, a_high], axis=0)
    b = jnp.concatenate([b_high, b_high, b_low], axis=0)
    return fast_dot(a, b, ((0,), (0,)))


def column_sum(x):
    return jnp.sum(x, axis=0, keepdims=True)


class Rows:
    def __init__(self, meta, m, two, rows, which=0):
        place = lax.broadcasted_iota(jnp.int32, (rows, LANES), 0)
        if two:
            later = place >= HALF
            limit = jnp.where(later, HALF + meta[OWN + m], meta[m])
            self.mask = place < limit
        else:
            self.mask = place < meta[which * OWN + m]

    def keep(self, x):
        return jnp.where(self.mask, x, 0.0)


class Padded:
    def __init__(self, ref, two):
        self.ref = ref
        self.pieces = [(8, 0, HALF), (16 + HALF, HALF, HALF)] if two else [(8, 0, SLOT)]

    def put(self, x):
        zeros = jnp.zeros((8, LANES), F32)
        for at, start, rows in self.pieces:
            self.ref[at - 8 : at, :] = zeros
            self.ref[at : at + rows, :] = x[start : start + rows]
        self.ref[at + rows : at + rows + 8, :] = zeros

    def get(self, offset):
        parts = [self.ref[at + offset : at + offset + rows, :] for at, _, rows in self.pieces]
        return parts[0] if len(parts) == 1 else jnp.concatenate(parts, axis=0)

    def conv(self, kernel):
        total = kernel[0:1] * self.get(-2)
        for k in range(1, TAPS):
            total = total + kernel[k : k + 1] * self.get(k - 2)
        return total

    def conv_back(self, kernel):
        total = kernel[0:1] * self.get(2)
        for k in range(1, TAPS):
            total = total + kernel[k : k + 1] * self.get(2 - k)
        return total


def every_other(ref, x):
    ref[0:SLOT, :] = x
    ref[SLOT : 2 * KEPT, :] = jnp.zeros((2 * KEPT - SLOT, LANES), F32)
    return ref[pl.ds(0, KEPT, stride=2), :]


def spread_out(ref, x):
    ref[...] = jnp.zeros_like(ref)
    ref[pl.ds(0, KEPT, stride=2), :] = x
    return ref[0:SLOT, :]


def center_spread(sums, rows):
    center = sums[0:1] / rows
    return center, lax.rsqrt(sums[1:2] / rows - center * center + EPSILON)


def added(ref):
    return jnp.sum(ref[:, 0], axis=0)


def accumulate(ref, m, at, value):
    rows = slice(at, at + value.shape[0])
    ref[rows, :] = jnp.where(m == 0, value, ref[rows, :] + value)


def send(ref, rows):
    for copy in range(ref.shape[0]):
        for row, x in enumerate(rows):
            ref[copy, 0, row : row + 1, 0 : x.shape[1]] = x


def pad_scratch():
    return pltpu.VMEM((len(CHUNKS), SLOT + 24, LANES), F32)


def stride_scratch():
    return pltpu.VMEM((len(CHUNKS), 2 * KEPT, LANES), F32)


def slots(rows, cols=C):
    return pl.BlockSpec((1, rows, cols), lambda m, *_: (m, 0, 0))


def copies(count, rows, cols=C):
    return pl.BlockSpec((count, 1, rows, cols), lambda m, *_: (0, m, 0, 0))


def whole(*shape):
    return pl.BlockSpec(shape, lambda m, *_: (0,) * len(shape))


def layer(i, *shape):
    return pl.BlockSpec((1,) + shape, lambda m, *_: (i,) + (0,) * len(shape))


def f32(*shape):
    return jax.ShapeDtypeStruct(shape, F32)


def bf16(*shape):
    return jax.ShapeDtypeStruct(shape, BF16)


def call(body, meta, args, outs, scratch=(), name=None, flops=0, steps=OWN, after=(), into=()):
    arrays, in_specs = [a for a, _ in args], [s for _, s in args]
    shapes, out_specs = [a for a, _ in outs], [s for _, s in outs]
    size = sum(a.size * a.dtype.itemsize for a in arrays + shapes)
    extra = list(after) + list(into)
    count = len(arrays)

    def inner(meta, *refs):
        body(meta, *refs[:count], *refs[count + len(extra) :])

    return pl.pallas_call(
        inner,
        out_shape=shapes,
        grid_spec=pltpu.PrefetchScalarGridSpec(
            num_scalar_prefetch=1,
            grid=(steps,),
            in_specs=in_specs + [pl.BlockSpec(memory_space=pl.ANY)] * len(extra),
            out_specs=out_specs,
            scratch_shapes=list(scratch),
        ),
        input_output_aliases={1 + count + len(after) + j: j for j in range(len(into))},
        compiler_params=pltpu.CompilerParams(vmem_limit_bytes=VMEM_BYTES),
        cost_estimate=pl.CostEstimate(flops=flops, bytes_accessed=size, transcendentals=0),
        name=name,
    )(meta, *arrays, *extra)


def choose(meta, block, own, far):
    return jnp.where(meta[2 * OWN] == 1 - block, own, far)


def prepare(meta, own, far, block, start, stop):
    def body(meta, *refs):
        pair = [ref[0] for ref in refs[:2]]
        if stop == 6:
            last = pl.program_id(0) == 5 - start
            pair = [jnp.where(last, ref[...], w) for ref, w in zip(refs[2:4], pair)]
        out = refs[-1]
        out[0, 0], out[0, 1] = halves(choose(meta, block, *pair))

    matrix = pl.BlockSpec((1, C, C), lambda j, *_: (jnp.minimum(j + start, 4), 0, 0))
    args = [(own[0], matrix), (far[0], matrix)]
    if stop == 6:
        args += [(own[1], whole(C, C)), (far[1], whole(C, C))]
    out = pl.BlockSpec((1, 2, C, C), lambda j, *_: (j, 0, 0, 0))
    name = f"prepare_{block}_{start}"
    return call(body, meta, args, [(bf16(stop - start, 2, C, C), out)], name=name, steps=stop - start)[0]


class Block:
    def __init__(self, two, meta, weights, ready, stages):
        self.done = ()
        self.two, self.meta, self.stages = two, meta, stages
        self.dw, self.gain, self.bias, self.down, self.down_b, self.up, self.up_b = weights
        self.ready = ready
        self.tail_rows = SLOT if two else KEPT
        self.first, self.last = stages[0], stages[-1]
        self.tag = "c15" if two else "c14"

    def rows_of(self, i):
        return self.tail_rows if i == 4 else SLOT

    def valid(self, meta, m, i):
        last = i == 4 and not self.two
        return Rows(meta, m, self.two, self.rows_of(i), which=1 if last else 0)

    def matrix(self, i):
        array, at = self.ready[i]
        return (array, layer(at, 2, C, C))

    def source_args(self):
        if not self.two:
            return [(self.x, slots(SLOT)), (self.x_far, whole(SLOT, C))]
        far = pl.BlockSpec((HALF, C), lambda m, *_: (m, 0))
        near = pl.BlockSpec((1, 1, HALF, C), lambda m, meta: (meta[2 * OWN + 1], 1, 0, 0))
        return [(self.arrived, slots(HALF)), (self.joined_far, far), (self.joined, near)]

    def source(self, meta, refs, cs):
        lower = meta[2 * OWN] == 1
        if not self.two:
            return jnp.where(lower, refs[0][0, :, cs], refs[1][:, cs])
        joined = jnp.where(lower, refs[1][:, cs], refs[2][0, 0, :, cs])
        return jnp.concatenate([refs[0][0, :, cs], joined], axis=0)

    def before_args(self, i):
        if i == 0:
            return self.source_args()
        return [(self.z[i - 1], slots(SLOT)), (self.stats[i - 1], slots(2))]


    def forward_layer(self, i, after=()):
        two, count = self.two, self.first
        strided = i == 4 and not two
        rows = self.rows_of(i)
        n_src = len(self.source_args())
        width = C + LANES if i == 0 else C
        sent = 4 if i == 3 else 2
        makes = i == 0 and not two

        def body(meta, *refs):
            refs = list(refs)
            take = lambda n: [refs.pop(0) for _ in range(n)]
            m = pl.program_id(0)
            if i == 0:
                src = take(n_src)
            else:
                z_ref, got_ref = take(2)
                n_ref, = take(1) if i > 1 else (None,)
                gain_ref, bias_ref = take(2)
                res_sum, = take(1) if i == 3 else (None,)
            dw_ref, = take(1)
            if makes:
                own_ref, far_ref, z_out, pay, w_ref = take(5)

                @pl.when(m == 0)
                def _():
                    w_ref[0, 0], w_ref[0, 1] = halves(choose(meta, 0, own_ref[0], far_ref[0]))

            else:
                w_ref, z_out, pay = take(3)
            if i:
                stat_out, = take(1)
            if i == 1:
                n_out, = take(1)
            pad, y_ref = take(2)
            alt, = take(1) if strided else (None,)
            valid_in = self.valid(meta, m, 0)
            if i:
                sums = added(got_ref)
                if i == 1:
                    count_in = jnp.maximum(jnp.concatenate([sums[0:1, C:]] * len(CHUNKS), axis=1), 1.0)
                    count_out = jnp.maximum(jnp.concatenate([sums[1:2, C:]] * len(CHUNKS), axis=1), 1.0)
                    n_out[0, 0:1, :] = count_in
                    n_out[0, 1:2, :] = count_out
                else:
                    count_in = n_ref[0, 0:1, :]
                center, spread = center_spread(sums[:, :C], count_in)
                stat_out[0, 0:1, :] = center
                stat_out[0, 1:2, :] = spread
                scale = gain_ref[i - 1 : i] * spread
                shift = bias_ref[i - 1 : i] - center * scale
            for c, cs in enumerate(CHUNKS):
                if i == 0:
                    h = valid_in.keep(self.source(meta, src, cs))
                else:
                    u = z_ref[0, :, cs] * scale[:, cs] + shift[:, cs]
                    h = valid_in.keep(u * sigmoid(u))
                padded = Padded(pad.at[c], two)
                padded.put(h)
                y = padded.conv(dw_ref[0, :, cs])
                if strided:
                    y = every_other(alt.at[c], y)
                high, low = halves(y)
                y_ref[:, cs] = high
                y_ref[:, C + cs.start : C + cs.stop] = low
            w = w_ref.at[0] if makes else w_ref.at[0]
            z = stacked_dot(y_ref[:, 0:C], y_ref[:, C : 2 * C], w)
            z_out[0] = z
            valid = self.valid(meta, m, i)
            one, square = [], []
            for cs in CHUNKS:
                kept = valid.keep(z[:, cs])
                one.append(column_sum(kept))
                square.append(column_sum(kept * kept))
            if i == 0:
                if two:
                    number = (meta[m] + meta[OWN + m]).astype(F32)
                    numbers = number, number
                else:
                    numbers = meta[m].astype(F32), meta[OWN + m].astype(F32)
                one.append(jnp.full((1, LANES), numbers[0], F32))
                square.append(jnp.full((1, LANES), numbers[1], F32))
            out = [jnp.concatenate(one, axis=1), jnp.concatenate(square, axis=1)]
            if i == 3:
                out += [res_sum[0, 0:1, :], res_sum[0, 1:2, :]]
            send(pay, out)

        if i == 0:
            args = list(self.source_args())
        else:
            got = 4 if i == 4 else 2
            args = [(self.z[i - 1], slots(SLOT)), (self.got[i - 1], copies(self.last, got, C + LANES if i == 1 else C))]
            if i > 1:
                args.append((self.number, slots(2)))
            args += [(self.gain, whole(6, C)), (self.bias, whole(6, C))]
            if i == 3:
                args.append((self.res_sum, slots(2)))
        args.append((self.dw, layer(i, TAPS, C)))
        args += [(w, layer(0, C, C)) for w in self.first_matrix] if makes else [self.matrix(i)]
        outs = [(f32(OWN, rows, C), slots(rows)), (f32(count, OWN, sent, width), copies(count, sent, width))]
        if i:
            outs.append((f32(OWN, 2, C), slots(2)))
        if i == 1:
            outs.append((f32(OWN, 2, C), slots(2)))
        if makes:
            outs.append((bf16(1, 2, C, C), layer(0, 2, C, C)))
        scratch = [pad_scratch(), pltpu.VMEM((rows, 2 * C), BF16)]
        if strided:
            scratch.append(stride_scratch())
        result = call(body, self.meta, args, outs, scratch, f"{self.tag}_forward_{i}", 6 * OWN * rows * C * C, after=after)
        self.z.append(result[0])
        if makes:
            self.ready[0] = (result[2], 0)
        if i:
            self.stats.append(result[2])
        if i == 1:
            self.number = result[3]
        self.got.append(shared(result[1], self.stages))

    def residual(self):
        two, rows = self.two, self.tail_rows

        def body(meta, *refs):
            refs = list(refs)
            src = [refs.pop(0) for _ in self.source_args()]
            w_ref, r_out, x_out, sum_out = refs[:4]
            alt = refs[4] if not two else None
            m = pl.program_id(0)
            valid_in = self.valid(meta, m, 0)
            for c, cs in enumerate(CHUNKS):
                x = valid_in.keep(self.source(meta, src, cs))
                if not two:
                    x = every_other(alt.at[c], x)
                high, low = halves(x)
                x_out[0, :, cs] = high
                x_out[0, :, C + cs.start : C + cs.stop] = low
            r = stacked_dot(x_out[0, :, 0:C], x_out[0, :, C : 2 * C], w_ref.at[0])
            r_out[0] = r
            valid = self.valid(meta, m, 4)
            for cs in CHUNKS:
                kept = valid.keep(r[:, cs])
                sum_out[0, 0:1, cs] = column_sum(kept)
                sum_out[0, 1:2, cs] = column_sum(kept * kept)

        args = self.source_args() + [self.matrix(5)]
        outs = [
            (f32(OWN, rows, C), slots(rows)),
            (bf16(OWN, rows, 2 * C), slots(rows, 2 * C)),
            (f32(OWN, 2, C), slots(2)),
        ]
        scratch = [] if two else [stride_scratch()]
        self.r, self.picked, self.res_sum = call(
            body, self.meta, args, outs, scratch, f"{self.tag}_residual", 6 * OWN * rows * C * C
        )

    def forward(self, after=None):
        self.z, self.got, self.stats = [], [], []
        for i in range(5):
            if i == 2:
                self.residual()
            self.forward_layer(i, (after or {}).get(i, ()))


    def segments(self):
        return [(0, HALF), (HALF, HALF)] if self.two else [(0, self.tail_rows)]

    def lengths(self, meta, m):
        if self.two:
            return [meta[m], meta[OWN + m]]
        return [meta[OWN + m]]

    def squeeze(self, sums, counts, se_refs):
        down_t, down_b, up, up_b = se_refs
        means = [s / jnp.maximum(jnp.full((1, C), n.astype(F32)), 1.0) for s, n in zip(sums, counts)]
        ps = [jnp.sum(down_t[...] * mean, axis=1, keepdims=True) + down_b[...] for mean in means]
        gates = [sigmoid(column_sum(up[...] * (p * sigmoid(p))) + up_b[...]) for p in ps]
        return means, ps, gates

    def squeeze_back(self, des, ps, gates, counts, se_refs, means, small, m):
        down_t, down_b, up, up_b = se_refs
        shares, up_grad, down_grad, dq_sum, dp_sum = [], 0.0, 0.0, 0.0, 0.0
        for de, p, gate, n, mean in zip(des, ps, gates, counts, means):
            dq = de * gate * (1.0 - gate)
            s = sigmoid(p)
            dp = jnp.sum(up[...] * dq, axis=1, keepdims=True) * (s * (1.0 + p * (1.0 - s)))
            shares.append(column_sum(down_t[...] * dp) / jnp.maximum(jnp.full((1, C), n.astype(F32)), 1.0))
            up_grad, down_grad = up_grad + (p * s) * dq, down_grad + dp * mean
            dq_sum, dp_sum = dq_sum + dq, dp_sum + dp
        row, col = (lax.broadcasted_iota(jnp.int32, (SE, C), axis) for axis in (0, 1))
        dp_row = column_sum(jnp.where(row == col, dp_sum, 0.0))
        accumulate(small, m, 0, up_grad)
        accumulate(small, m, SE, down_grad)
        accumulate(small, m, 2 * SE, dq_sum)
        accumulate(small, m, 2 * SE + 1, dp_row)
        return shares

    def last_norm(self, m, dt_out, du_out, z_ref, slope_ref, gates, shares, center, spread, res_bias, res_gain, pay, small):
        bias_sum, gain_sum = [], []
        for cs in CHUNKS:
            dh = dt_out[0, :, cs] * self.by_segment(gates, cs) + self.by_segment(shares, cs)
            du = dh * slope_ref[:, cs]
            du_out[0, :, cs] = du
            bias_sum.append(column_sum(du))
            gain_sum.append(column_sum(du * ((z_ref[0, :, cs] - center[:, cs]) * spread[:, cs])))
        rows = [jnp.concatenate(x, axis=1) for x in (bias_sum, gain_sum, res_bias, res_gain)]
        send(pay, rows)
        for j, row in enumerate(rows):
            accumulate(small, m, 2 * SE + 2 + j, row)

    def se_args(self):
        return [(self.down, whole(SE, C)), (self.down_b, whole(SE, 1)), (self.up, whole(SE, C)), (self.up_b, whole(1, C))]

    def store_rows(self, ref, rows):
        ref[0] = jnp.concatenate(rows + [jnp.zeros((8 - len(rows), C), F32)], axis=0)

    def store_columns(self, ref, columns):
        ref[0] = jnp.zeros((SE, 8), F32)
        for j, column in enumerate(columns):
            ref[0, :, j : j + 1] = column

    def by_segment(self, rows, cs):
        parts = [jnp.broadcast_to(row[:, cs], (n, LANES)) for row, (_, n) in zip(rows, self.segments())]
        return parts[0] if len(parts) == 1 else jnp.concatenate(parts, axis=0)

    def seg_sums(self, x):
        return [column_sum(x[at : at + n]) for at, n in self.segments()]

    def tail(self, cotangent=None, far=None, after=()):
        two, rows = self.two, self.tail_rows
        back = cotangent is not None

        def body(meta, *refs):
            refs = list(refs)
            take = lambda n: [refs.pop(0) for _ in range(n)]
            m = pl.program_id(0)
            z_ref, got4, r_ref, got3, n_ref, gain, bias = take(7)
            se_refs = take(4)
            if back:
                cot_ref, far_ref = take(2)
            out, stat_out, rstat_out, means_out, p_out, gate_out = take(6)
            if back:
                small, du_out, dt_out, pay = take(4)
            h_ref, = take(1)
            if back:
                slope_ref, = take(1)
            valid = self.valid(meta, m, 4)
            number = n_ref[0, 1:2, :]
            center, spread = center_spread(added(got4), number)
            rcenter, rspread = center_spread(added(got3)[2:4], number)
            stat_out[0, 0:1, :] = center
            stat_out[0, 1:2, :] = spread
            rstat_out[0, 0:1, :] = rcenter
            rstat_out[0, 1:2, :] = rspread
            scale = gain[4:5] * spread
            shift = bias[4:5] - center * scale
            sums = []
            for cs in CHUNKS:
                u = z_ref[0, :, cs] * scale[:, cs] + shift[:, cs]
                s = sigmoid(u)
                h = valid.keep(u * s)
                h_ref[:, cs] = h
                if back:
                    slope_ref[:, cs] = valid.keep(s * (1.0 + u * (1.0 - s)))
                sums.append(self.seg_sums(h))
            sums = [jnp.concatenate([s[j] for s in sums], axis=1) for j in range(len(self.segments()))]
            counts = self.lengths(meta, m)
            means, ps, gates = self.squeeze(sums, counts, se_refs)
            self.store_rows(means_out, means)
            self.store_columns(p_out, ps)
            self.store_rows(gate_out, gates)
            res_gain, res_bias, gate_grad = [], [], []
            for cs in CHUNKS:
                h = h_ref[:, cs]
                rh = (r_ref[0, :, cs] - rcenter[:, cs]) * rspread[:, cs]
                t = h * self.by_segment(gates, cs) + gain[5:6, cs] * rh + bias[5:6, cs]
                s = sigmoid(t)
                out[0, 0:rows, cs] = valid.keep(t * s)
                if rows < SLOT:
                    out[0, rows:SLOT, cs] = jnp.zeros((SLOT - rows, LANES), F32)
                if back:
                    cot = jnp.where(meta[2 * OWN] == 1, far_ref[0, :, cs], cot_ref[0, :, cs])
                    dt = valid.keep(cot * (s * (1.0 + t * (1.0 - s))))
                    dt_out[0, :, cs] = dt
                    res_bias.append(column_sum(dt))
                    res_gain.append(column_sum(dt * rh))
                    gate_grad.append(self.seg_sums(dt * h))
            if not back:
                return
            des = [jnp.concatenate([g[j] for g in gate_grad], axis=1) for j in range(len(counts))]
            shares = self.squeeze_back(des, ps, gates, counts, se_refs, means, small, m)
            self.last_norm(m, dt_out, du_out, z_ref, slope_ref, gates, shares, center, spread, res_bias, res_gain, pay, small)

        args = [
            (self.z[4], slots(rows)), (self.got[4], copies(self.last, 2)), (self.r, slots(rows)),
            (self.got[3], copies(self.last, 4)), (self.number, slots(2)),
            (self.gain, whole(6, C)), (self.bias, whole(6, C)),
        ] + self.se_args()
        outs = [
            (f32(OWN, SLOT, C), slots(SLOT)), (f32(OWN, 2, C), slots(2)), (f32(OWN, 2, C), slots(2)),
            (f32(OWN, 8, C), slots(8)), (f32(OWN, SE, 8), slots(SE, 8)), (f32(OWN, 8, C), slots(8)),
        ]
        scratch = [pltpu.VMEM((rows, C), F32)]
        if back:
            args += [(cotangent, layer(MB - 1, SLOT, C)), (far, slots(SLOT))]
            outs += self.tail_outs()
            scratch.append(pltpu.VMEM((rows, C), F32))
        result = call(body, self.meta, args, outs, scratch, f"{self.tag}_tail", after=after)
        self.stats.append(result[1])
        self.rstat, self.se_state = result[2], result[3:6]
        if back:
            self.tail_results(result[6:])
        return result[0]

    def tail_outs(self):
        rows, count = self.tail_rows, self.first
        return [
            (f32(SMALL, C), whole(TAIL_ROWS, C)), (f32(OWN, rows, C), slots(rows)), (f32(OWN, rows, C), slots(rows)),
            (f32(count, OWN, 4, C), copies(count, 4)),
        ]

    def tail_results(self, result):
        self.small, self.du, self.dt, pay = result
        self.back_got = shared(pay, self.stages)

    def tail_backward(self, cotangent, far, back):
        rows = self.tail_rows

        def body(meta, z_ref, r_ref, stat, rstat, gain, bias, means_ref, p_ref, gate_ref, down, down_b, up, up_b, cot_ref, far_ref, back_ref,
                 small, du_out, dt_out, pay, slope_ref):
            m = pl.program_id(0)
            valid = self.valid(meta, m, 4)
            center, spread, rcenter, rspread = stat[0, 0:1], stat[0, 1:2], rstat[0, 0:1], rstat[0, 1:2]
            scale = gain[4:5] * spread
            shift = bias[4:5] - center * scale
            zeros = jnp.zeros((rows - HALF, LANES), F32)
            counts = self.lengths(meta, m)
            ps = [p_ref[0, :, j : j + 1] for j in range(len(counts))]
            gates = [gate_ref[0, j : j + 1, :] for j in range(len(counts))]
            means = [means_ref[0, j : j + 1, :] for j in range(len(counts))]
            res_gain, res_bias, gate_grad = [], [], []
            for cs in CHUNKS:
                u = z_ref[0, :, cs] * scale[:, cs] + shift[:, cs]
                s = sigmoid(u)
                h = valid.keep(u * s)
                slope_ref[:, cs] = valid.keep(s * (1.0 + u * (1.0 - s)))
                rh = (r_ref[0, :, cs] - rcenter[:, cs]) * rspread[:, cs]
                t = h * self.by_segment(gates, cs) + gain[5:6, cs] * rh + bias[5:6, cs]
                s = sigmoid(t)
                here = jnp.where(meta[2 * OWN] == 1, cot_ref[0, 0:HALF, cs], far_ref[:, cs])
                cot = jnp.concatenate([here + back_ref[0, :, cs], zeros], axis=0)
                dt = valid.keep(cot * (s * (1.0 + t * (1.0 - s))))
                dt_out[0, :, cs] = dt
                res_bias.append(column_sum(dt))
                res_gain.append(column_sum(dt * rh))
                gate_grad.append(self.seg_sums(dt * h))
            des = [jnp.concatenate([g[j] for g in gate_grad], axis=1) for j in range(len(counts))]
            shares = self.squeeze_back(des, ps, gates, counts, (down, down_b, up, up_b), means, small, m)
            self.last_norm(m, dt_out, du_out, z_ref, slope_ref, gates, shares, center, spread, res_bias, res_gain, pay, small)

        args = [
            (self.z[4], slots(rows)), (self.r, slots(rows)), (self.stats[4], slots(2)), (self.rstat, slots(2)),
            (self.gain, whole(6, C)), (self.bias, whole(6, C)),
            (self.se_state[0], slots(8)), (self.se_state[1], slots(SE, 8)), (self.se_state[2], slots(8)),
        ] + self.se_args() + [(cotangent, slots(SLOT)), (far, whole(HALF, C)), (back, slots(HALF))]
        scratch = [pltpu.VMEM((rows, C), F32)]
        self.tail_results(call(body, self.meta, args, self.tail_outs(), scratch, f"{self.tag}_tail_back"))


    def norm_grad(self, du, zh, scale, sums, number, cs):
        return scale[:, cs] * (du - sums[0:1, cs] / number[:, cs] - zh * (sums[1:2, cs] / number[:, cs]))

    def backward_layer(self, i):
        two, count = self.two, self.first
        strided = i == 4 and not two
        rows = self.rows_of(i)
        n_src = len(self.source_args())

        def body(meta, *refs):
            refs = list(refs)
            take = lambda n: [refs.pop(0) for _ in range(n)]
            m = pl.program_id(0)
            du_ref, z_ref, w_ref, got, n_ref, stat, gain, bias, dw_ref = take(9)
            if i:
                zp_ref, statp = take(2)
            else:
                dxr_ref, = take(1)
                src = take(n_src)
            small, dz_out = take(2)
            if i:
                du_out, pay = take(2)
            elif two:
                back_out, dx_out = take(2)
            else:
                dx_out, = take(1)
            pad, = take(1)
            alt, = take(1) if refs else (None,)
            sums = added(got)
            number = n_ref[0, 1:2, :] if i == 4 else n_ref[0, 0:1, :]
            center, spread = stat[0, 0:1], stat[0, 1:2]
            scale = gain[i : i + 1] * spread
            valid = self.valid(meta, m, i)
            for cs in CHUNKS:
                zh = (z_ref[0, :, cs] - center[:, cs]) * spread[:, cs]
                dz = valid.keep(self.norm_grad(du_ref[0, :, cs], zh, scale, sums, number, cs))
                high, low = halves(dz)
                dz_out[0, :, cs] = high
                dz_out[0, :, C + cs.start : C + cs.stop] = low
            dy = stacked_dot(dz_out[0, :, 0:C], dz_out[0, :, C : 2 * C], w_ref.at[0], True)
            valid_in = self.valid(meta, m, 0)
            if i:
                pcenter, pspread = statp[0, 0:1], statp[0, 1:2]
                pscale = gain[i - 1 : i] * pspread
                pshift = bias[i - 1 : i] - pcenter * pscale
            taps, bias_sum, gain_sum = [[] for _ in range(TAPS)], [], []
            for c, cs in enumerate(CHUNKS):
                grad = dy[:, cs]
                if strided:
                    grad = spread_out(alt.at[c], grad)
                padded = Padded(pad.at[c], two)
                padded.put(grad)
                if i:
                    z = zp_ref[0, :, cs]
                    u = z * pscale[:, cs] + pshift[:, cs]
                    s = sigmoid(u)
                    h = valid_in.keep(u * s)
                else:
                    h = valid_in.keep(self.source(meta, src, cs))
                dh = None
                for k in range(TAPS):
                    moved = padded.get(2 - k)
                    taps[k].append(column_sum(h * moved))
                    term = dw_ref[0, k : k + 1, cs] * moved
                    dh = term if dh is None else dh + term
                if i:
                    du = valid_in.keep(dh * (s * (1.0 + u * (1.0 - s))))
                    du_out[0, :, cs] = du
                    bias_sum.append(column_sum(du))
                    gain_sum.append(column_sum(du * ((z - pcenter[:, cs]) * pspread[:, cs])))
                    continue
                dxr = dxr_ref[0, :, cs]
                if not two:
                    dxr = spread_out(alt.at[c], dxr)
                dx = valid_in.keep(dh) + dxr
                if two:
                    back_out[0, :, cs] = dx[:HALF]
                    dx = dx[HALF:]
                dx_out[0, :, cs] = dx
            rows = taps + [bias_sum, gain_sum] if i else taps
            rows = [jnp.concatenate(x, axis=1) for x in rows]
            for j, row in enumerate(rows):
                accumulate(small, m, j, row)
            if i:
                send(pay, rows[TAPS:])

        sent = 4 if i == 4 else 2
        args = [
            (self.du, slots(rows)), (self.z[i], slots(rows)), self.matrix(i), (self.back_got, copies(self.last, sent)),
            (self.number, slots(2)), (self.stats[i], slots(2)), (self.gain, whole(6, C)), (self.bias, whole(6, C)),
            (self.dw, layer(i, TAPS, C)),
        ]
        if not i:
            args.append((self.dxr, slots(self.tail_rows)))
        args += self.before_args(i)
        place = TAIL_ROWS // 8 + i
        outs = [(f32(SMALL, C), pl.BlockSpec((8, C), lambda m, *_: (place, 0))), (bf16(OWN, rows, 2 * C), slots(rows, 2 * C))]
        if i:
            outs += [(f32(OWN, SLOT, C), slots(SLOT)), (f32(count, OWN, 2, C), copies(count, 2))]
        elif two:
            outs += [(f32(OWN, HALF, C), slots(HALF)), (f32(OWN, HALF, C), slots(HALF))]
        else:
            outs += [(f32(OWN, SLOT, C), slots(SLOT))]
        scratch = [pad_scratch()]
        if strided or (i == 0 and not two):
            scratch.append(stride_scratch())
        self.small, dz, *result = call(
            body, self.meta, args, outs, scratch, f"{self.tag}_backward_{i}", 6 * OWN * rows * C * C,
            after=self.done, into=(self.small,),
        )
        got = self.back_got
        if i:
            self.du = result[0]
            self.back_got = shared(result[1], self.stages)
        self.weight_grad(i, dz)
        if i == 4:
            self.residual_back(got)
        return result

    def residual_back(self, got):
        rows = self.tail_rows

        def body(meta, got, n_ref, dt_ref, r_ref, rstat, gain, w_ref, x_ref, kept_out, away_out, dxr_out, dr, total):
            m = pl.program_id(0)
            sums = added(got)[2:4]
            number = n_ref[0, 1:2, :]
            center, spread = rstat[0, 0:1], rstat[0, 1:2]
            scale = gain[5:6] * spread
            valid = self.valid(meta, m, 4)
            for cs in CHUNKS:
                rh = (r_ref[0, :, cs] - center[:, cs]) * spread[:, cs]
                high, low = halves(valid.keep(self.norm_grad(dt_ref[0, :, cs], rh, scale, sums, number, cs)))
                dr[:, cs] = high
                dr[:, C + cs.start : C + cs.stop] = low
            high, low = dr[:, 0:C], dr[:, C : 2 * C]
            dxr_out[0] = stacked_dot(high, low, w_ref.at[0], True)
            grad = stacked_outer(x_ref[0, :, 0:C], x_ref[0, :, C : 2 * C], high, low)
            self.add_halves(meta, m, grad, total, kept_out, away_out)

        args = [
            (got, copies(self.last, 4)), (self.number, slots(2)), (self.dt, slots(rows)), (self.r, slots(rows)),
            (self.rstat, slots(2)), (self.gain, whole(6, C)), self.matrix(5), (self.picked, slots(rows, 2 * C)),
        ]
        outs = self.piece_out(5) + [(f32(OWN, rows, C), slots(rows))]
        which = PLACES[self.tag][5][0]
        *self.pieces[which], self.dxr = call(
            body, self.meta, args, outs, [pltpu.VMEM((rows, 2 * C), BF16), pltpu.VMEM((C, C), F32)],
            f"{self.tag}_residual_back", 12 * OWN * rows * C * C, into=self.pieces[which],
        )

    def piece_out(self, i):
        which, place = PLACES[self.tag][i]
        rows = PIECE_ROWS[self.tag][which]
        return [(f32(rows, C), pl.BlockSpec((C // 2, C), lambda m, *_: (place, 0)))] * 2

    def add_halves(self, meta, m, grad, total, kept_out, away_out):
        @pl.when(m == 0)
        def _():
            total[...] = grad

        @pl.when(m > 0)
        def _():
            top, bottom = total[0 : C // 2] + grad[0 : C // 2], total[C // 2 : C] + grad[C // 2 : C]
            lower = meta[2 * OWN] == 1
            kept_out[...] = jnp.where(lower, top, bottom)
            away_out[...] = jnp.where(lower, bottom, top)

    def weight_grad(self, i, dz):
        two = self.two
        strided = i == 4 and not two
        rows = self.rows_of(i)
        n_src = len(self.source_args())

        def body(meta, *refs):
            refs = list(refs)
            take = lambda n: [refs.pop(0) for _ in range(n)]
            m = pl.program_id(0)
            if i:
                zp_ref, statp, gain, bias = take(4)
                center, spread = statp[0, 0:1], statp[0, 1:2]
                scale = gain[i - 1 : i] * spread
                shift = bias[i - 1 : i] - center * scale
            else:
                src = take(n_src)
            dz_ref, dw_ref, kept_out, away_out, pad, yh, yl, total = take(8)
            alt, = take(1) if strided else (None,)
            valid_in = self.valid(meta, m, 0)
            for c, cs in enumerate(CHUNKS):
                if i:
                    u = zp_ref[0, :, cs] * scale[:, cs] + shift[:, cs]
                    h = valid_in.keep(u * sigmoid(u))
                else:
                    h = valid_in.keep(self.source(meta, src, cs))
                padded = Padded(pad.at[c], two)
                padded.put(h)
                y = padded.conv(dw_ref[0, :, cs])
                if strided:
                    y = every_other(alt.at[c], y)
                yh[:, cs], yl[:, cs] = halves(y)
            grad = stacked_outer(yh[...], yl[...], dz_ref[0, :, 0:C], dz_ref[0, :, C : 2 * C])
            self.add_halves(meta, m, grad, total, kept_out, away_out)

        args = self.before_args(i)
        if i:
            args += [(self.gain, whole(6, C)), (self.bias, whole(6, C))]
        args += [(dz, slots(rows, 2 * C)), (self.dw, layer(i, TAPS, C))]
        scratch = [pad_scratch(), pltpu.VMEM((rows, C), BF16), pltpu.VMEM((rows, C), BF16), pltpu.VMEM((C, C), F32)]
        if strided:
            scratch.append(stride_scratch())
        which = PLACES[self.tag][i][0]
        self.pieces[which] = call(
            body, self.meta, args, self.piece_out(i), scratch, f"{self.tag}_weights_{i}", 6 * OWN * rows * C * C,
            into=self.pieces[which],
        )
        self.done = (self.pieces[which][0],)

    def backward(self, layers):
        if layers[0] == 4:
            self.pieces = [[], []]
        for i in layers:
            result = self.backward_layer(i)
        return result

    def fork(self, state=None):
        other = copy.copy(self)
        other.__dict__.update(state or {})
        if "pieces" in other.__dict__:
            other.pieces = list(other.pieces)
        return other

    def state(self):
        return {name: getattr(self, name) for name in ("du", "dxr", "back_got", "pieces", "small")}

    def half(self, no, first, later=None):
        kept, away = self.pieces[no]
        if no:
            parts = self.small[: SMALL // 2], self.small[SMALL // 2 :]
            at = kept.shape[0] - SMALL // 2
            kept = lax.dynamic_update_slice_in_dim(kept, jnp.where(first, *parts), at, 0)
            away = lax.dynamic_update_slice_in_dim(away, jnp.where(first, *parts[::-1]), at, 0)
        if later is not None:
            kept, _ = lax.optimization_barrier((kept, later))
        return kept + swap(away)


PLACES = {
    "c15": {2: (0, 0), 3: (0, 1), 4: (0, 2), 5: (0, 3), 0: (1, 0), 1: (1, 1)},
    "c14": {3: (0, 0), 4: (0, 1), 5: (0, 2), 0: (1, 0), 1: (1, 1), 2: (1, 2)},
}
PIECE_ROWS = {"c15": (2 * C, C + SMALL // 2), "c14": (3 * C // 2, 3 * C // 2 + SMALL // 2)}


def swap(x):
    return lax.ppermute(x, "section", [(0, 1), (1, 0)])


def fenced(always, work, x):
    shapes = jax.eval_shape(work, x)
    return lax.cond(always, work, lambda x: jax.tree.map(lambda y: jnp.zeros(y.shape, y.dtype), shapes), x)


class Reduction:
    def __init__(self, x, stages):
        self.x = x
        self.todo = []
        stride = 1
        for radix in stages:
            self.todo.append((True, radix, stride))
            stride *= radix
        self.todo += [(False, radix, stride) for _, radix, stride in reversed(self.todo)]

    def step(self):
        scatter, radix, stride = self.todo.pop(0)
        rows = self.x.shape[0]
        if scatter:
            parts = exchange(self.x.reshape(radix, rows // radix, C), radix, stride)
            self.x = jnp.sum(parts, axis=0)
        else:
            parts = exchange(jnp.broadcast_to(self.x, (radix,) + self.x.shape), radix, stride)
            self.x = parts.reshape(radix * rows, C)
        return (self.x,)

    def finish(self):
        while self.todo:
            self.step()
        return self.x


def per_device(features, out_grad, lengths, join_pick, dw, pw, gain, bias, res_w, down, down_b, up, up_b):
    first = lax.axis_index("section") == 0
    size = lax.axis_size("dp")
    inputs = features.reshape(MB, SLOT, C)
    cotangent = out_grad.reshape(MB, SLOT, C)
    own, picks = lengths[0, 0], join_pick[0]
    to_upper = lambda x: lax.ppermute(x, "section", [(0, 1)])
    to_lower = lambda x: lax.ppermute(x, "section", [(1, 0)])

    far_len = swap(own)
    joining = jnp.concatenate([lax.dynamic_index_in_dim(inputs, picks[m], 0, False)[HALF:] for m in range(OWN)], axis=0)
    far_rows = swap(jnp.where(first, inputs[MB - 1], joining))
    far_w0 = swap(pw[0, 0:1])
    taps = jnp.concatenate([dw[0].reshape(5 * TAPS, C), gain[0], bias[0]], axis=0)
    far_taps = swap(taps)
    far_pw, far_res = swap(pw[0]), swap(res_w[0])
    wide = jnp.pad(down_b, ((0, 0), (0, C - SE)))
    squeeze = jnp.concatenate([down[0].T, up[0], up_b, wide], axis=0)
    far_squeeze = swap(squeeze)
    far_cot = to_lower(cotangent[:OWN])
    far_cot0 = to_upper(cotangent[MB - 1, :HALF])

    flag = first.astype(jnp.int32)[None]
    mine = lambda v: jnp.where(first, v[:OWN], jnp.concatenate([v[OWN:], jnp.zeros((1,), v.dtype)]))
    length = mine(jnp.where(first, own, far_len))
    half_len = (length + 1) // 2
    join_len = mine(jnp.where(first, far_len, own)[picks])
    meta1 = jnp.concatenate([length, half_len, flag])
    meta2 = jnp.concatenate([half_len, join_len, flag, picks[MB - 1 :]])

    def small(block):
        t = jnp.where(first == (block == 0), taps, far_taps)
        q = jnp.where(first == (block == 0), squeeze, far_squeeze)
        return (
            t[: 5 * TAPS].reshape(5, TAPS, C), t[5 * TAPS : 5 * TAPS + 6], t[5 * TAPS + 6 :],
            q[:SE], q[2 * SE + 1, :SE][:, None], q[SE : 2 * SE], q[2 * SE : 2 * SE + 1],
        )

    def prepared(block, start, stop):
        array = prepare(meta1, (pw[0], res_w[0]), (far_pw, far_res), block, start, stop)
        return array, {i: (array, i - start) for i in range(start, stop)}

    parts0 = [prepared(0, 1, 3), prepared(0, 3, 6)]
    parts1 = [prepared(1, 0, 3), prepared(1, 3, 6)]

    stages, deep = radices(size, 16), radices(size, 4)
    c14 = Block(False, meta1, small(0), {**parts0[0][1], **parts0[1][1]}, stages)
    c14.x, c14.x_far, c14.first_matrix = inputs, far_rows, (pw[0], far_w0)
    c14.forward({2: (parts0[1][0],), 4: (parts1[0][0],)})
    out0 = c14.tail(after=(parts1[1][0],))
    c15 = Block(True, meta2, small(1), {**parts1[0][1], **parts1[1][1]}, stages)
    c15.arrived, c15.joined_far, c15.joined = out0, far_rows, features.reshape(MB, 2, HALF, C)
    c15.forward()
    out1 = c15.tail(cotangent, far_cot)
    c15.backward((4, 3, 2))
    always = own[0] > 0

    half0 = c15.half(0, first, c15.back_got)
    sum0 = lax.psum(half0, "dp")

    def middle(half0):
        upper, lower = c15.fork({"done": c15.done + (half0,)}), c14.fork()
        back, dx1 = upper.backward((1, 0))
        lower.tail_backward(cotangent, far_cot0, back)
        lower.done = upper.done
        half1 = upper.half(1, first)
        lower.backward((4, 3, 2))
        return dx1, half1, lower.half(0, first), lower.state()

    dx1, half1, half2, state = fenced(always, middle, half0)
    sum0, half2 = lax.optimization_barrier((sum0, half2))
    sum1, sum2 = lax.psum((half1, half2), "dp")
    came0 = to_upper(sum0)

    def ending(half2):
        last = c14.fork({**state, "done": (half2,)})
        dx0, = last.backward((1, 0))
        reduction = Reduction(last.half(1, first), deep)
        reduction.step()
        pad = jnp.zeros((1, HALF, C), F32)
        lower = jnp.concatenate([out0, jnp.concatenate([to_lower(out0[0:1, :HALF]), pad], axis=1)], axis=0)
        upper = jnp.concatenate([to_upper(out1), out1[0:1]], axis=0)
        block_out = jnp.where(first, lower, upper)
        lower = jnp.concatenate([dx0, to_lower(dx0[0:1])], axis=0)
        joins = jnp.concatenate([to_upper(dx1), dx1[0:1]], axis=0)
        joins = jnp.stack([lax.dynamic_index_in_dim(joins, jnp.argmax(picks == s), 0, False) for s in range(MB)])
        upper = jnp.concatenate([jnp.zeros_like(joins), joins], axis=1)
        dx = jnp.where(first, lower, upper)
        reduction.x, block_out, dx = lax.optimization_barrier((reduction.x, block_out, dx))
        sum3 = reduction.finish()
        return block_out, dx, sum3

    block_out, dx, sum3 = fenced(always, ending, half2)
    sum1, sum2, sum3 = lax.optimization_barrier((sum1, sum2, sum3))
    came1, came2, came3 = to_upper(sum1), to_lower(sum2), to_lower(sum3)

    size3, size1 = 3 * C // 2, C
    mats14 = lambda a, b: jnp.concatenate([b[:size3], a[:C], a[C:size3]], axis=0)
    mats15 = lambda a, b: jnp.concatenate([b[:size1], a], axis=0)
    near = jnp.where(first, mats14(sum2, sum3), mats15(sum0, sum1)).reshape(6, 1, C // 2, C)
    far = jnp.where(first, mats14(came2, came3), mats15(came0, came1)).reshape(6, 1, C // 2, C)
    matrices = jnp.where(first, jnp.concatenate([near, far], axis=1), jnp.concatenate([far, near], axis=1))
    pw_grad, res_grad = matrices[:5].reshape(1, 5, C, C), matrices[5].reshape(1, C, C)
    near, far = jnp.where(first, sum3[size3:], sum1[size1:]), jnp.where(first, came3[size3:], came1[size1:])
    rows = jnp.where(first, jnp.concatenate([near, far], axis=0), jnp.concatenate([far, near], axis=0))
    dw_grad = rows[TAIL_ROWS : TAIL_ROWS + 40].reshape(1, 5, 8, C)
    norms = jnp.concatenate([dw_grad[0, 1:, TAPS : TAPS + 2], rows[None, 2 * SE + 2 : 2 * SE + 4], rows[None, 2 * SE + 4 : 2 * SE + 6]], axis=0)
    return (
        block_out.reshape(features.shape), dx.reshape(features.shape), dw_grad[:, :, :TAPS], pw_grad,
        norms[None, :, 1], norms[None, :, 0], res_grad, rows[SE : 2 * SE].T[None], rows[2 * SE + 1 : 2 * SE + 2, :SE],
        rows[:SE][None], rows[2 * SE : 2 * SE + 1],
    )


def solution(mesh):
    rows = P("section", "dp", None)
    own = lambda dims: P("section", *([None] * dims))
    weights = (own(3), own(3), own(2), own(2), own(2), own(2), own(1), own(2), own(1))
    in_specs = (rows, rows, rows, P("dp", None), *weights)
    out_specs = (rows, rows, *weights)
    return jax.shard_map(per_device, mesh=mesh, in_specs=in_specs, out_specs=out_specs, check_vma=False)
```

```python
import copy

import jax
import jax.numpy as jnp
from jax import lax
from jax.experimental import pallas as pl
from jax.experimental.pallas import tpu as pltpu
from jax.sharding import PartitionSpec as P

EPSILON = 1e-05
EXACT = lax.Precision.HIGHEST
TAPS = 5
MB = 3
OWN = 2
SLOT = 400
HALF = 200
KEPT = 208
C = 512
LANES = 128
CHUNKS = [slice(c, c + LANES) for c in range(0, C, LANES)]
SE = 64
BF16, F32 = jnp.bfloat16, jnp.float32
VMEM_BYTES = 60 << 20
TAIL_ROWS = 2 * SE + 8
SMALL = 256


def radices(size, most):
    stages, left = [], size
    while left > 1:
        radix = min(most, left)
        while left % radix:
            radix -= 1
        stages.append(radix)
        left //= radix
    return stages


def exchange(block, radix, stride):
    size = lax.axis_size("dp")
    if radix == size:
        return lax.all_to_all(block, "dp", 0, 0)
    groups = []
    for base in range(size):
        if (base // stride) % radix == 0:
            groups.append([base + j * stride for j in range(radix)])
    return lax.all_to_all(block, "dp", 0, 0, axis_index_groups=groups)


def shared(block, stages):
    stride = 1
    for no, radix in enumerate(stages):
        if no:
            block = jnp.broadcast_to(jnp.sum(block, axis=0), (radix,) + block.shape[1:])
        block = exchange(block, radix, stride)
        stride *= radix
    return block


def halves(x):
    high = x.astype(BF16)
    return high, (x - high.astype(F32)).astype(BF16)


def sigmoid(x):
    return 0.5 * jnp.tanh(0.5 * x) + 0.5


def exact_dot(a, b, dims=((1,), (0,))):
    return lax.dot_general(a, b, (dims, ((), ())), precision=EXACT, preferred_element_type=F32)


def fast_dot(a, b, dims=((1,), (0,))):
    return lax.dot_general(a, b, (dims, ((), ())), preferred_element_type=F32)


def stacked_dot(high, low, w, back=False):
    w_high, w_low = w[0], w[1]
    w = jnp.concatenate([w_high, w_high, w_low], axis=1 if back else 0)
    x = jnp.concatenate([high, low, high], axis=1)
    return fast_dot(x, w, ((1,), (1 if back else 0,)))


def stacked_outer(a_high, a_low, b_high, b_low):
    a = jnp.concatenate([a_high, a_low, a_high], axis=0)
    b = jnp.concatenate([b_high, b_high, b_low], axis=0)
    return fast_dot(a, b, ((0,), (0,)))


def column_sum(x):
    return jnp.sum(x, axis=0, keepdims=True)


class Rows:
    def __init__(self, meta, m, two, rows, which=0):
        place = lax.broadcasted_iota(jnp.int32, (rows, LANES), 0)
        if two:
            later = place >= HALF
            limit = jnp.where(later, HALF + meta[OWN + m], meta[m])
            self.mask = place < limit
        else:
            self.mask = place < meta[which * OWN + m]

    def keep(self, x):
        return jnp.where(self.mask, x, 0.0)


class Padded:
    def __init__(self, ref, two):
        self.ref = ref
        self.pieces = [(8, 0, HALF), (16 + HALF, HALF, HALF)] if two else [(8, 0, SLOT)]

    def put(self, x):
        zeros = jnp.zeros((8, LANES), F32)
        for at, start, rows in self.pieces:
            self.ref[at - 8 : at, :] = zeros
            self.ref[at : at + rows, :] = x[start : start + rows]
        self.ref[at + rows : at + rows + 8, :] = zeros

    def get(self, offset):
        parts = [self.ref[at + offset : at + offset + rows, :] for at, _, rows in self.pieces]
        return parts[0] if len(parts) == 1 else jnp.concatenate(parts, axis=0)

    def conv(self, kernel):
        total = kernel[0:1] * self.get(-2)
        for k in range(1, TAPS):
            total = total + kernel[k : k + 1] * self.get(k - 2)
        return total

    def conv_back(self, kernel):
        total = kernel[0:1] * self.get(2)
        for k in range(1, TAPS):
            total = total + kernel[k : k + 1] * self.get(2 - k)
        return total


def every_other(ref, x):
    ref[0:SLOT, :] = x
    ref[SLOT : 2 * KEPT, :] = jnp.zeros((2 * KEPT - SLOT, LANES), F32)
    return ref[pl.ds(0, KEPT, stride=2), :]


def spread_out(ref, x):
    ref[...] = jnp.zeros_like(ref)
    ref[pl.ds(0, KEPT, stride=2), :] = x
    return ref[0:SLOT, :]


def center_spread(sums, rows):
    center = sums[0:1] / rows
    return center, lax.rsqrt(sums[1:2] / rows - center * center + EPSILON)


def added(ref):
    return jnp.sum(ref[:, 0], axis=0)


def accumulate(ref, m, at, value):
    rows = slice(at, at + value.shape[0])
    ref[rows, :] = jnp.where(m == 0, value, ref[rows, :] + value)


def send(ref, rows):
    for copy in range(ref.shape[0]):
        for row, x in enumerate(rows):
            ref[copy, 0, row : row + 1, 0 : x.shape[1]] = x


def pad_scratch():
    return pltpu.VMEM((len(CHUNKS), SLOT + 24, LANES), F32)


def stride_scratch():
    return pltpu.VMEM((len(CHUNKS), 2 * KEPT, LANES), F32)


def slots(rows, cols=C):
    return pl.BlockSpec((1, rows, cols), lambda m, *_: (m, 0, 0))


def copies(count, rows, cols=C):
    return pl.BlockSpec((count, 1, rows, cols), lambda m, *_: (0, m, 0, 0))


def whole(*shape):
    return pl.BlockSpec(shape, lambda m, *_: (0,) * len(shape))


def layer(i, *shape):
    return pl.BlockSpec((1,) + shape, lambda m, *_: (i,) + (0,) * len(shape))


def f32(*shape):
    return jax.ShapeDtypeStruct(shape, F32)


def bf16(*shape):
    return jax.ShapeDtypeStruct(shape, BF16)


def call(body, meta, args, outs, scratch=(), name=None, flops=0, steps=OWN, after=(), into=()):
    arrays, in_specs = [a for a, _ in args], [s for _, s in args]
    shapes, out_specs = [a for a, _ in outs], [s for _, s in outs]
    size = sum(a.size * a.dtype.itemsize for a in arrays + shapes)
    extra = list(after) + list(into)
    count = len(arrays)

    def inner(meta, *refs):
        body(meta, *refs[:count], *refs[count + len(extra) :])

    return pl.pallas_call(
        inner,
        out_shape=shapes,
        grid_spec=pltpu.PrefetchScalarGridSpec(
            num_scalar_prefetch=1,
            grid=(steps,),
            in_specs=in_specs + [pl.BlockSpec(memory_space=pl.ANY)] * len(extra),
            out_specs=out_specs,
            scratch_shapes=list(scratch),
        ),
        input_output_aliases={1 + count + len(after) + j: j for j in range(len(into))},
        compiler_params=pltpu.CompilerParams(vmem_limit_bytes=VMEM_BYTES),
        cost_estimate=pl.CostEstimate(flops=flops, bytes_accessed=size, transcendentals=0),
        name=name,
    )(meta, *arrays, *extra)


def choose(meta, block, own, far):
    return jnp.where(meta[2 * OWN] == 1 - block, own, far)


def prepare(meta, own, far, block, start, stop):
    def body(meta, *refs):
        pair = [ref[0] for ref in refs[:2]]
        if stop == 6:
            last = pl.program_id(0) == 5 - start
            pair = [jnp.where(last, ref[...], w) for ref, w in zip(refs[2:4], pair)]
        out = refs[-1]
        out[0, 0], out[0, 1] = halves(choose(meta, block, *pair))

    matrix = pl.BlockSpec((1, C, C), lambda j, *_: (jnp.minimum(j + start, 4), 0, 0))
    args = [(own[0], matrix), (far[0], matrix)]
    if stop == 6:
        args += [(own[1], whole(C, C)), (far[1], whole(C, C))]
    out = pl.BlockSpec((1, 2, C, C), lambda j, *_: (j, 0, 0, 0))
    name = f"prepare_{block}_{start}"
    return call(body, meta, args, [(bf16(stop - start, 2, C, C), out)], name=name, steps=stop - start)[0]


class Block:
    def __init__(self, two, meta, weights, ready, stages):
        self.done, self.stop, self.pending = (), None, None
        self.two, self.meta, self.stages = two, meta, stages
        self.dw, self.gain, self.bias, self.down, self.down_b, self.up, self.up_b = weights
        self.ready = ready
        self.tail_rows = SLOT if two else KEPT
        self.first, self.last = stages[0], stages[-1]
        self.tag = "c15" if two else "c14"

    def rows_of(self, i):
        return self.tail_rows if i == 4 else SLOT

    def valid(self, meta, m, i):
        last = i == 4 and not self.two
        return Rows(meta, m, self.two, self.rows_of(i), which=1 if last else 0)

    def matrix(self, i):
        array, at = self.ready[i]
        return (array, layer(at, 2, C, C))

    def source_args(self):
        if not self.two:
            return [(self.x, slots(SLOT)), (self.x_far, whole(SLOT, C))]
        far = pl.BlockSpec((HALF, C), lambda m, *_: (m, 0))
        near = pl.BlockSpec((1, 1, HALF, C), lambda m, meta: (meta[2 * OWN + 1], 1, 0, 0))
        return [(self.arrived, slots(HALF)), (self.joined_far, far), (self.joined, near)]

    def source(self, meta, refs, cs):
        lower = meta[2 * OWN] == 1
        if not self.two:
            return jnp.where(lower, refs[0][0, :, cs], refs[1][:, cs])
        joined = jnp.where(lower, refs[1][:, cs], refs[2][0, 0, :, cs])
        return jnp.concatenate([refs[0][0, :, cs], joined], axis=0)

    def before_args(self, i):
        if i == 0:
            return self.source_args()
        return [(self.z[i - 1], slots(SLOT)), (self.stats[i - 1], slots(2))]


    def forward_layer(self, i, after=()):
        two, count = self.two, self.first
        strided = i == 4 and not two
        rows = self.rows_of(i)
        n_src = len(self.source_args())
        width = C + LANES if i == 0 else C
        sent = 4 if i == 3 else 2
        makes = i == 0 and not two

        def body(meta, *refs):
            refs = list(refs)
            take = lambda n: [refs.pop(0) for _ in range(n)]
            m = pl.program_id(0)
            if i == 0:
                src = take(n_src)
            else:
                z_ref, got_ref = take(2)
                n_ref, = take(1) if i > 1 else (None,)
                gain_ref, bias_ref = take(2)
                res_sum, = take(1) if i == 3 else (None,)
            dw_ref, = take(1)
            if makes:
                own_ref, far_ref, z_out, pay, w_ref = take(5)

                @pl.when(m == 0)
                def _():
                    w_ref[0, 0], w_ref[0, 1] = halves(choose(meta, 0, own_ref[0], far_ref[0]))

            else:
                w_ref, z_out, pay = take(3)
            if i:
                stat_out, = take(1)
            if i == 1:
                n_out, = take(1)
            pad, y_ref = take(2)
            alt, = take(1) if strided else (None,)
            valid_in = self.valid(meta, m, 0)
            if i:
                sums = added(got_ref)
                if i == 1:
                    count_in = jnp.maximum(jnp.concatenate([sums[0:1, C:]] * len(CHUNKS), axis=1), 1.0)
                    count_out = jnp.maximum(jnp.concatenate([sums[1:2, C:]] * len(CHUNKS), axis=1), 1.0)
                    n_out[0, 0:1, :] = count_in
                    n_out[0, 1:2, :] = count_out
                else:
                    count_in = n_ref[0, 0:1, :]
                center, spread = center_spread(sums[:, :C], count_in)
                stat_out[0, 0:1, :] = center
                stat_out[0, 1:2, :] = spread
                scale = gain_ref[i - 1 : i] * spread
                shift = bias_ref[i - 1 : i] - center * scale
            for c, cs in enumerate(CHUNKS):
                if i == 0:
                    h = valid_in.keep(self.source(meta, src, cs))
                else:
                    u = z_ref[0, :, cs] * scale[:, cs] + shift[:, cs]
                    h = valid_in.keep(u * sigmoid(u))
                padded = Padded(pad.at[c], two)
                padded.put(h)
                y = padded.conv(dw_ref[0, :, cs])
                if strided:
                    y = every_other(alt.at[c], y)
                high, low = halves(y)
                y_ref[:, cs] = high
                y_ref[:, C + cs.start : C + cs.stop] = low
            w = w_ref.at[0] if makes else w_ref.at[0]
            z = stacked_dot(y_ref[:, 0:C], y_ref[:, C : 2 * C], w)
            z_out[0] = z
            valid = self.valid(meta, m, i)
            one, square = [], []
            for cs in CHUNKS:
                kept = valid.keep(z[:, cs])
                one.append(column_sum(kept))
                square.append(column_sum(kept * kept))
            if i == 0:
                if two:
                    number = (meta[m] + meta[OWN + m]).astype(F32)
                    numbers = number, number
                else:
                    numbers = meta[m].astype(F32), meta[OWN + m].astype(F32)
                one.append(jnp.full((1, LANES), numbers[0], F32))
                square.append(jnp.full((1, LANES), numbers[1], F32))
            out = [jnp.concatenate(one, axis=1), jnp.concatenate(square, axis=1)]
            if i == 3:
                out += [res_sum[0, 0:1, :], res_sum[0, 1:2, :]]
            send(pay, out)

        if i == 0:
            args = list(self.source_args())
        else:
            got = 4 if i == 4 else 2
            args = [(self.z[i - 1], slots(SLOT)), (self.got[i - 1], copies(self.last, got, C + LANES if i == 1 else C))]
            if i > 1:
                args.append((self.number, slots(2)))
            args += [(self.gain, whole(6, C)), (self.bias, whole(6, C))]
            if i == 3:
                args.append((self.res_sum, slots(2)))
        args.append((self.dw, layer(i, TAPS, C)))
        args += [(w, layer(0, C, C)) for w in self.first_matrix] if makes else [self.matrix(i)]
        outs = [(f32(OWN, rows, C), slots(rows)), (f32(count, OWN, sent, width), copies(count, sent, width))]
        if i:
            outs.append((f32(OWN, 2, C), slots(2)))
        if i == 1:
            outs.append((f32(OWN, 2, C), slots(2)))
        if makes:
            outs.append((bf16(1, 2, C, C), layer(0, 2, C, C)))
        scratch = [pad_scratch(), pltpu.VMEM((rows, 2 * C), BF16)]
        if strided:
            scratch.append(stride_scratch())
        result = call(body, self.meta, args, outs, scratch, f"{self.tag}_forward_{i}", 6 * OWN * rows * C * C, after=after)
        self.z.append(result[0])
        if makes:
            self.ready[0] = (result[2], 0)
        if i:
            self.stats.append(result[2])
        if i == 1:
            self.number = result[3]
        self.got.append(shared(result[1], self.stages))

    def residual(self):
        two, rows = self.two, self.tail_rows

        def body(meta, *refs):
            refs = list(refs)
            src = [refs.pop(0) for _ in self.source_args()]
            w_ref, r_out, x_out, sum_out = refs[:4]
            alt = refs[4] if not two else None
            m = pl.program_id(0)
            valid_in = self.valid(meta, m, 0)
            for c, cs in enumerate(CHUNKS):
                x = valid_in.keep(self.source(meta, src, cs))
                if not two:
                    x = every_other(alt.at[c], x)
                high, low = halves(x)
                x_out[0, :, cs] = high
                x_out[0, :, C + cs.start : C + cs.stop] = low
            r = stacked_dot(x_out[0, :, 0:C], x_out[0, :, C : 2 * C], w_ref.at[0])
            r_out[0] = r
            valid = self.valid(meta, m, 4)
            for cs in CHUNKS:
                kept = valid.keep(r[:, cs])
                sum_out[0, 0:1, cs] = column_sum(kept)
                sum_out[0, 1:2, cs] = column_sum(kept * kept)

        args = self.source_args() + [self.matrix(5)]
        outs = [
            (f32(OWN, rows, C), slots(rows)),
            (bf16(OWN, rows, 2 * C), slots(rows, 2 * C)),
            (f32(OWN, 2, C), slots(2)),
        ]
        scratch = [] if two else [stride_scratch()]
        self.r, self.picked, self.res_sum = call(
            body, self.meta, args, outs, scratch, f"{self.tag}_residual", 6 * OWN * rows * C * C
        )

    def forward(self, after=None):
        self.z, self.got, self.stats = [], [], []
        for i in range(5):
            if i == 2:
                self.residual()
            self.forward_layer(i, (after or {}).get(i, ()))


    def segments(self):
        return [(0, HALF), (HALF, HALF)] if self.two else [(0, self.tail_rows)]

    def lengths(self, meta, m):
        if self.two:
            return [meta[m], meta[OWN + m]]
        return [meta[OWN + m]]

    def squeeze(self, sums, counts, se_refs):
        down_t, down_b, up, up_b = se_refs
        means = [s / jnp.maximum(jnp.full((1, C), n.astype(F32)), 1.0) for s, n in zip(sums, counts)]
        ps = [jnp.sum(down_t[...] * mean, axis=1, keepdims=True) + down_b[...] for mean in means]
        gates = [sigmoid(column_sum(up[...] * (p * sigmoid(p))) + up_b[...]) for p in ps]
        return means, ps, gates

    def squeeze_back(self, des, ps, gates, counts, se_refs, means, small, m):
        down_t, down_b, up, up_b = se_refs
        shares, up_grad, down_grad, dq_sum, dp_sum = [], 0.0, 0.0, 0.0, 0.0
        for de, p, gate, n, mean in zip(des, ps, gates, counts, means):
            dq = de * gate * (1.0 - gate)
            s = sigmoid(p)
            dp = jnp.sum(up[...] * dq, axis=1, keepdims=True) * (s * (1.0 + p * (1.0 - s)))
            shares.append(column_sum(down_t[...] * dp) / jnp.maximum(jnp.full((1, C), n.astype(F32)), 1.0))
            up_grad, down_grad = up_grad + (p * s) * dq, down_grad + dp * mean
            dq_sum, dp_sum = dq_sum + dq, dp_sum + dp
        row, col = (lax.broadcasted_iota(jnp.int32, (SE, C), axis) for axis in (0, 1))
        dp_row = column_sum(jnp.where(row == col, dp_sum, 0.0))
        accumulate(small, m, 0, up_grad)
        accumulate(small, m, SE, down_grad)
        accumulate(small, m, 2 * SE, dq_sum)
        accumulate(small, m, 2 * SE + 1, dp_row)
        return shares

    def last_norm(self, m, dt_out, du_out, z_ref, slope_ref, gates, shares, center, spread, res_bias, res_gain, pay, small):
        bias_sum, gain_sum = [], []
        for cs in CHUNKS:
            dh = dt_out[0, :, cs] * self.by_segment(gates, cs) + self.by_segment(shares, cs)
            du = dh * slope_ref[:, cs]
            du_out[0, :, cs] = du
            bias_sum.append(column_sum(du))
            gain_sum.append(column_sum(du * ((z_ref[0, :, cs] - center[:, cs]) * spread[:, cs])))
        rows = [jnp.concatenate(x, axis=1) for x in (bias_sum, gain_sum, res_bias, res_gain)]
        send(pay, rows)
        for j, row in enumerate(rows):
            accumulate(small, m, 2 * SE + 2 + j, row)

    def se_args(self):
        return [(self.down, whole(SE, C)), (self.down_b, whole(SE, 1)), (self.up, whole(SE, C)), (self.up_b, whole(1, C))]

    def store_rows(self, ref, rows):
        ref[0] = jnp.concatenate(rows + [jnp.zeros((8 - len(rows), C), F32)], axis=0)

    def store_columns(self, ref, columns):
        ref[0] = jnp.zeros((SE, 8), F32)
        for j, column in enumerate(columns):
            ref[0, :, j : j + 1] = column

    def by_segment(self, rows, cs):
        parts = [jnp.broadcast_to(row[:, cs], (n, LANES)) for row, (_, n) in zip(rows, self.segments())]
        return parts[0] if len(parts) == 1 else jnp.concatenate(parts, axis=0)

    def seg_sums(self, x):
        return [column_sum(x[at : at + n]) for at, n in self.segments()]

    def tail(self, cotangent=None, far=None, after=()):
        two, rows = self.two, self.tail_rows
        back = cotangent is not None

        def body(meta, *refs):
            refs = list(refs)
            take = lambda n: [refs.pop(0) for _ in range(n)]
            m = pl.program_id(0)
            z_ref, got4, r_ref, got3, n_ref, gain, bias = take(7)
            se_refs = take(4)
            if back:
                cot_ref, far_ref = take(2)
            out, stat_out, rstat_out, means_out, p_out, gate_out = take(6)
            if back:
                small, du_out, dt_out, pay = take(4)
            h_ref, = take(1)
            if back:
                slope_ref, = take(1)
            valid = self.valid(meta, m, 4)
            number = n_ref[0, 1:2, :]
            center, spread = center_spread(added(got4), number)
            rcenter, rspread = center_spread(added(got3)[2:4], number)
            stat_out[0, 0:1, :] = center
            stat_out[0, 1:2, :] = spread
            rstat_out[0, 0:1, :] = rcenter
            rstat_out[0, 1:2, :] = rspread
            scale = gain[4:5] * spread
            shift = bias[4:5] - center * scale
            sums = []
            for cs in CHUNKS:
                u = z_ref[0, :, cs] * scale[:, cs] + shift[:, cs]
                s = sigmoid(u)
                h = valid.keep(u * s)
                h_ref[:, cs] = h
                if back:
                    slope_ref[:, cs] = valid.keep(s * (1.0 + u * (1.0 - s)))
                sums.append(self.seg_sums(h))
            sums = [jnp.concatenate([s[j] for s in sums], axis=1) for j in range(len(self.segments()))]
            counts = self.lengths(meta, m)
            means, ps, gates = self.squeeze(sums, counts, se_refs)
            self.store_rows(means_out, means)
            self.store_columns(p_out, ps)
            self.store_rows(gate_out, gates)
            res_gain, res_bias, gate_grad = [], [], []
            for cs in CHUNKS:
                h = h_ref[:, cs]
                rh = (r_ref[0, :, cs] - rcenter[:, cs]) * rspread[:, cs]
                t = h * self.by_segment(gates, cs) + gain[5:6, cs] * rh + bias[5:6, cs]
                s = sigmoid(t)
                out[0, 0:rows, cs] = valid.keep(t * s)
                if rows < SLOT:
                    out[0, rows:SLOT, cs] = jnp.zeros((SLOT - rows, LANES), F32)
                if back:
                    cot = jnp.where(meta[2 * OWN] == 1, far_ref[0, :, cs], cot_ref[0, :, cs])
                    dt = valid.keep(cot * (s * (1.0 + t * (1.0 - s))))
                    dt_out[0, :, cs] = dt
                    res_bias.append(column_sum(dt))
                    res_gain.append(column_sum(dt * rh))
                    gate_grad.append(self.seg_sums(dt * h))
            if not back:
                return
            des = [jnp.concatenate([g[j] for g in gate_grad], axis=1) for j in range(len(counts))]
            shares = self.squeeze_back(des, ps, gates, counts, se_refs, means, small, m)
            self.last_norm(m, dt_out, du_out, z_ref, slope_ref, gates, shares, center, spread, res_bias, res_gain, pay, small)

        args = [
            (self.z[4], slots(rows)), (self.got[4], copies(self.last, 2)), (self.r, slots(rows)),
            (self.got[3], copies(self.last, 4)), (self.number, slots(2)),
            (self.gain, whole(6, C)), (self.bias, whole(6, C)),
        ] + self.se_args()
        outs = [
            (f32(OWN, SLOT, C), slots(SLOT)), (f32(OWN, 2, C), slots(2)), (f32(OWN, 2, C), slots(2)),
            (f32(OWN, 8, C), slots(8)), (f32(OWN, SE, 8), slots(SE, 8)), (f32(OWN, 8, C), slots(8)),
        ]
        scratch = [pltpu.VMEM((rows, C), F32)]
        if back:
            args += [(cotangent, layer(MB - 1, SLOT, C)), (far, slots(SLOT))]
            outs += self.tail_outs()
            scratch.append(pltpu.VMEM((rows, C), F32))
        result = call(body, self.meta, args, outs, scratch, f"{self.tag}_tail", after=after)
        self.stats.append(result[1])
        self.rstat, self.se_state = result[2], result[3:6]
        if back:
            self.tail_results(result[6:])
        return result[0]

    def tail_outs(self):
        rows, count = self.tail_rows, self.first
        return [
            (f32(SMALL, C), whole(TAIL_ROWS, C)), (f32(OWN, rows, C), slots(rows)), (f32(OWN, rows, C), slots(rows)),
            (f32(count, OWN, 4, C), copies(count, 4)),
        ]

    def tail_results(self, result):
        self.small, self.du, self.dt, pay = result
        self.back_got = shared(pay, self.stages)

    def tail_backward(self, cotangent, far, back):
        rows = self.tail_rows

        def body(meta, z_ref, r_ref, stat, rstat, gain, bias, means_ref, p_ref, gate_ref, down, down_b, up, up_b, cot_ref, far_ref, back_ref,
                 small, du_out, dt_out, pay, slope_ref):
            m = pl.program_id(0)
            valid = self.valid(meta, m, 4)
            center, spread, rcenter, rspread = stat[0, 0:1], stat[0, 1:2], rstat[0, 0:1], rstat[0, 1:2]
            scale = gain[4:5] * spread
            shift = bias[4:5] - center * scale
            zeros = jnp.zeros((rows - HALF, LANES), F32)
            counts = self.lengths(meta, m)
            ps = [p_ref[0, :, j : j + 1] for j in range(len(counts))]
            gates = [gate_ref[0, j : j + 1, :] for j in range(len(counts))]
            means = [means_ref[0, j : j + 1, :] for j in range(len(counts))]
            res_gain, res_bias, gate_grad = [], [], []
            for cs in CHUNKS:
                u = z_ref[0, :, cs] * scale[:, cs] + shift[:, cs]
                s = sigmoid(u)
                h = valid.keep(u * s)
                slope_ref[:, cs] = valid.keep(s * (1.0 + u * (1.0 - s)))
                rh = (r_ref[0, :, cs] - rcenter[:, cs]) * rspread[:, cs]
                t = h * self.by_segment(gates, cs) + gain[5:6, cs] * rh + bias[5:6, cs]
                s = sigmoid(t)
                here = jnp.where(meta[2 * OWN] == 1, cot_ref[0, 0:HALF, cs], far_ref[:, cs])
                cot = jnp.concatenate([here + back_ref[0, :, cs], zeros], axis=0)
                dt = valid.keep(cot * (s * (1.0 + t * (1.0 - s))))
                dt_out[0, :, cs] = dt
                res_bias.append(column_sum(dt))
                res_gain.append(column_sum(dt * rh))
                gate_grad.append(self.seg_sums(dt * h))
            des = [jnp.concatenate([g[j] for g in gate_grad], axis=1) for j in range(len(counts))]
            shares = self.squeeze_back(des, ps, gates, counts, (down, down_b, up, up_b), means, small, m)
            self.last_norm(m, dt_out, du_out, z_ref, slope_ref, gates, shares, center, spread, res_bias, res_gain, pay, small)

        args = [
            (self.z[4], slots(rows)), (self.r, slots(rows)), (self.stats[4], slots(2)), (self.rstat, slots(2)),
            (self.gain, whole(6, C)), (self.bias, whole(6, C)),
            (self.se_state[0], slots(8)), (self.se_state[1], slots(SE, 8)), (self.se_state[2], slots(8)),
        ] + self.se_args() + [(cotangent, slots(SLOT)), (far, whole(HALF, C)), (back, slots(HALF))]
        scratch = [pltpu.VMEM((rows, C), F32)]
        self.tail_results(call(body, self.meta, args, self.tail_outs(), scratch, f"{self.tag}_tail_back"))


    def norm_grad(self, du, zh, scale, sums, number, cs):
        return scale[:, cs] * (du - sums[0:1, cs] / number[:, cs] - zh * (sums[1:2, cs] / number[:, cs]))

    def backward_layer(self, i):
        two, count = self.two, self.first
        strided = i == 4 and not two
        rows = self.rows_of(i)
        n_src = len(self.source_args())

        def body(meta, *refs):
            refs = list(refs)
            take = lambda n: [refs.pop(0) for _ in range(n)]
            m = pl.program_id(0)
            du_ref, z_ref, w_ref, got, n_ref, stat, gain, bias, dw_ref = take(9)
            if i:
                zp_ref, statp = take(2)
            else:
                dxr_ref, = take(1)
                src = take(n_src)
            small, dz_out = take(2)
            if i:
                du_out, pay = take(2)
            elif two:
                back_out, dx_out = take(2)
            else:
                dx_out, = take(1)
            pad, = take(1)
            alt, = take(1) if refs else (None,)
            sums = added(got)
            number = n_ref[0, 1:2, :] if i == 4 else n_ref[0, 0:1, :]
            center, spread = stat[0, 0:1], stat[0, 1:2]
            scale = gain[i : i + 1] * spread
            valid = self.valid(meta, m, i)
            for cs in CHUNKS:
                zh = (z_ref[0, :, cs] - center[:, cs]) * spread[:, cs]
                dz = valid.keep(self.norm_grad(du_ref[0, :, cs], zh, scale, sums, number, cs))
                high, low = halves(dz)
                dz_out[0, :, cs] = high
                dz_out[0, :, C + cs.start : C + cs.stop] = low
            dy = stacked_dot(dz_out[0, :, 0:C], dz_out[0, :, C : 2 * C], w_ref.at[0], True)
            valid_in = self.valid(meta, m, 0)
            if i:
                pcenter, pspread = statp[0, 0:1], statp[0, 1:2]
                pscale = gain[i - 1 : i] * pspread
                pshift = bias[i - 1 : i] - pcenter * pscale
            taps, bias_sum, gain_sum = [[] for _ in range(TAPS)], [], []
            for c, cs in enumerate(CHUNKS):
                grad = dy[:, cs]
                if strided:
                    grad = spread_out(alt.at[c], grad)
                padded = Padded(pad.at[c], two)
                padded.put(grad)
                if i:
                    z = zp_ref[0, :, cs]
                    u = z * pscale[:, cs] + pshift[:, cs]
                    s = sigmoid(u)
                    h = valid_in.keep(u * s)
                else:
                    h = valid_in.keep(self.source(meta, src, cs))
                dh = None
                for k in range(TAPS):
                    moved = padded.get(2 - k)
                    taps[k].append(column_sum(h * moved))
                    term = dw_ref[0, k : k + 1, cs] * moved
                    dh = term if dh is None else dh + term
                if i:
                    du = valid_in.keep(dh * (s * (1.0 + u * (1.0 - s))))
                    du_out[0, :, cs] = du
                    bias_sum.append(column_sum(du))
                    gain_sum.append(column_sum(du * ((z - pcenter[:, cs]) * pspread[:, cs])))
                    continue
                dxr = dxr_ref[0, :, cs]
                if not two:
                    dxr = spread_out(alt.at[c], dxr)
                dx = valid_in.keep(dh) + dxr
                if two:
                    back_out[0, :, cs] = dx[:HALF]
                    dx = dx[HALF:]
                dx_out[0, :, cs] = dx
            rows = taps + [bias_sum, gain_sum] if i else taps
            rows = [jnp.concatenate(x, axis=1) for x in rows]
            for j, row in enumerate(rows):
                accumulate(small, m, j, row)
            if i:
                send(pay, rows[TAPS:])

        sent = 4 if i == 4 else 2
        args = [
            (self.du, slots(rows)), (self.z[i], slots(rows)), self.matrix(i), (self.back_got, copies(self.last, sent)),
            (self.number, slots(2)), (self.stats[i], slots(2)), (self.gain, whole(6, C)), (self.bias, whole(6, C)),
            (self.dw, layer(i, TAPS, C)),
        ]
        if not i:
            args.append((self.dxr, slots(self.tail_rows)))
        args += self.before_args(i)
        place = TAIL_ROWS // 8 + i
        outs = [(f32(SMALL, C), pl.BlockSpec((8, C), lambda m, *_: (place, 0))), (bf16(OWN, rows, 2 * C), slots(rows, 2 * C))]
        if i:
            outs += [(f32(OWN, SLOT, C), slots(SLOT)), (f32(count, OWN, 2, C), copies(count, 2))]
        elif two:
            outs += [(f32(OWN, HALF, C), slots(HALF)), (f32(OWN, HALF, C), slots(HALF))]
        else:
            outs += [(f32(OWN, SLOT, C), slots(SLOT))]
        scratch = [pad_scratch()]
        if strided or (i == 0 and not two):
            scratch.append(stride_scratch())
        self.small, dz, *result = call(
            body, self.meta, args, outs, scratch, f"{self.tag}_backward_{i}", 6 * OWN * rows * C * C,
            after=self.done, into=(self.small,),
        )
        got = self.back_got
        if i:
            self.du = result[0]
            if i == self.stop:
                self.pending = dz, result[1]
                return result
            self.back_got = shared(result[1], self.stages)
        self.weight_grad(i, dz)
        if i == 4:
            self.residual_back(got)
        return result

    def residual_back(self, got):
        rows = self.tail_rows

        def body(meta, got, n_ref, dt_ref, r_ref, rstat, gain, w_ref, x_ref, kept_out, away_out, dxr_out, dr, total):
            m = pl.program_id(0)
            sums = added(got)[2:4]
            number = n_ref[0, 1:2, :]
            center, spread = rstat[0, 0:1], rstat[0, 1:2]
            scale = gain[5:6] * spread
            valid = self.valid(meta, m, 4)
            for cs in CHUNKS:
                rh = (r_ref[0, :, cs] - center[:, cs]) * spread[:, cs]
                high, low = halves(valid.keep(self.norm_grad(dt_ref[0, :, cs], rh, scale, sums, number, cs)))
                dr[:, cs] = high
                dr[:, C + cs.start : C + cs.stop] = low
            high, low = dr[:, 0:C], dr[:, C : 2 * C]
            dxr_out[0] = stacked_dot(high, low, w_ref.at[0], True)
            grad = stacked_outer(x_ref[0, :, 0:C], x_ref[0, :, C : 2 * C], high, low)
            self.add_halves(meta, m, grad, total, kept_out, away_out)

        args = [
            (got, copies(self.last, 4)), (self.number, slots(2)), (self.dt, slots(rows)), (self.r, slots(rows)),
            (self.rstat, slots(2)), (self.gain, whole(6, C)), self.matrix(5), (self.picked, slots(rows, 2 * C)),
        ]
        outs = self.piece_out(5) + [(f32(OWN, rows, C), slots(rows))]
        which = PLACES[self.tag][5][0]
        *self.pieces[which], self.dxr = call(
            body, self.meta, args, outs, [pltpu.VMEM((rows, 2 * C), BF16), pltpu.VMEM((C, C), F32)],
            f"{self.tag}_residual_back", 12 * OWN * rows * C * C, into=self.pieces[which],
        )

    def piece_out(self, i):
        which, place = PLACES[self.tag][i]
        rows = PIECE_ROWS[self.tag][which]
        return [(f32(rows, C), pl.BlockSpec((C // 2, C), lambda m, *_: (place, 0)))] * 2

    def add_halves(self, meta, m, grad, total, kept_out, away_out):
        @pl.when(m == 0)
        def _():
            total[...] = grad

        @pl.when(m > 0)
        def _():
            top, bottom = total[0 : C // 2] + grad[0 : C // 2], total[C // 2 : C] + grad[C // 2 : C]
            lower = meta[2 * OWN] == 1
            kept_out[...] = jnp.where(lower, top, bottom)
            away_out[...] = jnp.where(lower, bottom, top)

    def weight_grad(self, i, dz):
        two = self.two
        strided = i == 4 and not two
        rows = self.rows_of(i)
        n_src = len(self.source_args())

        def body(meta, *refs):
            refs = list(refs)
            take = lambda n: [refs.pop(0) for _ in range(n)]
            m = pl.program_id(0)
            if i:
                zp_ref, statp, gain, bias = take(4)
                center, spread = statp[0, 0:1], statp[0, 1:2]
                scale = gain[i - 1 : i] * spread
                shift = bias[i - 1 : i] - center * scale
            else:
                src = take(n_src)
            dz_ref, dw_ref, kept_out, away_out, pad, yh, yl, total = take(8)
            alt, = take(1) if strided else (None,)
            valid_in = self.valid(meta, m, 0)
            for c, cs in enumerate(CHUNKS):
                if i:
                    u = zp_ref[0, :, cs] * scale[:, cs] + shift[:, cs]
                    h = valid_in.keep(u * sigmoid(u))
                else:
                    h = valid_in.keep(self.source(meta, src, cs))
                padded = Padded(pad.at[c], two)
                padded.put(h)
                y = padded.conv(dw_ref[0, :, cs])
                if strided:
                    y = every_other(alt.at[c], y)
                yh[:, cs], yl[:, cs] = halves(y)
            grad = stacked_outer(yh[...], yl[...], dz_ref[0, :, 0:C], dz_ref[0, :, C : 2 * C])
            self.add_halves(meta, m, grad, total, kept_out, away_out)

        args = self.before_args(i)
        if i:
            args += [(self.gain, whole(6, C)), (self.bias, whole(6, C))]
        args += [(dz, slots(rows, 2 * C)), (self.dw, layer(i, TAPS, C))]
        scratch = [pad_scratch(), pltpu.VMEM((rows, C), BF16), pltpu.VMEM((rows, C), BF16), pltpu.VMEM((C, C), F32)]
        if strided:
            scratch.append(stride_scratch())
        which = PLACES[self.tag][i][0]
        self.pieces[which] = call(
            body, self.meta, args, self.piece_out(i), scratch, f"{self.tag}_weights_{i}", 6 * OWN * rows * C * C,
            into=self.pieces[which],
        )
        self.done = (self.pieces[which][0],)

    def backward(self, layers):
        if layers[0] == 4:
            self.pieces = [[] for _ in PIECE_ROWS[self.tag]]
        for i in layers:
            result = self.backward_layer(i)
        return result

    def resume(self, i):
        dz, payload = self.pending
        self.back_got = shared(payload, self.stages)
        self.weight_grad(i, dz)

    def fork(self, state=None):
        other = copy.copy(self)
        other.__dict__.update(state or {})
        if "pieces" in other.__dict__:
            other.pieces = list(other.pieces)
        return other

    def state(self):
        return {name: getattr(self, name) for name in ("du", "dxr", "pieces", "small", "pending")}

    def half(self, no, first, later=None):
        kept, away = self.pieces[no]
        if no == len(self.pieces) - 1:
            parts = self.small[: SMALL // 2], self.small[SMALL // 2 :]
            at = kept.shape[0] - SMALL // 2
            kept = lax.dynamic_update_slice_in_dim(kept, jnp.where(first, *parts), at, 0)
            away = lax.dynamic_update_slice_in_dim(away, jnp.where(first, *parts[::-1]), at, 0)
        if later is not None:
            kept, _ = lax.optimization_barrier((kept, later))
        return kept + swap(away)


PLACES = {
    "c15": {3: (0, 0), 4: (0, 1), 5: (0, 2), 0: (1, 0), 1: (1, 1), 2: (1, 2)},
    "c14": {4: (0, 0), 5: (0, 1), 2: (1, 0), 3: (1, 1), 0: (2, 0), 1: (2, 1)},
}
PIECE_ROWS = {"c15": (3 * C // 2, 3 * C // 2 + SMALL // 2), "c14": (C, C, C + SMALL // 2)}


def swap(x):
    return lax.ppermute(x, "section", [(0, 1), (1, 0)])


def fenced(always, work, x):
    shapes = jax.eval_shape(work, x)
    return lax.cond(always, work, lambda x: jax.tree.map(lambda y: jnp.zeros(y.shape, y.dtype), shapes), x)


class Reduction:
    def __init__(self, x, stages):
        self.x = x
        self.todo = []
        stride = 1
        for radix in stages:
            self.todo.append((True, radix, stride))
            stride *= radix
        self.todo += [(False, radix, stride) for _, radix, stride in reversed(self.todo)]

    def step(self):
        scatter, radix, stride = self.todo.pop(0)
        rows = self.x.shape[0]
        if scatter:
            parts = exchange(self.x.reshape(radix, rows // radix, C), radix, stride)
            self.x = jnp.sum(parts, axis=0)
        else:
            parts = exchange(jnp.broadcast_to(self.x, (radix,) + self.x.shape), radix, stride)
            self.x = parts.reshape(radix * rows, C)
        return (self.x,)

    def finish(self):
        while self.todo:
            self.step()
        return self.x


def per_device(features, out_grad, lengths, join_pick, dw, pw, gain, bias, res_w, down, down_b, up, up_b):
    first = lax.axis_index("section") == 0
    size = lax.axis_size("dp")
    inputs = features.reshape(MB, SLOT, C)
    cotangent = out_grad.reshape(MB, SLOT, C)
    own, picks = lengths[0, 0], join_pick[0]
    to_upper = lambda x: lax.ppermute(x, "section", [(0, 1)])
    to_lower = lambda x: lax.ppermute(x, "section", [(1, 0)])

    far_len = swap(own)
    joining = jnp.concatenate([lax.dynamic_index_in_dim(inputs, picks[m], 0, False)[HALF:] for m in range(OWN)], axis=0)
    far_rows = to_upper(inputs[MB - 1])
    far_w0 = swap(pw[0, 0:1])
    taps = jnp.concatenate([dw[0].reshape(5 * TAPS, C), gain[0], bias[0]], axis=0)
    far_taps = swap(taps)
    far_pw, far_res = swap(pw[0]), swap(res_w[0])
    wide = jnp.pad(down_b, ((0, 0), (0, C - SE)))
    squeeze = jnp.concatenate([down[0].T, up[0], up_b, wide], axis=0)
    far_squeeze = swap(squeeze)
    far_cot = to_lower(cotangent[:OWN])
    far_joining = to_lower(joining)
    far_cot0 = to_upper(cotangent[MB - 1, :HALF])

    flag = first.astype(jnp.int32)[None]
    mine = lambda v: jnp.where(first, v[:OWN], jnp.concatenate([v[OWN:], jnp.zeros((1,), v.dtype)]))
    length = mine(jnp.where(first, own, far_len))
    half_len = (length + 1) // 2
    join_len = mine(jnp.where(first, far_len, own)[picks])
    meta1 = jnp.concatenate([length, half_len, flag])
    meta2 = jnp.concatenate([half_len, join_len, flag, picks[MB - 1 :]])

    def small(block):
        t = jnp.where(first == (block == 0), taps, far_taps)
        q = jnp.where(first == (block == 0), squeeze, far_squeeze)
        return (
            t[: 5 * TAPS].reshape(5, TAPS, C), t[5 * TAPS : 5 * TAPS + 6], t[5 * TAPS + 6 :],
            q[:SE], q[2 * SE + 1, :SE][:, None], q[SE : 2 * SE], q[2 * SE : 2 * SE + 1],
        )

    def prepared(block, start, stop):
        array = prepare(meta1, (pw[0], res_w[0]), (far_pw, far_res), block, start, stop)
        return array, {i: (array, i - start) for i in range(start, stop)}

    parts0 = [prepared(0, 1, 3), prepared(0, 3, 6)]
    parts1 = [prepared(1, 0, 1), prepared(1, 1, 3), prepared(1, 3, 6)]

    stages, deep = radices(size, 16), radices(size, 4)
    c14 = Block(False, meta1, small(0), {**parts0[0][1], **parts0[1][1]}, stages)
    c14.x, c14.x_far, c14.first_matrix = inputs, far_rows, (pw[0], far_w0)
    c14.forward({2: (parts0[1][0],)})
    out0 = c14.tail()
    c15 = Block(True, meta2, small(1), {**parts1[0][1], **parts1[1][1], **parts1[2][1]}, stages)
    c15.arrived, c15.joined_far, c15.joined = out0, far_joining, features.reshape(MB, 2, HALF, C)
    c15.forward()
    out1 = c15.tail(cotangent, far_cot)
    c15.stop = 2
    c15.backward((4, 3, 2))
    always = own[0] > 0

    half0 = c15.half(0, first, c15.du)
    sum0 = lax.psum(half0, "dp")

    def middle(half0):
        upper, lower = c15.fork(), c14.fork()
        upper.resume(2)
        upper.done += (half0,)
        back, dx1 = upper.backward((1, 0))
        lower.tail_backward(cotangent, far_cot0, back)
        lower.done = upper.done
        half1 = upper.half(1, first)
        lower.stop = 3
        lower.backward((4, 3))
        return dx1, half1, lower.half(0, first, lower.du), lower.state()

    dx1, half1, half2, state = fenced(always, middle, half0)
    sum0, half2 = lax.optimization_barrier((sum0, half2))
    sum1, sum2 = lax.psum((half1, half2), "dp")
    came0 = to_upper(sum0)

    def ending(half2):
        last = c14.fork(state)
        last.resume(3)
        pad = jnp.zeros((1, HALF, C), F32)
        lower = jnp.concatenate([out0, jnp.concatenate([to_lower(out0[0:1, :HALF]), pad], axis=1)], axis=0)
        block_out = jnp.where(first, lower, jnp.concatenate([to_upper(out1), out1[0:1]], axis=0))
        last.done += (half2, block_out)
        last.backward((2,))
        early = Reduction(last.half(1, first), deep)
        last.backward((1,))
        last.done += early.step()
        dx0, = last.backward((0,))
        late = Reduction(last.half(2, first), deep)
        late.step()
        joins = jnp.concatenate([to_upper(dx1), dx1[0:1]], axis=0)
        joins = jnp.stack([lax.dynamic_index_in_dim(joins, jnp.argmax(picks == s), 0, False) for s in range(MB)])
        upper = jnp.concatenate([jnp.zeros_like(joins), joins], axis=1)
        dx = jnp.where(first, jnp.concatenate([dx0, to_lower(dx0[0:1])], axis=0), upper)
        late.x, dx = lax.optimization_barrier((late.x, dx))
        left = size // deep[0]
        rows = early.x.shape[0] // left
        late.x = jnp.concatenate([early.x.reshape(left, -1, C), late.x.reshape(left, -1, C)], axis=1).reshape(-1, C)
        both = late.finish().reshape(size, -1, C)
        sum3, sum4 = both[:, :rows].reshape(-1, C), both[:, rows:].reshape(-1, C)
        return block_out, dx, sum3, sum4, to_lower(sum3), to_lower(sum4)

    block_out, dx, sum3, sum4, came3, came4 = fenced(always, ending, half2)
    sum1, sum2, sum3 = lax.optimization_barrier((sum1, sum2, sum3))
    came1, came2 = to_upper(sum1), to_lower(sum2)

    mats14 = lambda last, mid, lead: jnp.concatenate([last[:C], mid, lead], axis=0)
    mats15 = lambda rest, lead: jnp.concatenate([rest[: 3 * C // 2], lead], axis=0)
    near = jnp.where(first, mats14(sum4, sum3, sum2), mats15(sum1, sum0)).reshape(6, 1, C // 2, C)
    far = jnp.where(first, mats14(came4, came3, came2), mats15(came1, came0)).reshape(6, 1, C // 2, C)
    matrices = jnp.where(first, jnp.concatenate([near, far], axis=1), jnp.concatenate([far, near], axis=1))
    pw_grad, res_grad = matrices[:5].reshape(1, 5, C, C), matrices[5].reshape(1, C, C)
    near = jnp.where(first, sum4[C:], sum1[3 * C // 2 :])
    far = jnp.where(first, came4[C:], came1[3 * C // 2 :])
    rows = jnp.where(first, jnp.concatenate([near, far], axis=0), jnp.concatenate([far, near], axis=0))
    dw_grad = rows[TAIL_ROWS : TAIL_ROWS + 40].reshape(1, 5, 8, C)
    norms = jnp.concatenate([dw_grad[0, 1:, TAPS : TAPS + 2], rows[None, 2 * SE + 2 : 2 * SE + 4], rows[None, 2 * SE + 4 : 2 * SE + 6]], axis=0)
    return (
        block_out.reshape(features.shape), dx.reshape(features.shape), dw_grad[:, :, :TAPS], pw_grad,
        norms[None, :, 1], norms[None, :, 0], res_grad, rows[SE : 2 * SE].T[None], rows[2 * SE + 1 : 2 * SE + 2, :SE],
        rows[:SE][None], rows[2 * SE : 2 * SE + 1],
    )


def solution(mesh):
    rows = P("section", "dp", None)
    own = lambda dims: P("section", *([None] * dims))
    weights = (own(3), own(3), own(2), own(2), own(2), own(2), own(1), own(2), own(1))
    in_specs = (rows, rows, rows, P("dp", None), *weights)
    out_specs = (rows, rows, *weights)
    return jax.shard_map(per_device, mesh=mesh, in_specs=in_specs, out_specs=out_specs, check_vma=False)
```

```python
import copy

import jax
import jax.numpy as jnp
from jax import lax
from jax.experimental import pallas as pl
from jax.experimental.pallas import tpu as pltpu
from jax.sharding import PartitionSpec as P

EPSILON = 1e-05
EXACT = lax.Precision.HIGHEST
TAPS = 5
MB = 3
OWN = 2
SLOT = 400
HALF = 200
KEPT = 208
C = 512
LANES = 128
CHUNKS = [slice(c, c + LANES) for c in range(0, C, LANES)]
SE = 64
BF16, F32 = jnp.bfloat16, jnp.float32
VMEM_BYTES = 60 << 20
TAIL_ROWS = 2 * SE + 8
SMALL = 256


def radices(size, most):
    stages, left = [], size
    while left > 1:
        radix = min(most, left)
        while left % radix:
            radix -= 1
        stages.append(radix)
        left //= radix
    return stages


def exchange(block, radix, stride):
    size = lax.axis_size("dp")
    if radix == size:
        return lax.all_to_all(block, "dp", 0, 0)
    groups = []
    for base in range(size):
        if (base // stride) % radix == 0:
            groups.append([base + j * stride for j in range(radix)])
    return lax.all_to_all(block, "dp", 0, 0, axis_index_groups=groups)


def shared(block, stages):
    stride = 1
    for no, radix in enumerate(stages):
        if no:
            block = jnp.broadcast_to(jnp.sum(block, axis=0), (radix,) + block.shape[1:])
        block = exchange(block, radix, stride)
        stride *= radix
    return block


def halves(x):
    high = x.astype(BF16)
    return high, (x - high.astype(F32)).astype(BF16)


def sigmoid(x):
    return 0.5 * jnp.tanh(0.5 * x) + 0.5


def exact_dot(a, b, dims=((1,), (0,))):
    return lax.dot_general(a, b, (dims, ((), ())), precision=EXACT, preferred_element_type=F32)


def fast_dot(a, b, dims=((1,), (0,))):
    return lax.dot_general(a, b, (dims, ((), ())), preferred_element_type=F32)


def stacked_dot(high, low, w, back=False):
    w_high, w_low = w[0], w[1]
    w = jnp.concatenate([w_high, w_high, w_low], axis=1 if back else 0)
    x = jnp.concatenate([high, low, high], axis=1)
    return fast_dot(x, w, ((1,), (1 if back else 0,)))


def stacked_outer(a_high, a_low, b_high, b_low):
    a = jnp.concatenate([a_high, a_low, a_high], axis=0)
    b = jnp.concatenate([b_high, b_high, b_low], axis=0)
    return fast_dot(a, b, ((0,), (0,)))


def column_sum(x):
    return jnp.sum(x, axis=0, keepdims=True)


class Rows:
    def __init__(self, meta, m, two, rows, which=0):
        place = lax.broadcasted_iota(jnp.int32, (rows, LANES), 0)
        if two:
            later = place >= HALF
            limit = jnp.where(later, HALF + meta[OWN + m], meta[m])
            self.mask = place < limit
        else:
            self.mask = place < meta[which * OWN + m]

    def keep(self, x):
        return jnp.where(self.mask, x, 0.0)


class Padded:
    def __init__(self, ref, two):
        self.ref = ref
        self.pieces = [(8, 0, HALF), (16 + HALF, HALF, HALF)] if two else [(8, 0, SLOT)]

    def put(self, x):
        zeros = jnp.zeros((8, LANES), F32)
        for at, start, rows in self.pieces:
            self.ref[at - 8 : at, :] = zeros
            self.ref[at : at + rows, :] = x[start : start + rows]
        self.ref[at + rows : at + rows + 8, :] = zeros

    def get(self, offset):
        parts = [self.ref[at + offset : at + offset + rows, :] for at, _, rows in self.pieces]
        return parts[0] if len(parts) == 1 else jnp.concatenate(parts, axis=0)

    def conv(self, kernel):
        total = kernel[0:1] * self.get(-2)
        for k in range(1, TAPS):
            total = total + kernel[k : k + 1] * self.get(k - 2)
        return total

    def conv_back(self, kernel):
        total = kernel[0:1] * self.get(2)
        for k in range(1, TAPS):
            total = total + kernel[k : k + 1] * self.get(2 - k)
        return total


def every_other(ref, x):
    ref[0:SLOT, :] = x
    ref[SLOT : 2 * KEPT, :] = jnp.zeros((2 * KEPT - SLOT, LANES), F32)
    return ref[pl.ds(0, KEPT, stride=2), :]


def spread_out(ref, x):
    ref[...] = jnp.zeros_like(ref)
    ref[pl.ds(0, KEPT, stride=2), :] = x
    return ref[0:SLOT, :]


def center_spread(sums, rows):
    center = sums[0:1] / rows
    return center, lax.rsqrt(sums[1:2] / rows - center * center + EPSILON)


def added(ref):
    return jnp.sum(ref[:, 0], axis=0)


def accumulate(ref, m, at, value):
    rows = slice(at, at + value.shape[0])
    ref[rows, :] = jnp.where(m == 0, value, ref[rows, :] + value)


def send(ref, rows):
    for copy in range(ref.shape[0]):
        for row, x in enumerate(rows):
            ref[copy, 0, row : row + 1, 0 : x.shape[1]] = x


def pad_scratch():
    return pltpu.VMEM((len(CHUNKS), SLOT + 24, LANES), F32)


def stride_scratch():
    return pltpu.VMEM((len(CHUNKS), 2 * KEPT, LANES), F32)


def slots(rows, cols=C):
    return pl.BlockSpec((1, rows, cols), lambda m, *_: (m, 0, 0))


def copies(count, rows, cols=C):
    return pl.BlockSpec((count, 1, rows, cols), lambda m, *_: (0, m, 0, 0))


def whole(*shape):
    return pl.BlockSpec(shape, lambda m, *_: (0,) * len(shape))


def layer(i, *shape):
    return pl.BlockSpec((1,) + shape, lambda m, *_: (i,) + (0,) * len(shape))


def f32(*shape):
    return jax.ShapeDtypeStruct(shape, F32)


def bf16(*shape):
    return jax.ShapeDtypeStruct(shape, BF16)


def call(body, meta, args, outs, scratch=(), name=None, flops=0, steps=OWN, after=(), into=()):
    arrays, in_specs = [a for a, _ in args], [s for _, s in args]
    shapes, out_specs = [a for a, _ in outs], [s for _, s in outs]
    size = sum(a.size * a.dtype.itemsize for a in arrays + shapes)
    extra = list(after) + list(into)
    count = len(arrays)

    def inner(meta, *refs):
        body(meta, *refs[:count], *refs[count + len(extra) :])

    return pl.pallas_call(
        inner,
        out_shape=shapes,
        grid_spec=pltpu.PrefetchScalarGridSpec(
            num_scalar_prefetch=1,
            grid=(steps,),
            in_specs=in_specs + [pl.BlockSpec(memory_space=pl.ANY)] * len(extra),
            out_specs=out_specs,
            scratch_shapes=list(scratch),
        ),
        input_output_aliases={1 + count + len(after) + j: j for j in range(len(into))},
        compiler_params=pltpu.CompilerParams(vmem_limit_bytes=VMEM_BYTES),
        cost_estimate=pl.CostEstimate(flops=flops, bytes_accessed=size, transcendentals=0),
        name=name,
    )(meta, *arrays, *extra)


def choose(meta, block, own, far):
    return jnp.where(meta[2 * OWN] == 1 - block, own, far)


def prepare(meta, own, far, block, start, stop):
    def body(meta, *refs):
        pair = [ref[0] for ref in refs[:2]]
        if stop == 6:
            last = pl.program_id(0) == 5 - start
            pair = [jnp.where(last, ref[...], w) for ref, w in zip(refs[2:4], pair)]
        out = refs[-1]
        out[0, 0], out[0, 1] = halves(choose(meta, block, *pair))

    matrix = pl.BlockSpec((1, C, C), lambda j, *_: (jnp.minimum(j + start, 4), 0, 0))
    args = [(own[0], matrix), (far[0], matrix)]
    if stop == 6:
        args += [(own[1], whole(C, C)), (far[1], whole(C, C))]
    out = pl.BlockSpec((1, 2, C, C), lambda j, *_: (j, 0, 0, 0))
    name = f"prepare_{block}_{start}"
    return call(body, meta, args, [(bf16(stop - start, 2, C, C), out)], name=name, steps=stop - start)[0]


class Block:
    def __init__(self, two, meta, weights, ready, stages):
        self.done, self.stop, self.pending = (), None, None
        self.two, self.meta, self.stages = two, meta, stages
        self.dw, self.gain, self.bias, self.down, self.down_b, self.up, self.up_b = weights
        self.ready = ready
        self.tail_rows = SLOT if two else KEPT
        self.first, self.last = stages[0], stages[-1]
        self.tag = "c15" if two else "c14"

    def rows_of(self, i):
        return self.tail_rows if i == 4 else SLOT

    def valid(self, meta, m, i):
        last = i == 4 and not self.two
        return Rows(meta, m, self.two, self.rows_of(i), which=1 if last else 0)

    def matrix(self, i):
        array, at = self.ready[i]
        return (array, layer(at, 2, C, C))

    def source_args(self):
        if not self.two:
            return [(self.x, slots(SLOT)), (self.x_far, whole(SLOT, C))]
        far = pl.BlockSpec((HALF, C), lambda m, *_: (m, 0))
        near = pl.BlockSpec((1, 1, HALF, C), lambda m, meta: (meta[2 * OWN + 1], 1, 0, 0))
        return [(self.arrived, slots(HALF)), (self.joined_far, far), (self.joined, near)]

    def source(self, meta, refs, cs):
        lower = meta[2 * OWN] == 1
        if not self.two:
            return jnp.where(lower, refs[0][0, :, cs], refs[1][:, cs])
        joined = jnp.where(lower, refs[1][:, cs], refs[2][0, 0, :, cs])
        return jnp.concatenate([refs[0][0, :, cs], joined], axis=0)

    def before_args(self, i):
        if i == 0:
            return self.source_args()
        return [(self.z[i - 1], slots(SLOT)), (self.stats[i - 1], slots(2))]


    def forward_layer(self, i, after=()):
        two, count = self.two, self.first
        strided = i == 4 and not two
        rows = self.rows_of(i)
        n_src = len(self.source_args())
        width = C + LANES if i == 0 else C
        sent = 4 if i == 3 else 2
        makes = i == 0 and not two

        def body(meta, *refs):
            refs = list(refs)
            take = lambda n: [refs.pop(0) for _ in range(n)]
            m = pl.program_id(0)
            if i == 0:
                src = take(n_src)
            else:
                z_ref, got_ref = take(2)
                n_ref, = take(1) if i > 1 else (None,)
                gain_ref, bias_ref = take(2)
                res_sum, = take(1) if i == 3 else (None,)
            dw_ref, = take(1)
            if makes:
                own_ref, far_ref, z_out, pay, w_ref = take(5)

                @pl.when(m == 0)
                def _():
                    w_ref[0, 0], w_ref[0, 1] = halves(choose(meta, 0, own_ref[0], far_ref[0]))

            else:
                w_ref, z_out, pay = take(3)
            if i:
                stat_out, = take(1)
            if i == 1:
                n_out, = take(1)
            pad, y_ref = take(2)
            alt, = take(1) if strided else (None,)
            valid_in = self.valid(meta, m, 0)
            if i:
                sums = added(got_ref)
                if i == 1:
                    count_in = jnp.maximum(jnp.concatenate([sums[0:1, C:]] * len(CHUNKS), axis=1), 1.0)
                    count_out = jnp.maximum(jnp.concatenate([sums[1:2, C:]] * len(CHUNKS), axis=1), 1.0)
                    n_out[0, 0:1, :] = count_in
                    n_out[0, 1:2, :] = count_out
                else:
                    count_in = n_ref[0, 0:1, :]
                center, spread = center_spread(sums[:, :C], count_in)
                stat_out[0, 0:1, :] = center
                stat_out[0, 1:2, :] = spread
                scale = gain_ref[i - 1 : i] * spread
                shift = bias_ref[i - 1 : i] - center * scale
            for c, cs in enumerate(CHUNKS):
                if i == 0:
                    h = valid_in.keep(self.source(meta, src, cs))
                else:
                    u = z_ref[0, :, cs] * scale[:, cs] + shift[:, cs]
                    h = valid_in.keep(u * sigmoid(u))
                padded = Padded(pad.at[c], two)
                padded.put(h)
                y = padded.conv(dw_ref[0, :, cs])
                if strided:
                    y = every_other(alt.at[c], y)
                high, low = halves(y)
                y_ref[:, cs] = high
                y_ref[:, C + cs.start : C + cs.stop] = low
            w = w_ref.at[0] if makes else w_ref.at[0]
            z = stacked_dot(y_ref[:, 0:C], y_ref[:, C : 2 * C], w)
            z_out[0] = z
            valid = self.valid(meta, m, i)
            one, square = [], []
            for cs in CHUNKS:
                kept = valid.keep(z[:, cs])
                one.append(column_sum(kept))
                square.append(column_sum(kept * kept))
            if i == 0:
                if two:
                    number = (meta[m] + meta[OWN + m]).astype(F32)
                    numbers = number, number
                else:
                    numbers = meta[m].astype(F32), meta[OWN + m].astype(F32)
                one.append(jnp.full((1, LANES), numbers[0], F32))
                square.append(jnp.full((1, LANES), numbers[1], F32))
            out = [jnp.concatenate(one, axis=1), jnp.concatenate(square, axis=1)]
            if i == 3:
                out += [res_sum[0, 0:1, :], res_sum[0, 1:2, :]]
            send(pay, out)

        if i == 0:
            args = list(self.source_args())
        else:
            got = 4 if i == 4 else 2
            args = [(self.z[i - 1], slots(SLOT)), (self.got[i - 1], copies(self.last, got, C + LANES if i == 1 else C))]
            if i > 1:
                args.append((self.number, slots(2)))
            args += [(self.gain, whole(6, C)), (self.bias, whole(6, C))]
            if i == 3:
                args.append((self.res_sum, slots(2)))
        args.append((self.dw, layer(i, TAPS, C)))
        args += [(w, layer(0, C, C)) for w in self.first_matrix] if makes else [self.matrix(i)]
        outs = [(f32(OWN, rows, C), slots(rows)), (f32(count, OWN, sent, width), copies(count, sent, width))]
        if i:
            outs.append((f32(OWN, 2, C), slots(2)))
        if i == 1:
            outs.append((f32(OWN, 2, C), slots(2)))
        if makes:
            outs.append((bf16(1, 2, C, C), layer(0, 2, C, C)))
        scratch = [pad_scratch(), pltpu.VMEM((rows, 2 * C), BF16)]
        if strided:
            scratch.append(stride_scratch())
        result = call(body, self.meta, args, outs, scratch, f"{self.tag}_forward_{i}", 6 * OWN * rows * C * C, after=after)
        self.z.append(result[0])
        if makes:
            self.ready[0] = (result[2], 0)
        if i:
            self.stats.append(result[2])
        if i == 1:
            self.number = result[3]
        self.got.append(shared(result[1], self.stages))

    def residual(self):
        two, rows = self.two, self.tail_rows

        def body(meta, *refs):
            refs = list(refs)
            src = [refs.pop(0) for _ in self.source_args()]
            w_ref, r_out, x_out, sum_out = refs[:4]
            alt = refs[4] if not two else None
            m = pl.program_id(0)
            valid_in = self.valid(meta, m, 0)
            for c, cs in enumerate(CHUNKS):
                x = valid_in.keep(self.source(meta, src, cs))
                if not two:
                    x = every_other(alt.at[c], x)
                high, low = halves(x)
                x_out[0, :, cs] = high
                x_out[0, :, C + cs.start : C + cs.stop] = low
            r = stacked_dot(x_out[0, :, 0:C], x_out[0, :, C : 2 * C], w_ref.at[0])
            r_out[0] = r
            valid = self.valid(meta, m, 4)
            for cs in CHUNKS:
                kept = valid.keep(r[:, cs])
                sum_out[0, 0:1, cs] = column_sum(kept)
                sum_out[0, 1:2, cs] = column_sum(kept * kept)

        args = self.source_args() + [self.matrix(5)]
        outs = [
            (f32(OWN, rows, C), slots(rows)),
            (bf16(OWN, rows, 2 * C), slots(rows, 2 * C)),
            (f32(OWN, 2, C), slots(2)),
        ]
        scratch = [] if two else [stride_scratch()]
        self.r, self.picked, self.res_sum = call(
            body, self.meta, args, outs, scratch, f"{self.tag}_residual", 6 * OWN * rows * C * C
        )

    def forward(self, after=None):
        self.z, self.got, self.stats = [], [], []
        for i in range(5):
            if i == 2:
                self.residual()
            self.forward_layer(i, (after or {}).get(i, ()))


    def segments(self):
        return [(0, HALF), (HALF, HALF)] if self.two else [(0, self.tail_rows)]

    def lengths(self, meta, m):
        if self.two:
            return [meta[m], meta[OWN + m]]
        return [meta[OWN + m]]

    def squeeze(self, sums, counts, se_refs):
        down_t, down_b, up, up_b = se_refs
        means = [s / jnp.maximum(jnp.full((1, C), n.astype(F32)), 1.0) for s, n in zip(sums, counts)]
        ps = [jnp.sum(down_t[...] * mean, axis=1, keepdims=True) + down_b[...] for mean in means]
        gates = [sigmoid(column_sum(up[...] * (p * sigmoid(p))) + up_b[...]) for p in ps]
        return means, ps, gates

    def squeeze_back(self, des, ps, gates, counts, se_refs, means, small, m):
        down_t, down_b, up, up_b = se_refs
        shares, up_grad, down_grad, dq_sum, dp_sum = [], 0.0, 0.0, 0.0, 0.0
        for de, p, gate, n, mean in zip(des, ps, gates, counts, means):
            dq = de * gate * (1.0 - gate)
            s = sigmoid(p)
            dp = jnp.sum(up[...] * dq, axis=1, keepdims=True) * (s * (1.0 + p * (1.0 - s)))
            shares.append(column_sum(down_t[...] * dp) / jnp.maximum(jnp.full((1, C), n.astype(F32)), 1.0))
            up_grad, down_grad = up_grad + (p * s) * dq, down_grad + dp * mean
            dq_sum, dp_sum = dq_sum + dq, dp_sum + dp
        row, col = (lax.broadcasted_iota(jnp.int32, (SE, C), axis) for axis in (0, 1))
        dp_row = column_sum(jnp.where(row == col, dp_sum, 0.0))
        accumulate(small, m, 0, up_grad)
        accumulate(small, m, SE, down_grad)
        accumulate(small, m, 2 * SE, dq_sum)
        accumulate(small, m, 2 * SE + 1, dp_row)
        return shares

    def last_norm(self, m, dt_out, du_out, z_ref, slope_ref, gates, shares, center, spread, res_bias, res_gain, pay, small):
        bias_sum, gain_sum = [], []
        for cs in CHUNKS:
            dh = dt_out[0, :, cs] * self.by_segment(gates, cs) + self.by_segment(shares, cs)
            du = dh * slope_ref[:, cs]
            du_out[0, :, cs] = du
            bias_sum.append(column_sum(du))
            gain_sum.append(column_sum(du * ((z_ref[0, :, cs] - center[:, cs]) * spread[:, cs])))
        rows = [jnp.concatenate(x, axis=1) for x in (bias_sum, gain_sum, res_bias, res_gain)]
        send(pay, rows)
        for j, row in enumerate(rows):
            accumulate(small, m, 2 * SE + 2 + j, row)

    def se_args(self):
        return [(self.down, whole(SE, C)), (self.down_b, whole(SE, 1)), (self.up, whole(SE, C)), (self.up_b, whole(1, C))]

    def store_rows(self, ref, rows):
        ref[0] = jnp.concatenate(rows + [jnp.zeros((8 - len(rows), C), F32)], axis=0)

    def store_columns(self, ref, columns):
        ref[0] = jnp.zeros((SE, 8), F32)
        for j, column in enumerate(columns):
            ref[0, :, j : j + 1] = column

    def by_segment(self, rows, cs):
        parts = [jnp.broadcast_to(row[:, cs], (n, LANES)) for row, (_, n) in zip(rows, self.segments())]
        return parts[0] if len(parts) == 1 else jnp.concatenate(parts, axis=0)

    def seg_sums(self, x):
        return [column_sum(x[at : at + n]) for at, n in self.segments()]

    def tail(self, cotangent=None, far=None, after=()):
        two, rows = self.two, self.tail_rows
        back = cotangent is not None

        def body(meta, *refs):
            refs = list(refs)
            take = lambda n: [refs.pop(0) for _ in range(n)]
            m = pl.program_id(0)
            z_ref, got4, r_ref, got3, n_ref, gain, bias = take(7)
            se_refs = take(4)
            if back:
                cot_ref, far_ref = take(2)
            out, stat_out, rstat_out, means_out, p_out, gate_out = take(6)
            if back:
                small, du_out, dt_out, pay = take(4)
            h_ref, = take(1)
            if back:
                slope_ref, = take(1)
            valid = self.valid(meta, m, 4)
            number = n_ref[0, 1:2, :]
            center, spread = center_spread(added(got4), number)
            rcenter, rspread = center_spread(added(got3)[2:4], number)
            stat_out[0, 0:1, :] = center
            stat_out[0, 1:2, :] = spread
            rstat_out[0, 0:1, :] = rcenter
            rstat_out[0, 1:2, :] = rspread
            scale = gain[4:5] * spread
            shift = bias[4:5] - center * scale
            sums = []
            for cs in CHUNKS:
                u = z_ref[0, :, cs] * scale[:, cs] + shift[:, cs]
                s = sigmoid(u)
                h = valid.keep(u * s)
                h_ref[:, cs] = h
                if back:
                    slope_ref[:, cs] = valid.keep(s * (1.0 + u * (1.0 - s)))
                sums.append(self.seg_sums(h))
            sums = [jnp.concatenate([s[j] for s in sums], axis=1) for j in range(len(self.segments()))]
            counts = self.lengths(meta, m)
            means, ps, gates = self.squeeze(sums, counts, se_refs)
            self.store_rows(means_out, means)
            self.store_columns(p_out, ps)
            self.store_rows(gate_out, gates)
            res_gain, res_bias, gate_grad = [], [], []
            for cs in CHUNKS:
                h = h_ref[:, cs]
                rh = (r_ref[0, :, cs] - rcenter[:, cs]) * rspread[:, cs]
                t = h * self.by_segment(gates, cs) + gain[5:6, cs] * rh + bias[5:6, cs]
                s = sigmoid(t)
                out[0, 0:rows, cs] = valid.keep(t * s)
                if rows < SLOT:
                    out[0, rows:SLOT, cs] = jnp.zeros((SLOT - rows, LANES), F32)
                if back:
                    cot = jnp.where(meta[2 * OWN] == 1, far_ref[0, :, cs], cot_ref[0, :, cs])
                    dt = valid.keep(cot * (s * (1.0 + t * (1.0 - s))))
                    dt_out[0, :, cs] = dt
                    res_bias.append(column_sum(dt))
                    res_gain.append(column_sum(dt * rh))
                    gate_grad.append(self.seg_sums(dt * h))
            if not back:
                return
            des = [jnp.concatenate([g[j] for g in gate_grad], axis=1) for j in range(len(counts))]
            shares = self.squeeze_back(des, ps, gates, counts, se_refs, means, small, m)
            self.last_norm(m, dt_out, du_out, z_ref, slope_ref, gates, shares, center, spread, res_bias, res_gain, pay, small)

        args = [
            (self.z[4], slots(rows)), (self.got[4], copies(self.last, 2)), (self.r, slots(rows)),
            (self.got[3], copies(self.last, 4)), (self.number, slots(2)),
            (self.gain, whole(6, C)), (self.bias, whole(6, C)),
        ] + self.se_args()
        outs = [
            (f32(OWN, SLOT, C), slots(SLOT)), (f32(OWN, 2, C), slots(2)), (f32(OWN, 2, C), slots(2)),
            (f32(OWN, 8, C), slots(8)), (f32(OWN, SE, 8), slots(SE, 8)), (f32(OWN, 8, C), slots(8)),
        ]
        scratch = [pltpu.VMEM((rows, C), F32)]
        if back:
            args += [(cotangent, layer(MB - 1, SLOT, C)), (far, slots(SLOT))]
            outs += self.tail_outs()
            scratch.append(pltpu.VMEM((rows, C), F32))
        result = call(body, self.meta, args, outs, scratch, f"{self.tag}_tail", after=after)
        self.stats.append(result[1])
        self.rstat, self.se_state = result[2], result[3:6]
        if back:
            self.tail_results(result[6:])
        return result[0]

    def tail_outs(self):
        rows, count = self.tail_rows, self.first
        return [
            (f32(SMALL, C), whole(TAIL_ROWS, C)), (f32(OWN, rows, C), slots(rows)), (f32(OWN, rows, C), slots(rows)),
            (f32(count, OWN, 4, C), copies(count, 4)),
        ]

    def tail_results(self, result):
        self.small, self.du, self.dt, pay = result
        self.back_got = shared(pay, self.stages)

    def tail_backward(self, cotangent, far, back):
        rows = self.tail_rows

        def body(meta, z_ref, r_ref, stat, rstat, gain, bias, means_ref, p_ref, gate_ref, down, down_b, up, up_b, cot_ref, far_ref, back_ref,
                 small, du_out, dt_out, pay, slope_ref):
            m = pl.program_id(0)
            valid = self.valid(meta, m, 4)
            center, spread, rcenter, rspread = stat[0, 0:1], stat[0, 1:2], rstat[0, 0:1], rstat[0, 1:2]
            scale = gain[4:5] * spread
            shift = bias[4:5] - center * scale
            zeros = jnp.zeros((rows - HALF, LANES), F32)
            counts = self.lengths(meta, m)
            ps = [p_ref[0, :, j : j + 1] for j in range(len(counts))]
            gates = [gate_ref[0, j : j + 1, :] for j in range(len(counts))]
            means = [means_ref[0, j : j + 1, :] for j in range(len(counts))]
            res_gain, res_bias, gate_grad = [], [], []
            for cs in CHUNKS:
                u = z_ref[0, :, cs] * scale[:, cs] + shift[:, cs]
                s = sigmoid(u)
                h = valid.keep(u * s)
                slope_ref[:, cs] = valid.keep(s * (1.0 + u * (1.0 - s)))
                rh = (r_ref[0, :, cs] - rcenter[:, cs]) * rspread[:, cs]
                t = h * self.by_segment(gates, cs) + gain[5:6, cs] * rh + bias[5:6, cs]
                s = sigmoid(t)
                here = jnp.where(meta[2 * OWN] == 1, cot_ref[0, 0:HALF, cs], far_ref[:, cs])
                cot = jnp.concatenate([here + back_ref[0, :, cs], zeros], axis=0)
                dt = valid.keep(cot * (s * (1.0 + t * (1.0 - s))))
                dt_out[0, :, cs] = dt
                res_bias.append(column_sum(dt))
                res_gain.append(column_sum(dt * rh))
                gate_grad.append(self.seg_sums(dt * h))
            des = [jnp.concatenate([g[j] for g in gate_grad], axis=1) for j in range(len(counts))]
            shares = self.squeeze_back(des, ps, gates, counts, (down, down_b, up, up_b), means, small, m)
            self.last_norm(m, dt_out, du_out, z_ref, slope_ref, gates, shares, center, spread, res_bias, res_gain, pay, small)

        args = [
            (self.z[4], slots(rows)), (self.r, slots(rows)), (self.stats[4], slots(2)), (self.rstat, slots(2)),
            (self.gain, whole(6, C)), (self.bias, whole(6, C)),
            (self.se_state[0], slots(8)), (self.se_state[1], slots(SE, 8)), (self.se_state[2], slots(8)),
        ] + self.se_args() + [(cotangent, slots(SLOT)), (far, whole(HALF, C)), (back, slots(HALF))]
        scratch = [pltpu.VMEM((rows, C), F32)]
        self.tail_results(call(body, self.meta, args, self.tail_outs(), scratch, f"{self.tag}_tail_back"))


    def norm_grad(self, du, zh, scale, sums, number, cs):
        return scale[:, cs] * (du - sums[0:1, cs] / number[:, cs] - zh * (sums[1:2, cs] / number[:, cs]))

    def backward_layer(self, i):
        two, count = self.two, self.first
        strided = i == 4 and not two
        rows = self.rows_of(i)
        n_src = len(self.source_args())

        def body(meta, *refs):
            refs = list(refs)
            take = lambda n: [refs.pop(0) for _ in range(n)]
            m = pl.program_id(0)
            du_ref, z_ref, w_ref, got, n_ref, stat, gain, bias, dw_ref = take(9)
            if i:
                zp_ref, statp = take(2)
            else:
                dxr_ref, = take(1)
                src = take(n_src)
            small, dz_out = take(2)
            if i:
                du_out, pay = take(2)
            elif two:
                back_out, dx_out = take(2)
            else:
                dx_out, = take(1)
            pad, = take(1)
            alt, = take(1) if refs else (None,)
            sums = added(got)
            number = n_ref[0, 1:2, :] if i == 4 else n_ref[0, 0:1, :]
            center, spread = stat[0, 0:1], stat[0, 1:2]
            scale = gain[i : i + 1] * spread
            valid = self.valid(meta, m, i)
            for cs in CHUNKS:
                zh = (z_ref[0, :, cs] - center[:, cs]) * spread[:, cs]
                dz = valid.keep(self.norm_grad(du_ref[0, :, cs], zh, scale, sums, number, cs))
                high, low = halves(dz)
                dz_out[0, :, cs] = high
                dz_out[0, :, C + cs.start : C + cs.stop] = low
            dy = stacked_dot(dz_out[0, :, 0:C], dz_out[0, :, C : 2 * C], w_ref.at[0], True)
            valid_in = self.valid(meta, m, 0)
            if i:
                pcenter, pspread = statp[0, 0:1], statp[0, 1:2]
                pscale = gain[i - 1 : i] * pspread
                pshift = bias[i - 1 : i] - pcenter * pscale
            taps, bias_sum, gain_sum = [[] for _ in range(TAPS)], [], []
            for c, cs in enumerate(CHUNKS):
                grad = dy[:, cs]
                if strided:
                    grad = spread_out(alt.at[c], grad)
                padded = Padded(pad.at[c], two)
                padded.put(grad)
                if i:
                    z = zp_ref[0, :, cs]
                    u = z * pscale[:, cs] + pshift[:, cs]
                    s = sigmoid(u)
                    h = valid_in.keep(u * s)
                else:
                    h = valid_in.keep(self.source(meta, src, cs))
                dh = None
                for k in range(TAPS):
                    moved = padded.get(2 - k)
                    taps[k].append(column_sum(h * moved))
                    term = dw_ref[0, k : k + 1, cs] * moved
                    dh = term if dh is None else dh + term
                if i:
                    du = valid_in.keep(dh * (s * (1.0 + u * (1.0 - s))))
                    du_out[0, :, cs] = du
                    bias_sum.append(column_sum(du))
                    gain_sum.append(column_sum(du * ((z - pcenter[:, cs]) * pspread[:, cs])))
                    continue
                dxr = dxr_ref[0, :, cs]
                if not two:
                    dxr = spread_out(alt.at[c], dxr)
                dx = valid_in.keep(dh) + dxr
                if two:
                    back_out[0, :, cs] = dx[:HALF]
                    dx = dx[HALF:]
                dx_out[0, :, cs] = dx
            rows = taps + [bias_sum, gain_sum] if i else taps
            rows = [jnp.concatenate(x, axis=1) for x in rows]
            for j, row in enumerate(rows):
                accumulate(small, m, j, row)
            if i:
                send(pay, rows[TAPS:])

        sent = 4 if i == 4 else 2
        args = [
            (self.du, slots(rows)), (self.z[i], slots(rows)), self.matrix(i), (self.back_got, copies(self.last, sent)),
            (self.number, slots(2)), (self.stats[i], slots(2)), (self.gain, whole(6, C)), (self.bias, whole(6, C)),
            (self.dw, layer(i, TAPS, C)),
        ]
        if not i:
            args.append((self.dxr, slots(self.tail_rows)))
        args += self.before_args(i)
        place = TAIL_ROWS // 8 + i
        outs = [(f32(SMALL, C), pl.BlockSpec((8, C), lambda m, *_: (place, 0))), (bf16(OWN, rows, 2 * C), slots(rows, 2 * C))]
        if i:
            outs += [(f32(OWN, SLOT, C), slots(SLOT)), (f32(count, OWN, 2, C), copies(count, 2))]
        elif two:
            outs += [(f32(OWN, HALF, C), slots(HALF)), (f32(OWN, HALF, C), slots(HALF))]
        else:
            outs += [(f32(OWN, SLOT, C), slots(SLOT))]
        scratch = [pad_scratch()]
        if strided or (i == 0 and not two):
            scratch.append(stride_scratch())
        self.small, dz, *result = call(
            body, self.meta, args, outs, scratch, f"{self.tag}_backward_{i}", 6 * OWN * rows * C * C,
            after=self.done, into=(self.small,),
        )
        got = self.back_got
        if i:
            self.du = result[0]
            if i == self.stop:
                self.pending = dz, result[1]
                return result
            self.back_got = shared(result[1], self.stages)
        self.weight_grad(i, dz)
        if i == 4:
            self.residual_back(got)
        return result

    def residual_back(self, got):
        rows = self.tail_rows

        def body(meta, got, n_ref, dt_ref, r_ref, rstat, gain, w_ref, x_ref, kept_out, away_out, dxr_out, dr, total):
            m = pl.program_id(0)
            sums = added(got)[2:4]
            number = n_ref[0, 1:2, :]
            center, spread = rstat[0, 0:1], rstat[0, 1:2]
            scale = gain[5:6] * spread
            valid = self.valid(meta, m, 4)
            for cs in CHUNKS:
                rh = (r_ref[0, :, cs] - center[:, cs]) * spread[:, cs]
                high, low = halves(valid.keep(self.norm_grad(dt_ref[0, :, cs], rh, scale, sums, number, cs)))
                dr[:, cs] = high
                dr[:, C + cs.start : C + cs.stop] = low
            high, low = dr[:, 0:C], dr[:, C : 2 * C]
            dxr_out[0] = stacked_dot(high, low, w_ref.at[0], True)
            grad = stacked_outer(x_ref[0, :, 0:C], x_ref[0, :, C : 2 * C], high, low)
            self.add_halves(meta, m, grad, total, kept_out, away_out)

        args = [
            (got, copies(self.last, 4)), (self.number, slots(2)), (self.dt, slots(rows)), (self.r, slots(rows)),
            (self.rstat, slots(2)), (self.gain, whole(6, C)), self.matrix(5), (self.picked, slots(rows, 2 * C)),
        ]
        outs = self.piece_out(5) + [(f32(OWN, rows, C), slots(rows))]
        which = PLACES[5][0]
        *self.pieces[which], self.dxr = call(
            body, self.meta, args, outs, [pltpu.VMEM((rows, 2 * C), BF16), pltpu.VMEM((C, C), F32)],
            f"{self.tag}_residual_back", 12 * OWN * rows * C * C, into=self.pieces[which],
        )

    def piece_out(self, i):
        which, place = PLACES[i]
        rows = PIECE_ROWS[which]
        return [(f32(rows, C), pl.BlockSpec((C // 2, C), lambda m, *_: (place, 0)))] * 2

    def add_halves(self, meta, m, grad, total, kept_out, away_out):
        @pl.when(m == 0)
        def _():
            total[...] = grad

        @pl.when(m > 0)
        def _():
            top, bottom = total[0 : C // 2] + grad[0 : C // 2], total[C // 2 : C] + grad[C // 2 : C]
            lower = meta[2 * OWN] == 1
            kept_out[...] = jnp.where(lower, top, bottom)
            away_out[...] = jnp.where(lower, bottom, top)

    def weight_grad(self, i, dz):
        two = self.two
        strided = i == 4 and not two
        rows = self.rows_of(i)
        n_src = len(self.source_args())

        def body(meta, *refs):
            refs = list(refs)
            take = lambda n: [refs.pop(0) for _ in range(n)]
            m = pl.program_id(0)
            if i:
                zp_ref, statp, gain, bias = take(4)
                center, spread = statp[0, 0:1], statp[0, 1:2]
                scale = gain[i - 1 : i] * spread
                shift = bias[i - 1 : i] - center * scale
            else:
                src = take(n_src)
            dz_ref, dw_ref, kept_out, away_out, pad, yh, yl, total = take(8)
            alt, = take(1) if strided else (None,)
            valid_in = self.valid(meta, m, 0)
            for c, cs in enumerate(CHUNKS):
                if i:
                    u = zp_ref[0, :, cs] * scale[:, cs] + shift[:, cs]
                    h = valid_in.keep(u * sigmoid(u))
                else:
                    h = valid_in.keep(self.source(meta, src, cs))
                padded = Padded(pad.at[c], two)
                padded.put(h)
                y = padded.conv(dw_ref[0, :, cs])
                if strided:
                    y = every_other(alt.at[c], y)
                yh[:, cs], yl[:, cs] = halves(y)
            grad = stacked_outer(yh[...], yl[...], dz_ref[0, :, 0:C], dz_ref[0, :, C : 2 * C])
            self.add_halves(meta, m, grad, total, kept_out, away_out)

        args = self.before_args(i)
        if i:
            args += [(self.gain, whole(6, C)), (self.bias, whole(6, C))]
        args += [(dz, slots(rows, 2 * C)), (self.dw, layer(i, TAPS, C))]
        scratch = [pad_scratch(), pltpu.VMEM((rows, C), BF16), pltpu.VMEM((rows, C), BF16), pltpu.VMEM((C, C), F32)]
        if strided:
            scratch.append(stride_scratch())
        which = PLACES[i][0]
        self.pieces[which] = call(
            body, self.meta, args, self.piece_out(i), scratch, f"{self.tag}_weights_{i}", 6 * OWN * rows * C * C,
            into=self.pieces[which],
        )
        self.done = (self.pieces[which][0],)

    def backward(self, layers):
        if layers[0] == 4:
            self.pieces = [[], []]
        for i in layers:
            result = self.backward_layer(i)
        return result

    def resume(self, i):
        dz, payload = self.pending
        self.back_got = shared(payload, self.stages)
        self.weight_grad(i, dz)

    def fork(self, state=None):
        other = copy.copy(self)
        other.__dict__.update(state or {})
        if "pieces" in other.__dict__:
            other.pieces = list(other.pieces)
        return other

    def state(self):
        return {name: getattr(self, name) for name in ("du", "dxr", "pieces", "small", "pending")}

    def half(self, no, first, begin=None, end=None):
        kept, away = self.pieces[no]
        if no:
            parts = self.small[: SMALL // 2], self.small[SMALL // 2 :]
            at = kept.shape[0] - SMALL // 2
            kept = lax.dynamic_update_slice_in_dim(kept, jnp.where(first, *parts), at, 0)
            away = lax.dynamic_update_slice_in_dim(away, jnp.where(first, *parts[::-1]), at, 0)
        if begin is not None:
            away, _ = lax.optimization_barrier((away, begin))
            kept, _ = lax.optimization_barrier((kept, end))
        return kept + swap(away)


PLACES = {3: (0, 0), 4: (0, 1), 5: (0, 2), 0: (1, 0), 1: (1, 1), 2: (1, 2)}
PIECE_ROWS = (3 * C // 2, 3 * C // 2 + SMALL // 2)


def swap(x):
    return lax.ppermute(x, "section", [(0, 1), (1, 0)])


def fenced(always, work, x):
    shapes = jax.eval_shape(work, x)
    return lax.cond(always, work, lambda x: jax.tree.map(lambda y: jnp.zeros(y.shape, y.dtype), shapes), x)


class Reduction:
    def __init__(self, x, stages):
        self.x = x
        self.todo = []
        stride = 1
        for radix in stages:
            self.todo.append((True, radix, stride))
            stride *= radix
        self.todo += [(False, radix, stride) for _, radix, stride in reversed(self.todo)]

    def step(self):
        scatter, radix, stride = self.todo.pop(0)
        rows = self.x.shape[0]
        if scatter:
            parts = exchange(self.x.reshape(radix, rows // radix, C), radix, stride)
            self.x = jnp.sum(parts, axis=0)
        else:
            parts = exchange(jnp.broadcast_to(self.x, (radix,) + self.x.shape), radix, stride)
            self.x = parts.reshape(radix * rows, C)
        return (self.x,)

    def finish(self):
        while self.todo:
            self.step()
        return self.x


def per_device(features, out_grad, lengths, join_pick, dw, pw, gain, bias, res_w, down, down_b, up, up_b):
    first = lax.axis_index("section") == 0
    size = lax.axis_size("dp")
    inputs = features.reshape(MB, SLOT, C)
    cotangent = out_grad.reshape(MB, SLOT, C)
    own, picks = lengths[0, 0], join_pick[0]
    to_upper = lambda x: lax.ppermute(x, "section", [(0, 1)])
    to_lower = lambda x: lax.ppermute(x, "section", [(1, 0)])

    far_len = swap(own)
    joining = jnp.concatenate([lax.dynamic_index_in_dim(inputs, picks[m], 0, False)[HALF:] for m in range(OWN)], axis=0)
    far_rows = to_upper(inputs[MB - 1])
    far_w0 = swap(pw[0, 0:1])
    taps = jnp.concatenate([dw[0].reshape(5 * TAPS, C), gain[0], bias[0]], axis=0)
    far_taps = swap(taps)
    far_pw, far_res = swap(pw[0]), swap(res_w[0])
    wide = jnp.pad(down_b, ((0, 0), (0, C - SE)))
    squeeze = jnp.concatenate([down[0].T, up[0], up_b, wide], axis=0)
    far_squeeze = swap(squeeze)
    far_cot = to_lower(cotangent[:OWN])
    far_joining = to_lower(joining)
    far_cot0 = to_upper(cotangent[MB - 1, :HALF])

    flag = first.astype(jnp.int32)[None]
    mine = lambda v: jnp.where(first, v[:OWN], jnp.concatenate([v[OWN:], jnp.zeros((1,), v.dtype)]))
    length = mine(jnp.where(first, own, far_len))
    half_len = (length + 1) // 2
    join_len = mine(jnp.where(first, far_len, own)[picks])
    meta1 = jnp.concatenate([length, half_len, flag])
    meta2 = jnp.concatenate([half_len, join_len, flag, picks[MB - 1 :]])

    def small(block):
        t = jnp.where(first == (block == 0), taps, far_taps)
        q = jnp.where(first == (block == 0), squeeze, far_squeeze)
        return (
            t[: 5 * TAPS].reshape(5, TAPS, C), t[5 * TAPS : 5 * TAPS + 6], t[5 * TAPS + 6 :],
            q[:SE], q[2 * SE + 1, :SE][:, None], q[SE : 2 * SE], q[2 * SE : 2 * SE + 1],
        )

    def prepared(block, start, stop):
        array = prepare(meta1, (pw[0], res_w[0]), (far_pw, far_res), block, start, stop)
        return array, {i: (array, i - start) for i in range(start, stop)}

    parts0 = [prepared(0, 1, 3), prepared(0, 3, 6)]
    parts1 = [prepared(1, 0, 3), prepared(1, 3, 6)]

    stages, deep = radices(size, 16), radices(size, 4)
    c14 = Block(False, meta1, small(0), {**parts0[0][1], **parts0[1][1]}, stages)
    c14.x, c14.x_far, c14.first_matrix = inputs, far_rows, (pw[0], far_w0)
    c14.forward({2: (parts0[1][0],), 4: (parts1[0][0],)})
    out0 = c14.tail(after=(parts1[1][0],))
    c15 = Block(True, meta2, small(1), {**parts1[0][1], **parts1[1][1]}, stages)
    c15.arrived, c15.joined_far, c15.joined = out0, far_joining, features.reshape(MB, 2, HALF, C)
    c15.forward()
    out1 = c15.tail(cotangent, far_cot)
    c15.stop = 2
    c15.backward((4, 3))
    begin = c15.back_got
    c15.backward((2,))
    always = own[0] > 0

    half0 = c15.half(0, first, begin, c15.du)
    sum0 = lax.psum(half0, "dp")

    def middle(half0):
        upper, lower = c15.fork(), c14.fork()
        upper.resume(2)
        upper.done += (half0,)
        back, dx1 = upper.backward((1, 0))
        lower.tail_backward(cotangent, far_cot0, back)
        lower.done = upper.done
        lower.backward((4,))
        begin1 = lower.back_got
        lower.backward((3,))
        half1 = upper.half(1, first, begin1, lower.du)
        begin2 = lower.back_got
        lower.stop = 2
        lower.backward((2,))
        return dx1, half1, lower.half(0, first, begin2, lower.du), lower.state()

    dx1, half1, half2, state = fenced(always, middle, half0)
    sum0, half2 = lax.optimization_barrier((sum0, half2))
    sum1, sum2 = lax.psum((half1, half2), "dp")

    def ending(half2):
        last = c14.fork(state)
        last.resume(2)
        last.done += (half2,)
        came0 = to_upper(sum0)
        dx0, = last.backward((1, 0))
        reduction = Reduction(last.half(1, first), deep)
        reduction.step()
        pad = jnp.zeros((1, HALF, C), F32)
        lower = jnp.concatenate([out0, jnp.concatenate([to_lower(out0[0:1, :HALF]), pad], axis=1)], axis=0)
        upper = jnp.concatenate([to_upper(out1), out1[0:1]], axis=0)
        block_out = jnp.where(first, lower, upper)
        lower = jnp.concatenate([dx0, to_lower(dx0[0:1])], axis=0)
        joins = jnp.concatenate([to_upper(dx1), dx1[0:1]], axis=0)
        joins = jnp.stack([lax.dynamic_index_in_dim(joins, jnp.argmax(picks == s), 0, False) for s in range(MB)])
        upper = jnp.concatenate([jnp.zeros_like(joins), joins], axis=1)
        dx = jnp.where(first, lower, upper)
        reduction.x, block_out, dx, came0 = lax.optimization_barrier((reduction.x, block_out, dx, came0))
        return block_out, dx, came0, reduction.finish()

    block_out, dx, came0, sum3 = fenced(always, ending, half2)
    sum1, sum2, sum3 = lax.optimization_barrier((sum1, sum2, sum3))
    came1, came2, came3 = to_upper(sum1), to_lower(sum2), to_lower(sum3)

    size3 = size1 = 3 * C // 2
    mats = lambda rest, lead: jnp.concatenate([rest[:size3], lead], axis=0)
    near = jnp.where(first, mats(sum3, sum2), mats(sum1, sum0)).reshape(6, 1, C // 2, C)
    far = jnp.where(first, mats(came3, came2), mats(came1, came0)).reshape(6, 1, C // 2, C)
    matrices = jnp.where(first, jnp.concatenate([near, far], axis=1), jnp.concatenate([far, near], axis=1))
    pw_grad, res_grad = matrices[:5].reshape(1, 5, C, C), matrices[5].reshape(1, C, C)
    near, far = jnp.where(first, sum3[size3:], sum1[size1:]), jnp.where(first, came3[size3:], came1[size1:])
    rows = jnp.where(first, jnp.concatenate([near, far], axis=0), jnp.concatenate([far, near], axis=0))
    dw_grad = rows[TAIL_ROWS : TAIL_ROWS + 40].reshape(1, 5, 8, C)
    norms = jnp.concatenate([dw_grad[0, 1:, TAPS : TAPS + 2], rows[None, 2 * SE + 2 : 2 * SE + 4], rows[None, 2 * SE + 4 : 2 * SE + 6]], axis=0)
    return (
        block_out.reshape(features.shape), dx.reshape(features.shape), dw_grad[:, :, :TAPS], pw_grad,
        norms[None, :, 1], norms[None, :, 0], res_grad, rows[SE : 2 * SE].T[None], rows[2 * SE + 1 : 2 * SE + 2, :SE],
        rows[:SE][None], rows[2 * SE : 2 * SE + 1],
    )


def solution(mesh):
    rows = P("section", "dp", None)
    own = lambda dims: P("section", *([None] * dims))
    weights = (own(3), own(3), own(2), own(2), own(2), own(2), own(1), own(2), own(1))
    in_specs = (rows, rows, rows, P("dp", None), *weights)
    out_specs = (rows, rows, *weights)
    return jax.shard_map(per_device, mesh=mesh, in_specs=in_specs, out_specs=out_specs, check_vma=False)
```

```python
import copy

import jax
import jax.numpy as jnp
from jax import lax
from jax.experimental import pallas as pl
from jax.experimental.pallas import tpu as pltpu
from jax.sharding import PartitionSpec as P

EPSILON = 1e-05
EXACT = lax.Precision.HIGHEST
TAPS = 5
MB = 3
OWN = 2
SLOT = 400
HALF = 200
KEPT = 208
C = 512
LANES = 128
CHUNKS = [slice(c, c + LANES) for c in range(0, C, LANES)]
SE = 64
BF16, F32 = jnp.bfloat16, jnp.float32
VMEM_BYTES = 60 << 20
TAIL_ROWS = 2 * SE + 8
SMALL = 256


def radices(size, most):
    stages, left = [], size
    while left > 1:
        radix = min(most, left)
        while left % radix:
            radix -= 1
        stages.append(radix)
        left //= radix
    return stages


def exchange(block, radix, stride):
    size = lax.axis_size("dp")
    if radix == size:
        return lax.all_to_all(block, "dp", 0, 0)
    groups = []
    for base in range(size):
        if (base // stride) % radix == 0:
            groups.append([base + j * stride for j in range(radix)])
    return lax.all_to_all(block, "dp", 0, 0, axis_index_groups=groups)


def shared(block, stages):
    stride = 1
    for no, radix in enumerate(stages):
        if no:
            block = jnp.broadcast_to(jnp.sum(block, axis=0), (radix,) + block.shape[1:])
        block = exchange(block, radix, stride)
        stride *= radix
    return block


def halves(x):
    high = x.astype(BF16)
    return high, (x - high.astype(F32)).astype(BF16)


def sigmoid(x):
    return 0.5 * jnp.tanh(0.5 * x) + 0.5


def exact_dot(a, b, dims=((1,), (0,))):
    return lax.dot_general(a, b, (dims, ((), ())), precision=EXACT, preferred_element_type=F32)


def fast_dot(a, b, dims=((1,), (0,))):
    return lax.dot_general(a, b, (dims, ((), ())), preferred_element_type=F32)


def stacked_dot(high, low, w, back=False):
    w_high, w_low = w[0], w[1]
    w = jnp.concatenate([w_high, w_high, w_low], axis=1 if back else 0)
    x = jnp.concatenate([high, low, high], axis=1)
    return fast_dot(x, w, ((1,), (1 if back else 0,)))


def stacked_outer(a_high, a_low, b_high, b_low):
    a = jnp.concatenate([a_high, a_low, a_high], axis=0)
    b = jnp.concatenate([b_high, b_high, b_low], axis=0)
    return fast_dot(a, b, ((0,), (0,)))


def column_sum(x):
    return jnp.sum(x, axis=0, keepdims=True)


class Rows:
    def __init__(self, meta, m, two, rows, which=0):
        place = lax.broadcasted_iota(jnp.int32, (rows, LANES), 0)
        if two:
            later = place >= HALF
            limit = jnp.where(later, HALF + meta[OWN + m], meta[m])
            self.mask = place < limit
        else:
            self.mask = place < meta[which * OWN + m]

    def keep(self, x):
        return jnp.where(self.mask, x, 0.0)


class Padded:
    def __init__(self, ref, two):
        self.ref = ref
        self.pieces = [(8, 0, HALF), (16 + HALF, HALF, HALF)] if two else [(8, 0, SLOT)]

    def put(self, x):
        zeros = jnp.zeros((8, LANES), F32)
        for at, start, rows in self.pieces:
            self.ref[at - 8 : at, :] = zeros
            self.ref[at : at + rows, :] = x[start : start + rows]
        self.ref[at + rows : at + rows + 8, :] = zeros

    def get(self, offset):
        parts = [self.ref[at + offset : at + offset + rows, :] for at, _, rows in self.pieces]
        return parts[0] if len(parts) == 1 else jnp.concatenate(parts, axis=0)

    def conv(self, kernel):
        total = kernel[0:1] * self.get(-2)
        for k in range(1, TAPS):
            total = total + kernel[k : k + 1] * self.get(k - 2)
        return total

    def conv_back(self, kernel):
        total = kernel[0:1] * self.get(2)
        for k in range(1, TAPS):
            total = total + kernel[k : k + 1] * self.get(2 - k)
        return total


def every_other(ref, x):
    ref[0:SLOT, :] = x
    ref[SLOT : 2 * KEPT, :] = jnp.zeros((2 * KEPT - SLOT, LANES), F32)
    return ref[pl.ds(0, KEPT, stride=2), :]


def spread_out(ref, x):
    ref[...] = jnp.zeros_like(ref)
    ref[pl.ds(0, KEPT, stride=2), :] = x
    return ref[0:SLOT, :]


def center_spread(sums, rows):
    center = sums[0:1] / rows
    return center, lax.rsqrt(sums[1:2] / rows - center * center + EPSILON)


def added(ref):
    return jnp.sum(ref[:, 0], axis=0)


def accumulate(ref, m, at, value):
    rows = slice(at, at + value.shape[0])
    ref[rows, :] = jnp.where(m == 0, value, ref[rows, :] + value)


def send(ref, rows):
    for copy in range(ref.shape[0]):
        for row, x in enumerate(rows):
            ref[copy, 0, row : row + 1, 0 : x.shape[1]] = x


def pad_scratch():
    return pltpu.VMEM((len(CHUNKS), SLOT + 24, LANES), F32)


def stride_scratch():
    return pltpu.VMEM((len(CHUNKS), 2 * KEPT, LANES), F32)


def slots(rows, cols=C):
    return pl.BlockSpec((1, rows, cols), lambda m, *_: (m, 0, 0))


def copies(count, rows, cols=C):
    return pl.BlockSpec((count, 1, rows, cols), lambda m, *_: (0, m, 0, 0))


def whole(*shape):
    return pl.BlockSpec(shape, lambda m, *_: (0,) * len(shape))


def layer(i, *shape):
    return pl.BlockSpec((1,) + shape, lambda m, *_: (i,) + (0,) * len(shape))


def f32(*shape):
    return jax.ShapeDtypeStruct(shape, F32)


def bf16(*shape):
    return jax.ShapeDtypeStruct(shape, BF16)


def call(body, meta, args, outs, scratch=(), name=None, flops=0, steps=OWN, after=(), into=()):
    arrays, in_specs = [a for a, _ in args], [s for _, s in args]
    shapes, out_specs = [a for a, _ in outs], [s for _, s in outs]
    size = sum(a.size * a.dtype.itemsize for a in arrays + shapes)
    extra = list(after) + list(into)
    count = len(arrays)

    def inner(meta, *refs):
        body(meta, *refs[:count], *refs[count + len(extra) :])

    return pl.pallas_call(
        inner,
        out_shape=shapes,
        grid_spec=pltpu.PrefetchScalarGridSpec(
            num_scalar_prefetch=1,
            grid=(steps,),
            in_specs=in_specs + [pl.BlockSpec(memory_space=pl.ANY)] * len(extra),
            out_specs=out_specs,
            scratch_shapes=list(scratch),
        ),
        input_output_aliases={1 + count + len(after) + j: j for j in range(len(into))},
        compiler_params=pltpu.CompilerParams(vmem_limit_bytes=VMEM_BYTES),
        cost_estimate=pl.CostEstimate(flops=flops, bytes_accessed=size, transcendentals=0),
        name=name,
    )(meta, *arrays, *extra)


def choose(meta, block, own, far):
    return jnp.where(meta[2 * OWN] == 1 - block, own, far)


def prepare(meta, own, far, block, start, stop):
    def body(meta, *refs):
        pair = [ref[0] for ref in refs[:2]]
        if stop == 6:
            last = pl.program_id(0) == 5 - start
            pair = [jnp.where(last, ref[...], w) for ref, w in zip(refs[2:4], pair)]
        out = refs[-1]
        out[0, 0], out[0, 1] = halves(choose(meta, block, *pair))

    matrix = pl.BlockSpec((1, C, C), lambda j, *_: (jnp.minimum(j + start, 4), 0, 0))
    args = [(own[0], matrix), (far[0], matrix)]
    if stop == 6:
        args += [(own[1], whole(C, C)), (far[1], whole(C, C))]
    out = pl.BlockSpec((1, 2, C, C), lambda j, *_: (j, 0, 0, 0))
    name = f"prepare_{block}_{start}"
    return call(body, meta, args, [(bf16(stop - start, 2, C, C), out)], name=name, steps=stop - start)[0]


class Block:
    def __init__(self, two, meta, weights, ready, stages):
        self.done, self.stop, self.pending = (), None, None
        self.two, self.meta, self.stages = two, meta, stages
        self.dw, self.gain, self.bias, self.down, self.down_b, self.up, self.up_b = weights
        self.ready = ready
        self.tail_rows = SLOT if two else KEPT
        self.first, self.last = stages[0], stages[-1]
        self.tag = "c15" if two else "c14"

    def rows_of(self, i):
        return self.tail_rows if i == 4 else SLOT

    def valid(self, meta, m, i):
        last = i == 4 and not self.two
        return Rows(meta, m, self.two, self.rows_of(i), which=1 if last else 0)

    def matrix(self, i):
        array, at = self.ready[i]
        return (array, layer(at, 2, C, C))

    def source_args(self):
        if not self.two:
            return [(self.x, slots(SLOT)), (self.x_far, whole(SLOT, C))]
        far = pl.BlockSpec((HALF, C), lambda m, *_: (m, 0))
        near = pl.BlockSpec((1, 1, HALF, C), lambda m, meta: (meta[2 * OWN + 1], 1, 0, 0))
        return [(self.arrived, slots(HALF)), (self.joined_far, far), (self.joined, near)]

    def source(self, meta, refs, cs):
        lower = meta[2 * OWN] == 1
        if not self.two:
            return jnp.where(lower, refs[0][0, :, cs], refs[1][:, cs])
        joined = jnp.where(lower, refs[1][:, cs], refs[2][0, 0, :, cs])
        return jnp.concatenate([refs[0][0, :, cs], joined], axis=0)

    def before_args(self, i):
        if i == 0:
            return self.source_args()
        return [(self.z[i - 1], slots(SLOT)), (self.stats[i - 1], slots(2))]


    def forward_layer(self, i, after=()):
        two, count = self.two, self.first
        strided = i == 4 and not two
        rows = self.rows_of(i)
        n_src = len(self.source_args())
        width = C + LANES if i == 0 else C
        sent = 4 if i == 3 else 2
        makes = i == 0 and not two

        def body(meta, *refs):
            refs = list(refs)
            take = lambda n: [refs.pop(0) for _ in range(n)]
            m = pl.program_id(0)
            if i == 0:
                src = take(n_src)
            else:
                z_ref, got_ref = take(2)
                n_ref, = take(1) if i > 1 else (None,)
                gain_ref, bias_ref = take(2)
                res_sum, = take(1) if i == 3 else (None,)
            dw_ref, = take(1)
            if makes:
                own_ref, far_ref, z_out, pay, w_ref = take(5)

                @pl.when(m == 0)
                def _():
                    w_ref[0, 0], w_ref[0, 1] = halves(choose(meta, 0, own_ref[0], far_ref[0]))

            else:
                w_ref, z_out, pay = take(3)
            if i:
                stat_out, = take(1)
            if i == 1:
                n_out, = take(1)
            pad, y_ref = take(2)
            alt, = take(1) if strided else (None,)
            valid_in = self.valid(meta, m, 0)
            if i:
                sums = added(got_ref)
                if i == 1:
                    count_in = jnp.maximum(jnp.concatenate([sums[0:1, C:]] * len(CHUNKS), axis=1), 1.0)
                    count_out = jnp.maximum(jnp.concatenate([sums[1:2, C:]] * len(CHUNKS), axis=1), 1.0)
                    n_out[0, 0:1, :] = count_in
                    n_out[0, 1:2, :] = count_out
                else:
                    count_in = n_ref[0, 0:1, :]
                center, spread = center_spread(sums[:, :C], count_in)
                stat_out[0, 0:1, :] = center
                stat_out[0, 1:2, :] = spread
                scale = gain_ref[i - 1 : i] * spread
                shift = bias_ref[i - 1 : i] - center * scale
            for c, cs in enumerate(CHUNKS):
                if i == 0:
                    h = valid_in.keep(self.source(meta, src, cs))
                else:
                    u = z_ref[0, :, cs] * scale[:, cs] + shift[:, cs]
                    h = valid_in.keep(u * sigmoid(u))
                padded = Padded(pad.at[c], two)
                padded.put(h)
                y = padded.conv(dw_ref[0, :, cs])
                if strided:
                    y = every_other(alt.at[c], y)
                high, low = halves(y)
                y_ref[:, cs] = high
                y_ref[:, C + cs.start : C + cs.stop] = low
            w = w_ref.at[0] if makes else w_ref.at[0]
            z = stacked_dot(y_ref[:, 0:C], y_ref[:, C : 2 * C], w)
            z_out[0] = z
            valid = self.valid(meta, m, i)
            one, square = [], []
            for cs in CHUNKS:
                kept = valid.keep(z[:, cs])
                one.append(column_sum(kept))
                square.append(column_sum(kept * kept))
            if i == 0:
                if two:
                    number = (meta[m] + meta[OWN + m]).astype(F32)
                    numbers = number, number
                else:
                    numbers = meta[m].astype(F32), meta[OWN + m].astype(F32)
                one.append(jnp.full((1, LANES), numbers[0], F32))
                square.append(jnp.full((1, LANES), numbers[1], F32))
            out = [jnp.concatenate(one, axis=1), jnp.concatenate(square, axis=1)]
            if i == 3:
                out += [res_sum[0, 0:1, :], res_sum[0, 1:2, :]]
            send(pay, out)

        if i == 0:
            args = list(self.source_args())
        else:
            got = 4 if i == 4 else 2
            args = [(self.z[i - 1], slots(SLOT)), (self.got[i - 1], copies(self.last, got, C + LANES if i == 1 else C))]
            if i > 1:
                args.append((self.number, slots(2)))
            args += [(self.gain, whole(6, C)), (self.bias, whole(6, C))]
            if i == 3:
                args.append((self.res_sum, slots(2)))
        args.append((self.dw, layer(i, TAPS, C)))
        args += [(w, layer(0, C, C)) for w in self.first_matrix] if makes else [self.matrix(i)]
        outs = [(f32(OWN, rows, C), slots(rows)), (f32(count, OWN, sent, width), copies(count, sent, width))]
        if i:
            outs.append((f32(OWN, 2, C), slots(2)))
        if i == 1:
            outs.append((f32(OWN, 2, C), slots(2)))
        if makes:
            outs.append((bf16(1, 2, C, C), layer(0, 2, C, C)))
        scratch = [pad_scratch(), pltpu.VMEM((rows, 2 * C), BF16)]
        if strided:
            scratch.append(stride_scratch())
        result = call(body, self.meta, args, outs, scratch, f"{self.tag}_forward_{i}", 6 * OWN * rows * C * C, after=after)
        self.z.append(result[0])
        if makes:
            self.ready[0] = (result[2], 0)
        if i:
            self.stats.append(result[2])
        if i == 1:
            self.number = result[3]
        self.got.append(shared(result[1], self.stages))

    def residual(self):
        two, rows = self.two, self.tail_rows

        def body(meta, *refs):
            refs = list(refs)
            src = [refs.pop(0) for _ in self.source_args()]
            w_ref, r_out, x_out, sum_out = refs[:4]
            alt = refs[4] if not two else None
            m = pl.program_id(0)
            valid_in = self.valid(meta, m, 0)
            for c, cs in enumerate(CHUNKS):
                x = valid_in.keep(self.source(meta, src, cs))
                if not two:
                    x = every_other(alt.at[c], x)
                high, low = halves(x)
                x_out[0, :, cs] = high
                x_out[0, :, C + cs.start : C + cs.stop] = low
            r = stacked_dot(x_out[0, :, 0:C], x_out[0, :, C : 2 * C], w_ref.at[0])
            r_out[0] = r
            valid = self.valid(meta, m, 4)
            for cs in CHUNKS:
                kept = valid.keep(r[:, cs])
                sum_out[0, 0:1, cs] = column_sum(kept)
                sum_out[0, 1:2, cs] = column_sum(kept * kept)

        args = self.source_args() + [self.matrix(5)]
        outs = [
            (f32(OWN, rows, C), slots(rows)),
            (bf16(OWN, rows, 2 * C), slots(rows, 2 * C)),
            (f32(OWN, 2, C), slots(2)),
        ]
        scratch = [] if two else [stride_scratch()]
        self.r, self.picked, self.res_sum = call(
            body, self.meta, args, outs, scratch, f"{self.tag}_residual", 6 * OWN * rows * C * C
        )

    def forward(self, after=None):
        self.z, self.got, self.stats = [], [], []
        for i in range(5):
            if i == 2:
                self.residual()
            self.forward_layer(i, (after or {}).get(i, ()))


    def segments(self):
        return [(0, HALF), (HALF, HALF)] if self.two else [(0, self.tail_rows)]

    def lengths(self, meta, m):
        if self.two:
            return [meta[m], meta[OWN + m]]
        return [meta[OWN + m]]

    def squeeze(self, sums, counts, se_refs):
        down_t, down_b, up, up_b = se_refs
        means = [s / jnp.maximum(jnp.full((1, C), n.astype(F32)), 1.0) for s, n in zip(sums, counts)]
        ps = [jnp.sum(down_t[...] * mean, axis=1, keepdims=True) + down_b[...] for mean in means]
        gates = [sigmoid(column_sum(up[...] * (p * sigmoid(p))) + up_b[...]) for p in ps]
        return means, ps, gates

    def squeeze_back(self, des, ps, gates, counts, se_refs, means, small, m):
        down_t, down_b, up, up_b = se_refs
        shares, up_grad, down_grad, dq_sum, dp_sum = [], 0.0, 0.0, 0.0, 0.0
        for de, p, gate, n, mean in zip(des, ps, gates, counts, means):
            dq = de * gate * (1.0 - gate)
            s = sigmoid(p)
            dp = jnp.sum(up[...] * dq, axis=1, keepdims=True) * (s * (1.0 + p * (1.0 - s)))
            shares.append(column_sum(down_t[...] * dp) / jnp.maximum(jnp.full((1, C), n.astype(F32)), 1.0))
            up_grad, down_grad = up_grad + (p * s) * dq, down_grad + dp * mean
            dq_sum, dp_sum = dq_sum + dq, dp_sum + dp
        row, col = (lax.broadcasted_iota(jnp.int32, (SE, C), axis) for axis in (0, 1))
        dp_row = column_sum(jnp.where(row == col, dp_sum, 0.0))
        accumulate(small, m, 0, up_grad)
        accumulate(small, m, SE, down_grad)
        accumulate(small, m, 2 * SE, dq_sum)
        accumulate(small, m, 2 * SE + 1, dp_row)
        return shares

    def last_norm(self, m, dt_out, du_out, z_ref, slope_ref, gates, shares, center, spread, res_bias, res_gain, pay, small):
        bias_sum, gain_sum = [], []
        for cs in CHUNKS:
            dh = dt_out[0, :, cs] * self.by_segment(gates, cs) + self.by_segment(shares, cs)
            du = dh * slope_ref[:, cs]
            du_out[0, :, cs] = du
            bias_sum.append(column_sum(du))
            gain_sum.append(column_sum(du * ((z_ref[0, :, cs] - center[:, cs]) * spread[:, cs])))
        rows = [jnp.concatenate(x, axis=1) for x in (bias_sum, gain_sum, res_bias, res_gain)]
        send(pay, rows)
        for j, row in enumerate(rows):
            accumulate(small, m, 2 * SE + 2 + j, row)

    def se_args(self):
        return [(self.down, whole(SE, C)), (self.down_b, whole(SE, 1)), (self.up, whole(SE, C)), (self.up_b, whole(1, C))]

    def store_rows(self, ref, rows):
        ref[0] = jnp.concatenate(rows + [jnp.zeros((8 - len(rows), C), F32)], axis=0)

    def store_columns(self, ref, columns):
        ref[0] = jnp.zeros((SE, 8), F32)
        for j, column in enumerate(columns):
            ref[0, :, j : j + 1] = column

    def by_segment(self, rows, cs):
        parts = [jnp.broadcast_to(row[:, cs], (n, LANES)) for row, (_, n) in zip(rows, self.segments())]
        return parts[0] if len(parts) == 1 else jnp.concatenate(parts, axis=0)

    def seg_sums(self, x):
        return [column_sum(x[at : at + n]) for at, n in self.segments()]

    def tail(self, cotangent=None, far=None, after=()):
        two, rows = self.two, self.tail_rows
        back = cotangent is not None

        def body(meta, *refs):
            refs = list(refs)
            take = lambda n: [refs.pop(0) for _ in range(n)]
            m = pl.program_id(0)
            z_ref, got4, r_ref, got3, n_ref, gain, bias = take(7)
            se_refs = take(4)
            if back:
                cot_ref, far_ref = take(2)
            out, stat_out, rstat_out, means_out, p_out, gate_out = take(6)
            if back:
                small, du_out, dt_out, pay = take(4)
            h_ref, = take(1)
            if back:
                slope_ref, = take(1)
            valid = self.valid(meta, m, 4)
            number = n_ref[0, 1:2, :]
            center, spread = center_spread(added(got4), number)
            rcenter, rspread = center_spread(added(got3)[2:4], number)
            stat_out[0, 0:1, :] = center
            stat_out[0, 1:2, :] = spread
            rstat_out[0, 0:1, :] = rcenter
            rstat_out[0, 1:2, :] = rspread
            scale = gain[4:5] * spread
            shift = bias[4:5] - center * scale
            sums = []
            for cs in CHUNKS:
                u = z_ref[0, :, cs] * scale[:, cs] + shift[:, cs]
                s = sigmoid(u)
                h = valid.keep(u * s)
                h_ref[:, cs] = h
                if back:
                    slope_ref[:, cs] = valid.keep(s * (1.0 + u * (1.0 - s)))
                sums.append(self.seg_sums(h))
            sums = [jnp.concatenate([s[j] for s in sums], axis=1) for j in range(len(self.segments()))]
            counts = self.lengths(meta, m)
            means, ps, gates = self.squeeze(sums, counts, se_refs)
            self.store_rows(means_out, means)
            self.store_columns(p_out, ps)
            self.store_rows(gate_out, gates)
            res_gain, res_bias, gate_grad = [], [], []
            for cs in CHUNKS:
                h = h_ref[:, cs]
                rh = (r_ref[0, :, cs] - rcenter[:, cs]) * rspread[:, cs]
                t = h * self.by_segment(gates, cs) + gain[5:6, cs] * rh + bias[5:6, cs]
                s = sigmoid(t)
                out[0, 0:rows, cs] = valid.keep(t * s)
                if rows < SLOT:
                    out[0, rows:SLOT, cs] = jnp.zeros((SLOT - rows, LANES), F32)
                if back:
                    cot = jnp.where(meta[2 * OWN] == 1, far_ref[0, :, cs], cot_ref[0, :, cs])
                    dt = valid.keep(cot * (s * (1.0 + t * (1.0 - s))))
                    dt_out[0, :, cs] = dt
                    res_bias.append(column_sum(dt))
                    res_gain.append(column_sum(dt * rh))
                    gate_grad.append(self.seg_sums(dt * h))
            if not back:
                return
            des = [jnp.concatenate([g[j] for g in gate_grad], axis=1) for j in range(len(counts))]
            shares = self.squeeze_back(des, ps, gates, counts, se_refs, means, small, m)
            self.last_norm(m, dt_out, du_out, z_ref, slope_ref, gates, shares, center, spread, res_bias, res_gain, pay, small)

        args = [
            (self.z[4], slots(rows)), (self.got[4], copies(self.last, 2)), (self.r, slots(rows)),
            (self.got[3], copies(self.last, 4)), (self.number, slots(2)),
            (self.gain, whole(6, C)), (self.bias, whole(6, C)),
        ] + self.se_args()
        outs = [
            (f32(OWN, SLOT, C), slots(SLOT)), (f32(OWN, 2, C), slots(2)), (f32(OWN, 2, C), slots(2)),
            (f32(OWN, 8, C), slots(8)), (f32(OWN, SE, 8), slots(SE, 8)), (f32(OWN, 8, C), slots(8)),
        ]
        scratch = [pltpu.VMEM((rows, C), F32)]
        if back:
            args += [(cotangent, layer(MB - 1, SLOT, C)), (far, slots(SLOT))]
            outs += self.tail_outs()
            scratch.append(pltpu.VMEM((rows, C), F32))
        result = call(body, self.meta, args, outs, scratch, f"{self.tag}_tail", after=after)
        self.stats.append(result[1])
        self.rstat, self.se_state = result[2], result[3:6]
        if back:
            self.tail_results(result[6:])
        return result[0]

    def tail_outs(self):
        rows, count = self.tail_rows, self.first
        return [
            (f32(SMALL, C), whole(TAIL_ROWS, C)), (f32(OWN, rows, C), slots(rows)), (f32(OWN, rows, C), slots(rows)),
            (f32(count, OWN, 4, C), copies(count, 4)),
        ]

    def tail_results(self, result):
        self.small, self.du, self.dt, pay = result
        self.back_got = shared(pay, self.stages)

    def tail_backward(self, cotangent, far, back):
        rows = self.tail_rows

        def body(meta, z_ref, r_ref, stat, rstat, gain, bias, means_ref, p_ref, gate_ref, down, down_b, up, up_b, cot_ref, far_ref, back_ref,
                 small, du_out, dt_out, pay, slope_ref):
            m = pl.program_id(0)
            valid = self.valid(meta, m, 4)
            center, spread, rcenter, rspread = stat[0, 0:1], stat[0, 1:2], rstat[0, 0:1], rstat[0, 1:2]
            scale = gain[4:5] * spread
            shift = bias[4:5] - center * scale
            zeros = jnp.zeros((rows - HALF, LANES), F32)
            counts = self.lengths(meta, m)
            ps = [p_ref[0, :, j : j + 1] for j in range(len(counts))]
            gates = [gate_ref[0, j : j + 1, :] for j in range(len(counts))]
            means = [means_ref[0, j : j + 1, :] for j in range(len(counts))]
            res_gain, res_bias, gate_grad = [], [], []
            for cs in CHUNKS:
                u = z_ref[0, :, cs] * scale[:, cs] + shift[:, cs]
                s = sigmoid(u)
                h = valid.keep(u * s)
                slope_ref[:, cs] = valid.keep(s * (1.0 + u * (1.0 - s)))
                rh = (r_ref[0, :, cs] - rcenter[:, cs]) * rspread[:, cs]
                t = h * self.by_segment(gates, cs) + gain[5:6, cs] * rh + bias[5:6, cs]
                s = sigmoid(t)
                here = jnp.where(meta[2 * OWN] == 1, cot_ref[0, 0:HALF, cs], far_ref[:, cs])
                cot = jnp.concatenate([here + back_ref[0, :, cs], zeros], axis=0)
                dt = valid.keep(cot * (s * (1.0 + t * (1.0 - s))))
                dt_out[0, :, cs] = dt
                res_bias.append(column_sum(dt))
                res_gain.append(column_sum(dt * rh))
                gate_grad.append(self.seg_sums(dt * h))
            des = [jnp.concatenate([g[j] for g in gate_grad], axis=1) for j in range(len(counts))]
            shares = self.squeeze_back(des, ps, gates, counts, (down, down_b, up, up_b), means, small, m)
            self.last_norm(m, dt_out, du_out, z_ref, slope_ref, gates, shares, center, spread, res_bias, res_gain, pay, small)

        args = [
            (self.z[4], slots(rows)), (self.r, slots(rows)), (self.stats[4], slots(2)), (self.rstat, slots(2)),
            (self.gain, whole(6, C)), (self.bias, whole(6, C)),
            (self.se_state[0], slots(8)), (self.se_state[1], slots(SE, 8)), (self.se_state[2], slots(8)),
        ] + self.se_args() + [(cotangent, slots(SLOT)), (far, whole(HALF, C)), (back, slots(HALF))]
        scratch = [pltpu.VMEM((rows, C), F32)]
        self.tail_results(call(body, self.meta, args, self.tail_outs(), scratch, f"{self.tag}_tail_back"))


    def norm_grad(self, du, zh, scale, sums, number, cs):
        return scale[:, cs] * (du - sums[0:1, cs] / number[:, cs] - zh * (sums[1:2, cs] / number[:, cs]))

    def backward_layer(self, i):
        two, count = self.two, self.first
        strided = i == 4 and not two
        rows = self.rows_of(i)
        n_src = len(self.source_args())

        def body(meta, *refs):
            refs = list(refs)
            take = lambda n: [refs.pop(0) for _ in range(n)]
            m = pl.program_id(0)
            du_ref, z_ref, w_ref, got, n_ref, stat, gain, bias, dw_ref = take(9)
            if i:
                zp_ref, statp = take(2)
            else:
                dxr_ref, = take(1)
                src = take(n_src)
            small, dz_out = take(2)
            if i:
                du_out, pay = take(2)
            elif two:
                back_out, dx_out = take(2)
            else:
                dx_out, = take(1)
            pad, = take(1)
            alt, = take(1) if refs else (None,)
            sums = added(got)
            number = n_ref[0, 1:2, :] if i == 4 else n_ref[0, 0:1, :]
            center, spread = stat[0, 0:1], stat[0, 1:2]
            scale = gain[i : i + 1] * spread
            valid = self.valid(meta, m, i)
            for cs in CHUNKS:
                zh = (z_ref[0, :, cs] - center[:, cs]) * spread[:, cs]
                dz = valid.keep(self.norm_grad(du_ref[0, :, cs], zh, scale, sums, number, cs))
                high, low = halves(dz)
                dz_out[0, :, cs] = high
                dz_out[0, :, C + cs.start : C + cs.stop] = low
            dy = stacked_dot(dz_out[0, :, 0:C], dz_out[0, :, C : 2 * C], w_ref.at[0], True)
            valid_in = self.valid(meta, m, 0)
            if i:
                pcenter, pspread = statp[0, 0:1], statp[0, 1:2]
                pscale = gain[i - 1 : i] * pspread
                pshift = bias[i - 1 : i] - pcenter * pscale
            taps, bias_sum, gain_sum = [[] for _ in range(TAPS)], [], []
            for c, cs in enumerate(CHUNKS):
                grad = dy[:, cs]
                if strided:
                    grad = spread_out(alt.at[c], grad)
                padded = Padded(pad.at[c], two)
                padded.put(grad)
                if i:
                    z = zp_ref[0, :, cs]
                    u = z * pscale[:, cs] + pshift[:, cs]
                    s = sigmoid(u)
                    h = valid_in.keep(u * s)
                else:
                    h = valid_in.keep(self.source(meta, src, cs))
                dh = None
                for k in range(TAPS):
                    moved = padded.get(2 - k)
                    taps[k].append(column_sum(h * moved))
                    term = dw_ref[0, k : k + 1, cs] * moved
                    dh = term if dh is None else dh + term
                if i:
                    du = valid_in.keep(dh * (s * (1.0 + u * (1.0 - s))))
                    du_out[0, :, cs] = du
                    bias_sum.append(column_sum(du))
                    gain_sum.append(column_sum(du * ((z - pcenter[:, cs]) * pspread[:, cs])))
                    continue
                dxr = dxr_ref[0, :, cs]
                if not two:
                    dxr = spread_out(alt.at[c], dxr)
                dx = valid_in.keep(dh) + dxr
                if two:
                    back_out[0, :, cs] = dx[:HALF]
                    dx = dx[HALF:]
                dx_out[0, :, cs] = dx
            rows = taps + [bias_sum, gain_sum] if i else taps
            rows = [jnp.concatenate(x, axis=1) for x in rows]
            for j, row in enumerate(rows):
                accumulate(small, m, j, row)
            if i:
                send(pay, rows[TAPS:])

        sent = 4 if i == 4 else 2
        args = [
            (self.du, slots(rows)), (self.z[i], slots(rows)), self.matrix(i), (self.back_got, copies(self.last, sent)),
            (self.number, slots(2)), (self.stats[i], slots(2)), (self.gain, whole(6, C)), (self.bias, whole(6, C)),
            (self.dw, layer(i, TAPS, C)),
        ]
        if not i:
            args.append((self.dxr, slots(self.tail_rows)))
        args += self.before_args(i)
        place = TAIL_ROWS // 8 + i
        outs = [(f32(SMALL, C), pl.BlockSpec((8, C), lambda m, *_: (place, 0))), (bf16(OWN, rows, 2 * C), slots(rows, 2 * C))]
        if i:
            outs += [(f32(OWN, SLOT, C), slots(SLOT)), (f32(count, OWN, 2, C), copies(count, 2))]
        elif two:
            outs += [(f32(OWN, HALF, C), slots(HALF)), (f32(OWN, HALF, C), slots(HALF))]
        else:
            outs += [(f32(OWN, SLOT, C), slots(SLOT))]
        scratch = [pad_scratch()]
        if strided or (i == 0 and not two):
            scratch.append(stride_scratch())
        self.small, dz, *result = call(
            body, self.meta, args, outs, scratch, f"{self.tag}_backward_{i}", 6 * OWN * rows * C * C,
            after=self.done, into=(self.small,),
        )
        got = self.back_got
        if i:
            self.du = result[0]
            if i == self.stop:
                self.pending = dz, result[1]
                return result
            self.back_got = shared(result[1], self.stages)
        self.weight_grad(i, dz)
        if i == 4:
            self.residual_back(got)
        return result

    def residual_back(self, got):
        rows = self.tail_rows

        def body(meta, got, n_ref, dt_ref, r_ref, rstat, gain, w_ref, x_ref, kept_out, away_out, dxr_out, dr, total):
            m = pl.program_id(0)
            sums = added(got)[2:4]
            number = n_ref[0, 1:2, :]
            center, spread = rstat[0, 0:1], rstat[0, 1:2]
            scale = gain[5:6] * spread
            valid = self.valid(meta, m, 4)
            for cs in CHUNKS:
                rh = (r_ref[0, :, cs] - center[:, cs]) * spread[:, cs]
                high, low = halves(valid.keep(self.norm_grad(dt_ref[0, :, cs], rh, scale, sums, number, cs)))
                dr[:, cs] = high
                dr[:, C + cs.start : C + cs.stop] = low
            high, low = dr[:, 0:C], dr[:, C : 2 * C]
            dxr_out[0] = stacked_dot(high, low, w_ref.at[0], True)
            grad = stacked_outer(x_ref[0, :, 0:C], x_ref[0, :, C : 2 * C], high, low)
            self.add_halves(meta, m, grad, total, kept_out, away_out)

        args = [
            (got, copies(self.last, 4)), (self.number, slots(2)), (self.dt, slots(rows)), (self.r, slots(rows)),
            (self.rstat, slots(2)), (self.gain, whole(6, C)), self.matrix(5), (self.picked, slots(rows, 2 * C)),
        ]
        outs = self.piece_out(5) + [(f32(OWN, rows, C), slots(rows))]
        which = PLACES[5][0]
        *self.pieces[which], self.dxr = call(
            body, self.meta, args, outs, [pltpu.VMEM((rows, 2 * C), BF16), pltpu.VMEM((C, C), F32)],
            f"{self.tag}_residual_back", 12 * OWN * rows * C * C, into=self.pieces[which],
        )

    def piece_out(self, i):
        which, place = PLACES[i]
        rows = PIECE_ROWS[which]
        return [(f32(rows, C), pl.BlockSpec((C // 2, C), lambda m, *_: (place, 0)))] * 2

    def add_halves(self, meta, m, grad, total, kept_out, away_out):
        @pl.when(m == 0)
        def _():
            total[...] = grad

        @pl.when(m > 0)
        def _():
            top, bottom = total[0 : C // 2] + grad[0 : C // 2], total[C // 2 : C] + grad[C // 2 : C]
            lower = meta[2 * OWN] == 1
            kept_out[...] = jnp.where(lower, top, bottom)
            away_out[...] = jnp.where(lower, bottom, top)

    def weight_grad(self, i, dz):
        two = self.two
        strided = i == 4 and not two
        rows = self.rows_of(i)
        n_src = len(self.source_args())

        def body(meta, *refs):
            refs = list(refs)
            take = lambda n: [refs.pop(0) for _ in range(n)]
            m = pl.program_id(0)
            if i:
                zp_ref, statp, gain, bias = take(4)
                center, spread = statp[0, 0:1], statp[0, 1:2]
                scale = gain[i - 1 : i] * spread
                shift = bias[i - 1 : i] - center * scale
            else:
                src = take(n_src)
            dz_ref, dw_ref, kept_out, away_out, pad, yh, yl, total = take(8)
            alt, = take(1) if strided else (None,)
            valid_in = self.valid(meta, m, 0)
            for c, cs in enumerate(CHUNKS):
                if i:
                    u = zp_ref[0, :, cs] * scale[:, cs] + shift[:, cs]
                    h = valid_in.keep(u * sigmoid(u))
                else:
                    h = valid_in.keep(self.source(meta, src, cs))
                padded = Padded(pad.at[c], two)
                padded.put(h)
                y = padded.conv(dw_ref[0, :, cs])
                if strided:
                    y = every_other(alt.at[c], y)
                yh[:, cs], yl[:, cs] = halves(y)
            grad = stacked_outer(yh[...], yl[...], dz_ref[0, :, 0:C], dz_ref[0, :, C : 2 * C])
            self.add_halves(meta, m, grad, total, kept_out, away_out)

        args = self.before_args(i)
        if i:
            args += [(self.gain, whole(6, C)), (self.bias, whole(6, C))]
        args += [(dz, slots(rows, 2 * C)), (self.dw, layer(i, TAPS, C))]
        scratch = [pad_scratch(), pltpu.VMEM((rows, C), BF16), pltpu.VMEM((rows, C), BF16), pltpu.VMEM((C, C), F32)]
        if strided:
            scratch.append(stride_scratch())
        which = PLACES[i][0]
        self.pieces[which] = call(
            body, self.meta, args, self.piece_out(i), scratch, f"{self.tag}_weights_{i}", 6 * OWN * rows * C * C,
            into=self.pieces[which],
        )
        self.done = (self.pieces[which][0],)

    def backward(self, layers):
        if layers[0] == 4:
            self.pieces = [[], []]
        for i in layers:
            result = self.backward_layer(i)
        return result

    def resume(self, i):
        dz, payload = self.pending
        self.back_got = shared(payload, self.stages)
        self.weight_grad(i, dz)

    def fork(self, state=None):
        other = copy.copy(self)
        other.__dict__.update(state or {})
        if "pieces" in other.__dict__:
            other.pieces = list(other.pieces)
        return other

    def state(self):
        return {name: getattr(self, name) for name in ("du", "dxr", "pieces", "small", "pending")}

    def half(self, no, first, begin=None, end=None):
        kept, away = self.pieces[no]
        if no:
            parts = self.small[: SMALL // 2], self.small[SMALL // 2 :]
            at = kept.shape[0] - SMALL // 2
            kept = lax.dynamic_update_slice_in_dim(kept, jnp.where(first, *parts), at, 0)
            away = lax.dynamic_update_slice_in_dim(away, jnp.where(first, *parts[::-1]), at, 0)
        if begin is not None:
            away, _ = lax.optimization_barrier((away, begin))
            kept, _ = lax.optimization_barrier((kept, end))
        return kept + swap(away)


PLACES = {3: (0, 0), 4: (0, 1), 5: (0, 2), 0: (1, 0), 1: (1, 1), 2: (1, 2)}
PIECE_ROWS = (3 * C // 2, 3 * C // 2 + SMALL // 2)


def swap(x):
    return lax.ppermute(x, "section", [(0, 1), (1, 0)])


def fenced(always, work, x):
    shapes = jax.eval_shape(work, x)
    return lax.cond(always, work, lambda x: jax.tree.map(lambda y: jnp.zeros(y.shape, y.dtype), shapes), x)


class Reduction:
    def __init__(self, x, stages):
        self.x = x
        self.todo = []
        stride = 1
        for radix in stages:
            self.todo.append((True, radix, stride))
            stride *= radix
        self.todo += [(False, radix, stride) for _, radix, stride in reversed(self.todo)]

    def step(self):
        scatter, radix, stride = self.todo.pop(0)
        rows = self.x.shape[0]
        if scatter:
            parts = exchange(self.x.reshape(radix, rows // radix, C), radix, stride)
            self.x = jnp.sum(parts, axis=0)
        else:
            parts = exchange(jnp.broadcast_to(self.x, (radix,) + self.x.shape), radix, stride)
            self.x = parts.reshape(radix * rows, C)
        return (self.x,)

    def finish(self):
        while self.todo:
            self.step()
        return self.x


def per_device(features, out_grad, lengths, join_pick, dw, pw, gain, bias, res_w, down, down_b, up, up_b):
    first = lax.axis_index("section") == 0
    size = lax.axis_size("dp")
    inputs = features.reshape(MB, SLOT, C)
    cotangent = out_grad.reshape(MB, SLOT, C)
    own, picks = lengths[0, 0], join_pick[0]
    to_upper = lambda x: lax.ppermute(x, "section", [(0, 1)])
    to_lower = lambda x: lax.ppermute(x, "section", [(1, 0)])

    far_len = swap(own)
    far_rows = to_upper(inputs[MB - 1])
    far_w0 = swap(pw[0, 0:1])
    taps = jnp.concatenate([dw[0].reshape(5 * TAPS, C), gain[0], bias[0]], axis=0)
    far_taps = swap(taps)
    far_pw, far_res = swap(pw[0]), swap(res_w[0])
    wide = jnp.pad(down_b, ((0, 0), (0, C - SE)))
    squeeze = jnp.concatenate([down[0].T, up[0], up_b, wide], axis=0)
    far_squeeze = swap(squeeze)
    far_cot = to_lower(cotangent[:OWN])
    far_cot0 = to_upper(cotangent[MB - 1, :HALF])

    flag = first.astype(jnp.int32)[None]
    mine = lambda v: jnp.where(first, v[:OWN], jnp.concatenate([v[OWN:], jnp.zeros((1,), v.dtype)]))
    length = mine(jnp.where(first, own, far_len))
    half_len = (length + 1) // 2
    join_len = mine(jnp.where(first, far_len, own)[picks])
    meta1 = jnp.concatenate([length, half_len, flag])
    meta2 = jnp.concatenate([half_len, join_len, flag, picks[MB - 1 :]])

    def small(block):
        t = jnp.where(first == (block == 0), taps, far_taps)
        q = jnp.where(first == (block == 0), squeeze, far_squeeze)
        return (
            t[: 5 * TAPS].reshape(5, TAPS, C), t[5 * TAPS : 5 * TAPS + 6], t[5 * TAPS + 6 :],
            q[:SE], q[2 * SE + 1, :SE][:, None], q[SE : 2 * SE], q[2 * SE : 2 * SE + 1],
        )

    def prepared(block, start, stop):
        array = prepare(meta1, (pw[0], res_w[0]), (far_pw, far_res), block, start, stop)
        return array, {i: (array, i - start) for i in range(start, stop)}

    parts0 = [prepared(0, 1, 3), prepared(0, 3, 6)]
    parts1 = [prepared(1, 0, 1), prepared(1, 1, 4), prepared(1, 4, 6)]

    stages, deep = radices(size, 16), radices(size, 4)
    c14 = Block(False, meta1, small(0), {**parts0[0][1], **parts0[1][1]}, stages)
    c14.x, c14.x_far, c14.first_matrix = inputs, far_rows, (pw[0], far_w0)
    c14.forward({2: (parts0[1][0],)})
    out0 = c14.tail(after=(parts1[0][0],))
    late_picks, _ = lax.optimization_barrier((picks, c14.got[2]))
    joining = [lax.dynamic_index_in_dim(inputs, late_picks[m], 0, False)[HALF:] for m in range(OWN)]
    far_joining = to_lower(jnp.concatenate(joining, axis=0))
    c15 = Block(True, meta2, small(1), {**parts1[0][1], **parts1[1][1], **parts1[2][1]}, stages)
    c15.arrived, c15.joined_far, c15.joined = out0, far_joining, features.reshape(MB, 2, HALF, C)
    c15.forward({1: (parts1[1][0],), 2: (parts1[2][0],)})
    out1 = c15.tail(cotangent, far_cot)
    c15.stop = 2
    c15.backward((4, 3))
    begin = c15.back_got
    c15.backward((2,))
    always = own[0] > 0

    half0 = c15.half(0, first, begin, c15.du)
    sum0 = lax.psum(half0, "dp")

    def middle(half0):
        upper, lower = c15.fork(), c14.fork()
        upper.resume(2)
        upper.done += (half0,)
        back, dx1 = upper.backward((1, 0))
        lower.tail_backward(cotangent, far_cot0, back)
        lower.done = upper.done
        lower.backward((4,))
        begin1 = lower.back_got
        lower.backward((3,))
        half1 = upper.half(1, first, begin1, lower.du)
        begin2 = lower.back_got
        lower.stop = 2
        lower.backward((2,))
        return dx1, half1, lower.half(0, first, begin2, lower.du), lower.state()

    dx1, half1, half2, state = fenced(always, middle, half0)
    sum0, half2 = lax.optimization_barrier((sum0, half2))
    sum12 = lax.psum(jnp.concatenate([half1, half2], axis=0), "dp")

    def ending(half2):
        last = c14.fork(state)
        last.resume(2)
        last.done += (half2,)
        came0 = to_upper(sum0)
        dx0, = last.backward((1, 0))
        half3 = last.half(1, first)
        half3, dx0, *kept = lax.optimization_barrier((half3, dx0, out0, out1, dx1))
        reduction = Reduction(half3, deep)
        reduction.step()
        pad = jnp.zeros((1, HALF, C), F32)
        lower = jnp.concatenate([kept[0], jnp.concatenate([to_lower(kept[0][0:1, :HALF]), pad], axis=1)], axis=0)
        upper = jnp.concatenate([to_upper(kept[1]), kept[1][0:1]], axis=0)
        block_out = jnp.where(first, lower, upper)
        lower = jnp.concatenate([dx0, to_lower(dx0[0:1])], axis=0)
        joins = jnp.concatenate([to_upper(kept[2]), kept[2][0:1]], axis=0)
        joins = jnp.stack([lax.dynamic_index_in_dim(joins, jnp.argmax(picks == s), 0, False) for s in range(MB)])
        upper = jnp.concatenate([jnp.zeros_like(joins), joins], axis=1)
        dx = jnp.where(first, lower, upper)
        reduction.x, block_out, dx, came0 = lax.optimization_barrier((reduction.x, block_out, dx, came0))
        return block_out, dx, came0, reduction.finish()

    block_out, dx, came0, sum3 = fenced(always, ending, half2)
    sum12, sum3 = lax.optimization_barrier((sum12, sum3))
    sum1, sum2 = sum12[: half1.shape[0]], sum12[half1.shape[0] :]
    came1, came2, came3 = to_upper(sum1), to_lower(sum2), to_lower(sum3)

    lead = 3 * C // 2

    def joined(near, far):
        pair = [x.reshape(-1, 1, C // 2, C) for x in (near, far)]
        both = jnp.where(first, jnp.concatenate(pair, axis=1), jnp.concatenate(pair[::-1], axis=1))
        return both.reshape(-1, C, C)

    choose_mine = lambda a, b: jnp.where(first, a, b)
    rest_part = joined(choose_mine(sum3[:lead], sum1[:lead]), choose_mine(came3[:lead], came1[:lead]))
    lead_part = joined(choose_mine(sum2[:C], sum0[:C]), choose_mine(came2[:C], came0[:C]))
    pw_grad = jnp.concatenate([rest_part, lead_part], axis=0)[None]
    res_grad = joined(choose_mine(sum2[C:], sum0[C:]), choose_mine(came2[C:], came0[C:]))
    near, far = choose_mine(sum3[lead:], sum1[lead:]), choose_mine(came3[lead:], came1[lead:])
    rows = jnp.where(first, jnp.concatenate([near, far], axis=0), jnp.concatenate([far, near], axis=0))
    dw_grad = rows[TAIL_ROWS : TAIL_ROWS + 40].reshape(1, 5, 8, C)
    norms = jnp.concatenate([dw_grad[0, 1:, TAPS : TAPS + 2], rows[None, 2 * SE + 2 : 2 * SE + 4], rows[None, 2 * SE + 4 : 2 * SE + 6]], axis=0)
    return (
        block_out.reshape(features.shape), dx.reshape(features.shape), dw_grad[:, :, :TAPS], pw_grad,
        norms[None, :, 1], norms[None, :, 0], res_grad, rows[SE : 2 * SE].T[None], rows[2 * SE + 1 : 2 * SE + 2, :SE],
        rows[:SE][None], rows[2 * SE : 2 * SE + 1],
    )


def solution(mesh):
    rows = P("section", "dp", None)
    own = lambda dims: P("section", *([None] * dims))
    weights = (own(3), own(3), own(2), own(2), own(2), own(2), own(1), own(2), own(1))
    in_specs = (rows, rows, rows, P("dp", None), *weights)
    out_specs = (rows, rows, *weights)
    return jax.shard_map(per_device, mesh=mesh, in_specs=in_specs, out_specs=out_specs, check_vma=False)
```

```python
import copy

import jax
import jax.numpy as jnp
from jax import lax
from jax.experimental import pallas as pl
from jax.experimental.pallas import tpu as pltpu
from jax.sharding import PartitionSpec as P

EPSILON = 1e-05
EXACT = lax.Precision.HIGHEST
TAPS = 5
MB = 3
OWN = 2
SLOT = 400
HALF = 200
KEPT = 208
C = 512
LANES = 128
CHUNKS = [slice(c, c + LANES) for c in range(0, C, LANES)]
SE = 64
BF16, F32 = jnp.bfloat16, jnp.float32
VMEM_BYTES = 60 << 20
TAIL_ROWS = 2 * SE + 8
SMALL = 256


def radices(size, most):
    stages, left = [], size
    while left > 1:
        radix = min(most, left)
        while left % radix:
            radix -= 1
        stages.append(radix)
        left //= radix
    return stages


def exchange(block, radix, stride):
    size = lax.axis_size("dp")
    if radix == size:
        return lax.all_to_all(block, "dp", 0, 0)
    groups = []
    for base in range(size):
        if (base // stride) % radix == 0:
            groups.append([base + j * stride for j in range(radix)])
    return lax.all_to_all(block, "dp", 0, 0, axis_index_groups=groups)


def shared(block, stages):
    stride = 1
    for no, radix in enumerate(stages):
        if no:
            block = jnp.broadcast_to(jnp.sum(block, axis=0), (radix,) + block.shape[1:])
        block = exchange(block, radix, stride)
        stride *= radix
    return block


def halves(x):
    high = x.astype(BF16)
    return high, (x - high.astype(F32)).astype(BF16)


def sigmoid(x):
    return 0.5 * jnp.tanh(0.5 * x) + 0.5


def exact_dot(a, b, dims=((1,), (0,))):
    return lax.dot_general(a, b, (dims, ((), ())), precision=EXACT, preferred_element_type=F32)


def fast_dot(a, b, dims=((1,), (0,))):
    return lax.dot_general(a, b, (dims, ((), ())), preferred_element_type=F32)


def stacked_dot(high, low, w, back=False):
    w_high, w_low = w[0], w[1]
    w = jnp.concatenate([w_high, w_high, w_low], axis=1 if back else 0)
    x = jnp.concatenate([high, low, high], axis=1)
    return fast_dot(x, w, ((1,), (1 if back else 0,)))


def stacked_outer(a_high, a_low, b_high, b_low):
    a = jnp.concatenate([a_high, a_low, a_high], axis=0)
    b = jnp.concatenate([b_high, b_high, b_low], axis=0)
    return fast_dot(a, b, ((0,), (0,)))


def column_sum(x):
    return jnp.sum(x, axis=0, keepdims=True)


class Rows:
    def __init__(self, meta, m, two, rows, which=0):
        place = lax.broadcasted_iota(jnp.int32, (rows, LANES), 0)
        if two:
            later = place >= HALF
            limit = jnp.where(later, HALF + meta[OWN + m], meta[m])
            self.mask = place < limit
        else:
            self.mask = place < meta[which * OWN + m]

    def keep(self, x):
        return jnp.where(self.mask, x, 0.0)


class Padded:
    def __init__(self, ref, two):
        self.ref = ref
        self.pieces = [(8, 0, HALF), (16 + HALF, HALF, HALF)] if two else [(8, 0, SLOT)]

    def put(self, x):
        zeros = jnp.zeros((8, LANES), F32)
        for at, start, rows in self.pieces:
            self.ref[at - 8 : at, :] = zeros
            self.ref[at : at + rows, :] = x[start : start + rows]
        self.ref[at + rows : at + rows + 8, :] = zeros

    def get(self, offset):
        parts = [self.ref[at + offset : at + offset + rows, :] for at, _, rows in self.pieces]
        return parts[0] if len(parts) == 1 else jnp.concatenate(parts, axis=0)

    def conv(self, kernel):
        total = kernel[0:1] * self.get(-2)
        for k in range(1, TAPS):
            total = total + kernel[k : k + 1] * self.get(k - 2)
        return total

    def conv_back(self, kernel):
        total = kernel[0:1] * self.get(2)
        for k in range(1, TAPS):
            total = total + kernel[k : k + 1] * self.get(2 - k)
        return total


def every_other(ref, x):
    ref[0:SLOT, :] = x
    ref[SLOT : 2 * KEPT, :] = jnp.zeros((2 * KEPT - SLOT, LANES), F32)
    return ref[pl.ds(0, KEPT, stride=2), :]


def spread_out(ref, x):
    ref[...] = jnp.zeros_like(ref)
    ref[pl.ds(0, KEPT, stride=2), :] = x
    return ref[0:SLOT, :]


def center_spread(sums, rows):
    center = sums[0:1] / rows
    return center, lax.rsqrt(sums[1:2] / rows - center * center + EPSILON)


def added(ref):
    return jnp.sum(ref[:, 0], axis=0)


def accumulate(ref, m, at, value):
    rows = slice(at, at + value.shape[0])
    ref[rows, :] = jnp.where(m == 0, value, ref[rows, :] + value)


def send(ref, rows):
    for copy in range(ref.shape[0]):
        for row, x in enumerate(rows):
            ref[copy, 0, row : row + 1, 0 : x.shape[1]] = x


def pad_scratch():
    return pltpu.VMEM((len(CHUNKS), SLOT + 24, LANES), F32)


def stride_scratch():
    return pltpu.VMEM((len(CHUNKS), 2 * KEPT, LANES), F32)


def slots(rows, cols=C):
    return pl.BlockSpec((1, rows, cols), lambda m, *_: (m, 0, 0))


def copies(count, rows, cols=C):
    return pl.BlockSpec((count, 1, rows, cols), lambda m, *_: (0, m, 0, 0))


def whole(*shape):
    return pl.BlockSpec(shape, lambda m, *_: (0,) * len(shape))


def layer(i, *shape):
    return pl.BlockSpec((1,) + shape, lambda m, *_: (i,) + (0,) * len(shape))


def f32(*shape):
    return jax.ShapeDtypeStruct(shape, F32)


def bf16(*shape):
    return jax.ShapeDtypeStruct(shape, BF16)


def call(body, meta, args, outs, scratch=(), name=None, flops=0, steps=OWN, after=(), into=()):
    arrays, in_specs = [a for a, _ in args], [s for _, s in args]
    shapes, out_specs = [a for a, _ in outs], [s for _, s in outs]
    size = sum(a.size * a.dtype.itemsize for a in arrays + shapes)
    extra = list(after) + list(into)
    count = len(arrays)

    def inner(meta, *refs):
        body(meta, *refs[:count], *refs[count + len(extra) :])

    return pl.pallas_call(
        inner,
        out_shape=shapes,
        grid_spec=pltpu.PrefetchScalarGridSpec(
            num_scalar_prefetch=1,
            grid=(steps,),
            in_specs=in_specs + [pl.BlockSpec(memory_space=pl.ANY)] * len(extra),
            out_specs=out_specs,
            scratch_shapes=list(scratch),
        ),
        input_output_aliases={1 + count + len(after) + j: j for j in range(len(into))},
        compiler_params=pltpu.CompilerParams(vmem_limit_bytes=VMEM_BYTES),
        cost_estimate=pl.CostEstimate(flops=flops, bytes_accessed=size, transcendentals=0),
        name=name,
    )(meta, *arrays, *extra)


def choose(meta, block, own, far):
    return jnp.where(meta[2 * OWN] == 1 - block, own, far)


def prepare(meta, own, far, block, start, stop):
    def body(meta, *refs):
        pair = [ref[0] for ref in refs[:2]]
        if stop == 6:
            last = pl.program_id(0) == 5 - start
            pair = [jnp.where(last, ref[...], w) for ref, w in zip(refs[2:4], pair)]
        out = refs[-1]
        out[0, 0], out[0, 1] = halves(choose(meta, block, *pair))

    matrix = pl.BlockSpec((1, C, C), lambda j, *_: (jnp.minimum(j + start, 4), 0, 0))
    args = [(own[0], matrix), (far[0], matrix)]
    if stop == 6:
        args += [(own[1], whole(C, C)), (far[1], whole(C, C))]
    out = pl.BlockSpec((1, 2, C, C), lambda j, *_: (j, 0, 0, 0))
    name = f"prepare_{block}_{start}"
    return call(body, meta, args, [(bf16(stop - start, 2, C, C), out)], name=name, steps=stop - start)[0]


class Block:
    def __init__(self, two, meta, weights, ready, stages):
        self.done, self.stop, self.pending = (), None, None
        self.two, self.meta, self.stages = two, meta, stages
        self.dw, self.gain, self.bias = weights
        self.ready = ready
        self.tail_rows = SLOT if two else KEPT
        self.first, self.last = stages[0], stages[-1]
        self.tag = "c15" if two else "c14"

    def rows_of(self, i):
        return self.tail_rows if i == 4 else SLOT

    def valid(self, meta, m, i):
        last = i == 4 and not self.two
        return Rows(meta, m, self.two, self.rows_of(i), which=1 if last else 0)

    def matrix(self, i):
        array, at = self.ready[i]
        return (array, layer(at, 2, C, C))

    def source_args(self):
        if not self.two:
            return [(self.x, slots(SLOT)), (self.x_far, whole(SLOT, C))]
        far = pl.BlockSpec((HALF, C), lambda m, *_: (m, 0))
        near = pl.BlockSpec((1, 1, HALF, C), lambda m, meta: (meta[2 * OWN + 1], 1, 0, 0))
        return [(self.arrived, slots(HALF)), (self.joined_far, far), (self.joined, near)]

    def source(self, meta, refs, cs):
        lower = meta[2 * OWN] == 1
        if not self.two:
            return jnp.where(lower, refs[0][0, :, cs], refs[1][:, cs])
        joined = jnp.where(lower, refs[1][:, cs], refs[2][0, 0, :, cs])
        return jnp.concatenate([refs[0][0, :, cs], joined], axis=0)

    def before_args(self, i):
        if i == 0:
            return self.source_args()
        return [(self.z[i - 1], slots(SLOT)), (self.stats[i - 1], slots(2))]


    def forward_layer(self, i, after=()):
        two, count = self.two, self.first
        strided = i == 4 and not two
        rows = self.rows_of(i)
        n_src = len(self.source_args())
        width = C + LANES if i == 0 else C
        sent = 4 if i == 3 else 2
        makes = i == 0 and not two

        def body(meta, *refs):
            refs = list(refs)
            take = lambda n: [refs.pop(0) for _ in range(n)]
            m = pl.program_id(0)
            if i == 0:
                src = take(n_src)
            else:
                z_ref, got_ref = take(2)
                n_ref, = take(1) if i > 1 else (None,)
                gain_ref, bias_ref = take(2)
                res_sum, = take(1) if i == 3 else (None,)
            dw_ref, = take(1)
            if makes:
                own_ref, far_ref, z_out, pay, w_ref = take(5)

                @pl.when(m == 0)
                def _():
                    w_ref[0, 0], w_ref[0, 1] = halves(choose(meta, 0, own_ref[0], far_ref[0]))

            else:
                w_ref, z_out, pay = take(3)
            if i:
                stat_out, = take(1)
            if i == 1:
                n_out, = take(1)
            pad, y_ref = take(2)
            alt, = take(1) if strided else (None,)
            valid_in = self.valid(meta, m, 0)
            if i:
                sums = added(got_ref)
                if i == 1:
                    count_in = jnp.maximum(jnp.concatenate([sums[0:1, C:]] * len(CHUNKS), axis=1), 1.0)
                    count_out = jnp.maximum(jnp.concatenate([sums[1:2, C:]] * len(CHUNKS), axis=1), 1.0)
                    n_out[0, 0:1, :] = count_in
                    n_out[0, 1:2, :] = count_out
                else:
                    count_in = n_ref[0, 0:1, :]
                center, spread = center_spread(sums[:, :C], count_in)
                stat_out[0, 0:1, :] = center
                stat_out[0, 1:2, :] = spread
                scale = gain_ref[i - 1 : i] * spread
                shift = bias_ref[i - 1 : i] - center * scale
            for c, cs in enumerate(CHUNKS):
                if i == 0:
                    h = valid_in.keep(self.source(meta, src, cs))
                else:
                    u = z_ref[0, :, cs] * scale[:, cs] + shift[:, cs]
                    h = valid_in.keep(u * sigmoid(u))
                padded = Padded(pad.at[c], two)
                padded.put(h)
                y = padded.conv(dw_ref[0, :, cs])
                if strided:
                    y = every_other(alt.at[c], y)
                high, low = halves(y)
                y_ref[:, cs] = high
                y_ref[:, C + cs.start : C + cs.stop] = low
            w = w_ref.at[0] if makes else w_ref.at[0]
            z = stacked_dot(y_ref[:, 0:C], y_ref[:, C : 2 * C], w)
            z_out[0] = z
            valid = self.valid(meta, m, i)
            one, square = [], []
            for cs in CHUNKS:
                kept = valid.keep(z[:, cs])
                one.append(column_sum(kept))
                square.append(column_sum(kept * kept))
            if i == 0:
                if two:
                    number = (meta[m] + meta[OWN + m]).astype(F32)
                    numbers = number, number
                else:
                    numbers = meta[m].astype(F32), meta[OWN + m].astype(F32)
                one.append(jnp.full((1, LANES), numbers[0], F32))
                square.append(jnp.full((1, LANES), numbers[1], F32))
            out = [jnp.concatenate(one, axis=1), jnp.concatenate(square, axis=1)]
            if i == 3:
                out += [res_sum[0, 0:1, :], res_sum[0, 1:2, :]]
            send(pay, out)

        if i == 0:
            args = list(self.source_args())
        else:
            got = 4 if i == 4 else 2
            args = [(self.z[i - 1], slots(SLOT)), (self.got[i - 1], copies(self.last, got, C + LANES if i == 1 else C))]
            if i > 1:
                args.append((self.number, slots(2)))
            args += [(self.gain, whole(6, C)), (self.bias, whole(6, C))]
            if i == 3:
                args.append((self.res_sum, slots(2)))
        args.append((self.dw, layer(i, TAPS, C)))
        args += [(w, layer(0, C, C)) for w in self.first_matrix] if makes else [self.matrix(i)]
        outs = [(f32(OWN, rows, C), slots(rows)), (f32(count, OWN, sent, width), copies(count, sent, width))]
        if i:
            outs.append((f32(OWN, 2, C), slots(2)))
        if i == 1:
            outs.append((f32(OWN, 2, C), slots(2)))
        if makes:
            outs.append((bf16(1, 2, C, C), layer(0, 2, C, C)))
        scratch = [pad_scratch(), pltpu.VMEM((rows, 2 * C), BF16)]
        if strided:
            scratch.append(stride_scratch())
        result = call(body, self.meta, args, outs, scratch, f"{self.tag}_forward_{i}", 6 * OWN * rows * C * C, after=after)
        self.z.append(result[0])
        if makes:
            self.ready[0] = (result[2], 0)
        if i:
            self.stats.append(result[2])
        if i == 1:
            self.number = result[3]
        self.got.append(shared(result[1], self.stages))

    def residual(self):
        two, rows = self.two, self.tail_rows

        def body(meta, *refs):
            refs = list(refs)
            src = [refs.pop(0) for _ in self.source_args()]
            w_ref, r_out, x_out, sum_out = refs[:4]
            alt = refs[4] if not two else None
            m = pl.program_id(0)
            valid_in = self.valid(meta, m, 0)
            for c, cs in enumerate(CHUNKS):
                x = valid_in.keep(self.source(meta, src, cs))
                if not two:
                    x = every_other(alt.at[c], x)
                high, low = halves(x)
                x_out[0, :, cs] = high
                x_out[0, :, C + cs.start : C + cs.stop] = low
            r = stacked_dot(x_out[0, :, 0:C], x_out[0, :, C : 2 * C], w_ref.at[0])
            r_out[0] = r
            valid = self.valid(meta, m, 4)
            for cs in CHUNKS:
                kept = valid.keep(r[:, cs])
                sum_out[0, 0:1, cs] = column_sum(kept)
                sum_out[0, 1:2, cs] = column_sum(kept * kept)

        args = self.source_args() + [self.matrix(5)]
        outs = [
            (f32(OWN, rows, C), slots(rows)),
            (bf16(OWN, rows, 2 * C), slots(rows, 2 * C)),
            (f32(OWN, 2, C), slots(2)),
        ]
        scratch = [] if two else [stride_scratch()]
        self.r, self.picked, self.res_sum = call(
            body, self.meta, args, outs, scratch, f"{self.tag}_residual", 6 * OWN * rows * C * C
        )

    def forward(self, after=None):
        self.z, self.got, self.stats = [], [], []
        for i in range(5):
            first = after[i]() if after and i in after else ()
            if i == 2:
                self.residual()
            self.forward_layer(i, first)


    def segments(self):
        return [(0, HALF), (HALF, HALF)] if self.two else [(0, self.tail_rows)]

    def lengths(self, meta, m):
        if self.two:
            return [meta[m], meta[OWN + m]]
        return [meta[OWN + m]]

    def squeeze(self, sums, counts, se_refs):
        down_t, down_b, up, up_b = se_refs
        means = [s / jnp.maximum(jnp.full((1, C), n.astype(F32)), 1.0) for s, n in zip(sums, counts)]
        ps = [jnp.sum(down_t[...] * mean, axis=1, keepdims=True) + down_b[...] for mean in means]
        gates = [sigmoid(column_sum(up[...] * (p * sigmoid(p))) + up_b[...]) for p in ps]
        return means, ps, gates

    def squeeze_back(self, des, ps, gates, counts, se_refs, means, small, m):
        down_t, down_b, up, up_b = se_refs
        shares, up_grad, down_grad, dq_sum, dp_sum = [], 0.0, 0.0, 0.0, 0.0
        for de, p, gate, n, mean in zip(des, ps, gates, counts, means):
            dq = de * gate * (1.0 - gate)
            s = sigmoid(p)
            dp = jnp.sum(up[...] * dq, axis=1, keepdims=True) * (s * (1.0 + p * (1.0 - s)))
            shares.append(column_sum(down_t[...] * dp) / jnp.maximum(jnp.full((1, C), n.astype(F32)), 1.0))
            up_grad, down_grad = up_grad + (p * s) * dq, down_grad + dp * mean
            dq_sum, dp_sum = dq_sum + dq, dp_sum + dp
        row, col = (lax.broadcasted_iota(jnp.int32, (SE, C), axis) for axis in (0, 1))
        dp_row = column_sum(jnp.where(row == col, dp_sum, 0.0))
        accumulate(small, m, 0, up_grad)
        accumulate(small, m, SE, down_grad)
        accumulate(small, m, 2 * SE, dq_sum)
        accumulate(small, m, 2 * SE + 1, dp_row)
        return shares

    def last_norm(self, m, dt_out, du_out, z_ref, slope_ref, gates, shares, center, spread, res_bias, res_gain, pay, small):
        bias_sum, gain_sum = [], []
        for cs in CHUNKS:
            dh = dt_out[0, :, cs] * self.by_segment(gates, cs) + self.by_segment(shares, cs)
            du = dh * slope_ref[:, cs]
            du_out[0, :, cs] = du
            bias_sum.append(column_sum(du))
            gain_sum.append(column_sum(du * ((z_ref[0, :, cs] - center[:, cs]) * spread[:, cs])))
        rows = [jnp.concatenate(x, axis=1) for x in (bias_sum, gain_sum, res_bias, res_gain)]
        send(pay, rows)
        for j, row in enumerate(rows):
            accumulate(small, m, 2 * SE + 2 + j, row)

    def se_args(self):
        return list(zip(self.excitation, (whole(SE, C), whole(SE, 1), whole(SE, C), whole(1, C))))

    def store_rows(self, ref, rows):
        ref[0] = jnp.concatenate(rows + [jnp.zeros((8 - len(rows), C), F32)], axis=0)

    def store_columns(self, ref, columns):
        ref[0] = jnp.zeros((SE, 8), F32)
        for j, column in enumerate(columns):
            ref[0, :, j : j + 1] = column

    def by_segment(self, rows, cs):
        parts = [jnp.broadcast_to(row[:, cs], (n, LANES)) for row, (_, n) in zip(rows, self.segments())]
        return parts[0] if len(parts) == 1 else jnp.concatenate(parts, axis=0)

    def seg_sums(self, x):
        return [column_sum(x[at : at + n]) for at, n in self.segments()]

    def tail(self, cotangent=None, far=None, after=()):
        two, rows = self.two, self.tail_rows
        back = cotangent is not None

        def body(meta, *refs):
            refs = list(refs)
            take = lambda n: [refs.pop(0) for _ in range(n)]
            m = pl.program_id(0)
            z_ref, got4, r_ref, got3, n_ref, gain, bias = take(7)
            se_refs = take(4)
            if back:
                cot_ref, far_ref = take(2)
            out, stat_out, rstat_out, means_out, p_out, gate_out = take(6)
            if back:
                small, du_out, dt_out, pay = take(4)
            h_ref, = take(1)
            if back:
                slope_ref, = take(1)
            valid = self.valid(meta, m, 4)
            number = n_ref[0, 1:2, :]
            center, spread = center_spread(added(got4), number)
            rcenter, rspread = center_spread(added(got3)[2:4], number)
            stat_out[0, 0:1, :] = center
            stat_out[0, 1:2, :] = spread
            rstat_out[0, 0:1, :] = rcenter
            rstat_out[0, 1:2, :] = rspread
            scale = gain[4:5] * spread
            shift = bias[4:5] - center * scale
            sums = []
            for cs in CHUNKS:
                u = z_ref[0, :, cs] * scale[:, cs] + shift[:, cs]
                s = sigmoid(u)
                h = valid.keep(u * s)
                h_ref[:, cs] = h
                if back:
                    slope_ref[:, cs] = valid.keep(s * (1.0 + u * (1.0 - s)))
                sums.append(self.seg_sums(h))
            sums = [jnp.concatenate([s[j] for s in sums], axis=1) for j in range(len(self.segments()))]
            counts = self.lengths(meta, m)
            means, ps, gates = self.squeeze(sums, counts, se_refs)
            self.store_rows(means_out, means)
            self.store_columns(p_out, ps)
            self.store_rows(gate_out, gates)
            res_gain, res_bias, gate_grad = [], [], []
            for cs in CHUNKS:
                h = h_ref[:, cs]
                rh = (r_ref[0, :, cs] - rcenter[:, cs]) * rspread[:, cs]
                t = h * self.by_segment(gates, cs) + gain[5:6, cs] * rh + bias[5:6, cs]
                s = sigmoid(t)
                out[0, 0:rows, cs] = valid.keep(t * s)
                if rows < SLOT:
                    out[0, rows:SLOT, cs] = jnp.zeros((SLOT - rows, LANES), F32)
                if back:
                    cot = jnp.where(meta[2 * OWN] == 1, far_ref[0, :, cs], cot_ref[0, :, cs])
                    dt = valid.keep(cot * (s * (1.0 + t * (1.0 - s))))
                    dt_out[0, :, cs] = dt
                    res_bias.append(column_sum(dt))
                    res_gain.append(column_sum(dt * rh))
                    gate_grad.append(self.seg_sums(dt * h))
            if not back:
                return
            des = [jnp.concatenate([g[j] for g in gate_grad], axis=1) for j in range(len(counts))]
            shares = self.squeeze_back(des, ps, gates, counts, se_refs, means, small, m)
            self.last_norm(m, dt_out, du_out, z_ref, slope_ref, gates, shares, center, spread, res_bias, res_gain, pay, small)

        args = [
            (self.z[4], slots(rows)), (self.got[4], copies(self.last, 2)), (self.r, slots(rows)),
            (self.got[3], copies(self.last, 4)), (self.number, slots(2)),
            (self.gain, whole(6, C)), (self.bias, whole(6, C)),
        ] + self.se_args()
        outs = [
            (f32(OWN, SLOT, C), slots(SLOT)), (f32(OWN, 2, C), slots(2)), (f32(OWN, 2, C), slots(2)),
            (f32(OWN, 8, C), slots(8)), (f32(OWN, SE, 8), slots(SE, 8)), (f32(OWN, 8, C), slots(8)),
        ]
        scratch = [pltpu.VMEM((rows, C), F32)]
        if back:
            args += [(cotangent, layer(MB - 1, SLOT, C)), (far, slots(SLOT))]
            outs += self.tail_outs()
            scratch.append(pltpu.VMEM((rows, C), F32))
        result = call(body, self.meta, args, outs, scratch, f"{self.tag}_tail", after=after)
        self.stats.append(result[1])
        self.rstat, self.se_state = result[2], result[3:6]
        if back:
            self.tail_results(result[6:])
        return result[0]

    def tail_outs(self):
        rows, count = self.tail_rows, self.first
        return [
            (f32(SMALL, C), whole(TAIL_ROWS, C)), (f32(OWN, rows, C), slots(rows)), (f32(OWN, rows, C), slots(rows)),
            (f32(count, OWN, 4, C), copies(count, 4)),
        ]

    def tail_results(self, result):
        self.small, self.du, self.dt, pay = result
        self.back_got = shared(pay, self.stages)

    def tail_backward(self, cotangent, far, back):
        rows = self.tail_rows

        def body(meta, z_ref, r_ref, stat, rstat, gain, bias, means_ref, p_ref, gate_ref, down, down_b, up, up_b, cot_ref, far_ref, back_ref,
                 small, du_out, dt_out, pay, slope_ref):
            m = pl.program_id(0)
            valid = self.valid(meta, m, 4)
            center, spread, rcenter, rspread = stat[0, 0:1], stat[0, 1:2], rstat[0, 0:1], rstat[0, 1:2]
            scale = gain[4:5] * spread
            shift = bias[4:5] - center * scale
            zeros = jnp.zeros((rows - HALF, LANES), F32)
            counts = self.lengths(meta, m)
            ps = [p_ref[0, :, j : j + 1] for j in range(len(counts))]
            gates = [gate_ref[0, j : j + 1, :] for j in range(len(counts))]
            means = [means_ref[0, j : j + 1, :] for j in range(len(counts))]
            res_gain, res_bias, gate_grad = [], [], []
            for cs in CHUNKS:
                u = z_ref[0, :, cs] * scale[:, cs] + shift[:, cs]
                s = sigmoid(u)
                h = valid.keep(u * s)
                slope_ref[:, cs] = valid.keep(s * (1.0 + u * (1.0 - s)))
                rh = (r_ref[0, :, cs] - rcenter[:, cs]) * rspread[:, cs]
                t = h * self.by_segment(gates, cs) + gain[5:6, cs] * rh + bias[5:6, cs]
                s = sigmoid(t)
                here = jnp.where(meta[2 * OWN] == 1, cot_ref[0, 0:HALF, cs], far_ref[:, cs])
                cot = jnp.concatenate([here + back_ref[0, :, cs], zeros], axis=0)
                dt = valid.keep(cot * (s * (1.0 + t * (1.0 - s))))
                dt_out[0, :, cs] = dt
                res_bias.append(column_sum(dt))
                res_gain.append(column_sum(dt * rh))
                gate_grad.append(self.seg_sums(dt * h))
            des = [jnp.concatenate([g[j] for g in gate_grad], axis=1) for j in range(len(counts))]
            shares = self.squeeze_back(des, ps, gates, counts, (down, down_b, up, up_b), means, small, m)
            self.last_norm(m, dt_out, du_out, z_ref, slope_ref, gates, shares, center, spread, res_bias, res_gain, pay, small)

        args = [
            (self.z[4], slots(rows)), (self.r, slots(rows)), (self.stats[4], slots(2)), (self.rstat, slots(2)),
            (self.gain, whole(6, C)), (self.bias, whole(6, C)),
            (self.se_state[0], slots(8)), (self.se_state[1], slots(SE, 8)), (self.se_state[2], slots(8)),
        ] + self.se_args() + [(cotangent, slots(SLOT)), (far, whole(HALF, C)), (back, slots(HALF))]
        scratch = [pltpu.VMEM((rows, C), F32)]
        self.tail_results(call(body, self.meta, args, self.tail_outs(), scratch, f"{self.tag}_tail_back"))


    def norm_grad(self, du, zh, scale, sums, number, cs):
        return scale[:, cs] * (du - sums[0:1, cs] / number[:, cs] - zh * (sums[1:2, cs] / number[:, cs]))

    def backward_layer(self, i):
        two, count = self.two, self.first
        strided = i == 4 and not two
        rows = self.rows_of(i)
        n_src = len(self.source_args())

        def body(meta, *refs):
            refs = list(refs)
            take = lambda n: [refs.pop(0) for _ in range(n)]
            m = pl.program_id(0)
            du_ref, z_ref, w_ref, got, n_ref, stat, gain, bias, dw_ref = take(9)
            if i:
                zp_ref, statp = take(2)
            else:
                dxr_ref, = take(1)
                src = take(n_src)
            small, dz_out = take(2)
            if i:
                du_out, pay = take(2)
            elif two:
                back_out, dx_out = take(2)
            else:
                dx_out, = take(1)
            pad, = take(1)
            alt, = take(1) if refs else (None,)
            sums = added(got)
            number = n_ref[0, 1:2, :] if i == 4 else n_ref[0, 0:1, :]
            center, spread = stat[0, 0:1], stat[0, 1:2]
            scale = gain[i : i + 1] * spread
            valid = self.valid(meta, m, i)
            for cs in CHUNKS:
                zh = (z_ref[0, :, cs] - center[:, cs]) * spread[:, cs]
                dz = valid.keep(self.norm_grad(du_ref[0, :, cs], zh, scale, sums, number, cs))
                high, low = halves(dz)
                dz_out[0, :, cs] = high
                dz_out[0, :, C + cs.start : C + cs.stop] = low
            dy = stacked_dot(dz_out[0, :, 0:C], dz_out[0, :, C : 2 * C], w_ref.at[0], True)
            valid_in = self.valid(meta, m, 0)
            if i:
                pcenter, pspread = statp[0, 0:1], statp[0, 1:2]
                pscale = gain[i - 1 : i] * pspread
                pshift = bias[i - 1 : i] - pcenter * pscale
            taps, bias_sum, gain_sum = [[] for _ in range(TAPS)], [], []
            for c, cs in enumerate(CHUNKS):
                grad = dy[:, cs]
                if strided:
                    grad = spread_out(alt.at[c], grad)
                padded = Padded(pad.at[c], two)
                padded.put(grad)
                if i:
                    z = zp_ref[0, :, cs]
                    u = z * pscale[:, cs] + pshift[:, cs]
                    s = sigmoid(u)
                    h = valid_in.keep(u * s)
                else:
                    h = valid_in.keep(self.source(meta, src, cs))
                dh = None
                for k in range(TAPS):
                    moved = padded.get(2 - k)
                    taps[k].append(column_sum(h * moved))
                    term = dw_ref[0, k : k + 1, cs] * moved
                    dh = term if dh is None else dh + term
                if i:
                    du = valid_in.keep(dh * (s * (1.0 + u * (1.0 - s))))
                    du_out[0, :, cs] = du
                    bias_sum.append(column_sum(du))
                    gain_sum.append(column_sum(du * ((z - pcenter[:, cs]) * pspread[:, cs])))
                    continue
                dxr = dxr_ref[0, :, cs]
                if not two:
                    dxr = spread_out(alt.at[c], dxr)
                dx = valid_in.keep(dh) + dxr
                if two:
                    back_out[0, :, cs] = dx[:HALF]
                    dx = dx[HALF:]
                dx_out[0, :, cs] = dx
            rows = taps + [bias_sum, gain_sum] if i else taps
            rows = [jnp.concatenate(x, axis=1) for x in rows]
            for j, row in enumerate(rows):
                accumulate(small, m, j, row)
            if i:
                send(pay, rows[TAPS:])

        sent = 4 if i == 4 else 2
        args = [
            (self.du, slots(rows)), (self.z[i], slots(rows)), self.matrix(i), (self.back_got, copies(self.last, sent)),
            (self.number, slots(2)), (self.stats[i], slots(2)), (self.gain, whole(6, C)), (self.bias, whole(6, C)),
            (self.dw, layer(i, TAPS, C)),
        ]
        if not i:
            args.append((self.dxr, slots(self.tail_rows)))
        args += self.before_args(i)
        place = TAIL_ROWS // 8 + i
        outs = [(f32(SMALL, C), pl.BlockSpec((8, C), lambda m, *_: (place, 0))), (bf16(OWN, rows, 2 * C), slots(rows, 2 * C))]
        if i:
            outs += [(f32(OWN, SLOT, C), slots(SLOT)), (f32(count, OWN, 2, C), copies(count, 2))]
        elif two:
            outs += [(f32(OWN, HALF, C), slots(HALF)), (f32(OWN, HALF, C), slots(HALF))]
        else:
            outs += [(f32(OWN, SLOT, C), slots(SLOT))]
        scratch = [pad_scratch()]
        if strided or (i == 0 and not two):
            scratch.append(stride_scratch())
        self.small, dz, *result = call(
            body, self.meta, args, outs, scratch, f"{self.tag}_backward_{i}", 6 * OWN * rows * C * C,
            after=self.done, into=(self.small,),
        )
        got = self.back_got
        if i:
            self.du = result[0]
            if i == self.stop:
                self.pending = dz, result[1]
                return result
            self.back_got = shared(result[1], self.stages)
        self.weight_grad(i, dz)
        if i == 4:
            self.residual_back(got)
        return result

    def residual_back(self, got):
        rows = self.tail_rows

        def body(meta, got, n_ref, dt_ref, r_ref, rstat, gain, w_ref, x_ref, kept_out, away_out, dxr_out, dr, total):
            m = pl.program_id(0)
            sums = added(got)[2:4]
            number = n_ref[0, 1:2, :]
            center, spread = rstat[0, 0:1], rstat[0, 1:2]
            scale = gain[5:6] * spread
            valid = self.valid(meta, m, 4)
            for cs in CHUNKS:
                rh = (r_ref[0, :, cs] - center[:, cs]) * spread[:, cs]
                high, low = halves(valid.keep(self.norm_grad(dt_ref[0, :, cs], rh, scale, sums, number, cs)))
                dr[:, cs] = high
                dr[:, C + cs.start : C + cs.stop] = low
            high, low = dr[:, 0:C], dr[:, C : 2 * C]
            dxr_out[0] = stacked_dot(high, low, w_ref.at[0], True)
            grad = stacked_outer(x_ref[0, :, 0:C], x_ref[0, :, C : 2 * C], high, low)
            self.add_halves(meta, m, grad, total, kept_out, away_out)

        args = [
            (got, copies(self.last, 4)), (self.number, slots(2)), (self.dt, slots(rows)), (self.r, slots(rows)),
            (self.rstat, slots(2)), (self.gain, whole(6, C)), self.matrix(5), (self.picked, slots(rows, 2 * C)),
        ]
        outs = self.piece_out(5) + [(f32(OWN, rows, C), slots(rows))]
        which = PLACES[5][0]
        *self.pieces[which], self.dxr = call(
            body, self.meta, args, outs, [pltpu.VMEM((rows, 2 * C), BF16), pltpu.VMEM((C, C), F32)],
            f"{self.tag}_residual_back", 12 * OWN * rows * C * C, into=self.pieces[which],
        )

    def piece_out(self, i):
        which, place = PLACES[i]
        rows = PIECE_ROWS[which]
        return [(f32(rows, C), pl.BlockSpec((C // 2, C), lambda m, *_: (place, 0)))] * 2

    def add_halves(self, meta, m, grad, total, kept_out, away_out):
        @pl.when(m == 0)
        def _():
            total[...] = grad

        @pl.when(m > 0)
        def _():
            top, bottom = total[0 : C // 2] + grad[0 : C // 2], total[C // 2 : C] + grad[C // 2 : C]
            lower = meta[2 * OWN] == 1
            kept_out[...] = jnp.where(lower, top, bottom)
            away_out[...] = jnp.where(lower, bottom, top)

    def weight_grad(self, i, dz):
        two = self.two
        strided = i == 4 and not two
        rows = self.rows_of(i)
        n_src = len(self.source_args())

        def body(meta, *refs):
            refs = list(refs)
            take = lambda n: [refs.pop(0) for _ in range(n)]
            m = pl.program_id(0)
            if i:
                zp_ref, statp, gain, bias = take(4)
                center, spread = statp[0, 0:1], statp[0, 1:2]
                scale = gain[i - 1 : i] * spread
                shift = bias[i - 1 : i] - center * scale
            else:
                src = take(n_src)
            dz_ref, dw_ref, kept_out, away_out, pad, yh, yl, total = take(8)
            alt, = take(1) if strided else (None,)
            valid_in = self.valid(meta, m, 0)
            for c, cs in enumerate(CHUNKS):
                if i:
                    u = zp_ref[0, :, cs] * scale[:, cs] + shift[:, cs]
                    h = valid_in.keep(u * sigmoid(u))
                else:
                    h = valid_in.keep(self.source(meta, src, cs))
                padded = Padded(pad.at[c], two)
                padded.put(h)
                y = padded.conv(dw_ref[0, :, cs])
                if strided:
                    y = every_other(alt.at[c], y)
                yh[:, cs], yl[:, cs] = halves(y)
            grad = stacked_outer(yh[...], yl[...], dz_ref[0, :, 0:C], dz_ref[0, :, C : 2 * C])
            self.add_halves(meta, m, grad, total, kept_out, away_out)

        args = self.before_args(i)
        if i:
            args += [(self.gain, whole(6, C)), (self.bias, whole(6, C))]
        args += [(dz, slots(rows, 2 * C)), (self.dw, layer(i, TAPS, C))]
        scratch = [pad_scratch(), pltpu.VMEM((rows, C), BF16), pltpu.VMEM((rows, C), BF16), pltpu.VMEM((C, C), F32)]
        if strided:
            scratch.append(stride_scratch())
        which = PLACES[i][0]
        self.pieces[which] = call(
            body, self.meta, args, self.piece_out(i), scratch, f"{self.tag}_weights_{i}", 6 * OWN * rows * C * C,
            into=self.pieces[which],
        )
        self.done = (self.pieces[which][0],)

    def backward(self, layers):
        if layers[0] == 4:
            self.pieces = [[], []]
        for i in layers:
            result = self.backward_layer(i)
        return result

    def resume(self, i):
        dz, payload = self.pending
        self.back_got = shared(payload, self.stages)
        self.weight_grad(i, dz)

    def fork(self, state=None):
        other = copy.copy(self)
        other.__dict__.update(state or {})
        if "pieces" in other.__dict__:
            other.pieces = list(other.pieces)
        return other

    def state(self):
        return {name: getattr(self, name) for name in ("du", "dxr", "pieces", "small", "pending")}

    def half(self, no, first, begin=None, end=None):
        kept, away = self.pieces[no]
        if no:
            parts = self.small[: SMALL // 2], self.small[SMALL // 2 :]
            at = kept.shape[0] - SMALL // 2
            kept = lax.dynamic_update_slice_in_dim(kept, jnp.where(first, *parts), at, 0)
            away = lax.dynamic_update_slice_in_dim(away, jnp.where(first, *parts[::-1]), at, 0)
        if begin is not None:
            away, _ = lax.optimization_barrier((away, begin))
            kept, _ = lax.optimization_barrier((kept, end))
        return kept + swap(away)


PLACES = {3: (0, 0), 4: (0, 1), 5: (0, 2), 0: (1, 0), 1: (1, 1), 2: (1, 2)}
PIECE_ROWS = (3 * C // 2, 3 * C // 2 + SMALL // 2)


def pick_joining(picks, features):
    def body(picks, in_ref, out_ref):
        out_ref[...] = in_ref[0, 0]

    own = pl.BlockSpec((1, 1, HALF, C), lambda m, picks: (picks[m], 1, 0, 0))
    out = (f32(OWN * HALF, C), pl.BlockSpec((HALF, C), lambda m, *_: (m, 0)))
    return call(body, picks, [(features, own)], [out], name="pick_joining")[0]


def swap(x):
    return lax.ppermute(x, "section", [(0, 1), (1, 0)])


def fenced(always, work, x):
    shapes = jax.eval_shape(work, x)
    return lax.cond(always, work, lambda x: jax.tree.map(lambda y: jnp.zeros(y.shape, y.dtype), shapes), x)


class Reduction:
    def __init__(self, x, stages):
        self.x = x
        self.todo = []
        stride = 1
        for radix in stages:
            self.todo.append((True, radix, stride))
            stride *= radix
        self.todo += [(False, radix, stride) for _, radix, stride in reversed(self.todo)]

    def step(self):
        scatter, radix, stride = self.todo.pop(0)
        rows = self.x.shape[0]
        if scatter:
            parts = exchange(self.x.reshape(radix, rows // radix, C), radix, stride)
            self.x = jnp.sum(parts, axis=0)
        else:
            parts = exchange(jnp.broadcast_to(self.x, (radix,) + self.x.shape), radix, stride)
            self.x = parts.reshape(radix * rows, C)
        return (self.x,)

    def finish(self):
        while self.todo:
            self.step()
        return self.x


def per_device(features, out_grad, lengths, join_pick, dw, pw, gain, bias, res_w, down, down_b, up, up_b):
    first = lax.axis_index("section") == 0
    size = lax.axis_size("dp")
    inputs = features.reshape(MB, SLOT, C)
    cotangent = out_grad.reshape(MB, SLOT, C)
    own, picks = lengths[0, 0], join_pick[0]
    to_upper = lambda x: lax.ppermute(x, "section", [(0, 1)])
    to_lower = lambda x: lax.ppermute(x, "section", [(1, 0)])

    far_len = swap(own)
    far_rows = to_upper(inputs[MB - 1])
    far_w0 = swap(pw[0, 0:1])
    taps = jnp.concatenate([dw[0].reshape(5 * TAPS, C), gain[0], bias[0]], axis=0)
    far_taps = swap(taps)
    far_pw, far_res = swap(pw[0]), swap(res_w[0])
    wide = jnp.pad(down_b, ((0, 0), (0, C - SE)))
    squeeze = jnp.concatenate([down[0].T, up[0], up_b, wide], axis=0)
    far_squeeze = swap(squeeze)

    flag = first.astype(jnp.int32)[None]
    mine = lambda v: jnp.where(first, v[:OWN], jnp.concatenate([v[OWN:], jnp.zeros((1,), v.dtype)]))
    length = mine(jnp.where(first, own, far_len))
    half_len = (length + 1) // 2
    join_len = mine(jnp.where(first, far_len, own)[picks])
    meta1 = jnp.concatenate([length, half_len, flag])
    meta2 = jnp.concatenate([half_len, join_len, flag, picks[MB - 1 :]])

    def small(block):
        t = jnp.where(first == (block == 0), taps, far_taps)
        return t[: 5 * TAPS].reshape(5, TAPS, C), t[5 * TAPS : 5 * TAPS + 6], t[5 * TAPS + 6 :]

    def excitation(block, squeeze, far_squeeze):
        q = jnp.where(first == (block == 0), squeeze, far_squeeze)
        return q[:SE], q[2 * SE + 1, :SE][:, None], q[SE : 2 * SE], q[2 * SE : 2 * SE + 1]

    def prepared(block, start, stop, later=None):
        meta = meta1 if later is None else lax.optimization_barrier((meta1, later))[0]
        array = prepare(meta, (pw[0], res_w[0]), (far_pw, far_res), block, start, stop)
        return array, {i: (array, i - start) for i in range(start, stop)}

    parts0 = [prepared(0, 1, 3), prepared(0, 3, 6)]

    stages, deep = radices(size, 16), radices(size, 4)
    c14 = Block(False, meta1, small(0), {**parts0[0][1], **parts0[1][1]}, stages)
    c14.x, c14.x_far, c14.first_matrix = inputs, far_rows, (pw[0], far_w0)
    c14.excitation = excitation(0, squeeze, far_squeeze)
    c14.forward({2: lambda: (parts0[1][0],)})
    array, ready15 = prepared(1, 0, 1, c14.z[4])
    out0 = c14.tail(after=(array,))
    late_picks, _ = lax.optimization_barrier((picks, c14.z[3]))
    far_joining = to_lower(pick_joining(late_picks, features.reshape(MB, 2, HALF, C)))
    c15 = Block(True, meta2, small(1), ready15, stages)
    c15.arrived, c15.joined_far, c15.joined = out0, far_joining, features.reshape(MB, 2, HALF, C)
    far_cots = []

    def prepare_beside(start, stop):
        def go():
            array, ready = prepared(1, start, stop, c15.z[-1])
            c15.ready.update(ready)
            return (array,)

        return go

    def beside_third_sum():
        cots, q, far_q, _ = lax.optimization_barrier((cotangent, squeeze, far_squeeze, c15.z[3]))
        far_cots.extend([to_lower(cots[:OWN]), to_upper(cots[MB - 1, :HALF])])
        c15.excitation = excitation(1, q, far_q)
        return (*far_cots, *c15.excitation, *prepare_beside(4, 5)())

    c15.forward({1: prepare_beside(1, 4), 2: prepare_beside(5, 6), 4: beside_third_sum})
    far_cot, far_cot0 = far_cots
    out1 = c15.tail(cotangent, far_cot)

    pad = jnp.zeros((1, HALF, C), F32)
    lower = jnp.concatenate([out0, jnp.concatenate([to_lower(out0[0:1, :HALF]), pad], axis=1)], axis=0)
    upper = jnp.concatenate([to_upper(out1), out1[0:1]], axis=0)
    block_out = jnp.where(first, lower, upper)
    c15.done = (block_out,)
    c15.stop = 2
    c15.backward((4, 3))
    begin = c15.back_got
    c15.backward((2,))
    always = own[0] > 0

    half0 = c15.half(0, first, begin, c15.du)
    sum0 = lax.psum(half0, "dp")

    def middle(half0):
        upper, lower = c15.fork(), c14.fork()
        upper.resume(2)
        upper.done += (half0,)
        back, dx1 = upper.backward((1, 0))
        lower.tail_backward(cotangent, far_cot0, back)
        lower.done = upper.done
        lower.backward((4,))
        begin1 = lower.back_got
        lower.backward((3,))
        half1 = upper.half(1, first, begin1, lower.du)
        begin2 = lower.back_got
        lower.stop = 2
        lower.backward((2,))
        half2 = lower.half(0, first, begin2, lower.du)
        return dx1, jnp.concatenate([half1, half2], axis=0), lower.state()

    dx1, half12, state = fenced(always, middle, half0)
    sum0, half12 = lax.optimization_barrier((sum0, half12))
    sum12 = lax.psum(half12, "dp")

    def ending(half12):
        last = c14.fork(state)
        last.resume(2)
        last.done += (half12,)
        came0 = to_upper(sum0)
        dx0, = last.backward((1, 0))
        half3 = last.half(1, first)
        reduction = Reduction(half3, deep)
        reduction.step()
        lower = jnp.concatenate([dx0, to_lower(dx0[0:1])], axis=0)
        joins = jnp.concatenate([to_upper(dx1), dx1[0:1]], axis=0)
        joins = jnp.stack([lax.dynamic_index_in_dim(joins, jnp.argmax(picks == s), 0, False) for s in range(MB)])
        upper = jnp.concatenate([jnp.zeros_like(joins), joins], axis=1)
        dx = jnp.where(first, lower, upper)
        reduction.x, dx, came0 = lax.optimization_barrier((reduction.x, dx, came0))
        return dx, came0, reduction.finish()

    dx, came0, sum3 = fenced(always, ending, half12)
    sum12, sum3 = lax.optimization_barrier((sum12, sum3))
    sum1, sum2 = sum12[: PIECE_ROWS[1]], sum12[PIECE_ROWS[1] :]
    came1, came2, came3 = to_upper(sum1), to_lower(sum2), to_lower(sum3)

    lead = 3 * C // 2

    def joined(near, far):
        pair = [x.reshape(-1, 1, C // 2, C) for x in (near, far)]
        both = jnp.where(first, jnp.concatenate(pair, axis=1), jnp.concatenate(pair[::-1], axis=1))
        return both.reshape(-1, C, C)

    choose_mine = lambda a, b: jnp.where(first, a, b)
    rest_part = joined(choose_mine(sum3[:lead], sum1[:lead]), choose_mine(came3[:lead], came1[:lead]))
    lead_part = joined(choose_mine(sum2[:C], sum0[:C]), choose_mine(came2[:C], came0[:C]))
    pw_grad = jnp.concatenate([rest_part, lead_part], axis=0)[None]
    res_grad = joined(choose_mine(sum2[C:], sum0[C:]), choose_mine(came2[C:], came0[C:]))
    near, far = choose_mine(sum3[lead:], sum1[lead:]), choose_mine(came3[lead:], came1[lead:])
    rows = jnp.where(first, jnp.concatenate([near, far], axis=0), jnp.concatenate([far, near], axis=0))
    dw_grad = rows[TAIL_ROWS : TAIL_ROWS + 40].reshape(1, 5, 8, C)
    norms = jnp.concatenate([dw_grad[0, 1:, TAPS : TAPS + 2], rows[None, 2 * SE + 2 : 2 * SE + 4], rows[None, 2 * SE + 4 : 2 * SE + 6]], axis=0)
    return (
        block_out.reshape(features.shape), dx.reshape(features.shape), dw_grad[:, :, :TAPS], pw_grad,
        norms[None, :, 1], norms[None, :, 0], res_grad, rows[SE : 2 * SE].T[None], rows[2 * SE + 1 : 2 * SE + 2, :SE],
        rows[:SE][None], rows[2 * SE : 2 * SE + 1],
    )


def solution(mesh):
    rows = P("section", "dp", None)
    own = lambda dims: P("section", *([None] * dims))
    weights = (own(3), own(3), own(2), own(2), own(2), own(2), own(1), own(2), own(1))
    in_specs = (rows, rows, rows, P("dp", None), *weights)
    out_specs = (rows, rows, *weights)
    return jax.shard_map(per_device, mesh=mesh, in_specs=in_specs, out_specs=out_specs, check_vma=False)
```

```python
import copy

import jax
import jax.numpy as jnp
from jax import lax
from jax.experimental import pallas as pl
from jax.experimental.pallas import tpu as pltpu
from jax.sharding import PartitionSpec as P

EPSILON = 1e-05
EXACT = lax.Precision.HIGHEST
TAPS = 5
MB = 3
OWN = 2
SLOT = 400
HALF = 200
KEPT = 208
C = 512
LANES = 128
CHUNKS = [slice(c, c + LANES) for c in range(0, C, LANES)]
SE = 64
BF16, F32 = jnp.bfloat16, jnp.float32
VMEM_BYTES = 60 << 20
TAIL_ROWS = 2 * SE + 8
SMALL = 256


def radices(size, most):
    stages, left = [], size
    while left > 1:
        radix = min(most, left)
        while left % radix:
            radix -= 1
        stages.append(radix)
        left //= radix
    return stages


def exchange(block, radix, stride):
    size = lax.axis_size("dp")
    if radix == size:
        return lax.all_to_all(block, "dp", 0, 0)
    groups = []
    for base in range(size):
        if (base // stride) % radix == 0:
            groups.append([base + j * stride for j in range(radix)])
    return lax.all_to_all(block, "dp", 0, 0, axis_index_groups=groups)


def shared(block, stages):
    stride = 1
    for no, radix in enumerate(stages):
        if no:
            block = jnp.broadcast_to(jnp.sum(block, axis=0), (radix,) + block.shape[1:])
        block = exchange(block, radix, stride)
        stride *= radix
    return block


def halves(x):
    high = x.astype(BF16)
    return high, (x - high.astype(F32)).astype(BF16)


def sigmoid(x):
    return 0.5 * jnp.tanh(0.5 * x) + 0.5


def exact_dot(a, b, dims=((1,), (0,))):
    return lax.dot_general(a, b, (dims, ((), ())), precision=EXACT, preferred_element_type=F32)


def fast_dot(a, b, dims=((1,), (0,))):
    return lax.dot_general(a, b, (dims, ((), ())), preferred_element_type=F32)


def stacked_dot(high, low, w, back=False):
    w_high, w_low = w[0], w[1]
    w = jnp.concatenate([w_high, w_high, w_low], axis=1 if back else 0)
    x = jnp.concatenate([high, low, high], axis=1)
    return fast_dot(x, w, ((1,), (1 if back else 0,)))


def stacked_outer(a_high, a_low, b_high, b_low):
    a = jnp.concatenate([a_high, a_low, a_high], axis=0)
    b = jnp.concatenate([b_high, b_high, b_low], axis=0)
    return fast_dot(a, b, ((0,), (0,)))


def column_sum(x):
    return jnp.sum(x, axis=0, keepdims=True)


class Rows:
    def __init__(self, meta, m, two, rows, which=0):
        place = lax.broadcasted_iota(jnp.int32, (rows, LANES), 0)
        if two:
            later = place >= HALF
            limit = jnp.where(later, HALF + meta[OWN + m], meta[m])
            self.mask = place < limit
        else:
            self.mask = place < meta[which * OWN + m]

    def keep(self, x):
        return jnp.where(self.mask, x, 0.0)


class Padded:
    def __init__(self, ref, two):
        self.ref = ref
        self.pieces = [(8, 0, HALF), (16 + HALF, HALF, HALF)] if two else [(8, 0, SLOT)]

    def put(self, x):
        zeros = jnp.zeros((8, LANES), F32)
        for at, start, rows in self.pieces:
            self.ref[at - 8 : at, :] = zeros
            self.ref[at : at + rows, :] = x[start : start + rows]
        self.ref[at + rows : at + rows + 8, :] = zeros

    def get(self, offset):
        parts = [self.ref[at + offset : at + offset + rows, :] for at, _, rows in self.pieces]
        return parts[0] if len(parts) == 1 else jnp.concatenate(parts, axis=0)

    def conv(self, kernel):
        total = kernel[0:1] * self.get(-2)
        for k in range(1, TAPS):
            total = total + kernel[k : k + 1] * self.get(k - 2)
        return total

    def conv_back(self, kernel):
        total = kernel[0:1] * self.get(2)
        for k in range(1, TAPS):
            total = total + kernel[k : k + 1] * self.get(2 - k)
        return total


def every_other(ref, x):
    ref[0:SLOT, :] = x
    ref[SLOT : 2 * KEPT, :] = jnp.zeros((2 * KEPT - SLOT, LANES), F32)
    return ref[pl.ds(0, KEPT, stride=2), :]


def spread_out(ref, x):
    ref[...] = jnp.zeros_like(ref)
    ref[pl.ds(0, KEPT, stride=2), :] = x
    return ref[0:SLOT, :]


def center_spread(sums, rows):
    center = sums[0:1] / rows
    return center, lax.rsqrt(sums[1:2] / rows - center * center + EPSILON)


def added(ref):
    return jnp.sum(ref[:, 0], axis=0)


def accumulate(ref, m, at, value):
    rows = slice(at, at + value.shape[0])
    ref[rows, :] = jnp.where(m == 0, value, ref[rows, :] + value)


def send(ref, rows):
    for copy in range(ref.shape[0]):
        for row, x in enumerate(rows):
            ref[copy, 0, row : row + 1, 0 : x.shape[1]] = x


def pad_scratch():
    return pltpu.VMEM((len(CHUNKS), SLOT + 24, LANES), F32)


def stride_scratch():
    return pltpu.VMEM((len(CHUNKS), 2 * KEPT, LANES), F32)


def slots(rows, cols=C):
    return pl.BlockSpec((1, rows, cols), lambda m, *_: (m, 0, 0))


def copies(count, rows, cols=C):
    return pl.BlockSpec((count, 1, rows, cols), lambda m, *_: (0, m, 0, 0))


def whole(*shape):
    return pl.BlockSpec(shape, lambda m, *_: (0,) * len(shape))


def layer(i, *shape):
    return pl.BlockSpec((1,) + shape, lambda m, *_: (i,) + (0,) * len(shape))


def f32(*shape):
    return jax.ShapeDtypeStruct(shape, F32)


def bf16(*shape):
    return jax.ShapeDtypeStruct(shape, BF16)


def call(body, meta, args, outs, scratch=(), name=None, flops=0, steps=OWN, after=(), into=()):
    arrays, in_specs = [a for a, _ in args], [s for _, s in args]
    shapes, out_specs = [a for a, _ in outs], [s for _, s in outs]
    size = sum(a.size * a.dtype.itemsize for a in arrays + shapes)
    extra = list(after) + list(into)
    count = len(arrays)

    def inner(meta, *refs):
        body(meta, *refs[:count], *refs[count + len(extra) :])

    return pl.pallas_call(
        inner,
        out_shape=shapes,
        grid_spec=pltpu.PrefetchScalarGridSpec(
            num_scalar_prefetch=1,
            grid=(steps,),
            in_specs=in_specs + [pl.BlockSpec(memory_space=pl.ANY)] * len(extra),
            out_specs=out_specs,
            scratch_shapes=list(scratch),
        ),
        input_output_aliases={1 + count + len(after) + j: j for j in range(len(into))},
        compiler_params=pltpu.CompilerParams(vmem_limit_bytes=VMEM_BYTES),
        cost_estimate=pl.CostEstimate(flops=flops, bytes_accessed=size, transcendentals=0),
        name=name,
    )(meta, *arrays, *extra)


def choose(meta, block, own, far):
    return jnp.where(meta[2 * OWN] == 1 - block, own, far)


def prepare(meta, own, far, block, start, stop):
    def body(meta, *refs):
        pair = [ref[0] for ref in refs[:2]]
        if stop == 6:
            last = pl.program_id(0) == 5 - start
            pair = [jnp.where(last, ref[...], w) for ref, w in zip(refs[2:4], pair)]
        out = refs[-1]
        out[0, 0], out[0, 1] = halves(choose(meta, block, *pair))

    matrix = pl.BlockSpec((1, C, C), lambda j, *_: (jnp.minimum(j + start, 4), 0, 0))
    args = [(own[0], matrix), (far[0], matrix)]
    if stop == 6:
        args += [(own[1], whole(C, C)), (far[1], whole(C, C))]
    out = pl.BlockSpec((1, 2, C, C), lambda j, *_: (j, 0, 0, 0))
    name = f"prepare_{block}_{start}"
    return call(body, meta, args, [(bf16(stop - start, 2, C, C), out)], name=name, steps=stop - start)[0]


class Block:
    def __init__(self, two, meta, weights, ready, stages):
        self.done, self.stop, self.pending = (), None, None
        self.two, self.meta, self.stages = two, meta, stages
        self.dw, self.gain, self.bias, self.down, self.down_b, self.up, self.up_b = weights
        self.ready = ready
        self.tail_rows = SLOT if two else KEPT
        self.first, self.last = stages[0], stages[-1]
        self.tag = "c15" if two else "c14"

    def rows_of(self, i):
        return self.tail_rows if i == 4 else SLOT

    def valid(self, meta, m, i):
        last = i == 4 and not self.two
        return Rows(meta, m, self.two, self.rows_of(i), which=1 if last else 0)

    def matrix(self, i):
        array, at = self.ready[i]
        return (array, layer(at, 2, C, C))

    def source_args(self):
        if not self.two:
            return [(self.x, slots(SLOT)), (self.x_far, whole(SLOT, C))]
        far = pl.BlockSpec((HALF, C), lambda m, *_: (m, 0))
        near = pl.BlockSpec((1, 1, HALF, C), lambda m, meta: (meta[2 * OWN + 1], 1, 0, 0))
        return [(self.arrived, slots(HALF)), (self.joined_far, far), (self.joined, near)]

    def source(self, meta, refs, cs):
        lower = meta[2 * OWN] == 1
        if not self.two:
            return jnp.where(lower, refs[0][0, :, cs], refs[1][:, cs])
        joined = jnp.where(lower, refs[1][:, cs], refs[2][0, 0, :, cs])
        return jnp.concatenate([refs[0][0, :, cs], joined], axis=0)

    def before_args(self, i):
        if i == 0:
            return self.source_args()
        return [(self.z[i - 1], slots(SLOT)), (self.stats[i - 1], slots(2))]


    def forward_layer(self, i, after=()):
        two, count = self.two, self.first
        strided = i == 4 and not two
        rows = self.rows_of(i)
        n_src = len(self.source_args())
        width = C + LANES if i == 0 else C
        sent = 4 if i == 3 else 2
        makes = i == 0 and not two

        def body(meta, *refs):
            refs = list(refs)
            take = lambda n: [refs.pop(0) for _ in range(n)]
            m = pl.program_id(0)
            if i == 0:
                src = take(n_src)
            else:
                z_ref, got_ref = take(2)
                n_ref, = take(1) if i > 1 else (None,)
                gain_ref, bias_ref = take(2)
                res_sum, = take(1) if i == 3 else (None,)
            dw_ref, = take(1)
            if makes:
                own_ref, far_ref, z_out, pay, w_ref = take(5)

                @pl.when(m == 0)
                def _():
                    w_ref[0, 0], w_ref[0, 1] = halves(choose(meta, 0, own_ref[0], far_ref[0]))

            else:
                w_ref, z_out, pay = take(3)
            if i:
                stat_out, = take(1)
            if i == 1:
                n_out, = take(1)
            pad, y_ref = take(2)
            alt, = take(1) if strided else (None,)
            valid_in = self.valid(meta, m, 0)
            if i:
                sums = added(got_ref)
                if i == 1:
                    count_in = jnp.maximum(jnp.concatenate([sums[0:1, C:]] * len(CHUNKS), axis=1), 1.0)
                    count_out = jnp.maximum(jnp.concatenate([sums[1:2, C:]] * len(CHUNKS), axis=1), 1.0)
                    n_out[0, 0:1, :] = count_in
                    n_out[0, 1:2, :] = count_out
                else:
                    count_in = n_ref[0, 0:1, :]
                center, spread = center_spread(sums[:, :C], count_in)
                stat_out[0, 0:1, :] = center
                stat_out[0, 1:2, :] = spread
                scale = gain_ref[i - 1 : i] * spread
                shift = bias_ref[i - 1 : i] - center * scale
            for c, cs in enumerate(CHUNKS):
                if i == 0:
                    h = valid_in.keep(self.source(meta, src, cs))
                else:
                    u = z_ref[0, :, cs] * scale[:, cs] + shift[:, cs]
                    h = valid_in.keep(u * sigmoid(u))
                padded = Padded(pad.at[c], two)
                padded.put(h)
                y = padded.conv(dw_ref[0, :, cs])
                if strided:
                    y = every_other(alt.at[c], y)
                high, low = halves(y)
                y_ref[:, cs] = high
                y_ref[:, C + cs.start : C + cs.stop] = low
            w = w_ref.at[0] if makes else w_ref.at[0]
            z = stacked_dot(y_ref[:, 0:C], y_ref[:, C : 2 * C], w)
            z_out[0] = z
            valid = self.valid(meta, m, i)
            one, square = [], []
            for cs in CHUNKS:
                kept = valid.keep(z[:, cs])
                one.append(column_sum(kept))
                square.append(column_sum(kept * kept))
            if i == 0:
                if two:
                    number = (meta[m] + meta[OWN + m]).astype(F32)
                    numbers = number, number
                else:
                    numbers = meta[m].astype(F32), meta[OWN + m].astype(F32)
                one.append(jnp.full((1, LANES), numbers[0], F32))
                square.append(jnp.full((1, LANES), numbers[1], F32))
            out = [jnp.concatenate(one, axis=1), jnp.concatenate(square, axis=1)]
            if i == 3:
                out += [res_sum[0, 0:1, :], res_sum[0, 1:2, :]]
            send(pay, out)

        if i == 0:
            args = list(self.source_args())
        else:
            got = 4 if i == 4 else 2
            args = [(self.z[i - 1], slots(SLOT)), (self.got[i - 1], copies(self.last, got, C + LANES if i == 1 else C))]
            if i > 1:
                args.append((self.number, slots(2)))
            args += [(self.gain, whole(6, C)), (self.bias, whole(6, C))]
            if i == 3:
                args.append((self.res_sum, slots(2)))
        args.append((self.dw, layer(i, TAPS, C)))
        args += [(w, layer(0, C, C)) for w in self.first_matrix] if makes else [self.matrix(i)]
        outs = [(f32(OWN, rows, C), slots(rows)), (f32(count, OWN, sent, width), copies(count, sent, width))]
        if i:
            outs.append((f32(OWN, 2, C), slots(2)))
        if i == 1:
            outs.append((f32(OWN, 2, C), slots(2)))
        if makes:
            outs.append((bf16(1, 2, C, C), layer(0, 2, C, C)))
        scratch = [pad_scratch(), pltpu.VMEM((rows, 2 * C), BF16)]
        if strided:
            scratch.append(stride_scratch())
        result = call(body, self.meta, args, outs, scratch, f"{self.tag}_forward_{i}", 6 * OWN * rows * C * C, after=after)
        self.z.append(result[0])
        if makes:
            self.ready[0] = (result[2], 0)
        if i:
            self.stats.append(result[2])
        if i == 1:
            self.number = result[3]
        self.got.append(shared(result[1], self.stages))

    def residual(self):
        two, rows = self.two, self.tail_rows

        def body(meta, *refs):
            refs = list(refs)
            src = [refs.pop(0) for _ in self.source_args()]
            w_ref, r_out, x_out, sum_out = refs[:4]
            alt = refs[4] if not two else None
            m = pl.program_id(0)
            valid_in = self.valid(meta, m, 0)
            for c, cs in enumerate(CHUNKS):
                x = valid_in.keep(self.source(meta, src, cs))
                if not two:
                    x = every_other(alt.at[c], x)
                high, low = halves(x)
                x_out[0, :, cs] = high
                x_out[0, :, C + cs.start : C + cs.stop] = low
            r = stacked_dot(x_out[0, :, 0:C], x_out[0, :, C : 2 * C], w_ref.at[0])
            r_out[0] = r
            valid = self.valid(meta, m, 4)
            for cs in CHUNKS:
                kept = valid.keep(r[:, cs])
                sum_out[0, 0:1, cs] = column_sum(kept)
                sum_out[0, 1:2, cs] = column_sum(kept * kept)

        args = self.source_args() + [self.matrix(5)]
        outs = [
            (f32(OWN, rows, C), slots(rows)),
            (bf16(OWN, rows, 2 * C), slots(rows, 2 * C)),
            (f32(OWN, 2, C), slots(2)),
        ]
        scratch = [] if two else [stride_scratch()]
        self.r, self.picked, self.res_sum = call(
            body, self.meta, args, outs, scratch, f"{self.tag}_residual", 6 * OWN * rows * C * C
        )

    def forward(self, after=None):
        self.z, self.got, self.stats = [], [], []
        for i in range(5):
            if i == 2:
                self.residual()
            self.forward_layer(i, (after or {}).get(i, ()))


    def segments(self):
        return [(0, HALF), (HALF, HALF)] if self.two else [(0, self.tail_rows)]

    def lengths(self, meta, m):
        if self.two:
            return [meta[m], meta[OWN + m]]
        return [meta[OWN + m]]

    def squeeze(self, sums, counts, se_refs):
        down_t, down_b, up, up_b = se_refs
        means = [s / jnp.maximum(jnp.full((1, C), n.astype(F32)), 1.0) for s, n in zip(sums, counts)]
        ps = [jnp.sum(down_t[...] * mean, axis=1, keepdims=True) + down_b[...] for mean in means]
        gates = [sigmoid(column_sum(up[...] * (p * sigmoid(p))) + up_b[...]) for p in ps]
        return means, ps, gates

    def squeeze_back(self, des, ps, gates, counts, se_refs, means, small, m):
        down_t, down_b, up, up_b = se_refs
        shares, up_grad, down_grad, dq_sum, dp_sum = [], 0.0, 0.0, 0.0, 0.0
        for de, p, gate, n, mean in zip(des, ps, gates, counts, means):
            dq = de * gate * (1.0 - gate)
            s = sigmoid(p)
            dp = jnp.sum(up[...] * dq, axis=1, keepdims=True) * (s * (1.0 + p * (1.0 - s)))
            shares.append(column_sum(down_t[...] * dp) / jnp.maximum(jnp.full((1, C), n.astype(F32)), 1.0))
            up_grad, down_grad = up_grad + (p * s) * dq, down_grad + dp * mean
            dq_sum, dp_sum = dq_sum + dq, dp_sum + dp
        row, col = (lax.broadcasted_iota(jnp.int32, (SE, C), axis) for axis in (0, 1))
        dp_row = column_sum(jnp.where(row == col, dp_sum, 0.0))
        accumulate(small, m, 0, up_grad)
        accumulate(small, m, SE, down_grad)
        accumulate(small, m, 2 * SE, dq_sum)
        accumulate(small, m, 2 * SE + 1, dp_row)
        return shares

    def last_norm(self, m, dt_out, du_out, z_ref, slope_ref, gates, shares, center, spread, res_bias, res_gain, pay, small):
        bias_sum, gain_sum = [], []
        for cs in CHUNKS:
            dh = dt_out[0, :, cs] * self.by_segment(gates, cs) + self.by_segment(shares, cs)
            du = dh * slope_ref[:, cs]
            du_out[0, :, cs] = du
            bias_sum.append(column_sum(du))
            gain_sum.append(column_sum(du * ((z_ref[0, :, cs] - center[:, cs]) * spread[:, cs])))
        rows = [jnp.concatenate(x, axis=1) for x in (bias_sum, gain_sum, res_bias, res_gain)]
        send(pay, rows)
        for j, row in enumerate(rows):
            accumulate(small, m, 2 * SE + 2 + j, row)

    def se_args(self):
        return [(self.down, whole(SE, C)), (self.down_b, whole(SE, 1)), (self.up, whole(SE, C)), (self.up_b, whole(1, C))]

    def store_rows(self, ref, rows):
        ref[0] = jnp.concatenate(rows + [jnp.zeros((8 - len(rows), C), F32)], axis=0)

    def store_columns(self, ref, columns):
        ref[0] = jnp.zeros((SE, 8), F32)
        for j, column in enumerate(columns):
            ref[0, :, j : j + 1] = column

    def by_segment(self, rows, cs):
        parts = [jnp.broadcast_to(row[:, cs], (n, LANES)) for row, (_, n) in zip(rows, self.segments())]
        return parts[0] if len(parts) == 1 else jnp.concatenate(parts, axis=0)

    def seg_sums(self, x):
        return [column_sum(x[at : at + n]) for at, n in self.segments()]

    def tail(self, cotangent=None, far=None, after=()):
        two, rows = self.two, self.tail_rows
        back = cotangent is not None

        def body(meta, *refs):
            refs = list(refs)
            take = lambda n: [refs.pop(0) for _ in range(n)]
            m = pl.program_id(0)
            z_ref, got4, r_ref, got3, n_ref, gain, bias = take(7)
            se_refs = take(4)
            if back:
                cot_ref, far_ref = take(2)
            out, stat_out, rstat_out, means_out, p_out, gate_out = take(6)
            if back:
                small, du_out, dt_out, pay = take(4)
            h_ref, = take(1)
            if back:
                slope_ref, = take(1)
            valid = self.valid(meta, m, 4)
            number = n_ref[0, 1:2, :]
            center, spread = center_spread(added(got4), number)
            rcenter, rspread = center_spread(added(got3)[2:4], number)
            stat_out[0, 0:1, :] = center
            stat_out[0, 1:2, :] = spread
            rstat_out[0, 0:1, :] = rcenter
            rstat_out[0, 1:2, :] = rspread
            scale = gain[4:5] * spread
            shift = bias[4:5] - center * scale
            sums = []
            for cs in CHUNKS:
                u = z_ref[0, :, cs] * scale[:, cs] + shift[:, cs]
                s = sigmoid(u)
                h = valid.keep(u * s)
                h_ref[:, cs] = h
                if back:
                    slope_ref[:, cs] = valid.keep(s * (1.0 + u * (1.0 - s)))
                sums.append(self.seg_sums(h))
            sums = [jnp.concatenate([s[j] for s in sums], axis=1) for j in range(len(self.segments()))]
            counts = self.lengths(meta, m)
            means, ps, gates = self.squeeze(sums, counts, se_refs)
            self.store_rows(means_out, means)
            self.store_columns(p_out, ps)
            self.store_rows(gate_out, gates)
            res_gain, res_bias, gate_grad = [], [], []
            for cs in CHUNKS:
                h = h_ref[:, cs]
                rh = (r_ref[0, :, cs] - rcenter[:, cs]) * rspread[:, cs]
                t = h * self.by_segment(gates, cs) + gain[5:6, cs] * rh + bias[5:6, cs]
                s = sigmoid(t)
                out[0, 0:rows, cs] = valid.keep(t * s)
                if rows < SLOT:
                    out[0, rows:SLOT, cs] = jnp.zeros((SLOT - rows, LANES), F32)
                if back:
                    cot = jnp.where(meta[2 * OWN] == 1, far_ref[0, :, cs], cot_ref[0, :, cs])
                    dt = valid.keep(cot * (s * (1.0 + t * (1.0 - s))))
                    dt_out[0, :, cs] = dt
                    res_bias.append(column_sum(dt))
                    res_gain.append(column_sum(dt * rh))
                    gate_grad.append(self.seg_sums(dt * h))
            if not back:
                return
            des = [jnp.concatenate([g[j] for g in gate_grad], axis=1) for j in range(len(counts))]
            shares = self.squeeze_back(des, ps, gates, counts, se_refs, means, small, m)
            self.last_norm(m, dt_out, du_out, z_ref, slope_ref, gates, shares, center, spread, res_bias, res_gain, pay, small)

        args = [
            (self.z[4], slots(rows)), (self.got[4], copies(self.last, 2)), (self.r, slots(rows)),
            (self.got[3], copies(self.last, 4)), (self.number, slots(2)),
            (self.gain, whole(6, C)), (self.bias, whole(6, C)),
        ] + self.se_args()
        outs = [
            (f32(OWN, SLOT, C), slots(SLOT)), (f32(OWN, 2, C), slots(2)), (f32(OWN, 2, C), slots(2)),
            (f32(OWN, 8, C), slots(8)), (f32(OWN, SE, 8), slots(SE, 8)), (f32(OWN, 8, C), slots(8)),
        ]
        scratch = [pltpu.VMEM((rows, C), F32)]
        if back:
            args += [(cotangent, layer(MB - 1, SLOT, C)), (far, slots(SLOT))]
            outs += self.tail_outs()
            scratch.append(pltpu.VMEM((rows, C), F32))
        result = call(body, self.meta, args, outs, scratch, f"{self.tag}_tail", after=after)
        self.stats.append(result[1])
        self.rstat, self.se_state = result[2], result[3:6]
        if back:
            self.tail_results(result[6:])
        return result[0]

    def tail_outs(self):
        rows, count = self.tail_rows, self.first
        return [
            (f32(SMALL, C), whole(TAIL_ROWS, C)), (f32(OWN, rows, C), slots(rows)), (f32(OWN, rows, C), slots(rows)),
            (f32(count, OWN, 4, C), copies(count, 4)),
        ]

    def tail_results(self, result):
        self.small, self.du, self.dt, pay = result
        self.back_got = shared(pay, self.stages)

    def tail_backward(self, cotangent, far, back):
        rows = self.tail_rows

        def body(meta, z_ref, r_ref, stat, rstat, gain, bias, means_ref, p_ref, gate_ref, down, down_b, up, up_b, cot_ref, far_ref, back_ref,
                 small, du_out, dt_out, pay, slope_ref):
            m = pl.program_id(0)
            valid = self.valid(meta, m, 4)
            center, spread, rcenter, rspread = stat[0, 0:1], stat[0, 1:2], rstat[0, 0:1], rstat[0, 1:2]
            scale = gain[4:5] * spread
            shift = bias[4:5] - center * scale
            zeros = jnp.zeros((rows - HALF, LANES), F32)
            counts = self.lengths(meta, m)
            ps = [p_ref[0, :, j : j + 1] for j in range(len(counts))]
            gates = [gate_ref[0, j : j + 1, :] for j in range(len(counts))]
            means = [means_ref[0, j : j + 1, :] for j in range(len(counts))]
            res_gain, res_bias, gate_grad = [], [], []
            for cs in CHUNKS:
                u = z_ref[0, :, cs] * scale[:, cs] + shift[:, cs]
                s = sigmoid(u)
                h = valid.keep(u * s)
                slope_ref[:, cs] = valid.keep(s * (1.0 + u * (1.0 - s)))
                rh = (r_ref[0, :, cs] - rcenter[:, cs]) * rspread[:, cs]
                t = h * self.by_segment(gates, cs) + gain[5:6, cs] * rh + bias[5:6, cs]
                s = sigmoid(t)
                here = jnp.where(meta[2 * OWN] == 1, cot_ref[0, 0:HALF, cs], far_ref[0, :, cs])
                cot = jnp.concatenate([here + back_ref[0, :, cs], zeros], axis=0)
                dt = valid.keep(cot * (s * (1.0 + t * (1.0 - s))))
                dt_out[0, :, cs] = dt
                res_bias.append(column_sum(dt))
                res_gain.append(column_sum(dt * rh))
                gate_grad.append(self.seg_sums(dt * h))
            des = [jnp.concatenate([g[j] for g in gate_grad], axis=1) for j in range(len(counts))]
            shares = self.squeeze_back(des, ps, gates, counts, (down, down_b, up, up_b), means, small, m)
            self.last_norm(m, dt_out, du_out, z_ref, slope_ref, gates, shares, center, spread, res_bias, res_gain, pay, small)

        args = [
            (self.z[4], slots(rows)), (self.r, slots(rows)), (self.stats[4], slots(2)), (self.rstat, slots(2)),
            (self.gain, whole(6, C)), (self.bias, whole(6, C)),
            (self.se_state[0], slots(8)), (self.se_state[1], slots(SE, 8)), (self.se_state[2], slots(8)),
        ] + self.se_args() + [(cotangent, slots(HALF)), (far, layer(MB - 1, HALF, C)), (back, slots(HALF))]
        scratch = [pltpu.VMEM((rows, C), F32)]
        self.tail_results(call(body, self.meta, args, self.tail_outs(), scratch, f"{self.tag}_tail_back"))


    def norm_grad(self, du, zh, scale, sums, number, cs):
        return scale[:, cs] * (du - sums[0:1, cs] / number[:, cs] - zh * (sums[1:2, cs] / number[:, cs]))

    def backward_layer(self, i):
        two, count = self.two, self.first
        strided = i == 4 and not two
        rows = self.rows_of(i)
        n_src = len(self.source_args())

        def body(meta, *refs):
            refs = list(refs)
            take = lambda n: [refs.pop(0) for _ in range(n)]
            m = pl.program_id(0)
            du_ref, z_ref, w_ref, got, n_ref, stat, gain, bias, dw_ref = take(9)
            if i:
                zp_ref, statp = take(2)
            else:
                dxr_ref, = take(1)
                src = take(n_src)
            small, dz_out = take(2)
            if i:
                du_out, pay = take(2)
            elif two:
                back_out, dx_out = take(2)
            else:
                dx_out, = take(1)
            pad, = take(1)
            alt, = take(1) if refs else (None,)
            sums = added(got)
            number = n_ref[0, 1:2, :] if i == 4 else n_ref[0, 0:1, :]
            center, spread = stat[0, 0:1], stat[0, 1:2]
            scale = gain[i : i + 1] * spread
            valid = self.valid(meta, m, i)
            for cs in CHUNKS:
                zh = (z_ref[0, :, cs] - center[:, cs]) * spread[:, cs]
                dz = valid.keep(self.norm_grad(du_ref[0, :, cs], zh, scale, sums, number, cs))
                high, low = halves(dz)
                dz_out[0, :, cs] = high
                dz_out[0, :, C + cs.start : C + cs.stop] = low
            dy = stacked_dot(dz_out[0, :, 0:C], dz_out[0, :, C : 2 * C], w_ref.at[0], True)
            valid_in = self.valid(meta, m, 0)
            if i:
                pcenter, pspread = statp[0, 0:1], statp[0, 1:2]
                pscale = gain[i - 1 : i] * pspread
                pshift = bias[i - 1 : i] - pcenter * pscale
            taps, bias_sum, gain_sum = [[] for _ in range(TAPS)], [], []
            for c, cs in enumerate(CHUNKS):
                grad = dy[:, cs]
                if strided:
                    grad = spread_out(alt.at[c], grad)
                padded = Padded(pad.at[c], two)
                padded.put(grad)
                if i:
                    z = zp_ref[0, :, cs]
                    u = z * pscale[:, cs] + pshift[:, cs]
                    s = sigmoid(u)
                    h = valid_in.keep(u * s)
                else:
                    h = valid_in.keep(self.source(meta, src, cs))
                dh = None
                for k in range(TAPS):
                    moved = padded.get(2 - k)
                    taps[k].append(column_sum(h * moved))
                    term = dw_ref[0, k : k + 1, cs] * moved
                    dh = term if dh is None else dh + term
                if i:
                    du = valid_in.keep(dh * (s * (1.0 + u * (1.0 - s))))
                    du_out[0, :, cs] = du
                    bias_sum.append(column_sum(du))
                    gain_sum.append(column_sum(du * ((z - pcenter[:, cs]) * pspread[:, cs])))
                    continue
                dxr = dxr_ref[0, :, cs]
                if not two:
                    dxr = spread_out(alt.at[c], dxr)
                dx = valid_in.keep(dh) + dxr
                if two:
                    back_out[0, :, cs] = dx[:HALF]
                    dx = dx[HALF:]
                dx_out[0, :, cs] = dx
            rows = taps + [bias_sum, gain_sum] if i else taps
            rows = [jnp.concatenate(x, axis=1) for x in rows]
            for j, row in enumerate(rows):
                accumulate(small, m, j, row)
            if i:
                send(pay, rows[TAPS:])

        sent = 4 if i == 4 else 2
        args = [
            (self.du, slots(rows)), (self.z[i], slots(rows)), self.matrix(i), (self.back_got, copies(self.last, sent)),
            (self.number, slots(2)), (self.stats[i], slots(2)), (self.gain, whole(6, C)), (self.bias, whole(6, C)),
            (self.dw, layer(i, TAPS, C)),
        ]
        if not i:
            args.append((self.dxr, slots(self.tail_rows)))
        args += self.before_args(i)
        place = TAIL_ROWS // 8 + i
        outs = [(f32(SMALL, C), pl.BlockSpec((8, C), lambda m, *_: (place, 0))), (bf16(OWN, rows, 2 * C), slots(rows, 2 * C))]
        if i:
            outs += [(f32(OWN, SLOT, C), slots(SLOT)), (f32(count, OWN, 2, C), copies(count, 2))]
        elif two:
            outs += [(f32(OWN, HALF, C), slots(HALF)), (f32(OWN, HALF, C), slots(HALF))]
        else:
            outs += [(f32(OWN, SLOT, C), slots(SLOT))]
        scratch = [pad_scratch()]
        if strided or (i == 0 and not two):
            scratch.append(stride_scratch())
        self.small, dz, *result = call(
            body, self.meta, args, outs, scratch, f"{self.tag}_backward_{i}", 6 * OWN * rows * C * C,
            after=self.done, into=(self.small,),
        )
        got = self.back_got
        if i:
            self.du = result[0]
            if i == self.stop:
                self.pending = dz, result[1]
                return result
            self.back_got = shared(result[1], self.stages)
        self.weight_grad(i, dz)
        if i == 4:
            self.residual_back(got)
        return result

    def residual_back(self, got):
        rows = self.tail_rows

        def body(meta, got, n_ref, dt_ref, r_ref, rstat, gain, w_ref, x_ref, kept_out, away_out, dxr_out, dr, total):
            m = pl.program_id(0)
            sums = added(got)[2:4]
            number = n_ref[0, 1:2, :]
            center, spread = rstat[0, 0:1], rstat[0, 1:2]
            scale = gain[5:6] * spread
            valid = self.valid(meta, m, 4)
            for cs in CHUNKS:
                rh = (r_ref[0, :, cs] - center[:, cs]) * spread[:, cs]
                high, low = halves(valid.keep(self.norm_grad(dt_ref[0, :, cs], rh, scale, sums, number, cs)))
                dr[:, cs] = high
                dr[:, C + cs.start : C + cs.stop] = low
            high, low = dr[:, 0:C], dr[:, C : 2 * C]
            dxr_out[0] = stacked_dot(high, low, w_ref.at[0], True)
            grad = stacked_outer(x_ref[0, :, 0:C], x_ref[0, :, C : 2 * C], high, low)
            self.add_halves(meta, m, grad, total, kept_out, away_out)

        args = [
            (got, copies(self.last, 4)), (self.number, slots(2)), (self.dt, slots(rows)), (self.r, slots(rows)),
            (self.rstat, slots(2)), (self.gain, whole(6, C)), self.matrix(5), (self.picked, slots(rows, 2 * C)),
        ]
        outs = self.piece_out(5) + [(f32(OWN, rows, C), slots(rows))]
        which = PLACES[5][0]
        *self.pieces[which], self.dxr = call(
            body, self.meta, args, outs, [pltpu.VMEM((rows, 2 * C), BF16), pltpu.VMEM((C, C), F32)],
            f"{self.tag}_residual_back", 12 * OWN * rows * C * C, into=self.pieces[which],
        )

    def piece_out(self, i):
        which, place = PLACES[i]
        rows = PIECE_ROWS[which]
        return [(f32(rows, C), pl.BlockSpec((C // 2, C), lambda m, *_: (place, 0)))] * 2

    def add_halves(self, meta, m, grad, total, kept_out, away_out):
        @pl.when(m == 0)
        def _():
            total[...] = grad

        @pl.when(m > 0)
        def _():
            top, bottom = total[0 : C // 2] + grad[0 : C // 2], total[C // 2 : C] + grad[C // 2 : C]
            lower = meta[2 * OWN] == 1
            kept_out[...] = jnp.where(lower, top, bottom)
            away_out[...] = jnp.where(lower, bottom, top)

    def weight_grad(self, i, dz):
        two = self.two
        strided = i == 4 and not two
        rows = self.rows_of(i)
        n_src = len(self.source_args())

        def body(meta, *refs):
            refs = list(refs)
            take = lambda n: [refs.pop(0) for _ in range(n)]
            m = pl.program_id(0)
            if i:
                zp_ref, statp, gain, bias = take(4)
                center, spread = statp[0, 0:1], statp[0, 1:2]
                scale = gain[i - 1 : i] * spread
                shift = bias[i - 1 : i] - center * scale
            else:
                src = take(n_src)
            dz_ref, dw_ref, kept_out, away_out, pad, yh, yl, total = take(8)
            alt, = take(1) if strided else (None,)
            valid_in = self.valid(meta, m, 0)
            for c, cs in enumerate(CHUNKS):
                if i:
                    u = zp_ref[0, :, cs] * scale[:, cs] + shift[:, cs]
                    h = valid_in.keep(u * sigmoid(u))
                else:
                    h = valid_in.keep(self.source(meta, src, cs))
                padded = Padded(pad.at[c], two)
                padded.put(h)
                y = padded.conv(dw_ref[0, :, cs])
                if strided:
                    y = every_other(alt.at[c], y)
                yh[:, cs], yl[:, cs] = halves(y)
            grad = stacked_outer(yh[...], yl[...], dz_ref[0, :, 0:C], dz_ref[0, :, C : 2 * C])
            self.add_halves(meta, m, grad, total, kept_out, away_out)

        args = self.before_args(i)
        if i:
            args += [(self.gain, whole(6, C)), (self.bias, whole(6, C))]
        args += [(dz, slots(rows, 2 * C)), (self.dw, layer(i, TAPS, C))]
        scratch = [pad_scratch(), pltpu.VMEM((rows, C), BF16), pltpu.VMEM((rows, C), BF16), pltpu.VMEM((C, C), F32)]
        if strided:
            scratch.append(stride_scratch())
        which = PLACES[i][0]
        self.pieces[which] = call(
            body, self.meta, args, self.piece_out(i), scratch, f"{self.tag}_weights_{i}", 6 * OWN * rows * C * C,
            into=self.pieces[which],
        )
        self.done = (self.pieces[which][0],)

    def backward(self, layers):
        if layers[0] == 4:
            self.pieces = [[], []]
        for i in layers:
            result = self.backward_layer(i)
        return result

    def resume(self, i):
        dz, payload = self.pending
        self.back_got = shared(payload, self.stages)
        self.weight_grad(i, dz)

    def fork(self, state=None):
        other = copy.copy(self)
        other.__dict__.update(state or {})
        if "pieces" in other.__dict__:
            other.pieces = list(other.pieces)
        return other

    def state(self):
        return {name: getattr(self, name) for name in ("du", "dxr", "pieces", "small", "pending")}

    def half(self, no, first, begin=None, end=None):
        kept, away = self.pieces[no]
        if no:
            parts = self.small[: SMALL // 2], self.small[SMALL // 2 :]
            at = kept.shape[0] - SMALL // 2
            kept = lax.dynamic_update_slice_in_dim(kept, jnp.where(first, *parts), at, 0)
            away = lax.dynamic_update_slice_in_dim(away, jnp.where(first, *parts[::-1]), at, 0)
        if begin is not None:
            away, _ = lax.optimization_barrier((away, begin))
            kept, _ = lax.optimization_barrier((kept, end))
        return kept + swap(away)


PLACES = {3: (0, 0), 4: (0, 1), 5: (0, 2), 0: (1, 0), 1: (1, 1), 2: (1, 2)}
PIECE_ROWS = (3 * C // 2, 3 * C // 2 + SMALL // 2)


def pick_joining(picks, features):
    def body(picks, in_ref, out_ref):
        out_ref[...] = in_ref[0, 0]

    own = pl.BlockSpec((1, 1, HALF, C), lambda m, picks: (picks[m], 1, 0, 0))
    out = (f32(OWN * HALF, C), pl.BlockSpec((HALF, C), lambda m, *_: (m, 0)))
    return call(body, picks, [(features, own)], [out], name="pick_joining")[0]


def swap(x):
    return lax.ppermute(x, "section", [(0, 1), (1, 0)])


def fenced(always, work, x):
    shapes = jax.eval_shape(work, x)
    return lax.cond(always, work, lambda x: jax.tree.map(lambda y: jnp.zeros(y.shape, y.dtype), shapes), x)


class Reduction:
    def __init__(self, x, stages):
        self.x = x
        self.todo = []
        stride = 1
        for radix in stages:
            self.todo.append((True, radix, stride))
            stride *= radix
        self.todo += [(False, radix, stride) for _, radix, stride in reversed(self.todo)]

    def step(self):
        scatter, radix, stride = self.todo.pop(0)
        rows = self.x.shape[0]
        if scatter:
            parts = exchange(self.x.reshape(radix, rows // radix, C), radix, stride)
            self.x = jnp.sum(parts, axis=0)
        else:
            parts = exchange(jnp.broadcast_to(self.x, (radix,) + self.x.shape), radix, stride)
            self.x = parts.reshape(radix * rows, C)
        return (self.x,)

    def finish(self):
        while self.todo:
            self.step()
        return self.x


def per_device(features, out_grad, lengths, join_pick, dw, pw, gain, bias, res_w, down, down_b, up, up_b):
    first = lax.axis_index("section") == 0
    size = lax.axis_size("dp")
    inputs = features.reshape(MB, SLOT, C)
    cotangent = out_grad.reshape(MB, SLOT, C)
    own, picks = lengths[0, 0], join_pick[0]
    to_upper = lambda x: lax.ppermute(x, "section", [(0, 1)])
    to_lower = lambda x: lax.ppermute(x, "section", [(1, 0)])

    far_len = swap(own)
    far_rows = to_upper(inputs[MB - 1])
    far_w0 = swap(pw[0, 0:1])
    taps = jnp.concatenate([dw[0].reshape(5 * TAPS, C), gain[0], bias[0]], axis=0)
    far_taps = swap(taps)
    far_pw, far_res = swap(pw[0]), swap(res_w[0])
    wide = jnp.pad(down_b, ((0, 0), (0, C - SE)))
    squeeze = jnp.concatenate([down[0].T, up[0], up_b, wide], axis=0)
    far_squeeze = swap(squeeze)
    far_cot = swap(cotangent)

    flag = first.astype(jnp.int32)[None]
    mine = lambda v: jnp.where(first, v[:OWN], jnp.concatenate([v[OWN:], jnp.zeros((1,), v.dtype)]))
    length = mine(jnp.where(first, own, far_len))
    half_len = (length + 1) // 2
    join_len = mine(jnp.where(first, far_len, own)[picks])
    meta1 = jnp.concatenate([length, half_len, flag])
    meta2 = jnp.concatenate([half_len, join_len, flag, picks[MB - 1 :]])

    def small(block):
        t = jnp.where(first == (block == 0), taps, far_taps)
        q = jnp.where(first == (block == 0), squeeze, far_squeeze)
        return (
            t[: 5 * TAPS].reshape(5, TAPS, C), t[5 * TAPS : 5 * TAPS + 6], t[5 * TAPS + 6 :],
            q[:SE], q[2 * SE + 1, :SE][:, None], q[SE : 2 * SE], q[2 * SE : 2 * SE + 1],
        )

    def prepared(block, start, stop):
        array = prepare(meta1, (pw[0], res_w[0]), (far_pw, far_res), block, start, stop)
        return array, {i: (array, i - start) for i in range(start, stop)}

    parts0 = [prepared(0, 1, 3), prepared(0, 3, 6)]
    parts1 = [prepared(1, 0, 1), prepared(1, 1, 4), prepared(1, 4, 6)]

    stages, deep = radices(size, 16), radices(size, 4)
    c14 = Block(False, meta1, small(0), {**parts0[0][1], **parts0[1][1]}, stages)
    c14.x, c14.x_far, c14.first_matrix = inputs, far_rows, (pw[0], far_w0)
    c14.forward({2: (parts0[1][0],)})
    out0 = c14.tail(after=(parts1[0][0],))
    late_picks, _ = lax.optimization_barrier((picks, c14.z[3]))
    far_joining = to_lower(pick_joining(late_picks, features.reshape(MB, 2, HALF, C)))
    c15 = Block(True, meta2, small(1), {**parts1[0][1], **parts1[1][1], **parts1[2][1]}, stages)
    c15.arrived, c15.joined_far, c15.joined = out0, far_joining, features.reshape(MB, 2, HALF, C)
    c15.forward({1: (parts1[1][0],), 2: (parts1[2][0],)})
    out1 = c15.tail(cotangent, far_cot)
    c15.stop = 2
    c15.backward((4, 3))
    begin = c15.back_got
    c15.backward((2,))
    always = own[0] > 0

    half0 = c15.half(0, first, begin, c15.du)
    sum0 = lax.psum(half0, "dp")

    def middle(half0):
        upper, lower = c15.fork(), c14.fork()
        upper.resume(2)
        upper.done += (half0,)
        back, dx1 = upper.backward((1, 0))
        lower.tail_backward(cotangent, far_cot, back)
        lower.done = upper.done
        lower.backward((4,))
        begin1 = lower.back_got
        lower.backward((3,))
        half1 = upper.half(1, first, begin1, lower.du)
        begin2 = lower.back_got
        lower.stop = 2
        lower.backward((2,))
        half2 = lower.half(0, first, begin2, lower.du)
        return dx1, jnp.concatenate([half1, half2], axis=0), lower.state()

    dx1, half12, state = fenced(always, middle, half0)
    sum0, half12 = lax.optimization_barrier((sum0, half12))
    sum12 = lax.psum(half12, "dp")

    def ending(half12):
        last = c14.fork(state)
        last.resume(2)
        last.done += (half12,)
        came0 = to_upper(sum0)
        dx0, = last.backward((1, 0))
        half3 = last.half(1, first)
        half3, dx0, *kept = lax.optimization_barrier((half3, dx0, out0, out1, dx1))
        reduction = Reduction(half3, deep)
        reduction.step()
        pad = jnp.zeros((1, HALF, C), F32)
        lower = jnp.concatenate([kept[0], jnp.concatenate([to_lower(kept[0][0:1, :HALF]), pad], axis=1)], axis=0)
        upper = jnp.concatenate([to_upper(kept[1]), kept[1][0:1]], axis=0)
        block_out = jnp.where(first, lower, upper)
        lower = jnp.concatenate([dx0, to_lower(dx0[0:1])], axis=0)
        joins = jnp.concatenate([to_upper(kept[2]), kept[2][0:1]], axis=0)
        joins = jnp.stack([lax.dynamic_index_in_dim(joins, jnp.argmax(picks == s), 0, False) for s in range(MB)])
        upper = jnp.concatenate([jnp.zeros_like(joins), joins], axis=1)
        dx = jnp.where(first, lower, upper)
        reduction.x, block_out, dx, came0 = lax.optimization_barrier((reduction.x, block_out, dx, came0))
        return block_out, dx, came0, reduction.finish()

    block_out, dx, came0, sum3 = fenced(always, ending, half12)
    sum12, sum3 = lax.optimization_barrier((sum12, sum3))
    came12, came3 = swap(sum12), to_lower(sum3)
    split = PIECE_ROWS[1]
    sum1, sum2, came1, came2 = sum12[:split], sum12[split:], came12[:split], came12[split:]

    lead = 3 * C // 2

    def joined(near, far):
        pair = [x.reshape(-1, 1, C // 2, C) for x in (near, far)]
        both = jnp.where(first, jnp.concatenate(pair, axis=1), jnp.concatenate(pair[::-1], axis=1))
        return both.reshape(-1, C, C)

    choose_mine = lambda a, b: jnp.where(first, a, b)
    rest_part = joined(choose_mine(sum3[:lead], sum1[:lead]), choose_mine(came3[:lead], came1[:lead]))
    lead_part = joined(choose_mine(sum2[:C], sum0[:C]), choose_mine(came2[:C], came0[:C]))
    pw_grad = jnp.concatenate([rest_part, lead_part], axis=0)[None]
    res_grad = joined(choose_mine(sum2[C:], sum0[C:]), choose_mine(came2[C:], came0[C:]))
    near, far = choose_mine(sum3[lead:], sum1[lead:]), choose_mine(came3[lead:], came1[lead:])
    rows = jnp.where(first, jnp.concatenate([near, far], axis=0), jnp.concatenate([far, near], axis=0))
    dw_grad = rows[TAIL_ROWS : TAIL_ROWS + 40].reshape(1, 5, 8, C)
    norms = jnp.concatenate([dw_grad[0, 1:, TAPS : TAPS + 2], rows[None, 2 * SE + 2 : 2 * SE + 4], rows[None, 2 * SE + 4 : 2 * SE + 6]], axis=0)
    return (
        block_out.reshape(features.shape), dx.reshape(features.shape), dw_grad[:, :, :TAPS], pw_grad,
        norms[None, :, 1], norms[None, :, 0], res_grad, rows[SE : 2 * SE].T[None], rows[2 * SE + 1 : 2 * SE + 2, :SE],
        rows[:SE][None], rows[2 * SE : 2 * SE + 1],
    )


def solution(mesh):
    rows = P("section", "dp", None)
    own = lambda dims: P("section", *([None] * dims))
    weights = (own(3), own(3), own(2), own(2), own(2), own(2), own(1), own(2), own(1))
    in_specs = (rows, rows, rows, P("dp", None), *weights)
    out_specs = (rows, rows, *weights)
    return jax.shard_map(per_device, mesh=mesh, in_specs=in_specs, out_specs=out_specs, check_vma=False)
```

```python
import copy

import jax
import jax.numpy as jnp
from jax import lax
from jax.experimental import pallas as pl
from jax.experimental.pallas import tpu as pltpu
from jax.sharding import PartitionSpec as P

EPSILON = 1e-05
EXACT = lax.Precision.HIGHEST
TAPS = 5
MB = 3
OWN = 2
SLOT = 400
HALF = 200
KEPT = 208
C = 512
LANES = 128
CHUNKS = [slice(c, c + LANES) for c in range(0, C, LANES)]
SE = 64
BF16, F32 = jnp.bfloat16, jnp.float32
VMEM_BYTES = 60 << 20
TAIL_ROWS = 2 * SE + 8
SMALL = 256


def radices(size, most):
    stages, left = [], size
    while left > 1:
        radix = min(most, left)
        while left % radix:
            radix -= 1
        stages.append(radix)
        left //= radix
    return stages


def exchange(block, radix, stride):
    size = lax.axis_size("dp")
    if radix == size:
        return lax.all_to_all(block, "dp", 0, 0)
    groups = []
    for base in range(size):
        if (base // stride) % radix == 0:
            groups.append([base + j * stride for j in range(radix)])
    return lax.all_to_all(block, "dp", 0, 0, axis_index_groups=groups)


def shared(block, stages):
    stride = 1
    for no, radix in enumerate(stages):
        if no:
            block = jnp.broadcast_to(jnp.sum(block, axis=0), (radix,) + block.shape[1:])
        block = exchange(block, radix, stride)
        stride *= radix
    return block


def halves(x):
    high = x.astype(BF16)
    return high, (x - high.astype(F32)).astype(BF16)


def sigmoid(x):
    return 0.5 * jnp.tanh(0.5 * x) + 0.5


def exact_dot(a, b, dims=((1,), (0,))):
    return lax.dot_general(a, b, (dims, ((), ())), precision=EXACT, preferred_element_type=F32)


def fast_dot(a, b, dims=((1,), (0,))):
    return lax.dot_general(a, b, (dims, ((), ())), preferred_element_type=F32)


def stacked_dot(high, low, w, back=False):
    w_high, w_low = w[0], w[1]
    w = jnp.concatenate([w_high, w_high, w_low], axis=1 if back else 0)
    x = jnp.concatenate([high, low, high], axis=1)
    return fast_dot(x, w, ((1,), (1 if back else 0,)))


def stacked_outer(a_high, a_low, b_high, b_low):
    a = jnp.concatenate([a_high, a_low, a_high], axis=0)
    b = jnp.concatenate([b_high, b_high, b_low], axis=0)
    return fast_dot(a, b, ((0,), (0,)))


def column_sum(x):
    return jnp.sum(x, axis=0, keepdims=True)


class Rows:
    def __init__(self, meta, m, two, rows, which=0):
        place = lax.broadcasted_iota(jnp.int32, (rows, LANES), 0)
        if two:
            later = place >= HALF
            limit = jnp.where(later, HALF + meta[OWN + m], meta[m])
            self.mask = place < limit
        else:
            self.mask = place < meta[which * OWN + m]

    def keep(self, x):
        return jnp.where(self.mask, x, 0.0)


class Padded:
    def __init__(self, ref, two):
        self.ref = ref
        self.pieces = [(8, 0, HALF), (16 + HALF, HALF, HALF)] if two else [(8, 0, SLOT)]

    def put(self, x):
        zeros = jnp.zeros((8, LANES), F32)
        for at, start, rows in self.pieces:
            self.ref[at - 8 : at, :] = zeros
            self.ref[at : at + rows, :] = x[start : start + rows]
        self.ref[at + rows : at + rows + 8, :] = zeros

    def get(self, offset):
        parts = [self.ref[at + offset : at + offset + rows, :] for at, _, rows in self.pieces]
        return parts[0] if len(parts) == 1 else jnp.concatenate(parts, axis=0)

    def conv(self, kernel):
        total = kernel[0:1] * self.get(-2)
        for k in range(1, TAPS):
            total = total + kernel[k : k + 1] * self.get(k - 2)
        return total

    def conv_back(self, kernel):
        total = kernel[0:1] * self.get(2)
        for k in range(1, TAPS):
            total = total + kernel[k : k + 1] * self.get(2 - k)
        return total


def every_other(ref, x):
    ref[0:SLOT, :] = x
    ref[SLOT : 2 * KEPT, :] = jnp.zeros((2 * KEPT - SLOT, LANES), F32)
    return ref[pl.ds(0, KEPT, stride=2), :]


def spread_out(ref, x):
    ref[...] = jnp.zeros_like(ref)
    ref[pl.ds(0, KEPT, stride=2), :] = x
    return ref[0:SLOT, :]


def center_spread(sums, rows):
    center = sums[0:1] / rows
    return center, lax.rsqrt(sums[1:2] / rows - center * center + EPSILON)


def added(ref):
    return jnp.sum(ref[:, 0], axis=0)


def accumulate(ref, m, at, value):
    rows = slice(at, at + value.shape[0])
    ref[rows, :] = jnp.where(m == 0, value, ref[rows, :] + value)


def send(ref, rows):
    for copy in range(ref.shape[0]):
        for row, x in enumerate(rows):
            ref[copy, 0, row : row + 1, 0 : x.shape[1]] = x


def pad_scratch():
    return pltpu.VMEM((len(CHUNKS), SLOT + 24, LANES), F32)


def stride_scratch():
    return pltpu.VMEM((len(CHUNKS), 2 * KEPT, LANES), F32)


def slots(rows, cols=C):
    return pl.BlockSpec((1, rows, cols), lambda m, *_: (m, 0, 0))


def copies(count, rows, cols=C):
    return pl.BlockSpec((count, 1, rows, cols), lambda m, *_: (0, m, 0, 0))


def whole(*shape):
    return pl.BlockSpec(shape, lambda m, *_: (0,) * len(shape))


def layer(i, *shape):
    return pl.BlockSpec((1,) + shape, lambda m, *_: (i,) + (0,) * len(shape))


def f32(*shape):
    return jax.ShapeDtypeStruct(shape, F32)


def bf16(*shape):
    return jax.ShapeDtypeStruct(shape, BF16)


def call(body, meta, args, outs, scratch=(), name=None, flops=0, steps=OWN, after=(), into=()):
    arrays, in_specs = [a for a, _ in args], [s for _, s in args]
    shapes, out_specs = [a for a, _ in outs], [s for _, s in outs]
    size = sum(a.size * a.dtype.itemsize for a in arrays + shapes)
    extra = list(after) + list(into)
    count = len(arrays)

    def inner(meta, *refs):
        body(meta, *refs[:count], *refs[count + len(extra) :])

    return pl.pallas_call(
        inner,
        out_shape=shapes,
        grid_spec=pltpu.PrefetchScalarGridSpec(
            num_scalar_prefetch=1,
            grid=(steps,),
            in_specs=in_specs + [pl.BlockSpec(memory_space=pl.ANY)] * len(extra),
            out_specs=out_specs,
            scratch_shapes=list(scratch),
        ),
        input_output_aliases={1 + count + len(after) + j: j for j in range(len(into))},
        compiler_params=pltpu.CompilerParams(vmem_limit_bytes=VMEM_BYTES),
        cost_estimate=pl.CostEstimate(flops=flops, bytes_accessed=size, transcendentals=0),
        name=name,
    )(meta, *arrays, *extra)


class Linked:
    def __init__(self, index, rows):
        self.index, self.rows = index, rows


class Part:
    def __init__(self, ref, at):
        self.ref, self.at = ref, at

    def __getitem__(self, index):
        return self.ref[self.at + index]


def run(steps):
    body, meta, args, outs, scratch, name, flops, after, into = next(steps)
    return finish(steps, call(body, meta, args, outs, scratch, name, flops, after=after, into=into))


def finish(steps, results):
    try:
        steps.send(results)
    except StopIteration as stop:
        return stop.value


def run_joined(one, two):
    body1, meta1, args1, outs1, scratch1, name1, flops1, after1, into1 = next(one)
    body2, meta2, args2, outs2, scratch2, name2, flops2, after2, into2 = next(two)
    assert not into2
    own2 = [arg for arg in args2 if not isinstance(arg[0], Linked)]
    sizes = len(args1), len(own2), len(outs1), len(outs2), len(scratch1), len(scratch2)
    lead = meta1.shape[0]

    def body(meta, *refs):
        refs = list(refs)
        in1, in2, out1, out2, scr1, scr2 = [[refs.pop(0) for _ in range(n)] for n in sizes]
        body1(Part(meta, 0), *in1, *out1, *scr1)
        linked = []
        for arg in args2:
            link = arg[0]
            linked.append(out1[link.index].at[:, 0 : link.rows, :] if isinstance(link, Linked) else in2.pop(0))
        body2(Part(meta, lead), *linked, *out2, *scr2)

    def moved(spec):
        if spec.index_map is None:
            return spec
        return pl.BlockSpec(spec.block_shape, lambda m, meta: spec.index_map(m, Part(meta, lead)))

    meta = jnp.concatenate([meta1, meta2])
    args = args1 + [(a, moved(spec)) for a, spec in own2]
    results = call(
        body, meta, args, outs1 + outs2, list(scratch1) + list(scratch2), f"{name1}_{name2}", flops1 + flops2,
        after=(*after1, *after2), into=into1,
    )
    return finish(one, results[: len(outs1)]), finish(two, results[len(outs1) :])


def choose(meta, block, own, far):
    return jnp.where(meta[2 * OWN] == 1 - block, own, far)


def prepare(meta, own, far, block, start, stop):
    def body(meta, *refs):
        pair = [ref[0] for ref in refs[:2]]
        if stop == 6:
            last = pl.program_id(0) == 5 - start
            pair = [jnp.where(last, ref[...], w) for ref, w in zip(refs[2:4], pair)]
        out = refs[-1]
        out[0, 0], out[0, 1] = halves(choose(meta, block, *pair))

    matrix = pl.BlockSpec((1, C, C), lambda j, *_: (jnp.minimum(j + start, 4), 0, 0))
    args = [(own[0], matrix), (far[0], matrix)]
    if stop == 6:
        args += [(own[1], whole(C, C)), (far[1], whole(C, C))]
    out = pl.BlockSpec((1, 2, C, C), lambda j, *_: (j, 0, 0, 0))
    name = f"prepare_{block}_{start}"
    return call(body, meta, args, [(bf16(stop - start, 2, C, C), out)], name=name, steps=stop - start)[0]


class Block:
    def __init__(self, two, meta, weights, ready, stages):
        self.done, self.stop, self.pending = (), None, None
        self.two, self.meta, self.stages = two, meta, stages
        self.dw, self.gain, self.bias, self.down, self.down_b, self.up, self.up_b = weights
        self.ready = ready
        self.tail_rows = SLOT if two else KEPT
        self.first, self.last = stages[0], stages[-1]
        self.tag = "c15" if two else "c14"

    def rows_of(self, i):
        return self.tail_rows if i == 4 else SLOT

    def valid(self, meta, m, i):
        last = i == 4 and not self.two
        return Rows(meta, m, self.two, self.rows_of(i), which=1 if last else 0)

    def matrix(self, i):
        array, at = self.ready[i]
        return (array, layer(at, 2, C, C))

    def source_args(self):
        if not self.two:
            return [(self.x, slots(SLOT)), (self.x_far, whole(SLOT, C))]
        far = pl.BlockSpec((HALF, C), lambda m, *_: (m, 0))
        near = pl.BlockSpec((1, 1, HALF, C), lambda m, meta: (meta[2 * OWN + 1], 1, 0, 0))
        return [(self.arrived, slots(HALF)), (self.joined_far, far), (self.joined, near)]

    def source(self, meta, refs, cs):
        lower = meta[2 * OWN] == 1
        if not self.two:
            return jnp.where(lower, refs[0][0, :, cs], refs[1][:, cs])
        joined = jnp.where(lower, refs[1][:, cs], refs[2][0, 0, :, cs])
        return jnp.concatenate([refs[0][0, :, cs], joined], axis=0)

    def before_args(self, i):
        if i == 0:
            return self.source_args()
        return [(self.z[i - 1], slots(SLOT)), (self.stats[i - 1], slots(2))]


    def forward_layer(self, i, after=()):
        return run(self.forward_steps(i, after))

    def forward_steps(self, i, after=()):
        two, count = self.two, self.first
        strided = i == 4 and not two
        rows = self.rows_of(i)
        n_src = len(self.source_args())
        width = C + LANES if i == 0 else C
        sent = 4 if i == 3 else 2
        makes = i == 0 and not two

        def body(meta, *refs):
            refs = list(refs)
            take = lambda n: [refs.pop(0) for _ in range(n)]
            m = pl.program_id(0)
            if i == 0:
                src = take(n_src)
            else:
                z_ref, got_ref = take(2)
                n_ref, = take(1) if i > 1 else (None,)
                gain_ref, bias_ref = take(2)
                res_sum, = take(1) if i == 3 else (None,)
            dw_ref, = take(1)
            if makes:
                own_ref, far_ref, z_out, pay, w_ref = take(5)

                @pl.when(m == 0)
                def _():
                    w_ref[0, 0], w_ref[0, 1] = halves(choose(meta, 0, own_ref[0], far_ref[0]))

            else:
                w_ref, z_out, pay = take(3)
            if i:
                stat_out, = take(1)
            if i == 1:
                n_out, = take(1)
            pad, y_ref = take(2)
            alt, = take(1) if strided else (None,)
            valid_in = self.valid(meta, m, 0)
            if i:
                sums = added(got_ref)
                if i == 1:
                    count_in = jnp.maximum(jnp.concatenate([sums[0:1, C:]] * len(CHUNKS), axis=1), 1.0)
                    count_out = jnp.maximum(jnp.concatenate([sums[1:2, C:]] * len(CHUNKS), axis=1), 1.0)
                    n_out[0, 0:1, :] = count_in
                    n_out[0, 1:2, :] = count_out
                else:
                    count_in = n_ref[0, 0:1, :]
                center, spread = center_spread(sums[:, :C], count_in)
                stat_out[0, 0:1, :] = center
                stat_out[0, 1:2, :] = spread
                scale = gain_ref[i - 1 : i] * spread
                shift = bias_ref[i - 1 : i] - center * scale
            for c, cs in enumerate(CHUNKS):
                if i == 0:
                    h = valid_in.keep(self.source(meta, src, cs))
                else:
                    u = z_ref[0, :, cs] * scale[:, cs] + shift[:, cs]
                    h = valid_in.keep(u * sigmoid(u))
                padded = Padded(pad.at[c], two)
                padded.put(h)
                y = padded.conv(dw_ref[0, :, cs])
                if strided:
                    y = every_other(alt.at[c], y)
                high, low = halves(y)
                y_ref[:, cs] = high
                y_ref[:, C + cs.start : C + cs.stop] = low
            w = w_ref.at[0] if makes else w_ref.at[0]
            z = stacked_dot(y_ref[:, 0:C], y_ref[:, C : 2 * C], w)
            z_out[0] = z
            valid = self.valid(meta, m, i)
            one, square = [], []
            for cs in CHUNKS:
                kept = valid.keep(z[:, cs])
                one.append(column_sum(kept))
                square.append(column_sum(kept * kept))
            if i == 0:
                if two:
                    number = (meta[m] + meta[OWN + m]).astype(F32)
                    numbers = number, number
                else:
                    numbers = meta[m].astype(F32), meta[OWN + m].astype(F32)
                one.append(jnp.full((1, LANES), numbers[0], F32))
                square.append(jnp.full((1, LANES), numbers[1], F32))
            out = [jnp.concatenate(one, axis=1), jnp.concatenate(square, axis=1)]
            if i == 3:
                out += [res_sum[0, 0:1, :], res_sum[0, 1:2, :]]
            send(pay, out)

        if i == 0:
            args = list(self.source_args())
        else:
            got = 4 if i == 4 else 2
            args = [(self.z[i - 1], slots(SLOT)), (self.got[i - 1], copies(self.last, got, C + LANES if i == 1 else C))]
            if i > 1:
                args.append((self.number, slots(2)))
            args += [(self.gain, whole(6, C)), (self.bias, whole(6, C))]
            if i == 3:
                args.append((self.res_sum, slots(2)))
        args.append((self.dw, layer(i, TAPS, C)))
        args += [(w, layer(0, C, C)) for w in self.first_matrix] if makes else [self.matrix(i)]
        outs = [(f32(OWN, rows, C), slots(rows)), (f32(count, OWN, sent, width), copies(count, sent, width))]
        if i:
            outs.append((f32(OWN, 2, C), slots(2)))
        if i == 1:
            outs.append((f32(OWN, 2, C), slots(2)))
        if makes:
            outs.append((bf16(1, 2, C, C), layer(0, 2, C, C)))
        scratch = [pad_scratch(), pltpu.VMEM((rows, 2 * C), BF16)]
        if strided:
            scratch.append(stride_scratch())
        flops = 6 * OWN * rows * C * C
        result = yield body, self.meta, args, outs, scratch, f"{self.tag}_forward_{i}", flops, after, ()
        self.z.append(result[0])
        if makes:
            self.ready[0] = (result[2], 0)
        if i:
            self.stats.append(result[2])
        if i == 1:
            self.number = result[3]
        self.got.append(shared(result[1], self.stages))

    def residual(self):
        two, rows = self.two, self.tail_rows

        def body(meta, *refs):
            refs = list(refs)
            src = [refs.pop(0) for _ in self.source_args()]
            w_ref, r_out, x_out, sum_out = refs[:4]
            alt = refs[4] if not two else None
            m = pl.program_id(0)
            valid_in = self.valid(meta, m, 0)
            for c, cs in enumerate(CHUNKS):
                x = valid_in.keep(self.source(meta, src, cs))
                if not two:
                    x = every_other(alt.at[c], x)
                high, low = halves(x)
                x_out[0, :, cs] = high
                x_out[0, :, C + cs.start : C + cs.stop] = low
            r = stacked_dot(x_out[0, :, 0:C], x_out[0, :, C : 2 * C], w_ref.at[0])
            r_out[0] = r
            valid = self.valid(meta, m, 4)
            for cs in CHUNKS:
                kept = valid.keep(r[:, cs])
                sum_out[0, 0:1, cs] = column_sum(kept)
                sum_out[0, 1:2, cs] = column_sum(kept * kept)

        args = self.source_args() + [self.matrix(5)]
        outs = [
            (f32(OWN, rows, C), slots(rows)),
            (bf16(OWN, rows, 2 * C), slots(rows, 2 * C)),
            (f32(OWN, 2, C), slots(2)),
        ]
        scratch = [] if two else [stride_scratch()]
        self.r, self.picked, self.res_sum = call(
            body, self.meta, args, outs, scratch, f"{self.tag}_residual", 6 * OWN * rows * C * C
        )

    def start(self):
        self.z, self.got, self.stats = [], [], []

    def forward(self, after=None, joined=False):
        if not joined:
            self.start()
        for i in range(1 if joined else 0, 5):
            if i == 2:
                self.residual()
            self.forward_layer(i, (after or {}).get(i, ()))


    def segments(self):
        return [(0, HALF), (HALF, HALF)] if self.two else [(0, self.tail_rows)]

    def lengths(self, meta, m):
        if self.two:
            return [meta[m], meta[OWN + m]]
        return [meta[OWN + m]]

    def squeeze(self, sums, counts, se_refs):
        down_t, down_b, up, up_b = se_refs
        means = [s / jnp.maximum(jnp.full((1, C), n.astype(F32)), 1.0) for s, n in zip(sums, counts)]
        ps = [jnp.sum(down_t[...] * mean, axis=1, keepdims=True) + down_b[...] for mean in means]
        gates = [sigmoid(column_sum(up[...] * (p * sigmoid(p))) + up_b[...]) for p in ps]
        return means, ps, gates

    def squeeze_back(self, des, ps, gates, counts, se_refs, means, small, m):
        down_t, down_b, up, up_b = se_refs
        shares, up_grad, down_grad, dq_sum, dp_sum = [], 0.0, 0.0, 0.0, 0.0
        for de, p, gate, n, mean in zip(des, ps, gates, counts, means):
            dq = de * gate * (1.0 - gate)
            s = sigmoid(p)
            dp = jnp.sum(up[...] * dq, axis=1, keepdims=True) * (s * (1.0 + p * (1.0 - s)))
            shares.append(column_sum(down_t[...] * dp) / jnp.maximum(jnp.full((1, C), n.astype(F32)), 1.0))
            up_grad, down_grad = up_grad + (p * s) * dq, down_grad + dp * mean
            dq_sum, dp_sum = dq_sum + dq, dp_sum + dp
        row, col = (lax.broadcasted_iota(jnp.int32, (SE, C), axis) for axis in (0, 1))
        dp_row = column_sum(jnp.where(row == col, dp_sum, 0.0))
        accumulate(small, m, 0, up_grad)
        accumulate(small, m, SE, down_grad)
        accumulate(small, m, 2 * SE, dq_sum)
        accumulate(small, m, 2 * SE + 1, dp_row)
        return shares

    def last_norm(self, m, dt_out, du_out, z_ref, slope_ref, gates, shares, center, spread, res_bias, res_gain, pay, small):
        bias_sum, gain_sum = [], []
        for cs in CHUNKS:
            dh = dt_out[0, :, cs] * self.by_segment(gates, cs) + self.by_segment(shares, cs)
            du = dh * slope_ref[:, cs]
            du_out[0, :, cs] = du
            bias_sum.append(column_sum(du))
            gain_sum.append(column_sum(du * ((z_ref[0, :, cs] - center[:, cs]) * spread[:, cs])))
        rows = [jnp.concatenate(x, axis=1) for x in (bias_sum, gain_sum, res_bias, res_gain)]
        send(pay, rows)
        for j, row in enumerate(rows):
            accumulate(small, m, 2 * SE + 2 + j, row)

    def se_args(self):
        return [(self.down, whole(SE, C)), (self.down_b, whole(SE, 1)), (self.up, whole(SE, C)), (self.up_b, whole(1, C))]

    def store_rows(self, ref, rows):
        ref[0] = jnp.concatenate(rows + [jnp.zeros((8 - len(rows), C), F32)], axis=0)

    def store_columns(self, ref, columns):
        ref[0] = jnp.zeros((SE, 8), F32)
        for j, column in enumerate(columns):
            ref[0, :, j : j + 1] = column

    def by_segment(self, rows, cs):
        parts = [jnp.broadcast_to(row[:, cs], (n, LANES)) for row, (_, n) in zip(rows, self.segments())]
        return parts[0] if len(parts) == 1 else jnp.concatenate(parts, axis=0)

    def seg_sums(self, x):
        return [column_sum(x[at : at + n]) for at, n in self.segments()]

    def tail(self, cotangent=None, far=None, after=()):
        return run(self.tail_steps(cotangent, far, after))

    def tail_steps(self, cotangent=None, far=None, after=()):
        two, rows = self.two, self.tail_rows
        back = cotangent is not None

        def body(meta, *refs):
            refs = list(refs)
            take = lambda n: [refs.pop(0) for _ in range(n)]
            m = pl.program_id(0)
            z_ref, got4, r_ref, got3, n_ref, gain, bias = take(7)
            se_refs = take(4)
            if back:
                cot_ref, far_ref = take(2)
            out, stat_out, rstat_out, means_out, p_out, gate_out = take(6)
            if back:
                small, du_out, dt_out, pay = take(4)
            h_ref, = take(1)
            if back:
                slope_ref, = take(1)
            valid = self.valid(meta, m, 4)
            number = n_ref[0, 1:2, :]
            center, spread = center_spread(added(got4), number)
            rcenter, rspread = center_spread(added(got3)[2:4], number)
            stat_out[0, 0:1, :] = center
            stat_out[0, 1:2, :] = spread
            rstat_out[0, 0:1, :] = rcenter
            rstat_out[0, 1:2, :] = rspread
            scale = gain[4:5] * spread
            shift = bias[4:5] - center * scale
            sums = []
            for cs in CHUNKS:
                u = z_ref[0, :, cs] * scale[:, cs] + shift[:, cs]
                s = sigmoid(u)
                h = valid.keep(u * s)
                h_ref[:, cs] = h
                if back:
                    slope_ref[:, cs] = valid.keep(s * (1.0 + u * (1.0 - s)))
                sums.append(self.seg_sums(h))
            sums = [jnp.concatenate([s[j] for s in sums], axis=1) for j in range(len(self.segments()))]
            counts = self.lengths(meta, m)
            means, ps, gates = self.squeeze(sums, counts, se_refs)
            self.store_rows(means_out, means)
            self.store_columns(p_out, ps)
            self.store_rows(gate_out, gates)
            res_gain, res_bias, gate_grad = [], [], []
            for cs in CHUNKS:
                h = h_ref[:, cs]
                rh = (r_ref[0, :, cs] - rcenter[:, cs]) * rspread[:, cs]
                t = h * self.by_segment(gates, cs) + gain[5:6, cs] * rh + bias[5:6, cs]
                s = sigmoid(t)
                out[0, 0:rows, cs] = valid.keep(t * s)
                if rows < SLOT:
                    out[0, rows:SLOT, cs] = jnp.zeros((SLOT - rows, LANES), F32)
                if back:
                    cot = jnp.where(meta[2 * OWN] == 1, far_ref[0, :, cs], cot_ref[0, :, cs])
                    dt = valid.keep(cot * (s * (1.0 + t * (1.0 - s))))
                    dt_out[0, :, cs] = dt
                    res_bias.append(column_sum(dt))
                    res_gain.append(column_sum(dt * rh))
                    gate_grad.append(self.seg_sums(dt * h))
            if not back:
                return
            des = [jnp.concatenate([g[j] for g in gate_grad], axis=1) for j in range(len(counts))]
            shares = self.squeeze_back(des, ps, gates, counts, se_refs, means, small, m)
            self.last_norm(m, dt_out, du_out, z_ref, slope_ref, gates, shares, center, spread, res_bias, res_gain, pay, small)

        args = [
            (self.z[4], slots(rows)), (self.got[4], copies(self.last, 2)), (self.r, slots(rows)),
            (self.got[3], copies(self.last, 4)), (self.number, slots(2)),
            (self.gain, whole(6, C)), (self.bias, whole(6, C)),
        ] + self.se_args()
        outs = [
            (f32(OWN, SLOT, C), slots(SLOT)), (f32(OWN, 2, C), slots(2)), (f32(OWN, 2, C), slots(2)),
            (f32(OWN, 8, C), slots(8)), (f32(OWN, SE, 8), slots(SE, 8)), (f32(OWN, 8, C), slots(8)),
        ]
        scratch = [pltpu.VMEM((rows, C), F32)]
        if back:
            args += [(cotangent, layer(MB - 1, SLOT, C)), (far, slots(SLOT))]
            outs += self.tail_outs()
            scratch.append(pltpu.VMEM((rows, C), F32))
        result = yield body, self.meta, args, outs, scratch, f"{self.tag}_tail", 0, after, ()
        self.stats.append(result[1])
        self.rstat, self.se_state = result[2], result[3:6]
        if back:
            self.tail_results(result[6:])
        return result[0]

    def tail_outs(self):
        rows, count = self.tail_rows, self.first
        return [
            (f32(SMALL, C), whole(TAIL_ROWS, C)), (f32(OWN, rows, C), slots(rows)), (f32(OWN, rows, C), slots(rows)),
            (f32(count, OWN, 4, C), copies(count, 4)),
        ]

    def tail_results(self, result):
        self.small, self.du, self.dt, pay = result
        self.back_got = shared(pay, self.stages)

    def tail_backward_steps(self, cotangent, far, back):
        rows = self.tail_rows

        def body(meta, z_ref, r_ref, stat, rstat, gain, bias, means_ref, p_ref, gate_ref, down, down_b, up, up_b, cot_ref, far_ref, back_ref,
                 small, du_out, dt_out, pay, slope_ref):
            m = pl.program_id(0)
            valid = self.valid(meta, m, 4)
            center, spread, rcenter, rspread = stat[0, 0:1], stat[0, 1:2], rstat[0, 0:1], rstat[0, 1:2]
            scale = gain[4:5] * spread
            shift = bias[4:5] - center * scale
            zeros = jnp.zeros((rows - HALF, LANES), F32)
            counts = self.lengths(meta, m)
            ps = [p_ref[0, :, j : j + 1] for j in range(len(counts))]
            gates = [gate_ref[0, j : j + 1, :] for j in range(len(counts))]
            means = [means_ref[0, j : j + 1, :] for j in range(len(counts))]
            res_gain, res_bias, gate_grad = [], [], []
            for cs in CHUNKS:
                u = z_ref[0, :, cs] * scale[:, cs] + shift[:, cs]
                s = sigmoid(u)
                h = valid.keep(u * s)
                slope_ref[:, cs] = valid.keep(s * (1.0 + u * (1.0 - s)))
                rh = (r_ref[0, :, cs] - rcenter[:, cs]) * rspread[:, cs]
                t = h * self.by_segment(gates, cs) + gain[5:6, cs] * rh + bias[5:6, cs]
                s = sigmoid(t)
                here = jnp.where(meta[2 * OWN] == 1, cot_ref[0, 0:HALF, cs], far_ref[0, :, cs])
                cot = jnp.concatenate([here + back_ref[0, :, cs], zeros], axis=0)
                dt = valid.keep(cot * (s * (1.0 + t * (1.0 - s))))
                dt_out[0, :, cs] = dt
                res_bias.append(column_sum(dt))
                res_gain.append(column_sum(dt * rh))
                gate_grad.append(self.seg_sums(dt * h))
            des = [jnp.concatenate([g[j] for g in gate_grad], axis=1) for j in range(len(counts))]
            shares = self.squeeze_back(des, ps, gates, counts, (down, down_b, up, up_b), means, small, m)
            self.last_norm(m, dt_out, du_out, z_ref, slope_ref, gates, shares, center, spread, res_bias, res_gain, pay, small)

        args = [
            (self.z[4], slots(rows)), (self.r, slots(rows)), (self.stats[4], slots(2)), (self.rstat, slots(2)),
            (self.gain, whole(6, C)), (self.bias, whole(6, C)),
            (self.se_state[0], slots(8)), (self.se_state[1], slots(SE, 8)), (self.se_state[2], slots(8)),
        ] + self.se_args() + [(cotangent, slots(HALF)), (far, layer(MB - 1, HALF, C)), (back, slots(HALF))]
        scratch = [pltpu.VMEM((rows, C), F32)]
        result = yield body, self.meta, args, self.tail_outs(), scratch, f"{self.tag}_tail_back", 0, (), ()
        self.tail_results(result)


    def norm_grad(self, du, zh, scale, sums, number, cs):
        return scale[:, cs] * (du - sums[0:1, cs] / number[:, cs] - zh * (sums[1:2, cs] / number[:, cs]))

    def backward_layer(self, i):
        return run(self.backward_steps(i))

    def backward_steps(self, i):
        two, count = self.two, self.first
        strided = i == 4 and not two
        rows = self.rows_of(i)
        n_src = len(self.source_args())

        def body(meta, *refs):
            refs = list(refs)
            take = lambda n: [refs.pop(0) for _ in range(n)]
            m = pl.program_id(0)
            du_ref, z_ref, w_ref, got, n_ref, stat, gain, bias, dw_ref = take(9)
            if i:
                zp_ref, statp = take(2)
            else:
                dxr_ref, = take(1)
                src = take(n_src)
            small, dz_out = take(2)
            if i:
                du_out, pay = take(2)
            elif two:
                back_out, dx_out = take(2)
            else:
                dx_out, = take(1)
            pad, = take(1)
            alt, = take(1) if refs else (None,)
            sums = added(got)
            number = n_ref[0, 1:2, :] if i == 4 else n_ref[0, 0:1, :]
            center, spread = stat[0, 0:1], stat[0, 1:2]
            scale = gain[i : i + 1] * spread
            valid = self.valid(meta, m, i)
            for cs in CHUNKS:
                zh = (z_ref[0, :, cs] - center[:, cs]) * spread[:, cs]
                dz = valid.keep(self.norm_grad(du_ref[0, :, cs], zh, scale, sums, number, cs))
                high, low = halves(dz)
                dz_out[0, :, cs] = high
                dz_out[0, :, C + cs.start : C + cs.stop] = low
            dy = stacked_dot(dz_out[0, :, 0:C], dz_out[0, :, C : 2 * C], w_ref.at[0], True)
            valid_in = self.valid(meta, m, 0)
            if i:
                pcenter, pspread = statp[0, 0:1], statp[0, 1:2]
                pscale = gain[i - 1 : i] * pspread
                pshift = bias[i - 1 : i] - pcenter * pscale
            taps, bias_sum, gain_sum = [[] for _ in range(TAPS)], [], []
            for c, cs in enumerate(CHUNKS):
                grad = dy[:, cs]
                if strided:
                    grad = spread_out(alt.at[c], grad)
                padded = Padded(pad.at[c], two)
                padded.put(grad)
                if i:
                    z = zp_ref[0, :, cs]
                    u = z * pscale[:, cs] + pshift[:, cs]
                    s = sigmoid(u)
                    h = valid_in.keep(u * s)
                else:
                    h = valid_in.keep(self.source(meta, src, cs))
                dh = None
                for k in range(TAPS):
                    moved = padded.get(2 - k)
                    taps[k].append(column_sum(h * moved))
                    term = dw_ref[0, k : k + 1, cs] * moved
                    dh = term if dh is None else dh + term
                if i:
                    du = valid_in.keep(dh * (s * (1.0 + u * (1.0 - s))))
                    du_out[0, :, cs] = du
                    bias_sum.append(column_sum(du))
                    gain_sum.append(column_sum(du * ((z - pcenter[:, cs]) * pspread[:, cs])))
                    continue
                dxr = dxr_ref[0, :, cs]
                if not two:
                    dxr = spread_out(alt.at[c], dxr)
                dx = valid_in.keep(dh) + dxr
                if two:
                    back_out[0, :, cs] = dx[:HALF]
                    dx = dx[HALF:]
                dx_out[0, :, cs] = dx
            rows = taps + [bias_sum, gain_sum] if i else taps
            rows = [jnp.concatenate(x, axis=1) for x in rows]
            for j, row in enumerate(rows):
                accumulate(small, m, j, row)
            if i:
                send(pay, rows[TAPS:])

        sent = 4 if i == 4 else 2
        args = [
            (self.du, slots(rows)), (self.z[i], slots(rows)), self.matrix(i), (self.back_got, copies(self.last, sent)),
            (self.number, slots(2)), (self.stats[i], slots(2)), (self.gain, whole(6, C)), (self.bias, whole(6, C)),
            (self.dw, layer(i, TAPS, C)),
        ]
        if not i:
            args.append((self.dxr, slots(self.tail_rows)))
        args += self.before_args(i)
        place = TAIL_ROWS // 8 + i
        outs = [(f32(SMALL, C), pl.BlockSpec((8, C), lambda m, *_: (place, 0))), (bf16(OWN, rows, 2 * C), slots(rows, 2 * C))]
        if i:
            outs += [(f32(OWN, SLOT, C), slots(SLOT)), (f32(count, OWN, 2, C), copies(count, 2))]
        elif two:
            outs += [(f32(OWN, HALF, C), slots(HALF)), (f32(OWN, HALF, C), slots(HALF))]
        else:
            outs += [(f32(OWN, SLOT, C), slots(SLOT))]
        scratch = [pad_scratch()]
        if strided or (i == 0 and not two):
            scratch.append(stride_scratch())
        flops = 6 * OWN * rows * C * C
        self.small, dz, *result = yield (
            body, self.meta, args, outs, scratch, f"{self.tag}_backward_{i}", flops, self.done, (self.small,)
        )
        got = self.back_got
        if i:
            self.du = result[0]
            if i == self.stop:
                self.pending = dz, result[1]
                return result
            self.back_got = shared(result[1], self.stages)
        self.weight_grad(i, dz)
        if i == 4:
            self.residual_back(got)
        return result

    def residual_back(self, got):
        rows = self.tail_rows

        def body(meta, got, n_ref, dt_ref, r_ref, rstat, gain, w_ref, x_ref, kept_out, away_out, dxr_out, dr, total):
            m = pl.program_id(0)
            sums = added(got)[2:4]
            number = n_ref[0, 1:2, :]
            center, spread = rstat[0, 0:1], rstat[0, 1:2]
            scale = gain[5:6] * spread
            valid = self.valid(meta, m, 4)
            for cs in CHUNKS:
                rh = (r_ref[0, :, cs] - center[:, cs]) * spread[:, cs]
                high, low = halves(valid.keep(self.norm_grad(dt_ref[0, :, cs], rh, scale, sums, number, cs)))
                dr[:, cs] = high
                dr[:, C + cs.start : C + cs.stop] = low
            high, low = dr[:, 0:C], dr[:, C : 2 * C]
            dxr_out[0] = stacked_dot(high, low, w_ref.at[0], True)
            grad = stacked_outer(x_ref[0, :, 0:C], x_ref[0, :, C : 2 * C], high, low)
            self.add_halves(meta, m, grad, total, kept_out, away_out)

        args = [
            (got, copies(self.last, 4)), (self.number, slots(2)), (self.dt, slots(rows)), (self.r, slots(rows)),
            (self.rstat, slots(2)), (self.gain, whole(6, C)), self.matrix(5), (self.picked, slots(rows, 2 * C)),
        ]
        outs = self.piece_out(5) + [(f32(OWN, rows, C), slots(rows))]
        which = PLACES[5][0]
        *self.pieces[which], self.dxr = call(
            body, self.meta, args, outs, [pltpu.VMEM((rows, 2 * C), BF16), pltpu.VMEM((C, C), F32)],
            f"{self.tag}_residual_back", 12 * OWN * rows * C * C, into=self.pieces[which],
        )

    def piece_out(self, i):
        which, place = PLACES[i]
        rows = PIECE_ROWS[which]
        return [(f32(rows, C), pl.BlockSpec((C // 2, C), lambda m, *_: (place, 0)))] * 2

    def add_halves(self, meta, m, grad, total, kept_out, away_out):
        @pl.when(m == 0)
        def _():
            total[...] = grad

        @pl.when(m > 0)
        def _():
            top, bottom = total[0 : C // 2] + grad[0 : C // 2], total[C // 2 : C] + grad[C // 2 : C]
            lower = meta[2 * OWN] == 1
            kept_out[...] = jnp.where(lower, top, bottom)
            away_out[...] = jnp.where(lower, bottom, top)

    def weight_grad(self, i, dz):
        two = self.two
        strided = i == 4 and not two
        rows = self.rows_of(i)
        n_src = len(self.source_args())

        def body(meta, *refs):
            refs = list(refs)
            take = lambda n: [refs.pop(0) for _ in range(n)]
            m = pl.program_id(0)
            if i:
                zp_ref, statp, gain, bias = take(4)
                center, spread = statp[0, 0:1], statp[0, 1:2]
                scale = gain[i - 1 : i] * spread
                shift = bias[i - 1 : i] - center * scale
            else:
                src = take(n_src)
            dz_ref, dw_ref, kept_out, away_out, pad, yh, yl, total = take(8)
            alt, = take(1) if strided else (None,)
            valid_in = self.valid(meta, m, 0)
            for c, cs in enumerate(CHUNKS):
                if i:
                    u = zp_ref[0, :, cs] * scale[:, cs] + shift[:, cs]
                    h = valid_in.keep(u * sigmoid(u))
                else:
                    h = valid_in.keep(self.source(meta, src, cs))
                padded = Padded(pad.at[c], two)
                padded.put(h)
                y = padded.conv(dw_ref[0, :, cs])
                if strided:
                    y = every_other(alt.at[c], y)
                yh[:, cs], yl[:, cs] = halves(y)
            grad = stacked_outer(yh[...], yl[...], dz_ref[0, :, 0:C], dz_ref[0, :, C : 2 * C])
            self.add_halves(meta, m, grad, total, kept_out, away_out)

        args = self.before_args(i)
        if i:
            args += [(self.gain, whole(6, C)), (self.bias, whole(6, C))]
        args += [(dz, slots(rows, 2 * C)), (self.dw, layer(i, TAPS, C))]
        scratch = [pad_scratch(), pltpu.VMEM((rows, C), BF16), pltpu.VMEM((rows, C), BF16), pltpu.VMEM((C, C), F32)]
        if strided:
            scratch.append(stride_scratch())
        which = PLACES[i][0]
        self.pieces[which] = call(
            body, self.meta, args, self.piece_out(i), scratch, f"{self.tag}_weights_{i}", 6 * OWN * rows * C * C,
            into=self.pieces[which],
        )
        self.done = (self.pieces[which][0],)

    def backward(self, layers):
        if layers[0] == 4:
            self.pieces = [[], []]
        for i in layers:
            result = self.backward_layer(i)
        return result

    def resume(self, i):
        dz, payload = self.pending
        self.back_got = shared(payload, self.stages)
        self.weight_grad(i, dz)

    def fork(self, state=None):
        other = copy.copy(self)
        other.__dict__.update(state or {})
        if "pieces" in other.__dict__:
            other.pieces = list(other.pieces)
        return other

    def state(self):
        return {name: getattr(self, name) for name in ("du", "dxr", "pieces", "small", "pending")}

    def half(self, no, first, begin=None, end=None):
        kept, away = self.pieces[no]
        if no:
            parts = self.small[: SMALL // 2], self.small[SMALL // 2 :]
            at = kept.shape[0] - SMALL // 2
            kept = lax.dynamic_update_slice_in_dim(kept, jnp.where(first, *parts), at, 0)
            away = lax.dynamic_update_slice_in_dim(away, jnp.where(first, *parts[::-1]), at, 0)
        if begin is not None:
            away, _ = lax.optimization_barrier((away, begin))
            kept, _ = lax.optimization_barrier((kept, end))
        return kept + swap(away)


PLACES = {3: (0, 0), 4: (0, 1), 5: (0, 2), 0: (1, 0), 1: (1, 1), 2: (1, 2)}
PIECE_ROWS = (3 * C // 2, 3 * C // 2 + SMALL // 2)


def pick_joining(picks, features):
    def body(picks, in_ref, out_ref):
        out_ref[...] = in_ref[0, 0]

    own = pl.BlockSpec((1, 1, HALF, C), lambda m, picks: (picks[m], 1, 0, 0))
    out = (f32(OWN * HALF, C), pl.BlockSpec((HALF, C), lambda m, *_: (m, 0)))
    return call(body, picks, [(features, own)], [out], name="pick_joining")[0]


def swap(x):
    return lax.ppermute(x, "section", [(0, 1), (1, 0)])


def fenced(always, work, x):
    shapes = jax.eval_shape(work, x)
    return lax.cond(always, work, lambda x: jax.tree.map(lambda y: jnp.zeros(y.shape, y.dtype), shapes), x)


class Reduction:
    def __init__(self, x, stages):
        self.x = x
        self.todo = []
        stride = 1
        for radix in stages:
            self.todo.append((True, radix, stride))
            stride *= radix
        self.todo += [(False, radix, stride) for _, radix, stride in reversed(self.todo)]

    def step(self):
        scatter, radix, stride = self.todo.pop(0)
        rows = self.x.shape[0]
        if scatter:
            parts = exchange(self.x.reshape(radix, rows // radix, C), radix, stride)
            self.x = jnp.sum(parts, axis=0)
        else:
            parts = exchange(jnp.broadcast_to(self.x, (radix,) + self.x.shape), radix, stride)
            self.x = parts.reshape(radix * rows, C)
        return (self.x,)

    def finish(self):
        while self.todo:
            self.step()
        return self.x


def per_device(features, out_grad, lengths, join_pick, dw, pw, gain, bias, res_w, down, down_b, up, up_b):
    first = lax.axis_index("section") == 0
    size = lax.axis_size("dp")
    inputs = features.reshape(MB, SLOT, C)
    cotangent = out_grad.reshape(MB, SLOT, C)
    own, picks = lengths[0, 0], join_pick[0]
    to_upper = lambda x: lax.ppermute(x, "section", [(0, 1)])
    to_lower = lambda x: lax.ppermute(x, "section", [(1, 0)])

    far_len = swap(own)
    far_rows = to_upper(inputs[MB - 1])
    far_w0 = swap(pw[0, 0:1])
    taps = jnp.concatenate([dw[0].reshape(5 * TAPS, C), gain[0], bias[0]], axis=0)
    far_taps = swap(taps)
    far_pw, far_res = swap(pw[0]), swap(res_w[0])
    wide = jnp.pad(down_b, ((0, 0), (0, C - SE)))
    squeeze = jnp.concatenate([down[0].T, up[0], up_b, wide], axis=0)
    far_squeeze = swap(squeeze)
    far_cot = swap(cotangent)

    flag = first.astype(jnp.int32)[None]
    mine = lambda v: jnp.where(first, v[:OWN], jnp.concatenate([v[OWN:], jnp.zeros((1,), v.dtype)]))
    length = mine(jnp.where(first, own, far_len))
    half_len = (length + 1) // 2
    join_len = mine(jnp.where(first, far_len, own)[picks])
    meta1 = jnp.concatenate([length, half_len, flag])
    meta2 = jnp.concatenate([half_len, join_len, flag, picks[MB - 1 :]])

    def small(block):
        t = jnp.where(first == (block == 0), taps, far_taps)
        q = jnp.where(first == (block == 0), squeeze, far_squeeze)
        return (
            t[: 5 * TAPS].reshape(5, TAPS, C), t[5 * TAPS : 5 * TAPS + 6], t[5 * TAPS + 6 :],
            q[:SE], q[2 * SE + 1, :SE][:, None], q[SE : 2 * SE], q[2 * SE : 2 * SE + 1],
        )

    def prepared(block, start, stop):
        array = prepare(meta1, (pw[0], res_w[0]), (far_pw, far_res), block, start, stop)
        return array, {i: (array, i - start) for i in range(start, stop)}

    parts0 = [prepared(0, 1, 3), prepared(0, 3, 6)]
    parts1 = [prepared(1, 0, 1), prepared(1, 1, 4), prepared(1, 4, 6)]

    stages, deep = radices(size, 16), radices(size, 4)
    c14 = Block(False, meta1, small(0), {**parts0[0][1], **parts0[1][1]}, stages)
    c14.x, c14.x_far, c14.first_matrix = inputs, far_rows, (pw[0], far_w0)
    c14.forward({2: (parts0[1][0],)})
    late_picks, _ = lax.optimization_barrier((picks, c14.z[3]))
    far_joining = to_lower(pick_joining(late_picks, features.reshape(MB, 2, HALF, C)))
    c15 = Block(True, meta2, small(1), {**parts1[0][1], **parts1[1][1], **parts1[2][1]}, stages)
    c15.arrived, c15.joined_far, c15.joined = Linked(0, HALF), far_joining, features.reshape(MB, 2, HALF, C)
    c15.start()
    out0, _ = run_joined(c14.tail_steps(), c15.forward_steps(0))
    c15.arrived = out0
    c15.forward({1: (parts1[1][0],), 2: (parts1[2][0],)}, joined=True)
    out1 = c15.tail(cotangent, far_cot)
    c15.stop = 2
    c15.backward((4, 3))
    begin = c15.back_got
    c15.backward((2,))
    always = own[0] > 0

    half0 = c15.half(0, first, begin, c15.du)
    sum0 = lax.psum(half0, "dp")

    def middle(half0):
        upper, lower = c15.fork(), c14.fork()
        upper.resume(2)
        upper.done += (half0,)
        upper.backward((1,))
        (_, dx1), _ = run_joined(
            upper.backward_steps(0), lower.tail_backward_steps(cotangent, far_cot, Linked(2, HALF))
        )
        lower.done = upper.done
        lower.backward((4,))
        begin1 = lower.back_got
        lower.backward((3,))
        half1 = upper.half(1, first, begin1, lower.du)
        begin2 = lower.back_got
        lower.stop = 2
        lower.backward((2,))
        half2 = lower.half(0, first, begin2, lower.du)
        return dx1, half1, half2, lower.state()

    dx1, half1, half2, state = fenced(always, middle, half0)
    sum0, half2 = lax.optimization_barrier((sum0, half2))
    sum1, sum2 = lax.psum((half1, half2), "dp")

    def ending(half2):
        last = c14.fork(state)
        last.resume(2)
        last.done += (half2,)
        came0 = to_upper(sum0)
        dx0, = last.backward((1, 0))
        half3 = last.half(1, first)
        half3, dx0, *kept = lax.optimization_barrier((half3, dx0, out0, out1, dx1))
        reduction = Reduction(half3, deep)
        reduction.step()
        pad = jnp.zeros((1, HALF, C), F32)
        lower = jnp.concatenate([kept[0], jnp.concatenate([to_lower(kept[0][0:1, :HALF]), pad], axis=1)], axis=0)
        upper = jnp.concatenate([to_upper(kept[1]), kept[1][0:1]], axis=0)
        block_out = jnp.where(first, lower, upper)
        lower = jnp.concatenate([dx0, to_lower(dx0[0:1])], axis=0)
        joins = jnp.concatenate([to_upper(kept[2]), kept[2][0:1]], axis=0)
        joins = jnp.stack([lax.dynamic_index_in_dim(joins, jnp.argmax(picks == s), 0, False) for s in range(MB)])
        upper = jnp.concatenate([jnp.zeros_like(joins), joins], axis=1)
        dx = jnp.where(first, lower, upper)
        reduction.x, block_out, dx, came0 = lax.optimization_barrier((reduction.x, block_out, dx, came0))
        return block_out, dx, came0, reduction.finish()

    block_out, dx, came0, sum3 = fenced(always, ending, half2)
    came3 = to_lower(sum3)
    sum1, sum2, _ = lax.optimization_barrier((sum1, sum2, sum3))
    came1, came2 = to_upper(sum1), to_lower(sum2)

    lead = 3 * C // 2

    def joined(near, far):
        pair = [x.reshape(-1, 1, C // 2, C) for x in (near, far)]
        both = jnp.where(first, jnp.concatenate(pair, axis=1), jnp.concatenate(pair[::-1], axis=1))
        return both.reshape(-1, C, C)

    choose_mine = lambda a, b: jnp.where(first, a, b)
    rest_part = joined(choose_mine(sum3[:lead], sum1[:lead]), choose_mine(came3[:lead], came1[:lead]))
    lead_part = joined(choose_mine(sum2[:C], sum0[:C]), choose_mine(came2[:C], came0[:C]))
    pw_grad = jnp.concatenate([rest_part, lead_part], axis=0)[None]
    res_grad = joined(choose_mine(sum2[C:], sum0[C:]), choose_mine(came2[C:], came0[C:]))
    near, far = choose_mine(sum3[lead:], sum1[lead:]), choose_mine(came3[lead:], came1[lead:])
    rows = jnp.where(first, jnp.concatenate([near, far], axis=0), jnp.concatenate([far, near], axis=0))
    dw_grad = rows[TAIL_ROWS : TAIL_ROWS + 40].reshape(1, 5, 8, C)
    norms = jnp.concatenate([dw_grad[0, 1:, TAPS : TAPS + 2], rows[None, 2 * SE + 2 : 2 * SE + 4], rows[None, 2 * SE + 4 : 2 * SE + 6]], axis=0)
    return (
        block_out.reshape(features.shape), dx.reshape(features.shape), dw_grad[:, :, :TAPS], pw_grad,
        norms[None, :, 1], norms[None, :, 0], res_grad, rows[SE : 2 * SE].T[None], rows[2 * SE + 1 : 2 * SE + 2, :SE],
        rows[:SE][None], rows[2 * SE : 2 * SE + 1],
    )


def solution(mesh):
    rows = P("section", "dp", None)
    own = lambda dims: P("section", *([None] * dims))
    weights = (own(3), own(3), own(2), own(2), own(2), own(2), own(1), own(2), own(1))
    in_specs = (rows, rows, rows, P("dp", None), *weights)
    out_specs = (rows, rows, *weights)
    return jax.shard_map(per_device, mesh=mesh, in_specs=in_specs, out_specs=out_specs, check_vma=False)
```

```python
import copy

import jax
import jax.numpy as jnp
from jax import lax
from jax.experimental import pallas as pl
from jax.experimental.pallas import tpu as pltpu
from jax.sharding import PartitionSpec as P

EPSILON = 1e-05
EXACT = lax.Precision.HIGHEST
TAPS = 5
MB = 3
OWN = 2
SLOT = 400
HALF = 200
KEPT = 208
C = 512
LANES = 128
CHUNKS = [slice(c, c + LANES) for c in range(0, C, LANES)]
SE = 64
BF16, F32 = jnp.bfloat16, jnp.float32
VMEM_BYTES = 60 << 20
TAIL_ROWS = 2 * SE + 8
SMALL = 256


def radices(size, most):
    stages, left = [], size
    while left > 1:
        radix = min(most, left)
        while left % radix:
            radix -= 1
        stages.append(radix)
        left //= radix
    return stages


def exchange(block, radix, stride):
    size = lax.axis_size("dp")
    if radix == size:
        return lax.all_to_all(block, "dp", 0, 0)
    groups = []
    for base in range(size):
        if (base // stride) % radix == 0:
            groups.append([base + j * stride for j in range(radix)])
    return lax.all_to_all(block, "dp", 0, 0, axis_index_groups=groups)


def shared(block, stages):
    stride = 1
    for no, radix in enumerate(stages):
        if no:
            block = jnp.broadcast_to(jnp.sum(block, axis=0), (radix,) + block.shape[1:])
        block = exchange(block, radix, stride)
        stride *= radix
    return block


def halves(x):
    high = x.astype(BF16)
    return high, (x - high.astype(F32)).astype(BF16)


def sigmoid(x):
    return 0.5 * jnp.tanh(0.5 * x) + 0.5


def exact_dot(a, b, dims=((1,), (0,))):
    return lax.dot_general(a, b, (dims, ((), ())), precision=EXACT, preferred_element_type=F32)


def fast_dot(a, b, dims=((1,), (0,))):
    return lax.dot_general(a, b, (dims, ((), ())), preferred_element_type=F32)


def stacked_dot(high, low, w, back=False):
    w_high, w_low = w[0], w[1]
    w = jnp.concatenate([w_high, w_high, w_low], axis=1 if back else 0)
    x = jnp.concatenate([high, low, high], axis=1)
    return fast_dot(x, w, ((1,), (1 if back else 0,)))


def stacked_outer(a_high, a_low, b_high, b_low):
    a = jnp.concatenate([a_high, a_low, a_high], axis=0)
    b = jnp.concatenate([b_high, b_high, b_low], axis=0)
    return fast_dot(a, b, ((0,), (0,)))


def column_sum(x):
    return jnp.sum(x, axis=0, keepdims=True)


class Rows:
    def __init__(self, meta, m, two, rows, which=0):
        place = lax.broadcasted_iota(jnp.int32, (rows, LANES), 0)
        if two:
            later = place >= HALF
            limit = jnp.where(later, HALF + meta[OWN + m], meta[m])
            self.mask = place < limit
        else:
            self.mask = place < meta[which * OWN + m]

    def keep(self, x):
        return jnp.where(self.mask, x, 0.0)


class Padded:
    def __init__(self, ref, two):
        self.ref = ref
        self.pieces = [(8, 0, HALF), (16 + HALF, HALF, HALF)] if two else [(8, 0, SLOT)]

    def put(self, x):
        zeros = jnp.zeros((8, LANES), F32)
        for at, start, rows in self.pieces:
            self.ref[at - 8 : at, :] = zeros
            self.ref[at : at + rows, :] = x[start : start + rows]
        self.ref[at + rows : at + rows + 8, :] = zeros

    def get(self, offset):
        parts = [self.ref[at + offset : at + offset + rows, :] for at, _, rows in self.pieces]
        return parts[0] if len(parts) == 1 else jnp.concatenate(parts, axis=0)

    def conv(self, kernel):
        total = kernel[0:1] * self.get(-2)
        for k in range(1, TAPS):
            total = total + kernel[k : k + 1] * self.get(k - 2)
        return total

    def conv_back(self, kernel):
        total = kernel[0:1] * self.get(2)
        for k in range(1, TAPS):
            total = total + kernel[k : k + 1] * self.get(2 - k)
        return total


def every_other(ref, x):
    ref[0:SLOT, :] = x
    ref[SLOT : 2 * KEPT, :] = jnp.zeros((2 * KEPT - SLOT, LANES), F32)
    return ref[pl.ds(0, KEPT, stride=2), :]


def spread_out(ref, x):
    ref[...] = jnp.zeros_like(ref)
    ref[pl.ds(0, KEPT, stride=2), :] = x
    return ref[0:SLOT, :]


def center_spread(sums, rows):
    center = sums[0:1] / rows
    return center, lax.rsqrt(sums[1:2] / rows - center * center + EPSILON)


def added(ref):
    return jnp.sum(ref[:, 0], axis=0)


def accumulate(ref, m, at, value):
    rows = slice(at, at + value.shape[0])
    ref[rows, :] = jnp.where(m == 0, value, ref[rows, :] + value)


def send(ref, rows):
    for copy in range(ref.shape[0]):
        for row, x in enumerate(rows):
            ref[copy, 0, row : row + 1, 0 : x.shape[1]] = x


def pad_scratch():
    return pltpu.VMEM((len(CHUNKS), SLOT + 24, LANES), F32)


def stride_scratch():
    return pltpu.VMEM((len(CHUNKS), 2 * KEPT, LANES), F32)


def slots(rows, cols=C):
    return pl.BlockSpec((1, rows, cols), lambda m, *_: (m, 0, 0))


def copies(count, rows, cols=C):
    return pl.BlockSpec((count, 1, rows, cols), lambda m, *_: (0, m, 0, 0))


def whole(*shape):
    return pl.BlockSpec(shape, lambda m, *_: (0,) * len(shape))


def layer(i, *shape):
    return pl.BlockSpec((1,) + shape, lambda m, *_: (i,) + (0,) * len(shape))


def f32(*shape):
    return jax.ShapeDtypeStruct(shape, F32)


def bf16(*shape):
    return jax.ShapeDtypeStruct(shape, BF16)


def call(body, meta, args, outs, scratch=(), name=None, flops=0, steps=OWN, after=(), into=()):
    arrays, in_specs = [a for a, _ in args], [s for _, s in args]
    shapes, out_specs = [a for a, _ in outs], [s for _, s in outs]
    size = sum(a.size * a.dtype.itemsize for a in arrays + shapes)
    extra = list(after) + list(into)
    count = len(arrays)

    def inner(meta, *refs):
        body(meta, *refs[:count], *refs[count + len(extra) :])

    return pl.pallas_call(
        inner,
        out_shape=shapes,
        grid_spec=pltpu.PrefetchScalarGridSpec(
            num_scalar_prefetch=1,
            grid=(steps,),
            in_specs=in_specs + [pl.BlockSpec(memory_space=pl.ANY)] * len(extra),
            out_specs=out_specs,
            scratch_shapes=list(scratch),
        ),
        input_output_aliases={1 + count + len(after) + j: j for j in range(len(into))},
        compiler_params=pltpu.CompilerParams(vmem_limit_bytes=VMEM_BYTES),
        cost_estimate=pl.CostEstimate(flops=flops, bytes_accessed=size, transcendentals=0),
        name=name,
    )(meta, *arrays, *extra)


class Linked:
    def __init__(self, index, rows):
        self.index, self.rows = index, rows


class Part:
    def __init__(self, ref, at):
        self.ref, self.at = ref, at

    def __getitem__(self, index):
        return self.ref[self.at + index]


def run(steps):
    body, meta, args, outs, scratch, name, flops, after, into = next(steps)
    return finish(steps, call(body, meta, args, outs, scratch, name, flops, after=after, into=into))


def finish(steps, results):
    try:
        steps.send(results)
    except StopIteration as stop:
        return stop.value


def run_joined(one, two, scalars):
    meta, at1, at2 = scalars
    body1, _, args1, outs1, scratch1, name1, flops1, after1, into1 = next(one)
    body2, _, args2, outs2, scratch2, name2, flops2, after2, into2 = next(two)
    assert not into2
    own2 = [arg for arg in args2 if not isinstance(arg[0], Linked)]
    sizes = len(args1), len(own2), len(outs1), len(outs2), len(scratch1), len(scratch2)

    def body(meta, *refs):
        refs = list(refs)
        in1, in2, out1, out2, scr1, scr2 = [[refs.pop(0) for _ in range(n)] for n in sizes]
        body1(Part(meta, at1), *in1, *out1, *scr1)
        linked = []
        for arg in args2:
            link = arg[0]
            linked.append(out1[link.index].at[:, 0 : link.rows, :] if isinstance(link, Linked) else in2.pop(0))
        body2(Part(meta, at2), *linked, *out2, *scr2)

    def moved(spec, at):
        if spec.index_map is None:
            return spec
        return pl.BlockSpec(spec.block_shape, lambda m, meta: spec.index_map(m, Part(meta, at)))

    args = [(a, moved(spec, at1)) for a, spec in args1] + [(a, moved(spec, at2)) for a, spec in own2]
    results = call(
        body, meta, args, [(a, moved(spec, at1)) for a, spec in outs1] + [(a, moved(spec, at2)) for a, spec in outs2], list(scratch1) + list(scratch2), f"{name1}_{name2}", flops1 + flops2,
        after=(*after1, *after2), into=into1,
    )
    return finish(one, results[: len(outs1)]), finish(two, results[len(outs1) :])


def choose(meta, block, own, far):
    return jnp.where(meta[2 * OWN] == 1 - block, own, far)


def prepare(meta, own, far, block, start, stop):
    def body(meta, *refs):
        pair = [ref[0] for ref in refs[:2]]
        if stop == 6:
            last = pl.program_id(0) == 5 - start
            pair = [jnp.where(last, ref[...], w) for ref, w in zip(refs[2:4], pair)]
        out = refs[-1]
        out[0, 0], out[0, 1] = halves(choose(meta, block, *pair))

    matrix = pl.BlockSpec((1, C, C), lambda j, *_: (jnp.minimum(j + start, 4), 0, 0))
    args = [(own[0], matrix), (far[0], matrix)]
    if stop == 6:
        args += [(own[1], whole(C, C)), (far[1], whole(C, C))]
    out = pl.BlockSpec((1, 2, C, C), lambda j, *_: (j, 0, 0, 0))
    name = f"prepare_{block}_{start}"
    return call(body, meta, args, [(bf16(stop - start, 2, C, C), out)], name=name, steps=stop - start)[0]


class Block:
    def __init__(self, two, meta, weights, ready, stages):
        self.done, self.stop, self.pending = (), None, None
        self.two, self.meta, self.stages = two, meta, stages
        self.dw, self.gain, self.bias = weights
        self.ready = ready
        self.tail_rows = SLOT if two else KEPT
        self.first, self.last = stages[0], stages[-1]
        self.tag = "c15" if two else "c14"

    def rows_of(self, i):
        return self.tail_rows if i == 4 else SLOT

    def valid(self, meta, m, i):
        last = i == 4 and not self.two
        return Rows(meta, m, self.two, self.rows_of(i), which=1 if last else 0)

    def matrix(self, i):
        array, at = self.ready[i]
        return (array, layer(at, 2, C, C))

    def source_args(self):
        if not self.two:
            return [(self.x, slots(SLOT)), (self.x_far, whole(SLOT, C))]
        far = pl.BlockSpec((HALF, C), lambda m, *_: (m, 0))
        near = pl.BlockSpec((1, 1, HALF, C), lambda m, meta: (meta[2 * OWN + 1], 1, 0, 0))
        return [(self.arrived, slots(HALF)), (self.joined_far, far), (self.joined, near)]

    def source(self, meta, refs, cs):
        lower = meta[2 * OWN] == 1
        if not self.two:
            return jnp.where(lower, refs[0][0, :, cs], refs[1][:, cs])
        joined = jnp.where(lower, refs[1][:, cs], refs[2][0, 0, :, cs])
        return jnp.concatenate([refs[0][0, :, cs], joined], axis=0)

    def before_args(self, i):
        if i == 0:
            return self.source_args()
        return [(self.z[i - 1], slots(SLOT)), (self.stats[i - 1], slots(2))]


    def forward_layer(self, i, after=()):
        return run(self.forward_steps(i, after))

    def forward_steps(self, i, after=()):
        two, count = self.two, self.first
        strided = i == 4 and not two
        rows = self.rows_of(i)
        n_src = len(self.source_args())
        width = C + LANES if i == 0 else C
        sent = 4 if i == 3 else 2
        makes = i == 0 and not two

        def body(meta, *refs):
            refs = list(refs)
            take = lambda n: [refs.pop(0) for _ in range(n)]
            m = pl.program_id(0)
            if i == 0:
                src = take(n_src)
            else:
                z_ref, got_ref = take(2)
                n_ref, = take(1) if i > 1 else (None,)
                gain_ref, bias_ref = take(2)
                res_sum, = take(1) if i == 3 else (None,)
            dw_ref, = take(1)
            if makes:
                own_ref, far_ref, z_out, pay, w_ref = take(5)

                @pl.when(m == 0)
                def _():
                    w_ref[0, 0], w_ref[0, 1] = halves(choose(meta, 0, own_ref[0], far_ref[0]))

            else:
                w_ref, z_out, pay = take(3)
            if i:
                stat_out, = take(1)
            if i == 1:
                n_out, = take(1)
            pad, y_ref = take(2)
            alt, = take(1) if strided else (None,)
            valid_in = self.valid(meta, m, 0)
            if i:
                sums = added(got_ref)
                if i == 1:
                    count_in = jnp.maximum(jnp.concatenate([sums[0:1, C:]] * len(CHUNKS), axis=1), 1.0)
                    count_out = jnp.maximum(jnp.concatenate([sums[1:2, C:]] * len(CHUNKS), axis=1), 1.0)
                    n_out[0, 0:1, :] = count_in
                    n_out[0, 1:2, :] = count_out
                else:
                    count_in = n_ref[0, 0:1, :]
                center, spread = center_spread(sums[:, :C], count_in)
                stat_out[0, 0:1, :] = center
                stat_out[0, 1:2, :] = spread
                scale = gain_ref[i - 1 : i] * spread
                shift = bias_ref[i - 1 : i] - center * scale
            for c, cs in enumerate(CHUNKS):
                if i == 0:
                    h = valid_in.keep(self.source(meta, src, cs))
                else:
                    u = z_ref[0, :, cs] * scale[:, cs] + shift[:, cs]
                    h = valid_in.keep(u * sigmoid(u))
                padded = Padded(pad.at[c], two)
                padded.put(h)
                y = padded.conv(dw_ref[0, :, cs])
                if strided:
                    y = every_other(alt.at[c], y)
                high, low = halves(y)
                y_ref[:, cs] = high
                y_ref[:, C + cs.start : C + cs.stop] = low
            w = w_ref.at[0] if makes else w_ref.at[0]
            z = stacked_dot(y_ref[:, 0:C], y_ref[:, C : 2 * C], w)
            z_out[0] = z
            valid = self.valid(meta, m, i)
            one, square = [], []
            for cs in CHUNKS:
                kept = valid.keep(z[:, cs])
                one.append(column_sum(kept))
                square.append(column_sum(kept * kept))
            if i == 0:
                if two:
                    number = (meta[m] + meta[OWN + m]).astype(F32)
                    numbers = number, number
                else:
                    numbers = meta[m].astype(F32), meta[OWN + m].astype(F32)
                one.append(jnp.full((1, LANES), numbers[0], F32))
                square.append(jnp.full((1, LANES), numbers[1], F32))
            out = [jnp.concatenate(one, axis=1), jnp.concatenate(square, axis=1)]
            if i == 3:
                out += [res_sum[0, 0:1, :], res_sum[0, 1:2, :]]
            send(pay, out)

        if i == 0:
            args = list(self.source_args())
        else:
            got = 4 if i == 4 else 2
            args = [(self.z[i - 1], slots(SLOT)), (self.got[i - 1], copies(self.last, got, C + LANES if i == 1 else C))]
            if i > 1:
                args.append((self.number, slots(2)))
            args += [(self.gain, whole(6, C)), (self.bias, whole(6, C))]
            if i == 3:
                args.append((self.res_sum, slots(2)))
        args.append((self.dw, layer(i, TAPS, C)))
        args += [(w, layer(0, C, C)) for w in self.first_matrix] if makes else [self.matrix(i)]
        outs = [(f32(OWN, rows, C), slots(rows)), (f32(count, OWN, sent, width), copies(count, sent, width))]
        if i:
            outs.append((f32(OWN, 2, C), slots(2)))
        if i == 1:
            outs.append((f32(OWN, 2, C), slots(2)))
        if makes:
            outs.append((bf16(1, 2, C, C), layer(0, 2, C, C)))
        scratch = [pad_scratch(), pltpu.VMEM((rows, 2 * C), BF16)]
        if strided:
            scratch.append(stride_scratch())
        flops = 6 * OWN * rows * C * C
        result = yield body, self.meta, args, outs, scratch, f"{self.tag}_forward_{i}", flops, after, ()
        self.z.append(result[0])
        if makes:
            self.ready[0] = (result[2], 0)
        if i:
            self.stats.append(result[2])
        if i == 1:
            self.number = result[3]
        self.got.append(shared(result[1], self.stages))

    def residual(self):
        two, rows = self.two, self.tail_rows

        def body(meta, *refs):
            refs = list(refs)
            src = [refs.pop(0) for _ in self.source_args()]
            w_ref, r_out, x_out, sum_out = refs[:4]
            alt = refs[4] if not two else None
            m = pl.program_id(0)
            valid_in = self.valid(meta, m, 0)
            for c, cs in enumerate(CHUNKS):
                x = valid_in.keep(self.source(meta, src, cs))
                if not two:
                    x = every_other(alt.at[c], x)
                high, low = halves(x)
                x_out[0, :, cs] = high
                x_out[0, :, C + cs.start : C + cs.stop] = low
            r = stacked_dot(x_out[0, :, 0:C], x_out[0, :, C : 2 * C], w_ref.at[0])
            r_out[0] = r
            valid = self.valid(meta, m, 4)
            for cs in CHUNKS:
                kept = valid.keep(r[:, cs])
                sum_out[0, 0:1, cs] = column_sum(kept)
                sum_out[0, 1:2, cs] = column_sum(kept * kept)

        args = self.source_args() + [self.matrix(5)]
        outs = [
            (f32(OWN, rows, C), slots(rows)),
            (bf16(OWN, rows, 2 * C), slots(rows, 2 * C)),
            (f32(OWN, 2, C), slots(2)),
        ]
        scratch = [] if two else [stride_scratch()]
        self.r, self.picked, self.res_sum = call(
            body, self.meta, args, outs, scratch, f"{self.tag}_residual", 6 * OWN * rows * C * C
        )

    def start(self):
        self.z, self.got, self.stats = [], [], []

    def forward(self, after=None, joined=False):
        if not joined:
            self.start()
        for i in range(1 if joined else 0, 5):
            if i == 2:
                self.residual()
            self.forward_layer(i, (after or {}).get(i, ()))


    def segments(self):
        return [(0, HALF), (HALF, HALF)] if self.two else [(0, self.tail_rows)]

    def lengths(self, meta, m):
        if self.two:
            return [meta[m], meta[OWN + m]]
        return [meta[OWN + m]]

    def squeeze(self, sums, counts, se_refs):
        down_t, down_b, up, up_b = se_refs
        means = [s / jnp.maximum(jnp.full((1, C), n.astype(F32)), 1.0) for s, n in zip(sums, counts)]
        ps = [jnp.sum(down_t[...] * mean, axis=1, keepdims=True) + down_b[...] for mean in means]
        gates = [sigmoid(column_sum(up[...] * (p * sigmoid(p))) + up_b[...]) for p in ps]
        return means, ps, gates

    def squeeze_back(self, des, ps, gates, counts, se_refs, means, small, m):
        down_t, down_b, up, up_b = se_refs
        shares, up_grad, down_grad, dq_sum, dp_sum = [], 0.0, 0.0, 0.0, 0.0
        for de, p, gate, n, mean in zip(des, ps, gates, counts, means):
            dq = de * gate * (1.0 - gate)
            s = sigmoid(p)
            dp = jnp.sum(up[...] * dq, axis=1, keepdims=True) * (s * (1.0 + p * (1.0 - s)))
            shares.append(column_sum(down_t[...] * dp) / jnp.maximum(jnp.full((1, C), n.astype(F32)), 1.0))
            up_grad, down_grad = up_grad + (p * s) * dq, down_grad + dp * mean
            dq_sum, dp_sum = dq_sum + dq, dp_sum + dp
        row, col = (lax.broadcasted_iota(jnp.int32, (SE, C), axis) for axis in (0, 1))
        dp_row = column_sum(jnp.where(row == col, dp_sum, 0.0))
        accumulate(small, m, 0, up_grad)
        accumulate(small, m, SE, down_grad)
        accumulate(small, m, 2 * SE, dq_sum)
        accumulate(small, m, 2 * SE + 1, dp_row)
        return shares

    def last_norm(self, m, dt_out, du_out, z_ref, slope_ref, gates, shares, center, spread, res_bias, res_gain, pay, small):
        bias_sum, gain_sum = [], []
        for cs in CHUNKS:
            dh = dt_out[0, :, cs] * self.by_segment(gates, cs) + self.by_segment(shares, cs)
            du = dh * slope_ref[:, cs]
            du_out[0, :, cs] = du
            bias_sum.append(column_sum(du))
            gain_sum.append(column_sum(du * ((z_ref[0, :, cs] - center[:, cs]) * spread[:, cs])))
        rows = [jnp.concatenate(x, axis=1) for x in (bias_sum, gain_sum, res_bias, res_gain)]
        send(pay, rows)
        for j, row in enumerate(rows):
            accumulate(small, m, 2 * SE + 2 + j, row)

    def se_args(self):
        return list(zip(self.excitation, (whole(SE, C), whole(SE, 1), whole(SE, C), whole(1, C))))

    def store_rows(self, ref, rows):
        ref[0] = jnp.concatenate(rows + [jnp.zeros((8 - len(rows), C), F32)], axis=0)

    def store_columns(self, ref, columns):
        ref[0] = jnp.zeros((SE, 8), F32)
        for j, column in enumerate(columns):
            ref[0, :, j : j + 1] = column

    def by_segment(self, rows, cs):
        parts = [jnp.broadcast_to(row[:, cs], (n, LANES)) for row, (_, n) in zip(rows, self.segments())]
        return parts[0] if len(parts) == 1 else jnp.concatenate(parts, axis=0)

    def seg_sums(self, x):
        return [column_sum(x[at : at + n]) for at, n in self.segments()]

    def tail(self, cotangent=None, far=None, after=()):
        return run(self.tail_steps(cotangent, far, after))

    def tail_steps(self, cotangent=None, far=None, after=()):
        two, rows = self.two, self.tail_rows
        back = cotangent is not None

        def body(meta, *refs):
            refs = list(refs)
            take = lambda n: [refs.pop(0) for _ in range(n)]
            m = pl.program_id(0)
            z_ref, got4, r_ref, got3, n_ref, gain, bias = take(7)
            se_refs = take(4)
            if back:
                cot_ref, far_ref = take(2)
            out, stat_out, rstat_out, means_out, p_out, gate_out = take(6)
            if back:
                small, du_out, dt_out, pay = take(4)
            h_ref, = take(1)
            if back:
                slope_ref, = take(1)
            valid = self.valid(meta, m, 4)
            number = n_ref[0, 1:2, :]
            center, spread = center_spread(added(got4), number)
            rcenter, rspread = center_spread(added(got3)[2:4], number)
            stat_out[0, 0:1, :] = center
            stat_out[0, 1:2, :] = spread
            rstat_out[0, 0:1, :] = rcenter
            rstat_out[0, 1:2, :] = rspread
            scale = gain[4:5] * spread
            shift = bias[4:5] - center * scale
            sums = []
            for cs in CHUNKS:
                u = z_ref[0, :, cs] * scale[:, cs] + shift[:, cs]
                s = sigmoid(u)
                h = valid.keep(u * s)
                h_ref[:, cs] = h
                if back:
                    slope_ref[:, cs] = valid.keep(s * (1.0 + u * (1.0 - s)))
                sums.append(self.seg_sums(h))
            sums = [jnp.concatenate([s[j] for s in sums], axis=1) for j in range(len(self.segments()))]
            counts = self.lengths(meta, m)
            means, ps, gates = self.squeeze(sums, counts, se_refs)
            self.store_rows(means_out, means)
            self.store_columns(p_out, ps)
            self.store_rows(gate_out, gates)
            res_gain, res_bias, gate_grad = [], [], []
            for cs in CHUNKS:
                h = h_ref[:, cs]
                rh = (r_ref[0, :, cs] - rcenter[:, cs]) * rspread[:, cs]
                t = h * self.by_segment(gates, cs) + gain[5:6, cs] * rh + bias[5:6, cs]
                s = sigmoid(t)
                out[0, 0:rows, cs] = valid.keep(t * s)
                if rows < SLOT:
                    out[0, rows:SLOT, cs] = jnp.zeros((SLOT - rows, LANES), F32)
                if back:
                    cot = jnp.where(meta[2 * OWN] == 1, far_ref[0, :, cs], cot_ref[0, :, cs])
                    dt = valid.keep(cot * (s * (1.0 + t * (1.0 - s))))
                    dt_out[0, :, cs] = dt
                    res_bias.append(column_sum(dt))
                    res_gain.append(column_sum(dt * rh))
                    gate_grad.append(self.seg_sums(dt * h))
            if not back:
                return
            des = [jnp.concatenate([g[j] for g in gate_grad], axis=1) for j in range(len(counts))]
            shares = self.squeeze_back(des, ps, gates, counts, se_refs, means, small, m)
            self.last_norm(m, dt_out, du_out, z_ref, slope_ref, gates, shares, center, spread, res_bias, res_gain, pay, small)

        args = [
            (self.z[4], slots(rows)), (self.got[4], copies(self.last, 2)), (self.r, slots(rows)),
            (self.got[3], copies(self.last, 4)), (self.number, slots(2)),
            (self.gain, whole(6, C)), (self.bias, whole(6, C)),
        ] + self.se_args()
        outs = [
            (f32(OWN, SLOT, C), slots(SLOT)), (f32(OWN, 2, C), slots(2)), (f32(OWN, 2, C), slots(2)),
            (f32(OWN, 8, C), slots(8)), (f32(OWN, SE, 8), slots(SE, 8)), (f32(OWN, 8, C), slots(8)),
        ]
        scratch = [pltpu.VMEM((rows, C), F32)]
        if back:
            args += [(cotangent, layer(MB - 1, SLOT, C)), (far, slots(SLOT))]
            outs += self.tail_outs()
            scratch.append(pltpu.VMEM((rows, C), F32))
        result = yield body, self.meta, args, outs, scratch, f"{self.tag}_tail", 0, after, ()
        self.stats.append(result[1])
        self.rstat, self.se_state = result[2], result[3:6]
        if back:
            self.tail_results(result[6:])
        return result[0]

    def tail_outs(self):
        rows, count = self.tail_rows, self.first
        return [
            (f32(SMALL, C), whole(TAIL_ROWS, C)), (f32(OWN, rows, C), slots(rows)), (f32(OWN, rows, C), slots(rows)),
            (f32(count, OWN, 4, C), copies(count, 4)),
        ]

    def tail_results(self, result):
        self.small, self.du, self.dt, pay = result
        self.back_got = shared(pay, self.stages)

    def tail_backward_steps(self, cotangent, far, back):
        rows = self.tail_rows

        def body(meta, z_ref, r_ref, stat, rstat, gain, bias, means_ref, p_ref, gate_ref, down, down_b, up, up_b, cot_ref, far_ref, back_ref,
                 small, du_out, dt_out, pay, slope_ref):
            m = pl.program_id(0)
            valid = self.valid(meta, m, 4)
            center, spread, rcenter, rspread = stat[0, 0:1], stat[0, 1:2], rstat[0, 0:1], rstat[0, 1:2]
            scale = gain[4:5] * spread
            shift = bias[4:5] - center * scale
            zeros = jnp.zeros((rows - HALF, LANES), F32)
            counts = self.lengths(meta, m)
            ps = [p_ref[0, :, j : j + 1] for j in range(len(counts))]
            gates = [gate_ref[0, j : j + 1, :] for j in range(len(counts))]
            means = [means_ref[0, j : j + 1, :] for j in range(len(counts))]
            res_gain, res_bias, gate_grad = [], [], []
            for cs in CHUNKS:
                u = z_ref[0, :, cs] * scale[:, cs] + shift[:, cs]
                s = sigmoid(u)
                h = valid.keep(u * s)
                slope_ref[:, cs] = valid.keep(s * (1.0 + u * (1.0 - s)))
                rh = (r_ref[0, :, cs] - rcenter[:, cs]) * rspread[:, cs]
                t = h * self.by_segment(gates, cs) + gain[5:6, cs] * rh + bias[5:6, cs]
                s = sigmoid(t)
                here = jnp.where(meta[2 * OWN] == 1, cot_ref[0, 0:HALF, cs], far_ref[0, :, cs])
                cot = jnp.concatenate([here + back_ref[0, :, cs], zeros], axis=0)
                dt = valid.keep(cot * (s * (1.0 + t * (1.0 - s))))
                dt_out[0, :, cs] = dt
                res_bias.append(column_sum(dt))
                res_gain.append(column_sum(dt * rh))
                gate_grad.append(self.seg_sums(dt * h))
            des = [jnp.concatenate([g[j] for g in gate_grad], axis=1) for j in range(len(counts))]
            shares = self.squeeze_back(des, ps, gates, counts, (down, down_b, up, up_b), means, small, m)
            self.last_norm(m, dt_out, du_out, z_ref, slope_ref, gates, shares, center, spread, res_bias, res_gain, pay, small)

        args = [
            (self.z[4], slots(rows)), (self.r, slots(rows)), (self.stats[4], slots(2)), (self.rstat, slots(2)),
            (self.gain, whole(6, C)), (self.bias, whole(6, C)),
            (self.se_state[0], slots(8)), (self.se_state[1], slots(SE, 8)), (self.se_state[2], slots(8)),
        ] + self.se_args() + [(cotangent, slots(HALF)), (far, layer(MB - 1, HALF, C)), (back, slots(HALF))]
        scratch = [pltpu.VMEM((rows, C), F32)]
        result = yield body, self.meta, args, self.tail_outs(), scratch, f"{self.tag}_tail_back", 0, (), ()
        self.tail_results(result)


    def norm_grad(self, du, zh, scale, sums, number, cs):
        return scale[:, cs] * (du - sums[0:1, cs] / number[:, cs] - zh * (sums[1:2, cs] / number[:, cs]))

    def backward_layer(self, i):
        return run(self.backward_steps(i))

    def backward_steps(self, i):
        two, count = self.two, self.first
        strided = i == 4 and not two
        rows = self.rows_of(i)
        n_src = len(self.source_args())

        def body(meta, *refs):
            refs = list(refs)
            take = lambda n: [refs.pop(0) for _ in range(n)]
            m = pl.program_id(0)
            du_ref, z_ref, w_ref, got, n_ref, stat, gain, bias, dw_ref = take(9)
            if i:
                zp_ref, statp = take(2)
            else:
                dxr_ref, = take(1)
                src = take(n_src)
            small, dz_out = take(2)
            if i:
                du_out, pay = take(2)
            elif two:
                back_out, dx_out = take(2)
            else:
                dx_out, = take(1)
            pad, = take(1)
            alt, = take(1) if refs else (None,)
            sums = added(got)
            number = n_ref[0, 1:2, :] if i == 4 else n_ref[0, 0:1, :]
            center, spread = stat[0, 0:1], stat[0, 1:2]
            scale = gain[i : i + 1] * spread
            valid = self.valid(meta, m, i)
            for cs in CHUNKS:
                zh = (z_ref[0, :, cs] - center[:, cs]) * spread[:, cs]
                dz = valid.keep(self.norm_grad(du_ref[0, :, cs], zh, scale, sums, number, cs))
                high, low = halves(dz)
                dz_out[0, :, cs] = high
                dz_out[0, :, C + cs.start : C + cs.stop] = low
            dy = stacked_dot(dz_out[0, :, 0:C], dz_out[0, :, C : 2 * C], w_ref.at[0], True)
            valid_in = self.valid(meta, m, 0)
            if i:
                pcenter, pspread = statp[0, 0:1], statp[0, 1:2]
                pscale = gain[i - 1 : i] * pspread
                pshift = bias[i - 1 : i] - pcenter * pscale
            taps, bias_sum, gain_sum = [[] for _ in range(TAPS)], [], []
            for c, cs in enumerate(CHUNKS):
                grad = dy[:, cs]
                if strided:
                    grad = spread_out(alt.at[c], grad)
                padded = Padded(pad.at[c], two)
                padded.put(grad)
                if i:
                    z = zp_ref[0, :, cs]
                    u = z * pscale[:, cs] + pshift[:, cs]
                    s = sigmoid(u)
                    h = valid_in.keep(u * s)
                else:
                    h = valid_in.keep(self.source(meta, src, cs))
                dh = None
                for k in range(TAPS):
                    moved = padded.get(2 - k)
                    taps[k].append(column_sum(h * moved))
                    term = dw_ref[0, k : k + 1, cs] * moved
                    dh = term if dh is None else dh + term
                if i:
                    du = valid_in.keep(dh * (s * (1.0 + u * (1.0 - s))))
                    du_out[0, :, cs] = du
                    bias_sum.append(column_sum(du))
                    gain_sum.append(column_sum(du * ((z - pcenter[:, cs]) * pspread[:, cs])))
                    continue
                dxr = dxr_ref[0, :, cs]
                if not two:
                    dxr = spread_out(alt.at[c], dxr)
                dx = valid_in.keep(dh) + dxr
                if two:
                    back_out[0, :, cs] = dx[:HALF]
                    dx = dx[HALF:]
                dx_out[0, :, cs] = dx
            rows = taps + [bias_sum, gain_sum] if i else taps
            rows = [jnp.concatenate(x, axis=1) for x in rows]
            for j, row in enumerate(rows):
                accumulate(small, m, j, row)
            if i:
                send(pay, rows[TAPS:])

        sent = 4 if i == 4 else 2
        args = [
            (self.du, slots(rows)), (self.z[i], slots(rows)), self.matrix(i), (self.back_got, copies(self.last, sent)),
            (self.number, slots(2)), (self.stats[i], slots(2)), (self.gain, whole(6, C)), (self.bias, whole(6, C)),
            (self.dw, layer(i, TAPS, C)),
        ]
        if not i:
            args.append((self.dxr, slots(self.tail_rows)))
        args += self.before_args(i)
        place = TAIL_ROWS // 8 + i
        outs = [(f32(SMALL, C), pl.BlockSpec((8, C), lambda m, *_: (place, 0))), (bf16(OWN, rows, 2 * C), slots(rows, 2 * C))]
        if i:
            outs += [(f32(OWN, SLOT, C), slots(SLOT)), (f32(count, OWN, 2, C), copies(count, 2))]
        elif two:
            outs += [(f32(OWN, HALF, C), slots(HALF)), (f32(OWN, HALF, C), slots(HALF))]
        else:
            outs += [(f32(OWN, SLOT, C), slots(SLOT))]
        scratch = [pad_scratch()]
        if strided or (i == 0 and not two):
            scratch.append(stride_scratch())
        flops = 6 * OWN * rows * C * C
        self.small, dz, *result = yield (
            body, self.meta, args, outs, scratch, f"{self.tag}_backward_{i}", flops, self.done, (self.small,)
        )
        got = self.back_got
        if i:
            self.du = result[0]
            if i == self.stop:
                self.pending = dz, result[1]
                return result
            self.back_got = shared(result[1], self.stages)
        self.weight_grad(i, dz)
        if i == 4:
            self.residual_back(got)
        return result

    def residual_back(self, got):
        rows = self.tail_rows

        def body(meta, got, n_ref, dt_ref, r_ref, rstat, gain, w_ref, x_ref, kept_out, away_out, dxr_out, dr, total):
            m = pl.program_id(0)
            sums = added(got)[2:4]
            number = n_ref[0, 1:2, :]
            center, spread = rstat[0, 0:1], rstat[0, 1:2]
            scale = gain[5:6] * spread
            valid = self.valid(meta, m, 4)
            for cs in CHUNKS:
                rh = (r_ref[0, :, cs] - center[:, cs]) * spread[:, cs]
                high, low = halves(valid.keep(self.norm_grad(dt_ref[0, :, cs], rh, scale, sums, number, cs)))
                dr[:, cs] = high
                dr[:, C + cs.start : C + cs.stop] = low
            high, low = dr[:, 0:C], dr[:, C : 2 * C]
            dxr_out[0] = stacked_dot(high, low, w_ref.at[0], True)
            grad = stacked_outer(x_ref[0, :, 0:C], x_ref[0, :, C : 2 * C], high, low)
            self.add_halves(meta, m, grad, total, kept_out, away_out)

        args = [
            (got, copies(self.last, 4)), (self.number, slots(2)), (self.dt, slots(rows)), (self.r, slots(rows)),
            (self.rstat, slots(2)), (self.gain, whole(6, C)), self.matrix(5), (self.picked, slots(rows, 2 * C)),
        ]
        outs = self.piece_out(5) + [(f32(OWN, rows, C), slots(rows))]
        which = PLACES[5][0]
        *self.pieces[which], self.dxr = call(
            body, self.meta, args, outs, [pltpu.VMEM((rows, 2 * C), BF16), pltpu.VMEM((C, C), F32)],
            f"{self.tag}_residual_back", 12 * OWN * rows * C * C, into=self.pieces[which],
        )

    def piece_out(self, i):
        which, place = PLACES[i]
        rows = PIECE_ROWS[which]
        return [(f32(rows, C), pl.BlockSpec((C // 2, C), lambda m, *_: (place, 0)))] * 2

    def add_halves(self, meta, m, grad, total, kept_out, away_out):
        @pl.when(m == 0)
        def _():
            total[...] = grad

        @pl.when(m > 0)
        def _():
            top, bottom = total[0 : C // 2] + grad[0 : C // 2], total[C // 2 : C] + grad[C // 2 : C]
            lower = meta[2 * OWN] == 1
            kept_out[...] = jnp.where(lower, top, bottom)
            away_out[...] = jnp.where(lower, bottom, top)

    def weight_grad(self, i, dz):
        two = self.two
        strided = i == 4 and not two
        rows = self.rows_of(i)
        n_src = len(self.source_args())

        def body(meta, *refs):
            refs = list(refs)
            take = lambda n: [refs.pop(0) for _ in range(n)]
            m = pl.program_id(0)
            if i:
                zp_ref, statp, gain, bias = take(4)
                center, spread = statp[0, 0:1], statp[0, 1:2]
                scale = gain[i - 1 : i] * spread
                shift = bias[i - 1 : i] - center * scale
            else:
                src = take(n_src)
            dz_ref, dw_ref, kept_out, away_out, pad, yh, yl, total = take(8)
            alt, = take(1) if strided else (None,)
            valid_in = self.valid(meta, m, 0)
            for c, cs in enumerate(CHUNKS):
                if i:
                    u = zp_ref[0, :, cs] * scale[:, cs] + shift[:, cs]
                    h = valid_in.keep(u * sigmoid(u))
                else:
                    h = valid_in.keep(self.source(meta, src, cs))
                padded = Padded(pad.at[c], two)
                padded.put(h)
                y = padded.conv(dw_ref[0, :, cs])
                if strided:
                    y = every_other(alt.at[c], y)
                yh[:, cs], yl[:, cs] = halves(y)
            grad = stacked_outer(yh[...], yl[...], dz_ref[0, :, 0:C], dz_ref[0, :, C : 2 * C])
            self.add_halves(meta, m, grad, total, kept_out, away_out)

        args = self.before_args(i)
        if i:
            args += [(self.gain, whole(6, C)), (self.bias, whole(6, C))]
        args += [(dz, slots(rows, 2 * C)), (self.dw, layer(i, TAPS, C))]
        scratch = [pad_scratch(), pltpu.VMEM((rows, C), BF16), pltpu.VMEM((rows, C), BF16), pltpu.VMEM((C, C), F32)]
        if strided:
            scratch.append(stride_scratch())
        which = PLACES[i][0]
        self.pieces[which] = call(
            body, self.meta, args, self.piece_out(i), scratch, f"{self.tag}_weights_{i}", 6 * OWN * rows * C * C,
            into=self.pieces[which],
        )
        self.done = (self.pieces[which][0],)

    def backward(self, layers):
        if layers[0] == 4:
            self.pieces = [[], []]
        for i in layers:
            result = self.backward_layer(i)
        return result

    def resume(self, i):
        dz, payload = self.pending
        self.back_got = shared(payload, self.stages)
        self.weight_grad(i, dz)

    def fork(self, state=None):
        other = copy.copy(self)
        other.__dict__.update(state or {})
        if "pieces" in other.__dict__:
            other.pieces = list(other.pieces)
        return other

    def state(self):
        return {name: getattr(self, name) for name in ("du", "dxr", "pieces", "small", "pending")}

    def half(self, no, first, begin=None, end=None):
        kept, away = self.pieces[no]
        if no:
            parts = self.small[: SMALL // 2], self.small[SMALL // 2 :]
            at = kept.shape[0] - SMALL // 2
            kept = lax.dynamic_update_slice_in_dim(kept, jnp.where(first, *parts), at, 0)
            away = lax.dynamic_update_slice_in_dim(away, jnp.where(first, *parts[::-1]), at, 0)
        if begin is not None:
            away, _ = lax.optimization_barrier((away, begin))
            kept, _ = lax.optimization_barrier((kept, end))
        return kept + swap(away)


PLACES = {3: (0, 0), 4: (0, 1), 5: (0, 2), 0: (1, 0), 1: (1, 1), 2: (1, 2)}
PIECE_ROWS = (3 * C // 2, 3 * C // 2 + SMALL // 2)


def split_squeeze(meta, own, far):
    def body(meta, own_ref, far_ref, *outs):
        row, col = (lax.broadcasted_iota(jnp.int32, (SE, C), axis) for axis in (0, 1))
        for block in range(2):
            down, down_b, up, up_b = outs[4 * block : 4 * block + 4]
            down[...] = choose(meta, block, own_ref[0:SE, :], far_ref[0:SE, :])
            up[...] = choose(meta, block, own_ref[SE : 2 * SE, :], far_ref[SE : 2 * SE, :])
            up_b[...] = choose(meta, block, own_ref[2 * SE : 2 * SE + 1, :], far_ref[2 * SE : 2 * SE + 1, :])
            wide = choose(meta, block, own_ref[2 * SE + 1 : 2 * SE + 2, :], far_ref[2 * SE + 1 : 2 * SE + 2, :])
            down_b[...] = jnp.sum(jnp.where(row == col, wide, 0.0), axis=1, keepdims=True)

    shapes = [(SE, C), (SE, 1), (SE, C), (1, C)] * 2
    args = [(x, whole(*x.shape)) for x in (own, far)]
    outs = call(body, meta, args, [(f32(*shape), whole(*shape)) for shape in shapes], name="split_squeeze", steps=1)
    return tuple(outs[:4]), tuple(outs[4:])


def pick_joining(picks, features):
    def body(picks, in_ref, out_ref):
        out_ref[...] = in_ref[0, 0]

    own = pl.BlockSpec((1, 1, HALF, C), lambda m, picks: (picks[m], 1, 0, 0))
    out = (f32(OWN * HALF, C), pl.BlockSpec((HALF, C), lambda m, *_: (m, 0)))
    return call(body, picks, [(features, own)], [out], name="pick_joining")[0]


def swap(x):
    return lax.ppermute(x, "section", [(0, 1), (1, 0)])


def fenced(always, work, x):
    shapes = jax.eval_shape(work, x)
    return lax.cond(always, work, lambda x: jax.tree.map(lambda y: jnp.zeros(y.shape, y.dtype), shapes), x)


class Reduction:
    def __init__(self, x, stages):
        self.x = x
        self.todo = []
        stride = 1
        for radix in stages:
            self.todo.append((True, radix, stride))
            stride *= radix
        self.todo += [(False, radix, stride) for _, radix, stride in reversed(self.todo)]

    def step(self):
        scatter, radix, stride = self.todo.pop(0)
        rows = self.x.shape[0]
        if scatter:
            parts = exchange(self.x.reshape(radix, rows // radix, C), radix, stride)
            self.x = jnp.sum(parts, axis=0)
        else:
            parts = exchange(jnp.broadcast_to(self.x, (radix,) + self.x.shape), radix, stride)
            self.x = parts.reshape(radix * rows, C)
        return (self.x,)

    def finish(self):
        while self.todo:
            self.step()
        return self.x


def per_device(features, out_grad, lengths, join_pick, dw, pw, gain, bias, res_w, down, down_b, up, up_b):
    first = lax.axis_index("section") == 0
    size = lax.axis_size("dp")
    inputs = features.reshape(MB, SLOT, C)
    cotangent = out_grad.reshape(MB, SLOT, C)
    own, picks = lengths[0, 0], join_pick[0]
    to_upper = lambda x: lax.ppermute(x, "section", [(0, 1)])
    to_lower = lambda x: lax.ppermute(x, "section", [(1, 0)])

    far_len = swap(own)
    far_rows = to_upper(inputs[MB - 1])
    far_w0 = swap(pw[0, 0:1])
    taps = jnp.concatenate([dw[0].reshape(5 * TAPS, C), gain[0], bias[0]], axis=0)
    far_taps = swap(taps)
    far_pw, far_res = swap(pw[0]), swap(res_w[0])
    wide = jnp.pad(down_b, ((0, 0), (0, C - SE)))
    squeeze = jnp.concatenate([down[0].T, up[0], up_b, wide], axis=0)
    far_squeeze = swap(squeeze)
    far_cot = swap(cotangent)

    flag = first.astype(jnp.int32)[None]
    mine = lambda v: jnp.where(first, v[:OWN], jnp.concatenate([v[OWN:], jnp.zeros((1,), v.dtype)]))
    length = mine(jnp.where(first, own, far_len))
    half_len = (length + 1) // 2
    join_len = mine(jnp.where(first, far_len, own)[picks])
    meta1 = jnp.concatenate([length, half_len, flag])
    meta2 = jnp.concatenate([half_len, join_len, flag, picks[MB - 1 :]])
    both = jnp.concatenate([length, half_len, flag, half_len, join_len, flag, picks[MB - 1 :]])

    def small(block):
        t = jnp.where(first == (block == 0), taps, far_taps)
        return t[: 5 * TAPS].reshape(5, TAPS, C), t[5 * TAPS : 5 * TAPS + 6], t[5 * TAPS + 6 :]

    excitations = split_squeeze(meta1, squeeze, far_squeeze)

    def prepared(block, start, stop):
        array = prepare(meta1, (pw[0], res_w[0]), (far_pw, far_res), block, start, stop)
        return array, {i: (array, i - start) for i in range(start, stop)}

    parts0 = [prepared(0, 1, 3), prepared(0, 3, 6)]
    parts1 = [prepared(1, 0, 1), prepared(1, 1, 4), prepared(1, 4, 6)]

    stages, deep = radices(size, 16), radices(size, 4)
    c14 = Block(False, meta1, small(0), {**parts0[0][1], **parts0[1][1]}, stages)
    c14.x, c14.x_far, c14.first_matrix = inputs, far_rows, (pw[0], far_w0)
    c14.excitation = excitations[0]
    c14.forward({2: (parts0[1][0],)})
    late_picks, _ = lax.optimization_barrier((picks, c14.z[3]))
    far_joining = to_lower(pick_joining(late_picks, features.reshape(MB, 2, HALF, C)))
    c15 = Block(True, meta2, small(1), {**parts1[0][1], **parts1[1][1], **parts1[2][1]}, stages)
    c15.excitation = excitations[1]
    c15.arrived, c15.joined_far, c15.joined = Linked(0, HALF), far_joining, features.reshape(MB, 2, HALF, C)
    c15.start()
    out0, _ = run_joined(c14.tail_steps(), c15.forward_steps(0), (both, 0, meta1.shape[0]))
    c15.arrived = out0
    c15.forward({1: (parts1[1][0],), 2: (parts1[2][0],)}, joined=True)
    out1 = c15.tail(cotangent, far_cot)
    c15.stop = 2
    c15.backward((4, 3))
    begin = c15.back_got
    c15.backward((2,))
    always = own[0] > 0

    half0 = c15.half(0, first, begin, c15.du)
    sum0 = lax.psum(half0, "dp")

    def middle(half0):
        upper, lower = c15.fork(), c14.fork()
        upper.resume(2)
        upper.done += (half0,)
        upper.backward((1,))
        (_, dx1), _ = run_joined(
            upper.backward_steps(0), lower.tail_backward_steps(cotangent, far_cot, Linked(2, HALF)), (both, meta1.shape[0], 0)
        )
        lower.done = upper.done
        lower.backward((4,))
        begin1 = lower.back_got
        lower.backward((3,))
        half1 = upper.half(1, first, begin1, lower.du)
        begin2 = lower.back_got
        lower.stop = 2
        lower.backward((2,))
        half2 = lower.half(0, first, begin2, lower.du)
        return dx1, jnp.concatenate([half1, half2], axis=0), lower.state()

    dx1, half12, state = fenced(always, middle, half0)
    sum0, half12 = lax.optimization_barrier((sum0, half12))
    sum12 = lax.psum(half12, "dp")

    def ending(half12):
        last = c14.fork(state)
        last.resume(2)
        last.done += (half12,)
        came0 = to_upper(sum0)
        dx0, = last.backward((1, 0))
        half3 = last.half(1, first)
        half3, dx0, *kept = lax.optimization_barrier((half3, dx0, out0, out1, dx1))
        reduction = Reduction(half3, deep)
        reduction.step()
        pad = jnp.zeros((1, HALF, C), F32)
        lower = jnp.concatenate([kept[0], jnp.concatenate([to_lower(kept[0][0:1, :HALF]), pad], axis=1)], axis=0)
        upper = jnp.concatenate([to_upper(kept[1]), kept[1][0:1]], axis=0)
        block_out = jnp.where(first, lower, upper)
        lower = jnp.concatenate([dx0, to_lower(dx0[0:1])], axis=0)
        joins = jnp.concatenate([to_upper(kept[2]), kept[2][0:1]], axis=0)
        joins = jnp.stack([lax.dynamic_index_in_dim(joins, jnp.argmax(picks == s), 0, False) for s in range(MB)])
        upper = jnp.concatenate([jnp.zeros_like(joins), joins], axis=1)
        dx = jnp.where(first, lower, upper)
        reduction.x, block_out, dx, came0 = lax.optimization_barrier((reduction.x, block_out, dx, came0))
        return block_out, dx, came0, reduction.finish()

    block_out, dx, came0, sum3 = fenced(always, ending, half12)
    came3 = to_lower(sum3)
    sum12, _ = lax.optimization_barrier((sum12, sum3))
    came12 = swap(sum12)
    split = PIECE_ROWS[1]
    sum1, sum2, came1, came2 = sum12[:split], sum12[split:], came12[:split], came12[split:]

    lead = 3 * C // 2

    def joined(near, far):
        pair = [x.reshape(-1, 1, C // 2, C) for x in (near, far)]
        both = jnp.where(first, jnp.concatenate(pair, axis=1), jnp.concatenate(pair[::-1], axis=1))
        return both.reshape(-1, C, C)

    choose_mine = lambda a, b: jnp.where(first, a, b)
    rest_part = joined(choose_mine(sum3[:lead], sum1[:lead]), choose_mine(came3[:lead], came1[:lead]))
    lead_part = joined(choose_mine(sum2[:C], sum0[:C]), choose_mine(came2[:C], came0[:C]))
    pw_grad = jnp.concatenate([rest_part, lead_part], axis=0)[None]
    res_grad = joined(choose_mine(sum2[C:], sum0[C:]), choose_mine(came2[C:], came0[C:]))
    near, far = choose_mine(sum3[lead:], sum1[lead:]), choose_mine(came3[lead:], came1[lead:])
    rows = jnp.where(first, jnp.concatenate([near, far], axis=0), jnp.concatenate([far, near], axis=0))
    dw_grad = rows[TAIL_ROWS : TAIL_ROWS + 40].reshape(1, 5, 8, C)
    norms = jnp.concatenate([dw_grad[0, 1:, TAPS : TAPS + 2], rows[None, 2 * SE + 2 : 2 * SE + 4], rows[None, 2 * SE + 4 : 2 * SE + 6]], axis=0)
    return (
        block_out.reshape(features.shape), dx.reshape(features.shape), dw_grad[:, :, :TAPS], pw_grad,
        norms[None, :, 1], norms[None, :, 0], res_grad, rows[SE : 2 * SE].T[None], rows[2 * SE + 1 : 2 * SE + 2, :SE],
        rows[:SE][None], rows[2 * SE : 2 * SE + 1],
    )


def solution(mesh):
    rows = P("section", "dp", None)
    own = lambda dims: P("section", *([None] * dims))
    weights = (own(3), own(3), own(2), own(2), own(2), own(2), own(1), own(2), own(1))
    in_specs = (rows, rows, rows, P("dp", None), *weights)
    out_specs = (rows, rows, *weights)
    return jax.shard_map(per_device, mesh=mesh, in_specs=in_specs, out_specs=out_specs, check_vma=False)
```

```python
import copy

import jax
import jax.numpy as jnp
from jax import lax
from jax.experimental import pallas as pl
from jax.experimental.pallas import tpu as pltpu
from jax.sharding import PartitionSpec as P

EPSILON = 1e-05
EXACT = lax.Precision.HIGHEST
TAPS = 5
MB = 3
OWN = 2
SLOT = 400
HALF = 200
KEPT = 208
C = 512
LANES = 128
CHUNKS = [slice(c, c + LANES) for c in range(0, C, LANES)]
SE = 64
BF16, F32 = jnp.bfloat16, jnp.float32
VMEM_BYTES = 60 << 20
TAIL_ROWS = 2 * SE + 8
SMALL = 256


def radices(size, most):
    stages, left = [], size
    while left > 1:
        radix = min(most, left)
        while left % radix:
            radix -= 1
        stages.append(radix)
        left //= radix
    return stages


def exchange(block, radix, stride):
    size = lax.axis_size("dp")
    if radix == size:
        return lax.all_to_all(block, "dp", 0, 0)
    groups = []
    for base in range(size):
        if (base // stride) % radix == 0:
            groups.append([base + j * stride for j in range(radix)])
    return lax.all_to_all(block, "dp", 0, 0, axis_index_groups=groups)


def shared(block, stages):
    stride = 1
    for no, radix in enumerate(stages):
        if no:
            block = jnp.broadcast_to(jnp.sum(block, axis=0), (radix,) + block.shape[1:])
        block = exchange(block, radix, stride)
        stride *= radix
    return block


def halves(x):
    high = x.astype(BF16)
    return high, (x - high.astype(F32)).astype(BF16)


def sigmoid(x):
    return 0.5 * jnp.tanh(0.5 * x) + 0.5


def exact_dot(a, b, dims=((1,), (0,))):
    return lax.dot_general(a, b, (dims, ((), ())), precision=EXACT, preferred_element_type=F32)


def fast_dot(a, b, dims=((1,), (0,))):
    return lax.dot_general(a, b, (dims, ((), ())), preferred_element_type=F32)


def stacked_dot(high, low, w, back=False):
    w_high, w_low = w[0], w[1]
    w = jnp.concatenate([w_high, w_high, w_low], axis=1 if back else 0)
    x = jnp.concatenate([high, low, high], axis=1)
    return fast_dot(x, w, ((1,), (1 if back else 0,)))


def stacked_outer(a_high, a_low, b_high, b_low):
    a = jnp.concatenate([a_high, a_low, a_high], axis=0)
    b = jnp.concatenate([b_high, b_high, b_low], axis=0)
    return fast_dot(a, b, ((0,), (0,)))


def column_sum(x):
    return jnp.sum(x, axis=0, keepdims=True)


class Rows:
    def __init__(self, meta, m, two, rows, which=0):
        place = lax.broadcasted_iota(jnp.int32, (rows, LANES), 0)
        if two:
            later = place >= HALF
            limit = jnp.where(later, HALF + meta[OWN + m], meta[m])
            self.mask = place < limit
        else:
            self.mask = place < meta[which * OWN + m]

    def keep(self, x):
        return jnp.where(self.mask, x, 0.0)


class Padded:
    def __init__(self, ref, two):
        self.ref = ref
        self.pieces = [(8, 0, HALF), (16 + HALF, HALF, HALF)] if two else [(8, 0, SLOT)]

    def put(self, x):
        zeros = jnp.zeros((8, LANES), F32)
        for at, start, rows in self.pieces:
            self.ref[at - 8 : at, :] = zeros
            self.ref[at : at + rows, :] = x[start : start + rows]
        self.ref[at + rows : at + rows + 8, :] = zeros

    def get(self, offset):
        parts = [self.ref[at + offset : at + offset + rows, :] for at, _, rows in self.pieces]
        return parts[0] if len(parts) == 1 else jnp.concatenate(parts, axis=0)

    def conv(self, kernel):
        total = kernel[0:1] * self.get(-2)
        for k in range(1, TAPS):
            total = total + kernel[k : k + 1] * self.get(k - 2)
        return total

    def conv_back(self, kernel):
        total = kernel[0:1] * self.get(2)
        for k in range(1, TAPS):
            total = total + kernel[k : k + 1] * self.get(2 - k)
        return total


def every_other(ref, x):
    ref[0:SLOT, :] = x
    ref[SLOT : 2 * KEPT, :] = jnp.zeros((2 * KEPT - SLOT, LANES), F32)
    return ref[pl.ds(0, KEPT, stride=2), :]


def spread_out(ref, x):
    ref[...] = jnp.zeros_like(ref)
    ref[pl.ds(0, KEPT, stride=2), :] = x
    return ref[0:SLOT, :]


def center_spread(sums, rows):
    center = sums[0:1] / rows
    return center, lax.rsqrt(sums[1:2] / rows - center * center + EPSILON)


def added(ref):
    return jnp.sum(ref[:, 0], axis=0)


def accumulate(ref, m, at, value):
    rows = slice(at, at + value.shape[0])
    ref[rows, :] = jnp.where(m == 0, value, ref[rows, :] + value)


def send(ref, rows):
    for copy in range(ref.shape[0]):
        for row, x in enumerate(rows):
            ref[copy, 0, row : row + 1, 0 : x.shape[1]] = x


def pad_scratch():
    return pltpu.VMEM((len(CHUNKS), SLOT + 24, LANES), F32)


def stride_scratch():
    return pltpu.VMEM((len(CHUNKS), 2 * KEPT, LANES), F32)


def slots(rows, cols=C):
    return pl.BlockSpec((1, rows, cols), lambda m, *_: (m, 0, 0))


def copies(count, rows, cols=C):
    return pl.BlockSpec((count, 1, rows, cols), lambda m, *_: (0, m, 0, 0))


def whole(*shape):
    return pl.BlockSpec(shape, lambda m, *_: (0,) * len(shape))


def layer(i, *shape):
    return pl.BlockSpec((1,) + shape, lambda m, *_: (i,) + (0,) * len(shape))


def f32(*shape):
    return jax.ShapeDtypeStruct(shape, F32)


def bf16(*shape):
    return jax.ShapeDtypeStruct(shape, BF16)


def call(body, meta, args, outs, scratch=(), name=None, flops=0, steps=OWN, after=(), into=()):
    arrays, in_specs = [a for a, _ in args], [s for _, s in args]
    shapes, out_specs = [a for a, _ in outs], [s for _, s in outs]
    size = sum(a.size * a.dtype.itemsize for a in arrays + shapes)
    extra = list(after) + list(into)
    count = len(arrays)

    def inner(meta, *refs):
        body(meta, *refs[:count], *refs[count + len(extra) :])

    return pl.pallas_call(
        inner,
        out_shape=shapes,
        grid_spec=pltpu.PrefetchScalarGridSpec(
            num_scalar_prefetch=1,
            grid=(steps,),
            in_specs=in_specs + [pl.BlockSpec(memory_space=pl.ANY)] * len(extra),
            out_specs=out_specs,
            scratch_shapes=list(scratch),
        ),
        input_output_aliases={1 + count + len(after) + j: j for j in range(len(into))},
        compiler_params=pltpu.CompilerParams(vmem_limit_bytes=VMEM_BYTES),
        cost_estimate=pl.CostEstimate(flops=flops, bytes_accessed=size, transcendentals=0),
        name=name,
    )(meta, *arrays, *extra)


class Linked:
    def __init__(self, index, rows):
        self.index, self.rows = index, rows


class Part:
    def __init__(self, ref, at):
        self.ref, self.at = ref, at

    def __getitem__(self, index):
        return self.ref[self.at + index]


def run(steps):
    body, meta, args, outs, scratch, name, flops, after, into = next(steps)
    return finish(steps, call(body, meta, args, outs, scratch, name, flops, after=after, into=into))


def finish(steps, results):
    try:
        steps.send(results)
    except StopIteration as stop:
        return stop.value


def run_joined(one, two, scalars):
    meta, at1, at2 = scalars
    body1, _, args1, outs1, scratch1, name1, flops1, after1, into1 = next(one)
    body2, _, args2, outs2, scratch2, name2, flops2, after2, into2 = next(two)
    assert not into2
    own2 = [arg for arg in args2 if not isinstance(arg[0], Linked)]
    sizes = len(args1), len(own2), len(outs1), len(outs2), len(scratch1), len(scratch2)

    def body(meta, *refs):
        refs = list(refs)
        in1, in2, out1, out2, scr1, scr2 = [[refs.pop(0) for _ in range(n)] for n in sizes]
        body1(Part(meta, at1), *in1, *out1, *scr1)
        linked = []
        for arg in args2:
            link = arg[0]
            linked.append(out1[link.index].at[:, 0 : link.rows, :] if isinstance(link, Linked) else in2.pop(0))
        body2(Part(meta, at2), *linked, *out2, *scr2)

    def moved(spec, at):
        if spec.index_map is None:
            return spec
        return pl.BlockSpec(spec.block_shape, lambda m, meta: spec.index_map(m, Part(meta, at)))

    args = [(a, moved(spec, at1)) for a, spec in args1] + [(a, moved(spec, at2)) for a, spec in own2]
    results = call(
        body, meta, args, [(a, moved(spec, at1)) for a, spec in outs1] + [(a, moved(spec, at2)) for a, spec in outs2], list(scratch1) + list(scratch2), f"{name1}_{name2}", flops1 + flops2,
        after=(*after1, *after2), into=into1,
    )
    return finish(one, results[: len(outs1)]), finish(two, results[len(outs1) :])


def choose(meta, block, own, far):
    return jnp.where(meta[2 * OWN] == 1 - block, own, far)


def prepare(meta, own, far, block, start, stop):
    def body(meta, *refs):
        pair = [ref[0] for ref in refs[:2]]
        if stop == 6:
            last = pl.program_id(0) == 5 - start
            pair = [jnp.where(last, ref[...], w) for ref, w in zip(refs[2:4], pair)]
        out = refs[-1]
        out[0, 0], out[0, 1] = halves(choose(meta, block, *pair))

    matrix = pl.BlockSpec((1, C, C), lambda j, *_: (jnp.minimum(j + start, 4), 0, 0))
    args = [(own[0], matrix), (far[0], matrix)]
    if stop == 6:
        args += [(own[1], whole(C, C)), (far[1], whole(C, C))]
    out = pl.BlockSpec((1, 2, C, C), lambda j, *_: (j, 0, 0, 0))
    name = f"prepare_{block}_{start}"
    return call(body, meta, args, [(bf16(stop - start, 2, C, C), out)], name=name, steps=stop - start)[0]


class Block:
    def __init__(self, two, meta, weights, ready, stages):
        self.done, self.stop, self.pending = (), None, None
        self.two, self.meta, self.stages = two, meta, stages
        self.dw, self.gain, self.bias = weights
        self.ready = ready
        self.tail_rows = SLOT if two else KEPT
        self.first, self.last = stages[0], stages[-1]
        self.tag = "c15" if two else "c14"

    def rows_of(self, i):
        return self.tail_rows if i == 4 else SLOT

    def valid(self, meta, m, i):
        last = i == 4 and not self.two
        return Rows(meta, m, self.two, self.rows_of(i), which=1 if last else 0)

    def matrix(self, i):
        array, at = self.ready[i]
        return (array, layer(at, 2, C, C))

    def source_args(self):
        if not self.two:
            return [(self.x, slots(SLOT)), (self.x_far, whole(SLOT, C))]
        far = pl.BlockSpec((HALF, C), lambda m, *_: (m, 0))
        near = pl.BlockSpec((1, 1, HALF, C), lambda m, meta: (meta[2 * OWN + 1], 1, 0, 0))
        return [(self.arrived, slots(HALF)), (self.joined_far, far), (self.joined, near)]

    def source(self, meta, refs, cs):
        lower = meta[2 * OWN] == 1
        if not self.two:
            return jnp.where(lower, refs[0][0, :, cs], refs[1][:, cs])
        joined = jnp.where(lower, refs[1][:, cs], refs[2][0, 0, :, cs])
        return jnp.concatenate([refs[0][0, :, cs], joined], axis=0)

    def before_args(self, i):
        if i == 0:
            return self.source_args()
        return [(self.z[i - 1], slots(SLOT)), (self.stats[i - 1], slots(2))]


    def forward_layer(self, i, after=()):
        return run(self.forward_steps(i, after))

    def forward_steps(self, i, after=()):
        two, count = self.two, self.first
        strided = i == 4 and not two
        rows = self.rows_of(i)
        n_src = len(self.source_args())
        width = C + LANES if i == 0 else C
        sent = 4 if i == 3 else 2
        makes = i == 0 and not two

        def body(meta, *refs):
            refs = list(refs)
            take = lambda n: [refs.pop(0) for _ in range(n)]
            m = pl.program_id(0)
            if i == 0:
                src = take(n_src)
            else:
                z_ref, got_ref = take(2)
                n_ref, = take(1) if i > 1 else (None,)
                gain_ref, bias_ref = take(2)
                res_sum, = take(1) if i == 3 else (None,)
            dw_ref, = take(1)
            if makes:
                own_ref, far_ref, z_out, pay, w_ref = take(5)

                @pl.when(m == 0)
                def _():
                    w_ref[0, 0], w_ref[0, 1] = halves(choose(meta, 0, own_ref[0], far_ref[0]))

            else:
                w_ref, z_out, pay = take(3)
            if i:
                stat_out, = take(1)
            if i == 1:
                n_out, = take(1)
            pad, y_ref = take(2)
            alt, = take(1) if strided else (None,)
            valid_in = self.valid(meta, m, 0)
            if i:
                sums = added(got_ref)
                if i == 1:
                    count_in = jnp.maximum(jnp.concatenate([sums[0:1, C:]] * len(CHUNKS), axis=1), 1.0)
                    count_out = jnp.maximum(jnp.concatenate([sums[1:2, C:]] * len(CHUNKS), axis=1), 1.0)
                    n_out[0, 0:1, :] = count_in
                    n_out[0, 1:2, :] = count_out
                else:
                    count_in = n_ref[0, 0:1, :]
                center, spread = center_spread(sums[:, :C], count_in)
                stat_out[0, 0:1, :] = center
                stat_out[0, 1:2, :] = spread
                scale = gain_ref[i - 1 : i] * spread
                shift = bias_ref[i - 1 : i] - center * scale
            for c, cs in enumerate(CHUNKS):
                if i == 0:
                    h = valid_in.keep(self.source(meta, src, cs))
                else:
                    u = z_ref[0, :, cs] * scale[:, cs] + shift[:, cs]
                    h = valid_in.keep(u * sigmoid(u))
                padded = Padded(pad.at[c], two)
                padded.put(h)
                y = padded.conv(dw_ref[0, :, cs])
                if strided:
                    y = every_other(alt.at[c], y)
                high, low = halves(y)
                y_ref[:, cs] = high
                y_ref[:, C + cs.start : C + cs.stop] = low
            w = w_ref.at[0] if makes else w_ref.at[0]
            z = stacked_dot(y_ref[:, 0:C], y_ref[:, C : 2 * C], w)
            z_out[0] = z
            valid = self.valid(meta, m, i)
            one, square = [], []
            for cs in CHUNKS:
                kept = valid.keep(z[:, cs])
                one.append(column_sum(kept))
                square.append(column_sum(kept * kept))
            if i == 0:
                if two:
                    number = (meta[m] + meta[OWN + m]).astype(F32)
                    numbers = number, number
                else:
                    numbers = meta[m].astype(F32), meta[OWN + m].astype(F32)
                one.append(jnp.full((1, LANES), numbers[0], F32))
                square.append(jnp.full((1, LANES), numbers[1], F32))
            out = [jnp.concatenate(one, axis=1), jnp.concatenate(square, axis=1)]
            if i == 3:
                out += [res_sum[0, 0:1, :], res_sum[0, 1:2, :]]
            send(pay, out)

        if i == 0:
            args = list(self.source_args())
        else:
            got = 4 if i == 4 else 2
            args = [(self.z[i - 1], slots(SLOT)), (self.got[i - 1], copies(self.last, got, C + LANES if i == 1 else C))]
            if i > 1:
                args.append((self.number, slots(2)))
            args += [(self.gain, whole(6, C)), (self.bias, whole(6, C))]
            if i == 3:
                args.append((self.res_sum, slots(2)))
        args.append((self.dw, layer(i, TAPS, C)))
        args += [(w, layer(0, C, C)) for w in self.first_matrix] if makes else [self.matrix(i)]
        outs = [(f32(OWN, rows, C), slots(rows)), (f32(count, OWN, sent, width), copies(count, sent, width))]
        if i:
            outs.append((f32(OWN, 2, C), slots(2)))
        if i == 1:
            outs.append((f32(OWN, 2, C), slots(2)))
        if makes:
            outs.append((bf16(1, 2, C, C), layer(0, 2, C, C)))
        scratch = [pad_scratch(), pltpu.VMEM((rows, 2 * C), BF16)]
        if strided:
            scratch.append(stride_scratch())
        flops = 6 * OWN * rows * C * C
        result = yield body, self.meta, args, outs, scratch, f"{self.tag}_forward_{i}", flops, after, ()
        self.z.append(result[0])
        if makes:
            self.ready[0] = (result[2], 0)
        if i:
            self.stats.append(result[2])
        if i == 1:
            self.number = result[3]
        self.got.append(shared(result[1], self.stages))

    def residual(self):
        two, rows = self.two, self.tail_rows

        def body(meta, *refs):
            refs = list(refs)
            src = [refs.pop(0) for _ in self.source_args()]
            w_ref, r_out, x_out, sum_out = refs[:4]
            alt = refs[4] if not two else None
            m = pl.program_id(0)
            valid_in = self.valid(meta, m, 0)
            for c, cs in enumerate(CHUNKS):
                x = valid_in.keep(self.source(meta, src, cs))
                if not two:
                    x = every_other(alt.at[c], x)
                high, low = halves(x)
                x_out[0, :, cs] = high
                x_out[0, :, C + cs.start : C + cs.stop] = low
            r = stacked_dot(x_out[0, :, 0:C], x_out[0, :, C : 2 * C], w_ref.at[0])
            r_out[0] = r
            valid = self.valid(meta, m, 4)
            for cs in CHUNKS:
                kept = valid.keep(r[:, cs])
                sum_out[0, 0:1, cs] = column_sum(kept)
                sum_out[0, 1:2, cs] = column_sum(kept * kept)

        args = self.source_args() + [self.matrix(5)]
        outs = [
            (f32(OWN, rows, C), slots(rows)),
            (bf16(OWN, rows, 2 * C), slots(rows, 2 * C)),
            (f32(OWN, 2, C), slots(2)),
        ]
        scratch = [] if two else [stride_scratch()]
        self.r, self.picked, self.res_sum = call(
            body, self.meta, args, outs, scratch, f"{self.tag}_residual", 6 * OWN * rows * C * C
        )

    def start(self):
        self.z, self.got, self.stats = [], [], []

    def forward(self, after=None, joined=False):
        if not joined:
            self.start()
        for i in range(1 if joined else 0, 5):
            if i == 2:
                self.residual()
            self.forward_layer(i, (after or {}).get(i, ()))


    def segments(self):
        return [(0, HALF), (HALF, HALF)] if self.two else [(0, self.tail_rows)]

    def lengths(self, meta, m):
        if self.two:
            return [meta[m], meta[OWN + m]]
        return [meta[OWN + m]]

    def squeeze(self, sums, counts, se_refs):
        down_t, down_b, up, up_b = se_refs
        means = [s / jnp.maximum(jnp.full((1, C), n.astype(F32)), 1.0) for s, n in zip(sums, counts)]
        ps = [jnp.sum(down_t[...] * mean, axis=1, keepdims=True) + down_b[...] for mean in means]
        gates = [sigmoid(column_sum(up[...] * (p * sigmoid(p))) + up_b[...]) for p in ps]
        return means, ps, gates

    def squeeze_back(self, des, ps, gates, counts, se_refs, means, small, m):
        down_t, down_b, up, up_b = se_refs
        shares, up_grad, down_grad, dq_sum, dp_sum = [], 0.0, 0.0, 0.0, 0.0
        for de, p, gate, n, mean in zip(des, ps, gates, counts, means):
            dq = de * gate * (1.0 - gate)
            s = sigmoid(p)
            dp = jnp.sum(up[...] * dq, axis=1, keepdims=True) * (s * (1.0 + p * (1.0 - s)))
            shares.append(column_sum(down_t[...] * dp) / jnp.maximum(jnp.full((1, C), n.astype(F32)), 1.0))
            up_grad, down_grad = up_grad + (p * s) * dq, down_grad + dp * mean
            dq_sum, dp_sum = dq_sum + dq, dp_sum + dp
        row, col = (lax.broadcasted_iota(jnp.int32, (SE, C), axis) for axis in (0, 1))
        dp_row = column_sum(jnp.where(row == col, dp_sum, 0.0))
        accumulate(small, m, 0, up_grad)
        accumulate(small, m, SE, down_grad)
        accumulate(small, m, 2 * SE, dq_sum)
        accumulate(small, m, 2 * SE + 1, dp_row)
        return shares

    def last_norm(self, m, dt_out, du_out, z_ref, slope_ref, gates, shares, center, spread, res_bias, res_gain, pay, small):
        bias_sum, gain_sum = [], []
        for cs in CHUNKS:
            dh = dt_out[0, :, cs] * self.by_segment(gates, cs) + self.by_segment(shares, cs)
            du = dh * slope_ref[:, cs]
            du_out[0, :, cs] = du
            bias_sum.append(column_sum(du))
            gain_sum.append(column_sum(du * ((z_ref[0, :, cs] - center[:, cs]) * spread[:, cs])))
        rows = [jnp.concatenate(x, axis=1) for x in (bias_sum, gain_sum, res_bias, res_gain)]
        send(pay, rows)
        for j, row in enumerate(rows):
            accumulate(small, m, 2 * SE + 2 + j, row)

    def se_args(self):
        return list(zip(self.excitation, (whole(SE, C), whole(SE, 1), whole(SE, C), whole(1, C))))

    def store_rows(self, ref, rows):
        ref[0] = jnp.concatenate(rows + [jnp.zeros((8 - len(rows), C), F32)], axis=0)

    def store_columns(self, ref, columns):
        ref[0] = jnp.zeros((SE, 8), F32)
        for j, column in enumerate(columns):
            ref[0, :, j : j + 1] = column

    def by_segment(self, rows, cs):
        parts = [jnp.broadcast_to(row[:, cs], (n, LANES)) for row, (_, n) in zip(rows, self.segments())]
        return parts[0] if len(parts) == 1 else jnp.concatenate(parts, axis=0)

    def seg_sums(self, x):
        return [column_sum(x[at : at + n]) for at, n in self.segments()]

    def tail(self, cotangent=None, far=None, after=()):
        return run(self.tail_steps(cotangent, far, after))

    def tail_steps(self, cotangent=None, far=None, after=()):
        two, rows = self.two, self.tail_rows
        back = cotangent is not None

        def body(meta, *refs):
            refs = list(refs)
            take = lambda n: [refs.pop(0) for _ in range(n)]
            m = pl.program_id(0)
            z_ref, got4, r_ref, got3, n_ref, gain, bias = take(7)
            se_refs = take(4)
            if back:
                cot_ref, far_ref = take(2)
            out, stat_out, rstat_out, means_out, p_out, gate_out = take(6)
            if back:
                small, du_out, dt_out, pay = take(4)
            h_ref, = take(1)
            if back:
                slope_ref, = take(1)
            valid = self.valid(meta, m, 4)
            number = n_ref[0, 1:2, :]
            center, spread = center_spread(added(got4), number)
            rcenter, rspread = center_spread(added(got3)[2:4], number)
            stat_out[0, 0:1, :] = center
            stat_out[0, 1:2, :] = spread
            rstat_out[0, 0:1, :] = rcenter
            rstat_out[0, 1:2, :] = rspread
            scale = gain[4:5] * spread
            shift = bias[4:5] - center * scale
            sums = []
            for cs in CHUNKS:
                u = z_ref[0, :, cs] * scale[:, cs] + shift[:, cs]
                s = sigmoid(u)
                h = valid.keep(u * s)
                h_ref[:, cs] = h
                if back:
                    slope_ref[:, cs] = valid.keep(s * (1.0 + u * (1.0 - s)))
                sums.append(self.seg_sums(h))
            sums = [jnp.concatenate([s[j] for s in sums], axis=1) for j in range(len(self.segments()))]
            counts = self.lengths(meta, m)
            means, ps, gates = self.squeeze(sums, counts, se_refs)
            self.store_rows(means_out, means)
            self.store_columns(p_out, ps)
            self.store_rows(gate_out, gates)
            res_gain, res_bias, gate_grad = [], [], []
            for cs in CHUNKS:
                h = h_ref[:, cs]
                rh = (r_ref[0, :, cs] - rcenter[:, cs]) * rspread[:, cs]
                t = h * self.by_segment(gates, cs) + gain[5:6, cs] * rh + bias[5:6, cs]
                s = sigmoid(t)
                out[0, 0:rows, cs] = valid.keep(t * s)
                if rows < SLOT:
                    out[0, rows:SLOT, cs] = jnp.zeros((SLOT - rows, LANES), F32)
                if back:
                    cot = jnp.where(meta[2 * OWN] == 1, far_ref[0, :, cs], cot_ref[0, :, cs])
                    dt = valid.keep(cot * (s * (1.0 + t * (1.0 - s))))
                    dt_out[0, :, cs] = dt
                    res_bias.append(column_sum(dt))
                    res_gain.append(column_sum(dt * rh))
                    gate_grad.append(self.seg_sums(dt * h))
            if not back:
                return
            des = [jnp.concatenate([g[j] for g in gate_grad], axis=1) for j in range(len(counts))]
            shares = self.squeeze_back(des, ps, gates, counts, se_refs, means, small, m)
            self.last_norm(m, dt_out, du_out, z_ref, slope_ref, gates, shares, center, spread, res_bias, res_gain, pay, small)

        args = [
            (self.z[4], slots(rows)), (self.got[4], copies(self.last, 2)), (self.r, slots(rows)),
            (self.got[3], copies(self.last, 4)), (self.number, slots(2)),
            (self.gain, whole(6, C)), (self.bias, whole(6, C)),
        ] + self.se_args()
        outs = [
            (f32(OWN, SLOT, C), slots(SLOT)), (f32(OWN, 2, C), slots(2)), (f32(OWN, 2, C), slots(2)),
            (f32(OWN, 8, C), slots(8)), (f32(OWN, SE, 8), slots(SE, 8)), (f32(OWN, 8, C), slots(8)),
        ]
        scratch = [pltpu.VMEM((rows, C), F32)]
        if back:
            args += [(cotangent, layer(MB - 1, SLOT, C)), (far, slots(SLOT))]
            outs += self.tail_outs()
            scratch.append(pltpu.VMEM((rows, C), F32))
        result = yield body, self.meta, args, outs, scratch, f"{self.tag}_tail", 0, after, ()
        self.stats.append(result[1])
        self.rstat, self.se_state = result[2], result[3:6]
        if back:
            self.tail_results(result[6:])
        return result[0]

    def tail_outs(self):
        rows, count = self.tail_rows, self.first
        return [
            (f32(SMALL, C), whole(TAIL_ROWS, C)), (f32(OWN, rows, C), slots(rows)), (f32(OWN, rows, C), slots(rows)),
            (f32(count, OWN, 4, C), copies(count, 4)),
        ]

    def tail_results(self, result):
        self.small, self.du, self.dt, pay = result
        self.back_got = shared(pay, self.stages)

    def tail_backward_steps(self, cotangent, far, back):
        rows = self.tail_rows

        def body(meta, z_ref, r_ref, stat, rstat, gain, bias, means_ref, p_ref, gate_ref, down, down_b, up, up_b, cot_ref, far_ref, back_ref,
                 small, du_out, dt_out, pay, slope_ref):
            m = pl.program_id(0)
            valid = self.valid(meta, m, 4)
            center, spread, rcenter, rspread = stat[0, 0:1], stat[0, 1:2], rstat[0, 0:1], rstat[0, 1:2]
            scale = gain[4:5] * spread
            shift = bias[4:5] - center * scale
            zeros = jnp.zeros((rows - HALF, LANES), F32)
            counts = self.lengths(meta, m)
            ps = [p_ref[0, :, j : j + 1] for j in range(len(counts))]
            gates = [gate_ref[0, j : j + 1, :] for j in range(len(counts))]
            means = [means_ref[0, j : j + 1, :] for j in range(len(counts))]
            res_gain, res_bias, gate_grad = [], [], []
            for cs in CHUNKS:
                u = z_ref[0, :, cs] * scale[:, cs] + shift[:, cs]
                s = sigmoid(u)
                h = valid.keep(u * s)
                slope_ref[:, cs] = valid.keep(s * (1.0 + u * (1.0 - s)))
                rh = (r_ref[0, :, cs] - rcenter[:, cs]) * rspread[:, cs]
                t = h * self.by_segment(gates, cs) + gain[5:6, cs] * rh + bias[5:6, cs]
                s = sigmoid(t)
                here = jnp.where(meta[2 * OWN] == 1, cot_ref[0, 0:HALF, cs], far_ref[0, :, cs])
                cot = jnp.concatenate([here + back_ref[0, :, cs], zeros], axis=0)
                dt = valid.keep(cot * (s * (1.0 + t * (1.0 - s))))
                dt_out[0, :, cs] = dt
                res_bias.append(column_sum(dt))
                res_gain.append(column_sum(dt * rh))
                gate_grad.append(self.seg_sums(dt * h))
            des = [jnp.concatenate([g[j] for g in gate_grad], axis=1) for j in range(len(counts))]
            shares = self.squeeze_back(des, ps, gates, counts, (down, down_b, up, up_b), means, small, m)
            self.last_norm(m, dt_out, du_out, z_ref, slope_ref, gates, shares, center, spread, res_bias, res_gain, pay, small)

        args = [
            (self.z[4], slots(rows)), (self.r, slots(rows)), (self.stats[4], slots(2)), (self.rstat, slots(2)),
            (self.gain, whole(6, C)), (self.bias, whole(6, C)),
            (self.se_state[0], slots(8)), (self.se_state[1], slots(SE, 8)), (self.se_state[2], slots(8)),
        ] + self.se_args() + [(cotangent, slots(HALF)), (far, layer(MB - 1, HALF, C)), (back, slots(HALF))]
        scratch = [pltpu.VMEM((rows, C), F32)]
        result = yield body, self.meta, args, self.tail_outs(), scratch, f"{self.tag}_tail_back", 0, (), ()
        self.tail_results(result)


    def norm_grad(self, du, zh, scale, sums, number, cs):
        return scale[:, cs] * (du - sums[0:1, cs] / number[:, cs] - zh * (sums[1:2, cs] / number[:, cs]))

    def backward_layer(self, i):
        return run(self.backward_steps(i))

    def backward_steps(self, i):
        two, count = self.two, self.first
        strided = i == 4 and not two
        rows = self.rows_of(i)
        n_src = len(self.source_args())

        def body(meta, *refs):
            refs = list(refs)
            take = lambda n: [refs.pop(0) for _ in range(n)]
            m = pl.program_id(0)
            du_ref, z_ref, w_ref, got, n_ref, stat, gain, bias, dw_ref = take(9)
            if i:
                zp_ref, statp = take(2)
            else:
                dxr_ref, = take(1)
                src = take(n_src)
            small, dz_out = take(2)
            if i:
                du_out, pay = take(2)
            elif two:
                back_out, dx_out = take(2)
            else:
                dx_out, = take(1)
            pad, = take(1)
            alt, = take(1) if refs else (None,)
            sums = added(got)
            number = n_ref[0, 1:2, :] if i == 4 else n_ref[0, 0:1, :]
            center, spread = stat[0, 0:1], stat[0, 1:2]
            scale = gain[i : i + 1] * spread
            valid = self.valid(meta, m, i)
            for cs in CHUNKS:
                zh = (z_ref[0, :, cs] - center[:, cs]) * spread[:, cs]
                dz = valid.keep(self.norm_grad(du_ref[0, :, cs], zh, scale, sums, number, cs))
                high, low = halves(dz)
                dz_out[0, :, cs] = high
                dz_out[0, :, C + cs.start : C + cs.stop] = low
            dy = stacked_dot(dz_out[0, :, 0:C], dz_out[0, :, C : 2 * C], w_ref.at[0], True)
            valid_in = self.valid(meta, m, 0)
            if i:
                pcenter, pspread = statp[0, 0:1], statp[0, 1:2]
                pscale = gain[i - 1 : i] * pspread
                pshift = bias[i - 1 : i] - pcenter * pscale
            taps, bias_sum, gain_sum = [[] for _ in range(TAPS)], [], []
            for c, cs in enumerate(CHUNKS):
                grad = dy[:, cs]
                if strided:
                    grad = spread_out(alt.at[c], grad)
                padded = Padded(pad.at[c], two)
                padded.put(grad)
                if i:
                    z = zp_ref[0, :, cs]
                    u = z * pscale[:, cs] + pshift[:, cs]
                    s = sigmoid(u)
                    h = valid_in.keep(u * s)
                else:
                    h = valid_in.keep(self.source(meta, src, cs))
                dh = None
                for k in range(TAPS):
                    moved = padded.get(2 - k)
                    taps[k].append(column_sum(h * moved))
                    term = dw_ref[0, k : k + 1, cs] * moved
                    dh = term if dh is None else dh + term
                if i:
                    du = valid_in.keep(dh * (s * (1.0 + u * (1.0 - s))))
                    du_out[0, :, cs] = du
                    bias_sum.append(column_sum(du))
                    gain_sum.append(column_sum(du * ((z - pcenter[:, cs]) * pspread[:, cs])))
                    continue
                dxr = dxr_ref[0, :, cs]
                if not two:
                    dxr = spread_out(alt.at[c], dxr)
                dx = valid_in.keep(dh) + dxr
                if two:
                    back_out[0, :, cs] = dx[:HALF]
                    dx = dx[HALF:]
                dx_out[0, :, cs] = dx
            rows = taps + [bias_sum, gain_sum] if i else taps
            rows = [jnp.concatenate(x, axis=1) for x in rows]
            for j, row in enumerate(rows):
                accumulate(small, m, j, row)
            if i:
                send(pay, rows[TAPS:])

        sent = 4 if i == 4 else 2
        args = [
            (self.du, slots(rows)), (self.z[i], slots(rows)), self.matrix(i), (self.back_got, copies(self.last, sent)),
            (self.number, slots(2)), (self.stats[i], slots(2)), (self.gain, whole(6, C)), (self.bias, whole(6, C)),
            (self.dw, layer(i, TAPS, C)),
        ]
        if not i:
            args.append((self.dxr, slots(self.tail_rows)))
        args += self.before_args(i)
        place = TAIL_ROWS // 8 + i
        outs = [(f32(SMALL, C), pl.BlockSpec((8, C), lambda m, *_: (place, 0))), (bf16(OWN, rows, 2 * C), slots(rows, 2 * C))]
        if i:
            outs += [(f32(OWN, SLOT, C), slots(SLOT)), (f32(count, OWN, 2, C), copies(count, 2))]
        elif two:
            outs += [(f32(OWN, HALF, C), slots(HALF)), (f32(OWN, HALF, C), slots(HALF))]
        else:
            outs += [(f32(OWN, SLOT, C), slots(SLOT))]
        scratch = [pad_scratch()]
        if strided or (i == 0 and not two):
            scratch.append(stride_scratch())
        flops = 6 * OWN * rows * C * C
        self.small, dz, *result = yield (
            body, self.meta, args, outs, scratch, f"{self.tag}_backward_{i}", flops, self.done, (self.small,)
        )
        got = self.back_got
        if i:
            self.du = result[0]
            if i == self.stop:
                self.pending = dz, result[1]
                return result
            self.back_got = shared(result[1], self.stages)
        self.weight_grad(i, dz)
        if i == 4:
            self.residual_back(got)
        return result

    def residual_back(self, got):
        rows = self.tail_rows

        def body(meta, got, n_ref, dt_ref, r_ref, rstat, gain, w_ref, x_ref, kept_out, away_out, dxr_out, dr, total):
            m = pl.program_id(0)
            sums = added(got)[2:4]
            number = n_ref[0, 1:2, :]
            center, spread = rstat[0, 0:1], rstat[0, 1:2]
            scale = gain[5:6] * spread
            valid = self.valid(meta, m, 4)
            for cs in CHUNKS:
                rh = (r_ref[0, :, cs] - center[:, cs]) * spread[:, cs]
                high, low = halves(valid.keep(self.norm_grad(dt_ref[0, :, cs], rh, scale, sums, number, cs)))
                dr[:, cs] = high
                dr[:, C + cs.start : C + cs.stop] = low
            high, low = dr[:, 0:C], dr[:, C : 2 * C]
            dxr_out[0] = stacked_dot(high, low, w_ref.at[0], True)
            grad = stacked_outer(x_ref[0, :, 0:C], x_ref[0, :, C : 2 * C], high, low)
            self.add_halves(meta, m, grad, total, kept_out, away_out)

        args = [
            (got, copies(self.last, 4)), (self.number, slots(2)), (self.dt, slots(rows)), (self.r, slots(rows)),
            (self.rstat, slots(2)), (self.gain, whole(6, C)), self.matrix(5), (self.picked, slots(rows, 2 * C)),
        ]
        outs = self.piece_out(5) + [(f32(OWN, rows, C), slots(rows))]
        which = PLACES[5][0]
        *self.pieces[which], self.dxr = call(
            body, self.meta, args, outs, [pltpu.VMEM((rows, 2 * C), BF16), pltpu.VMEM((C, C), F32)],
            f"{self.tag}_residual_back", 12 * OWN * rows * C * C, into=self.pieces[which],
        )

    def piece_out(self, i):
        which, place = PLACES[i]
        rows = PIECE_ROWS[which]
        return [(f32(rows, C), pl.BlockSpec((C // 2, C), lambda m, *_: (place, 0)))] * 2

    def add_halves(self, meta, m, grad, total, kept_out, away_out):
        @pl.when(m == 0)
        def _():
            total[...] = grad

        @pl.when(m > 0)
        def _():
            top, bottom = total[0 : C // 2] + grad[0 : C // 2], total[C // 2 : C] + grad[C // 2 : C]
            lower = meta[2 * OWN] == 1
            kept_out[...] = jnp.where(lower, top, bottom)
            away_out[...] = jnp.where(lower, bottom, top)

    def weight_grad(self, i, dz):
        two = self.two
        strided = i == 4 and not two
        rows = self.rows_of(i)
        n_src = len(self.source_args())

        def body(meta, *refs):
            refs = list(refs)
            take = lambda n: [refs.pop(0) for _ in range(n)]
            m = pl.program_id(0)
            if i:
                zp_ref, statp, gain, bias = take(4)
                center, spread = statp[0, 0:1], statp[0, 1:2]
                scale = gain[i - 1 : i] * spread
                shift = bias[i - 1 : i] - center * scale
            else:
                src = take(n_src)
            dz_ref, dw_ref, kept_out, away_out, pad, yh, yl, total = take(8)
            alt, = take(1) if strided else (None,)
            valid_in = self.valid(meta, m, 0)
            for c, cs in enumerate(CHUNKS):
                if i:
                    u = zp_ref[0, :, cs] * scale[:, cs] + shift[:, cs]
                    h = valid_in.keep(u * sigmoid(u))
                else:
                    h = valid_in.keep(self.source(meta, src, cs))
                padded = Padded(pad.at[c], two)
                padded.put(h)
                y = padded.conv(dw_ref[0, :, cs])
                if strided:
                    y = every_other(alt.at[c], y)
                yh[:, cs], yl[:, cs] = halves(y)
            grad = stacked_outer(yh[...], yl[...], dz_ref[0, :, 0:C], dz_ref[0, :, C : 2 * C])
            self.add_halves(meta, m, grad, total, kept_out, away_out)

        args = self.before_args(i)
        if i:
            args += [(self.gain, whole(6, C)), (self.bias, whole(6, C))]
        args += [(dz, slots(rows, 2 * C)), (self.dw, layer(i, TAPS, C))]
        scratch = [pad_scratch(), pltpu.VMEM((rows, C), BF16), pltpu.VMEM((rows, C), BF16), pltpu.VMEM((C, C), F32)]
        if strided:
            scratch.append(stride_scratch())
        which = PLACES[i][0]
        self.pieces[which] = call(
            body, self.meta, args, self.piece_out(i), scratch, f"{self.tag}_weights_{i}", 6 * OWN * rows * C * C,
            into=self.pieces[which],
        )
        self.done = (self.pieces[which][0],)

    def backward(self, layers):
        if layers[0] == 4:
            self.pieces = [[], []]
        for i in layers:
            result = self.backward_layer(i)
        return result

    def resume(self, i):
        dz, payload = self.pending
        self.back_got = shared(payload, self.stages)
        self.weight_grad(i, dz)

    def fork(self, state=None):
        other = copy.copy(self)
        other.__dict__.update(state or {})
        if "pieces" in other.__dict__:
            other.pieces = list(other.pieces)
        return other

    def state(self):
        return {name: getattr(self, name) for name in ("du", "dxr", "pieces", "small", "pending")}

    def half(self, no, first, begin=None, end=None):
        kept, away = self.pieces[no]
        if no:
            parts = self.small[: SMALL // 2], self.small[SMALL // 2 :]
            at = kept.shape[0] - SMALL // 2
            kept = lax.dynamic_update_slice_in_dim(kept, jnp.where(first, *parts), at, 0)
            away = lax.dynamic_update_slice_in_dim(away, jnp.where(first, *parts[::-1]), at, 0)
        if begin is not None:
            away, _ = lax.optimization_barrier((away, begin))
            kept, _ = lax.optimization_barrier((kept, end))
        return kept + swap(away)


PLACES = {3: (0, 0), 4: (0, 1), 5: (0, 2), 0: (1, 0), 1: (1, 1), 2: (1, 2)}
PIECE_ROWS = (3 * C // 2, 3 * C // 2 + SMALL // 2)


def split_squeeze(meta, own, far):
    def body(meta, own_ref, far_ref, *outs):
        row, col = (lax.broadcasted_iota(jnp.int32, (SE, C), axis) for axis in (0, 1))
        for block in range(2):
            down, down_b, up, up_b = outs[4 * block : 4 * block + 4]
            down[...] = choose(meta, block, own_ref[0:SE, :], far_ref[0:SE, :])
            up[...] = choose(meta, block, own_ref[SE : 2 * SE, :], far_ref[SE : 2 * SE, :])
            up_b[...] = choose(meta, block, own_ref[2 * SE : 2 * SE + 1, :], far_ref[2 * SE : 2 * SE + 1, :])
            wide = choose(meta, block, own_ref[2 * SE + 1 : 2 * SE + 2, :], far_ref[2 * SE + 1 : 2 * SE + 2, :])
            down_b[...] = jnp.sum(jnp.where(row == col, wide, 0.0), axis=1, keepdims=True)

    shapes = [(SE, C), (SE, 1), (SE, C), (1, C)] * 2
    args = [(x, whole(*x.shape)) for x in (own, far)]
    outs = call(body, meta, args, [(f32(*shape), whole(*shape)) for shape in shapes], name="split_squeeze", steps=1)
    return tuple(outs[:4]), tuple(outs[4:])


def pick_joining(picks, features):
    def body(picks, in_ref, out_ref):
        out_ref[...] = in_ref[0, 0]

    own = pl.BlockSpec((1, 1, HALF, C), lambda m, picks: (picks[m], 1, 0, 0))
    out = (f32(OWN * HALF, C), pl.BlockSpec((HALF, C), lambda m, *_: (m, 0)))
    return call(body, picks, [(features, own)], [out], name="pick_joining")[0]


def swap(x):
    return lax.ppermute(x, "section", [(0, 1), (1, 0)])


def fenced(always, work, x):
    shapes = jax.eval_shape(work, x)
    return lax.cond(always, work, lambda x: jax.tree.map(lambda y: jnp.zeros(y.shape, y.dtype), shapes), x)


class Reduction:
    def __init__(self, x, stages):
        self.x = x
        self.todo = []
        stride = 1
        for radix in stages:
            self.todo.append((True, radix, stride))
            stride *= radix
        self.todo += [(False, radix, stride) for _, radix, stride in reversed(self.todo)]

    def step(self):
        scatter, radix, stride = self.todo.pop(0)
        rows = self.x.shape[0]
        if scatter:
            parts = exchange(self.x.reshape(radix, rows // radix, C), radix, stride)
            self.x = jnp.sum(parts, axis=0)
        else:
            parts = exchange(jnp.broadcast_to(self.x, (radix,) + self.x.shape), radix, stride)
            self.x = parts.reshape(radix * rows, C)
        return (self.x,)

    def finish(self):
        while self.todo:
            self.step()
        return self.x


def per_device(features, out_grad, lengths, join_pick, dw, pw, gain, bias, res_w, down, down_b, up, up_b):
    first = lax.axis_index("section") == 0
    size = lax.axis_size("dp")
    inputs = features.reshape(MB, SLOT, C)
    cotangent = out_grad.reshape(MB, SLOT, C)
    own, picks = lengths[0, 0], join_pick[0]
    to_upper = lambda x: lax.ppermute(x, "section", [(0, 1)])
    to_lower = lambda x: lax.ppermute(x, "section", [(1, 0)])

    far_len = swap(own)
    far_rows = to_upper(inputs[MB - 1])
    far_w0 = swap(pw[0, 0:1])
    taps = jnp.concatenate([dw[0].reshape(5 * TAPS, C), gain[0], bias[0]], axis=0)
    far_taps = swap(taps)
    far_pw, far_res = swap(pw[0]), swap(res_w[0])
    wide = jnp.pad(down_b, ((0, 0), (0, C - SE)))
    squeeze = jnp.concatenate([down[0].T, up[0], up_b, wide], axis=0)
    far_squeeze = swap(squeeze)
    far_cot = swap(cotangent)

    flag = first.astype(jnp.int32)[None]
    mine = lambda v: jnp.where(first, v[:OWN], jnp.concatenate([v[OWN:], jnp.zeros((1,), v.dtype)]))
    length = mine(jnp.where(first, own, far_len))
    half_len = (length + 1) // 2
    join_len = mine(jnp.where(first, far_len, own)[picks])
    meta1 = jnp.concatenate([length, half_len, flag])
    meta2 = jnp.concatenate([half_len, join_len, flag, picks[MB - 1 :]])
    both = jnp.concatenate([length, half_len, flag, half_len, join_len, flag, picks[MB - 1 :]])

    def small(block):
        own, far = taps, far_taps
        if block:
            own, far, _ = lax.optimization_barrier((taps, far_taps, c14.z[3]))
        t = jnp.where(first == (block == 0), own, far)
        return t[: 5 * TAPS].reshape(5, TAPS, C), t[5 * TAPS : 5 * TAPS + 6], t[5 * TAPS + 6 :]

    excitations = split_squeeze(meta1, squeeze, far_squeeze)

    def prepared(block, start, stop):
        array = prepare(meta1, (pw[0], res_w[0]), (far_pw, far_res), block, start, stop)
        return array, {i: (array, i - start) for i in range(start, stop)}

    parts0 = [prepared(0, 1, 3), prepared(0, 3, 6)]
    parts1 = [prepared(1, 0, 1), prepared(1, 1, 4), prepared(1, 4, 6)]

    stages, deep = radices(size, 16), radices(size, 4)
    c14 = Block(False, meta1, small(0), {**parts0[0][1], **parts0[1][1]}, stages)
    c14.x, c14.x_far, c14.first_matrix = inputs, far_rows, (pw[0], far_w0)
    c14.excitation = excitations[0]
    c14.forward({1: excitations[0], 2: (parts0[1][0],)})
    late_picks, _ = lax.optimization_barrier((picks, c14.z[3]))
    far_joining = to_lower(pick_joining(late_picks, features.reshape(MB, 2, HALF, C)))
    c15 = Block(True, meta2, small(1), {**parts1[0][1], **parts1[1][1], **parts1[2][1]}, stages)
    c15.excitation = excitations[1]
    c15.arrived, c15.joined_far, c15.joined = Linked(0, HALF), far_joining, features.reshape(MB, 2, HALF, C)
    c15.start()
    out0, _ = run_joined(c14.tail_steps(), c15.forward_steps(0), (both, 0, meta1.shape[0]))
    c15.arrived = out0
    c15.forward({1: (parts1[1][0],), 2: (parts1[2][0],)}, joined=True)
    out1 = c15.tail(cotangent, far_cot)
    c15.stop = 2
    c15.backward((4, 3))
    begin = c15.back_got
    c15.backward((2,))
    always = own[0] > 0

    half0 = c15.half(0, first, begin, c15.du)
    sum0 = lax.psum(half0, "dp")

    def middle(half0):
        upper, lower = c15.fork(), c14.fork()
        upper.resume(2)
        upper.done += (half0,)
        upper.backward((1,))
        (_, dx1), _ = run_joined(
            upper.backward_steps(0), lower.tail_backward_steps(cotangent, far_cot, Linked(2, HALF)), (both, meta1.shape[0], 0)
        )
        lower.done = upper.done
        lower.backward((4,))
        begin1 = lower.back_got
        lower.backward((3,))
        half1 = upper.half(1, first, begin1, lower.du)
        begin2 = lower.back_got
        lower.stop = 2
        lower.backward((2,))
        half2 = lower.half(0, first, begin2, lower.du)
        return dx1, jnp.concatenate([half1, half2], axis=0), lower.state()

    dx1, half12, state = fenced(always, middle, half0)
    sum0, half12 = lax.optimization_barrier((sum0, half12))
    sum12 = lax.psum(half12, "dp")

    def ending(half12):
        last = c14.fork(state)
        last.resume(2)
        last.done += (half12,)
        came0 = to_upper(sum0)
        dx0, = last.backward((1, 0))
        half3 = last.half(1, first)
        half3, dx0, *kept = lax.optimization_barrier((half3, dx0, out0, out1, dx1))
        reduction = Reduction(half3, deep)
        reduction.step()
        pad = jnp.zeros((1, HALF, C), F32)
        lower = jnp.concatenate([kept[0], jnp.concatenate([to_lower(kept[0][0:1, :HALF]), pad], axis=1)], axis=0)
        upper = jnp.concatenate([to_upper(kept[1]), kept[1][0:1]], axis=0)
        block_out = jnp.where(first, lower, upper)
        lower = jnp.concatenate([dx0, to_lower(dx0[0:1])], axis=0)
        joins = jnp.concatenate([to_upper(kept[2]), kept[2][0:1]], axis=0)
        joins = jnp.stack([lax.dynamic_index_in_dim(joins, jnp.argmax(picks == s), 0, False) for s in range(MB)])
        upper = jnp.concatenate([jnp.zeros_like(joins), joins], axis=1)
        dx = jnp.where(first, lower, upper)
        reduction.x, block_out, dx, came0 = lax.optimization_barrier((reduction.x, block_out, dx, came0))
        return block_out, dx, came0, reduction.finish()

    block_out, dx, came0, sum3 = fenced(always, ending, half12)
    came3 = to_lower(sum3)
    sum12, _ = lax.optimization_barrier((sum12, sum3))
    came12 = swap(sum12)
    split, lead = PIECE_ROWS[1], 3 * C // 2

    def assembled(rest_top, rest_bottom, lead_top, lead_bottom):
        halves_of = lambda x: x.reshape(-1, 1, C // 2, C)
        both = lambda top, bottom: jnp.concatenate([halves_of(top), halves_of(bottom)], axis=1).reshape(-1, C, C)
        rest, top = both(rest_top[:lead], rest_bottom[:lead]), both(lead_top[:C], lead_bottom[:C])
        res = both(lead_top[C:], lead_bottom[C:])
        return jnp.concatenate([rest, top], axis=0)[None], res, jnp.concatenate([rest_top[lead:], rest_bottom[lead:]], axis=0)

    pw_grad, res_grad, rows = lax.cond(
        first,
        lambda s3, c3, s12, c12, s0, c0: assembled(s3, c3, s12[split:], c12[split:]),
        lambda s3, c3, s12, c12, s0, c0: assembled(c12[:split], s12[:split], c0, s0),
        sum3, came3, sum12, came12, sum0, came0,
    )
    dw_grad = rows[TAIL_ROWS : TAIL_ROWS + 40].reshape(1, 5, 8, C)
    norms = jnp.concatenate([dw_grad[0, 1:, TAPS : TAPS + 2], rows[None, 2 * SE + 2 : 2 * SE + 4], rows[None, 2 * SE + 4 : 2 * SE + 6]], axis=0)
    return (
        block_out.reshape(features.shape), dx.reshape(features.shape), dw_grad[:, :, :TAPS], pw_grad,
        norms[None, :, 1], norms[None, :, 0], res_grad, rows[SE : 2 * SE].T[None], rows[2 * SE + 1 : 2 * SE + 2, :SE],
        rows[:SE][None], rows[2 * SE : 2 * SE + 1],
    )


def solution(mesh):
    rows = P("section", "dp", None)
    own = lambda dims: P("section", *([None] * dims))
    weights = (own(3), own(3), own(2), own(2), own(2), own(2), own(1), own(2), own(1))
    in_specs = (rows, rows, rows, P("dp", None), *weights)
    out_specs = (rows, rows, *weights)
    return jax.shard_map(per_device, mesh=mesh, in_specs=in_specs, out_specs=out_specs, check_vma=False)
```

```python
import copy

import jax
import jax.numpy as jnp
from jax import lax
from jax.experimental import pallas as pl
from jax.experimental.pallas import tpu as pltpu
from jax.sharding import PartitionSpec as P

EPSILON = 1e-05
EXACT = lax.Precision.HIGHEST
TAPS = 5
MB = 3
OWN = 2
SLOT = 400
HALF = 200
KEPT = 208
C = 512
LANES = 128
CHUNKS = [slice(c, c + LANES) for c in range(0, C, LANES)]
SE = 64
BF16, F32 = jnp.bfloat16, jnp.float32
VMEM_BYTES = 60 << 20
TAIL_ROWS = 2 * SE + 8
SMALL = 256


def radices(size, most):
    stages, left = [], size
    while left > 1:
        radix = min(most, left)
        while left % radix:
            radix -= 1
        stages.append(radix)
        left //= radix
    return stages


def exchange(block, radix, stride):
    size = lax.axis_size("dp")
    if radix == size:
        return lax.all_to_all(block, "dp", 0, 0)
    groups = []
    for base in range(size):
        if (base // stride) % radix == 0:
            groups.append([base + j * stride for j in range(radix)])
    return lax.all_to_all(block, "dp", 0, 0, axis_index_groups=groups)


def shared(block, stages):
    stride = 1
    for no, radix in enumerate(stages):
        if no:
            block = jnp.broadcast_to(jnp.sum(block, axis=0), (radix,) + block.shape[1:])
        block = exchange(block, radix, stride)
        stride *= radix
    return block


def halves(x):
    high = x.astype(BF16)
    return high, (x - high.astype(F32)).astype(BF16)


def sigmoid(x):
    return 0.5 * jnp.tanh(0.5 * x) + 0.5


def exact_dot(a, b, dims=((1,), (0,))):
    return lax.dot_general(a, b, (dims, ((), ())), precision=EXACT, preferred_element_type=F32)


def fast_dot(a, b, dims=((1,), (0,))):
    return lax.dot_general(a, b, (dims, ((), ())), preferred_element_type=F32)


def stacked_dot(high, low, w, back=False):
    w_high, w_low = w[0], w[1]
    w = jnp.concatenate([w_high, w_high, w_low], axis=1 if back else 0)
    x = jnp.concatenate([high, low, high], axis=1)
    return fast_dot(x, w, ((1,), (1 if back else 0,)))


def stacked_outer(a_high, a_low, b_high, b_low):
    a = jnp.concatenate([a_high, a_low, a_high], axis=0)
    b = jnp.concatenate([b_high, b_high, b_low], axis=0)
    return fast_dot(a, b, ((0,), (0,)))


def column_sum(x):
    return jnp.sum(x, axis=0, keepdims=True)


class Rows:
    def __init__(self, meta, m, two, rows, which=0):
        place = lax.broadcasted_iota(jnp.int32, (rows, LANES), 0)
        if two:
            later = place >= HALF
            limit = jnp.where(later, HALF + meta[OWN + m], meta[m])
            self.mask = place < limit
        else:
            self.mask = place < meta[which * OWN + m]

    def keep(self, x):
        return jnp.where(self.mask, x, 0.0)


class Padded:
    def __init__(self, ref, two):
        self.ref = ref
        self.pieces = [(8, 0, HALF), (16 + HALF, HALF, HALF)] if two else [(8, 0, SLOT)]

    def put(self, x):
        zeros = jnp.zeros((8, LANES), F32)
        for at, start, rows in self.pieces:
            self.ref[at - 8 : at, :] = zeros
            self.ref[at : at + rows, :] = x[start : start + rows]
        self.ref[at + rows : at + rows + 8, :] = zeros

    def get(self, offset):
        parts = [self.ref[at + offset : at + offset + rows, :] for at, _, rows in self.pieces]
        return parts[0] if len(parts) == 1 else jnp.concatenate(parts, axis=0)

    def conv(self, kernel):
        total = kernel[0:1] * self.get(-2)
        for k in range(1, TAPS):
            total = total + kernel[k : k + 1] * self.get(k - 2)
        return total

    def conv_back(self, kernel):
        total = kernel[0:1] * self.get(2)
        for k in range(1, TAPS):
            total = total + kernel[k : k + 1] * self.get(2 - k)
        return total


def every_other(ref, x):
    ref[0:SLOT, :] = x
    ref[SLOT : 2 * KEPT, :] = jnp.zeros((2 * KEPT - SLOT, LANES), F32)
    return ref[pl.ds(0, KEPT, stride=2), :]


def spread_out(ref, x):
    ref[...] = jnp.zeros_like(ref)
    ref[pl.ds(0, KEPT, stride=2), :] = x
    return ref[0:SLOT, :]


def center_spread(sums, rows):
    center = sums[0:1] / rows
    return center, lax.rsqrt(sums[1:2] / rows - center * center + EPSILON)


def added(ref):
    return jnp.sum(ref[:, 0], axis=0)


def accumulate(ref, m, at, value):
    rows = slice(at, at + value.shape[0])
    ref[rows, :] = jnp.where(m == 0, value, ref[rows, :] + value)


def send(ref, rows):
    for copy in range(ref.shape[0]):
        for row, x in enumerate(rows):
            ref[copy, 0, row : row + 1, 0 : x.shape[1]] = x


def pad_scratch():
    return pltpu.VMEM((len(CHUNKS), SLOT + 24, LANES), F32)


def stride_scratch():
    return pltpu.VMEM((len(CHUNKS), 2 * KEPT, LANES), F32)


def slots(rows, cols=C):
    return pl.BlockSpec((1, rows, cols), lambda m, *_: (m, 0, 0))


def copies(count, rows, cols=C):
    return pl.BlockSpec((count, 1, rows, cols), lambda m, *_: (0, m, 0, 0))


def whole(*shape):
    return pl.BlockSpec(shape, lambda m, *_: (0,) * len(shape))


def layer(i, *shape):
    return pl.BlockSpec((1,) + shape, lambda m, *_: (i,) + (0,) * len(shape))


def f32(*shape):
    return jax.ShapeDtypeStruct(shape, F32)


def bf16(*shape):
    return jax.ShapeDtypeStruct(shape, BF16)


def call(body, meta, args, outs, scratch=(), name=None, flops=0, steps=OWN, after=(), into=()):
    arrays, in_specs = [a for a, _ in args], [s for _, s in args]
    shapes, out_specs = [a for a, _ in outs], [s for _, s in outs]
    size = sum(a.size * a.dtype.itemsize for a in arrays + shapes)
    extra = list(after) + list(into)
    count = len(arrays)

    def inner(meta, *refs):
        body(meta, *refs[:count], *refs[count + len(extra) :])

    return pl.pallas_call(
        inner,
        out_shape=shapes,
        grid_spec=pltpu.PrefetchScalarGridSpec(
            num_scalar_prefetch=1,
            grid=(steps,),
            in_specs=in_specs + [pl.BlockSpec(memory_space=pl.ANY)] * len(extra),
            out_specs=out_specs,
            scratch_shapes=list(scratch),
        ),
        input_output_aliases={1 + count + len(after) + j: j for j in range(len(into))},
        compiler_params=pltpu.CompilerParams(vmem_limit_bytes=VMEM_BYTES),
        cost_estimate=pl.CostEstimate(flops=flops, bytes_accessed=size, transcendentals=0),
        name=name,
    )(meta, *arrays, *extra)


class Linked:
    def __init__(self, index, rows):
        self.index, self.rows = index, rows


class Part:
    def __init__(self, ref, at):
        self.ref, self.at = ref, at

    def __getitem__(self, index):
        return self.ref[self.at + index]


def run(steps):
    body, meta, args, outs, scratch, name, flops, after, into = next(steps)
    return finish(steps, call(body, meta, args, outs, scratch, name, flops, after=after, into=into))


def finish(steps, results):
    try:
        steps.send(results)
    except StopIteration as stop:
        return stop.value


def run_joined(one, two, scalars):
    meta, at1, at2 = scalars
    body1, _, args1, outs1, scratch1, name1, flops1, after1, into1 = next(one)
    body2, _, args2, outs2, scratch2, name2, flops2, after2, into2 = next(two)
    assert not into2
    own2 = [arg for arg in args2 if not isinstance(arg[0], Linked)]
    sizes = len(args1), len(own2), len(outs1), len(outs2), len(scratch1), len(scratch2)

    def body(meta, *refs):
        refs = list(refs)
        in1, in2, out1, out2, scr1, scr2 = [[refs.pop(0) for _ in range(n)] for n in sizes]
        body1(Part(meta, at1), *in1, *out1, *scr1)
        linked = []
        for arg in args2:
            link = arg[0]
            linked.append(out1[link.index].at[:, 0 : link.rows, :] if isinstance(link, Linked) else in2.pop(0))
        body2(Part(meta, at2), *linked, *out2, *scr2)

    def moved(spec, at):
        if spec.index_map is None:
            return spec
        return pl.BlockSpec(spec.block_shape, lambda m, meta: spec.index_map(m, Part(meta, at)))

    args = [(a, moved(spec, at1)) for a, spec in args1] + [(a, moved(spec, at2)) for a, spec in own2]
    results = call(
        body, meta, args, [(a, moved(spec, at1)) for a, spec in outs1] + [(a, moved(spec, at2)) for a, spec in outs2], list(scratch1) + list(scratch2), f"{name1}_{name2}", flops1 + flops2,
        after=(*after1, *after2), into=into1,
    )
    return finish(one, results[: len(outs1)]), finish(two, results[len(outs1) :])


def choose(meta, block, own, far):
    return jnp.where(meta[2 * OWN] == 1 - block, own, far)


def prepare(meta, own, far, block, start, stop):
    def body(meta, *refs):
        pair = [ref[0] for ref in refs[:2]]
        if stop == 6:
            last = pl.program_id(0) == 5 - start
            pair = [jnp.where(last, ref[...], w) for ref, w in zip(refs[2:4], pair)]
        out = refs[-1]
        out[0, 0], out[0, 1] = halves(choose(meta, block, *pair))

    matrix = pl.BlockSpec((1, C, C), lambda j, *_: (jnp.minimum(j + start, 4), 0, 0))
    args = [(own[0], matrix), (far[0], matrix)]
    if stop == 6:
        args += [(own[1], whole(C, C)), (far[1], whole(C, C))]
    out = pl.BlockSpec((1, 2, C, C), lambda j, *_: (j, 0, 0, 0))
    name = f"prepare_{block}_{start}"
    return call(body, meta, args, [(bf16(stop - start, 2, C, C), out)], name=name, steps=stop - start)[0]


class Block:
    def __init__(self, two, meta, weights, ready, stages):
        self.done, self.stop, self.pending = (), None, None
        self.two, self.meta, self.stages = two, meta, stages
        self.dw, self.gain, self.bias = weights
        self.ready = ready
        self.tail_rows = SLOT if two else KEPT
        self.first, self.last = stages[0], stages[-1]
        self.tag = "c15" if two else "c14"

    def rows_of(self, i):
        return self.tail_rows if i == 4 else SLOT

    def valid(self, meta, m, i):
        last = i == 4 and not self.two
        return Rows(meta, m, self.two, self.rows_of(i), which=1 if last else 0)

    def matrix(self, i):
        array, at = self.ready[i]
        return (array, layer(at, 2, C, C))

    def source_args(self):
        if not self.two:
            return [(self.x, slots(SLOT)), (self.x_far, whole(SLOT, C))]
        far = pl.BlockSpec((HALF, C), lambda m, *_: (m, 0))
        near = pl.BlockSpec((1, 1, HALF, C), lambda m, meta: (meta[2 * OWN + 1], 1, 0, 0))
        return [(self.arrived, slots(HALF)), (self.joined_far, far), (self.joined, near)]

    def source(self, meta, refs, cs):
        lower = meta[2 * OWN] == 1
        if not self.two:
            return jnp.where(lower, refs[0][0, :, cs], refs[1][:, cs])
        joined = jnp.where(lower, refs[1][:, cs], refs[2][0, 0, :, cs])
        return jnp.concatenate([refs[0][0, :, cs], joined], axis=0)

    def before_args(self, i):
        if i == 0:
            return self.source_args()
        return [(self.z[i - 1], slots(SLOT)), (self.stats[i - 1], slots(2))]


    def forward_layer(self, i, after=()):
        return run(self.forward_steps(i, after))

    def forward_steps(self, i, after=()):
        two, count = self.two, self.first
        strided = i == 4 and not two
        rows = self.rows_of(i)
        n_src = len(self.source_args())
        width = C + LANES if i == 0 else C
        sent = 4 if i == 3 else 2
        makes = i == 0 and not two

        def body(meta, *refs):
            refs = list(refs)
            take = lambda n: [refs.pop(0) for _ in range(n)]
            m = pl.program_id(0)
            if i == 0:
                src = take(n_src)
            else:
                z_ref, got_ref = take(2)
                n_ref, = take(1) if i > 1 else (None,)
                gain_ref, bias_ref = take(2)
                res_sum, = take(1) if i == 3 else (None,)
            dw_ref, = take(1)
            if makes:
                own_ref, far_ref, z_out, pay, w_ref = take(5)

                @pl.when(m == 0)
                def _():
                    w_ref[0, 0], w_ref[0, 1] = halves(choose(meta, 0, own_ref[0], far_ref[0]))

            else:
                w_ref, z_out, pay = take(3)
            if i:
                stat_out, = take(1)
            if i == 1:
                n_out, = take(1)
            pad, y_ref = take(2)
            alt, = take(1) if strided else (None,)
            valid_in = self.valid(meta, m, 0)
            if i:
                sums = added(got_ref)
                if i == 1:
                    count_in = jnp.maximum(jnp.concatenate([sums[0:1, C:]] * len(CHUNKS), axis=1), 1.0)
                    count_out = jnp.maximum(jnp.concatenate([sums[1:2, C:]] * len(CHUNKS), axis=1), 1.0)
                    n_out[0, 0:1, :] = count_in
                    n_out[0, 1:2, :] = count_out
                else:
                    count_in = n_ref[0, 0:1, :]
                center, spread = center_spread(sums[:, :C], count_in)
                stat_out[0, 0:1, :] = center
                stat_out[0, 1:2, :] = spread
                scale = gain_ref[i - 1 : i] * spread
                shift = bias_ref[i - 1 : i] - center * scale
            for c, cs in enumerate(CHUNKS):
                if i == 0:
                    h = valid_in.keep(self.source(meta, src, cs))
                else:
                    u = z_ref[0, :, cs] * scale[:, cs] + shift[:, cs]
                    h = valid_in.keep(u * sigmoid(u))
                padded = Padded(pad.at[c], two)
                padded.put(h)
                y = padded.conv(dw_ref[0, :, cs])
                if strided:
                    y = every_other(alt.at[c], y)
                high, low = halves(y)
                y_ref[:, cs] = high
                y_ref[:, C + cs.start : C + cs.stop] = low
            w = w_ref.at[0] if makes else w_ref.at[0]
            z = stacked_dot(y_ref[:, 0:C], y_ref[:, C : 2 * C], w)
            z_out[0] = z
            valid = self.valid(meta, m, i)
            one, square = [], []
            for cs in CHUNKS:
                kept = valid.keep(z[:, cs])
                one.append(column_sum(kept))
                square.append(column_sum(kept * kept))
            if i == 0:
                if two:
                    number = (meta[m] + meta[OWN + m]).astype(F32)
                    numbers = number, number
                else:
                    numbers = meta[m].astype(F32), meta[OWN + m].astype(F32)
                one.append(jnp.full((1, LANES), numbers[0], F32))
                square.append(jnp.full((1, LANES), numbers[1], F32))
            out = [jnp.concatenate(one, axis=1), jnp.concatenate(square, axis=1)]
            if i == 3:
                out += [res_sum[0, 0:1, :], res_sum[0, 1:2, :]]
            send(pay, out)

        if i == 0:
            args = list(self.source_args())
        else:
            got = 4 if i == 4 else 2
            args = [(self.z[i - 1], slots(SLOT)), (self.got[i - 1], copies(self.last, got, C + LANES if i == 1 else C))]
            if i > 1:
                args.append((self.number, slots(2)))
            args += [(self.gain, whole(6, C)), (self.bias, whole(6, C))]
            if i == 3:
                args.append((self.res_sum, slots(2)))
        args.append((self.dw, layer(i, TAPS, C)))
        args += [(w, layer(0, C, C)) for w in self.first_matrix] if makes else [self.matrix(i)]
        outs = [(f32(OWN, rows, C), slots(rows)), (f32(count, OWN, sent, width), copies(count, sent, width))]
        if i:
            outs.append((f32(OWN, 2, C), slots(2)))
        if i == 1:
            outs.append((f32(OWN, 2, C), slots(2)))
        if makes:
            outs.append((bf16(1, 2, C, C), layer(0, 2, C, C)))
        scratch = [pad_scratch(), pltpu.VMEM((rows, 2 * C), BF16)]
        if strided:
            scratch.append(stride_scratch())
        flops = 6 * OWN * rows * C * C
        result = yield body, self.meta, args, outs, scratch, f"{self.tag}_forward_{i}", flops, after, ()
        self.z.append(result[0])
        if makes:
            self.ready[0] = (result[2], 0)
        if i:
            self.stats.append(result[2])
        if i == 1:
            self.number = result[3]
        self.got.append(shared(result[1], self.stages))

    def residual(self):
        two, rows = self.two, self.tail_rows

        def body(meta, *refs):
            refs = list(refs)
            src = [refs.pop(0) for _ in self.source_args()]
            w_ref, r_out, x_out, sum_out = refs[:4]
            alt = refs[4] if not two else None
            m = pl.program_id(0)
            valid_in = self.valid(meta, m, 0)
            for c, cs in enumerate(CHUNKS):
                x = valid_in.keep(self.source(meta, src, cs))
                if not two:
                    x = every_other(alt.at[c], x)
                high, low = halves(x)
                x_out[0, :, cs] = high
                x_out[0, :, C + cs.start : C + cs.stop] = low
            r = stacked_dot(x_out[0, :, 0:C], x_out[0, :, C : 2 * C], w_ref.at[0])
            r_out[0] = r
            valid = self.valid(meta, m, 4)
            for cs in CHUNKS:
                kept = valid.keep(r[:, cs])
                sum_out[0, 0:1, cs] = column_sum(kept)
                sum_out[0, 1:2, cs] = column_sum(kept * kept)

        args = self.source_args() + [self.matrix(5)]
        outs = [
            (f32(OWN, rows, C), slots(rows)),
            (bf16(OWN, rows, 2 * C), slots(rows, 2 * C)),
            (f32(OWN, 2, C), slots(2)),
        ]
        scratch = [] if two else [stride_scratch()]
        self.r, self.picked, self.res_sum = call(
            body, self.meta, args, outs, scratch, f"{self.tag}_residual", 6 * OWN * rows * C * C
        )

    def start(self):
        self.z, self.got, self.stats = [], [], []

    def forward(self, after=None, joined=False):
        if not joined:
            self.start()
        for i in range(1 if joined else 0, 5):
            if i == 2:
                self.residual()
            self.forward_layer(i, (after or {}).get(i, ()))


    def segments(self):
        return [(0, HALF), (HALF, HALF)] if self.two else [(0, self.tail_rows)]

    def lengths(self, meta, m):
        if self.two:
            return [meta[m], meta[OWN + m]]
        return [meta[OWN + m]]

    def squeeze(self, sums, counts, se_refs):
        down_t, down_b, up, up_b = se_refs
        means = [s / jnp.maximum(jnp.full((1, C), n.astype(F32)), 1.0) for s, n in zip(sums, counts)]
        ps = [jnp.sum(down_t[...] * mean, axis=1, keepdims=True) + down_b[...] for mean in means]
        gates = [sigmoid(column_sum(up[...] * (p * sigmoid(p))) + up_b[...]) for p in ps]
        return means, ps, gates

    def squeeze_back(self, des, ps, gates, counts, se_refs, means, small, m):
        down_t, down_b, up, up_b = se_refs
        shares, up_grad, down_grad, dq_sum, dp_sum = [], 0.0, 0.0, 0.0, 0.0
        for de, p, gate, n, mean in zip(des, ps, gates, counts, means):
            dq = de * gate * (1.0 - gate)
            s = sigmoid(p)
            dp = jnp.sum(up[...] * dq, axis=1, keepdims=True) * (s * (1.0 + p * (1.0 - s)))
            shares.append(column_sum(down_t[...] * dp) / jnp.maximum(jnp.full((1, C), n.astype(F32)), 1.0))
            up_grad, down_grad = up_grad + (p * s) * dq, down_grad + dp * mean
            dq_sum, dp_sum = dq_sum + dq, dp_sum + dp
        row, col = (lax.broadcasted_iota(jnp.int32, (SE, C), axis) for axis in (0, 1))
        dp_row = column_sum(jnp.where(row == col, dp_sum, 0.0))
        accumulate(small, m, 0, up_grad)
        accumulate(small, m, SE, down_grad)
        accumulate(small, m, 2 * SE, dq_sum)
        accumulate(small, m, 2 * SE + 1, dp_row)
        return shares

    def last_norm(self, m, dt_out, du_out, z_ref, slope_ref, gates, shares, center, spread, res_bias, res_gain, pay, small):
        bias_sum, gain_sum = [], []
        for cs in CHUNKS:
            dh = dt_out[0, :, cs] * self.by_segment(gates, cs) + self.by_segment(shares, cs)
            du = dh * slope_ref[:, cs]
            du_out[0, :, cs] = du
            bias_sum.append(column_sum(du))
            gain_sum.append(column_sum(du * ((z_ref[0, :, cs] - center[:, cs]) * spread[:, cs])))
        rows = [jnp.concatenate(x, axis=1) for x in (bias_sum, gain_sum, res_bias, res_gain)]
        send(pay, rows)
        for j, row in enumerate(rows):
            accumulate(small, m, 2 * SE + 2 + j, row)

    def se_args(self):
        return list(zip(self.excitation, (whole(SE, C), whole(SE, 1), whole(SE, C), whole(1, C))))

    def store_rows(self, ref, rows):
        ref[0] = jnp.concatenate(rows + [jnp.zeros((8 - len(rows), C), F32)], axis=0)

    def store_columns(self, ref, columns):
        ref[0] = jnp.zeros((SE, 8), F32)
        for j, column in enumerate(columns):
            ref[0, :, j : j + 1] = column

    def by_segment(self, rows, cs):
        parts = [jnp.broadcast_to(row[:, cs], (n, LANES)) for row, (_, n) in zip(rows, self.segments())]
        return parts[0] if len(parts) == 1 else jnp.concatenate(parts, axis=0)

    def seg_sums(self, x):
        return [column_sum(x[at : at + n]) for at, n in self.segments()]

    def tail(self, cotangent=None, far=None, after=()):
        return run(self.tail_steps(cotangent, far, after))

    def tail_steps(self, cotangent=None, far=None, after=()):
        two, rows = self.two, self.tail_rows
        back = cotangent is not None

        def body(meta, *refs):
            refs = list(refs)
            take = lambda n: [refs.pop(0) for _ in range(n)]
            m = pl.program_id(0)
            z_ref, got4, r_ref, got3, n_ref, gain, bias = take(7)
            se_refs = take(4)
            if back:
                cot_ref, far_ref = take(2)
            out, stat_out, rstat_out, means_out, p_out, gate_out = take(6)
            if back:
                small, du_out, dt_out, pay = take(4)
            h_ref, = take(1)
            if back:
                slope_ref, = take(1)
            valid = self.valid(meta, m, 4)
            number = n_ref[0, 1:2, :]
            center, spread = center_spread(added(got4), number)
            rcenter, rspread = center_spread(added(got3)[2:4], number)
            stat_out[0, 0:1, :] = center
            stat_out[0, 1:2, :] = spread
            rstat_out[0, 0:1, :] = rcenter
            rstat_out[0, 1:2, :] = rspread
            scale = gain[4:5] * spread
            shift = bias[4:5] - center * scale
            sums = []
            for cs in CHUNKS:
                u = z_ref[0, :, cs] * scale[:, cs] + shift[:, cs]
                s = sigmoid(u)
                h = valid.keep(u * s)
                h_ref[:, cs] = h
                if back:
                    slope_ref[:, cs] = valid.keep(s * (1.0 + u * (1.0 - s)))
                sums.append(self.seg_sums(h))
            sums = [jnp.concatenate([s[j] for s in sums], axis=1) for j in range(len(self.segments()))]
            counts = self.lengths(meta, m)
            means, ps, gates = self.squeeze(sums, counts, se_refs)
            self.store_rows(means_out, means)
            self.store_columns(p_out, ps)
            self.store_rows(gate_out, gates)
            res_gain, res_bias, gate_grad = [], [], []
            for cs in CHUNKS:
                h = h_ref[:, cs]
                rh = (r_ref[0, :, cs] - rcenter[:, cs]) * rspread[:, cs]
                t = h * self.by_segment(gates, cs) + gain[5:6, cs] * rh + bias[5:6, cs]
                s = sigmoid(t)
                out[0, 0:rows, cs] = valid.keep(t * s)
                if rows < SLOT:
                    out[0, rows:SLOT, cs] = jnp.zeros((SLOT - rows, LANES), F32)
                if back:
                    cot = jnp.where(meta[2 * OWN] == 1, far_ref[0, :, cs], cot_ref[0, :, cs])
                    dt = valid.keep(cot * (s * (1.0 + t * (1.0 - s))))
                    dt_out[0, :, cs] = dt
                    res_bias.append(column_sum(dt))
                    res_gain.append(column_sum(dt * rh))
                    gate_grad.append(self.seg_sums(dt * h))
            if not back:
                return
            des = [jnp.concatenate([g[j] for g in gate_grad], axis=1) for j in range(len(counts))]
            shares = self.squeeze_back(des, ps, gates, counts, se_refs, means, small, m)
            self.last_norm(m, dt_out, du_out, z_ref, slope_ref, gates, shares, center, spread, res_bias, res_gain, pay, small)

        args = [
            (self.z[4], slots(rows)), (self.got[4], copies(self.last, 2)), (self.r, slots(rows)),
            (self.got[3], copies(self.last, 4)), (self.number, slots(2)),
            (self.gain, whole(6, C)), (self.bias, whole(6, C)),
        ] + self.se_args()
        outs = [
            (f32(OWN, SLOT, C), slots(SLOT)), (f32(OWN, 2, C), slots(2)), (f32(OWN, 2, C), slots(2)),
            (f32(OWN, 8, C), slots(8)), (f32(OWN, SE, 8), slots(SE, 8)), (f32(OWN, 8, C), slots(8)),
        ]
        scratch = [pltpu.VMEM((rows, C), F32)]
        if back:
            args += [(cotangent, layer(MB - 1, SLOT, C)), (far, slots(SLOT))]
            outs += self.tail_outs()
            scratch.append(pltpu.VMEM((rows, C), F32))
        result = yield body, self.meta, args, outs, scratch, f"{self.tag}_tail", 0, after, ()
        self.stats.append(result[1])
        self.rstat, self.se_state = result[2], result[3:6]
        if back:
            self.tail_results(result[6:])
        return result[0]

    def tail_outs(self):
        rows, count = self.tail_rows, self.first
        return [
            (f32(SMALL, C), whole(TAIL_ROWS, C)), (f32(OWN, rows, C), slots(rows)), (f32(OWN, rows, C), slots(rows)),
            (f32(count, OWN, 4, C), copies(count, 4)),
        ]

    def tail_results(self, result):
        self.small, self.du, self.dt, pay = result
        self.back_got = shared(pay, self.stages)

    def tail_backward_steps(self, cotangent, far, back):
        rows = self.tail_rows

        def body(meta, z_ref, r_ref, stat, rstat, gain, bias, means_ref, p_ref, gate_ref, down, down_b, up, up_b, cot_ref, far_ref, back_ref,
                 small, du_out, dt_out, pay, slope_ref):
            m = pl.program_id(0)
            valid = self.valid(meta, m, 4)
            center, spread, rcenter, rspread = stat[0, 0:1], stat[0, 1:2], rstat[0, 0:1], rstat[0, 1:2]
            scale = gain[4:5] * spread
            shift = bias[4:5] - center * scale
            zeros = jnp.zeros((rows - HALF, LANES), F32)
            counts = self.lengths(meta, m)
            ps = [p_ref[0, :, j : j + 1] for j in range(len(counts))]
            gates = [gate_ref[0, j : j + 1, :] for j in range(len(counts))]
            means = [means_ref[0, j : j + 1, :] for j in range(len(counts))]
            res_gain, res_bias, gate_grad = [], [], []
            for cs in CHUNKS:
                u = z_ref[0, :, cs] * scale[:, cs] + shift[:, cs]
                s = sigmoid(u)
                h = valid.keep(u * s)
                slope_ref[:, cs] = valid.keep(s * (1.0 + u * (1.0 - s)))
                rh = (r_ref[0, :, cs] - rcenter[:, cs]) * rspread[:, cs]
                t = h * self.by_segment(gates, cs) + gain[5:6, cs] * rh + bias[5:6, cs]
                s = sigmoid(t)
                here = jnp.where(meta[2 * OWN] == 1, cot_ref[0, 0:HALF, cs], far_ref[0, :, cs])
                cot = jnp.concatenate([here + back_ref[0, :, cs], zeros], axis=0)
                dt = valid.keep(cot * (s * (1.0 + t * (1.0 - s))))
                dt_out[0, :, cs] = dt
                res_bias.append(column_sum(dt))
                res_gain.append(column_sum(dt * rh))
                gate_grad.append(self.seg_sums(dt * h))
            des = [jnp.concatenate([g[j] for g in gate_grad], axis=1) for j in range(len(counts))]
            shares = self.squeeze_back(des, ps, gates, counts, (down, down_b, up, up_b), means, small, m)
            self.last_norm(m, dt_out, du_out, z_ref, slope_ref, gates, shares, center, spread, res_bias, res_gain, pay, small)

        args = [
            (self.z[4], slots(rows)), (self.r, slots(rows)), (self.stats[4], slots(2)), (self.rstat, slots(2)),
            (self.gain, whole(6, C)), (self.bias, whole(6, C)),
            (self.se_state[0], slots(8)), (self.se_state[1], slots(SE, 8)), (self.se_state[2], slots(8)),
        ] + self.se_args() + [(cotangent, slots(HALF)), (far, layer(MB - 1, HALF, C)), (back, slots(HALF))]
        scratch = [pltpu.VMEM((rows, C), F32)]
        result = yield body, self.meta, args, self.tail_outs(), scratch, f"{self.tag}_tail_back", 0, (), ()
        self.tail_results(result)


    def norm_grad(self, du, zh, scale, sums, number, cs):
        return scale[:, cs] * (du - sums[0:1, cs] / number[:, cs] - zh * (sums[1:2, cs] / number[:, cs]))

    def backward_layer(self, i):
        return run(self.backward_steps(i))

    def backward_steps(self, i):
        two, count = self.two, self.first
        strided = i == 4 and not two
        rows = self.rows_of(i)
        n_src = len(self.source_args())

        def body(meta, *refs):
            refs = list(refs)
            take = lambda n: [refs.pop(0) for _ in range(n)]
            m = pl.program_id(0)
            du_ref, z_ref, w_ref, got, n_ref, stat, gain, bias, dw_ref = take(9)
            if i:
                zp_ref, statp = take(2)
            else:
                dxr_ref, = take(1)
                src = take(n_src)
            small, dz_out = take(2)
            if i:
                du_out, pay = take(2)
            elif two:
                back_out, dx_out = take(2)
            else:
                dx_out, = take(1)
            pad, = take(1)
            alt, = take(1) if refs else (None,)
            sums = added(got)
            number = n_ref[0, 1:2, :] if i == 4 else n_ref[0, 0:1, :]
            center, spread = stat[0, 0:1], stat[0, 1:2]
            scale = gain[i : i + 1] * spread
            valid = self.valid(meta, m, i)
            for cs in CHUNKS:
                zh = (z_ref[0, :, cs] - center[:, cs]) * spread[:, cs]
                dz = valid.keep(self.norm_grad(du_ref[0, :, cs], zh, scale, sums, number, cs))
                high, low = halves(dz)
                dz_out[0, :, cs] = high
                dz_out[0, :, C + cs.start : C + cs.stop] = low
            dy = stacked_dot(dz_out[0, :, 0:C], dz_out[0, :, C : 2 * C], w_ref.at[0], True)
            valid_in = self.valid(meta, m, 0)
            if i:
                pcenter, pspread = statp[0, 0:1], statp[0, 1:2]
                pscale = gain[i - 1 : i] * pspread
                pshift = bias[i - 1 : i] - pcenter * pscale
            taps, bias_sum, gain_sum = [[] for _ in range(TAPS)], [], []
            for c, cs in enumerate(CHUNKS):
                grad = dy[:, cs]
                if strided:
                    grad = spread_out(alt.at[c], grad)
                padded = Padded(pad.at[c], two)
                padded.put(grad)
                if i:
                    z = zp_ref[0, :, cs]
                    u = z * pscale[:, cs] + pshift[:, cs]
                    s = sigmoid(u)
                    h = valid_in.keep(u * s)
                else:
                    h = valid_in.keep(self.source(meta, src, cs))
                dh = None
                for k in range(TAPS):
                    moved = padded.get(2 - k)
                    taps[k].append(column_sum(h * moved))
                    term = dw_ref[0, k : k + 1, cs] * moved
                    dh = term if dh is None else dh + term
                if i:
                    du = valid_in.keep(dh * (s * (1.0 + u * (1.0 - s))))
                    du_out[0, :, cs] = du
                    bias_sum.append(column_sum(du))
                    gain_sum.append(column_sum(du * ((z - pcenter[:, cs]) * pspread[:, cs])))
                    continue
                dxr = dxr_ref[0, :, cs]
                if not two:
                    dxr = spread_out(alt.at[c], dxr)
                dx = valid_in.keep(dh) + dxr
                if two:
                    back_out[0, :, cs] = dx[:HALF]
                    dx = dx[HALF:]
                dx_out[0, :, cs] = dx
            rows = taps + [bias_sum, gain_sum] if i else taps
            rows = [jnp.concatenate(x, axis=1) for x in rows]
            for j, row in enumerate(rows):
                accumulate(small, m, j, row)
            if i:
                send(pay, rows[TAPS:])

        sent = 4 if i == 4 else 2
        args = [
            (self.du, slots(rows)), (self.z[i], slots(rows)), self.matrix(i), (self.back_got, copies(self.last, sent)),
            (self.number, slots(2)), (self.stats[i], slots(2)), (self.gain, whole(6, C)), (self.bias, whole(6, C)),
            (self.dw, layer(i, TAPS, C)),
        ]
        if not i:
            args.append((self.dxr, slots(self.tail_rows)))
        args += self.before_args(i)
        place = TAIL_ROWS // 8 + i
        outs = [(f32(SMALL, C), pl.BlockSpec((8, C), lambda m, *_: (place, 0))), (bf16(OWN, rows, 2 * C), slots(rows, 2 * C))]
        if i:
            outs += [(f32(OWN, SLOT, C), slots(SLOT)), (f32(count, OWN, 2, C), copies(count, 2))]
        elif two:
            outs += [(f32(OWN, HALF, C), slots(HALF)), (f32(OWN, HALF, C), slots(HALF))]
        else:
            outs += [(f32(OWN, SLOT, C), slots(SLOT))]
        scratch = [pad_scratch()]
        if strided or (i == 0 and not two):
            scratch.append(stride_scratch())
        flops = 6 * OWN * rows * C * C
        self.small, dz, *result = yield (
            body, self.meta, args, outs, scratch, f"{self.tag}_backward_{i}", flops, self.done, (self.small,)
        )
        got = self.back_got
        if i:
            self.du = result[0]
            if i == self.stop:
                self.pending = dz, result[1]
                return result
            self.back_got = shared(result[1], self.stages)
        self.weight_grad(i, dz)
        if i == 4:
            self.residual_back(got)
        return result

    def residual_back(self, got):
        rows = self.tail_rows

        def body(meta, got, n_ref, dt_ref, r_ref, rstat, gain, w_ref, x_ref, kept_out, away_out, dxr_out, dr, total):
            m = pl.program_id(0)
            sums = added(got)[2:4]
            number = n_ref[0, 1:2, :]
            center, spread = rstat[0, 0:1], rstat[0, 1:2]
            scale = gain[5:6] * spread
            valid = self.valid(meta, m, 4)
            for cs in CHUNKS:
                rh = (r_ref[0, :, cs] - center[:, cs]) * spread[:, cs]
                high, low = halves(valid.keep(self.norm_grad(dt_ref[0, :, cs], rh, scale, sums, number, cs)))
                dr[:, cs] = high
                dr[:, C + cs.start : C + cs.stop] = low
            high, low = dr[:, 0:C], dr[:, C : 2 * C]
            dxr_out[0] = stacked_dot(high, low, w_ref.at[0], True)
            grad = stacked_outer(x_ref[0, :, 0:C], x_ref[0, :, C : 2 * C], high, low)
            self.add_halves(meta, m, grad, total, kept_out, away_out)

        args = [
            (got, copies(self.last, 4)), (self.number, slots(2)), (self.dt, slots(rows)), (self.r, slots(rows)),
            (self.rstat, slots(2)), (self.gain, whole(6, C)), self.matrix(5), (self.picked, slots(rows, 2 * C)),
        ]
        outs = self.piece_out(5) + [(f32(OWN, rows, C), slots(rows))]
        which = PLACES[5][0]
        *self.pieces[which], self.dxr = call(
            body, self.meta, args, outs, [pltpu.VMEM((rows, 2 * C), BF16), pltpu.VMEM((C, C), F32)],
            f"{self.tag}_residual_back", 12 * OWN * rows * C * C, into=self.pieces[which],
        )

    def piece_out(self, i):
        which, place = PLACES[i]
        rows = PIECE_ROWS[which]
        return [(f32(rows, C), pl.BlockSpec((C // 2, C), lambda m, *_: (place, 0)))] * 2

    def add_halves(self, meta, m, grad, total, kept_out, away_out):
        @pl.when(m == 0)
        def _():
            total[...] = grad

        @pl.when(m > 0)
        def _():
            top, bottom = total[0 : C // 2] + grad[0 : C // 2], total[C // 2 : C] + grad[C // 2 : C]
            lower = meta[2 * OWN] == 1
            kept_out[...] = jnp.where(lower, top, bottom)
            away_out[...] = jnp.where(lower, bottom, top)

    def weight_grad(self, i, dz):
        two = self.two
        strided = i == 4 and not two
        rows = self.rows_of(i)
        n_src = len(self.source_args())

        def body(meta, *refs):
            refs = list(refs)
            take = lambda n: [refs.pop(0) for _ in range(n)]
            m = pl.program_id(0)
            if i:
                zp_ref, statp, gain, bias = take(4)
                center, spread = statp[0, 0:1], statp[0, 1:2]
                scale = gain[i - 1 : i] * spread
                shift = bias[i - 1 : i] - center * scale
            else:
                src = take(n_src)
            dz_ref, dw_ref, kept_out, away_out, pad, yh, yl, total = take(8)
            alt, = take(1) if strided else (None,)
            valid_in = self.valid(meta, m, 0)
            for c, cs in enumerate(CHUNKS):
                if i:
                    u = zp_ref[0, :, cs] * scale[:, cs] + shift[:, cs]
                    h = valid_in.keep(u * sigmoid(u))
                else:
                    h = valid_in.keep(self.source(meta, src, cs))
                padded = Padded(pad.at[c], two)
                padded.put(h)
                y = padded.conv(dw_ref[0, :, cs])
                if strided:
                    y = every_other(alt.at[c], y)
                yh[:, cs], yl[:, cs] = halves(y)
            grad = stacked_outer(yh[...], yl[...], dz_ref[0, :, 0:C], dz_ref[0, :, C : 2 * C])
            self.add_halves(meta, m, grad, total, kept_out, away_out)

        args = self.before_args(i)
        if i:
            args += [(self.gain, whole(6, C)), (self.bias, whole(6, C))]
        args += [(dz, slots(rows, 2 * C)), (self.dw, layer(i, TAPS, C))]
        scratch = [pad_scratch(), pltpu.VMEM((rows, C), BF16), pltpu.VMEM((rows, C), BF16), pltpu.VMEM((C, C), F32)]
        if strided:
            scratch.append(stride_scratch())
        which = PLACES[i][0]
        self.pieces[which] = call(
            body, self.meta, args, self.piece_out(i), scratch, f"{self.tag}_weights_{i}", 6 * OWN * rows * C * C,
            into=self.pieces[which],
        )
        self.done = (self.pieces[which][0],)

    def backward(self, layers):
        if layers[0] == 4:
            self.pieces = [[], []]
        for i in layers:
            result = self.backward_layer(i)
        return result

    def resume(self, i):
        dz, payload = self.pending
        self.back_got = shared(payload, self.stages)
        self.weight_grad(i, dz)

    def fork(self, state=None):
        other = copy.copy(self)
        other.__dict__.update(state or {})
        if "pieces" in other.__dict__:
            other.pieces = list(other.pieces)
        return other

    def state(self):
        return {name: getattr(self, name) for name in ("du", "dxr", "pieces", "small", "pending")}

    def half(self, no, first, begin=None, end=None):
        kept, away = self.pieces[no]
        if no:
            parts = self.small[: SMALL // 2], self.small[SMALL // 2 :]
            at = kept.shape[0] - SMALL // 2
            kept = lax.dynamic_update_slice_in_dim(kept, jnp.where(first, *parts), at, 0)
            away = lax.dynamic_update_slice_in_dim(away, jnp.where(first, *parts[::-1]), at, 0)
        if begin is not None:
            away, _ = lax.optimization_barrier((away, begin))
            kept, _ = lax.optimization_barrier((kept, end))
        return kept + swap(away)


PLACES = {3: (0, 0), 4: (0, 1), 5: (0, 2), 0: (1, 0), 1: (1, 1), 2: (1, 2)}
PIECE_ROWS = (3 * C // 2, 3 * C // 2 + SMALL // 2)


def split_squeeze(meta, own, far):
    def body(meta, own_ref, far_ref, *outs):
        row, col = (lax.broadcasted_iota(jnp.int32, (SE, C), axis) for axis in (0, 1))
        for block in range(2):
            down, down_b, up, up_b = outs[4 * block : 4 * block + 4]
            down[...] = choose(meta, block, own_ref[0:SE, :], far_ref[0:SE, :])
            up[...] = choose(meta, block, own_ref[SE : 2 * SE, :], far_ref[SE : 2 * SE, :])
            up_b[...] = choose(meta, block, own_ref[2 * SE : 2 * SE + 1, :], far_ref[2 * SE : 2 * SE + 1, :])
            wide = choose(meta, block, own_ref[2 * SE + 1 : 2 * SE + 2, :], far_ref[2 * SE + 1 : 2 * SE + 2, :])
            down_b[...] = jnp.sum(jnp.where(row == col, wide, 0.0), axis=1, keepdims=True)

    shapes = [(SE, C), (SE, 1), (SE, C), (1, C)] * 2
    args = [(x, whole(*x.shape)) for x in (own, far)]
    outs = call(body, meta, args, [(f32(*shape), whole(*shape)) for shape in shapes], name="split_squeeze", steps=1)
    return tuple(outs[:4]), tuple(outs[4:])


def pick_joining(picks, features):
    def body(picks, in_ref, out_ref):
        out_ref[...] = in_ref[0, 0]

    own = pl.BlockSpec((1, 1, HALF, C), lambda m, picks: (picks[m], 1, 0, 0))
    out = (f32(OWN * HALF, C), pl.BlockSpec((HALF, C), lambda m, *_: (m, 0)))
    return call(body, picks, [(features, own)], [out], name="pick_joining")[0]


def swap(x):
    return lax.ppermute(x, "section", [(0, 1), (1, 0)])


def fenced(always, work, x):
    shapes = jax.eval_shape(work, x)
    return lax.cond(always, work, lambda x: jax.tree.map(lambda y: jnp.zeros(y.shape, y.dtype), shapes), x)


class Reduction:
    def __init__(self, x, stages):
        self.x = x
        self.todo = []
        stride = 1
        for radix in stages:
            self.todo.append((True, radix, stride))
            stride *= radix
        self.todo += [(False, radix, stride) for _, radix, stride in reversed(self.todo)]

    def step(self):
        scatter, radix, stride = self.todo.pop(0)
        rows = self.x.shape[0]
        if scatter:
            parts = exchange(self.x.reshape(radix, rows // radix, C), radix, stride)
            self.x = jnp.sum(parts, axis=0)
        else:
            parts = exchange(jnp.broadcast_to(self.x, (radix,) + self.x.shape), radix, stride)
            self.x = parts.reshape(radix * rows, C)
        return (self.x,)

    def finish(self):
        while self.todo:
            self.step()
        return self.x


def per_device(features, out_grad, lengths, join_pick, dw, pw, gain, bias, res_w, down, down_b, up, up_b):
    first = lax.axis_index("section") == 0
    size = lax.axis_size("dp")
    inputs = features.reshape(MB, SLOT, C)
    cotangent = out_grad.reshape(MB, SLOT, C)
    own, picks = lengths[0, 0], join_pick[0]
    to_upper = lambda x: lax.ppermute(x, "section", [(0, 1)])
    to_lower = lambda x: lax.ppermute(x, "section", [(1, 0)])

    far_len = swap(own)
    far_rows = to_upper(inputs[MB - 1])
    far_w0 = swap(pw[0, 0:1])
    taps = jnp.concatenate([dw[0].reshape(5 * TAPS, C), gain[0], bias[0]], axis=0)
    far_taps = swap(taps)
    far_pw, far_res = swap(pw[0]), swap(res_w[0])
    wide = jnp.pad(down_b, ((0, 0), (0, C - SE)))
    squeeze = jnp.concatenate([down[0].T, up[0], up_b, wide], axis=0)
    far_squeeze = swap(squeeze)
    far_cot = swap(cotangent)

    flag = first.astype(jnp.int32)[None]
    mine = lambda v: jnp.where(first, v[:OWN], jnp.concatenate([v[OWN:], jnp.zeros((1,), v.dtype)]))
    length = mine(jnp.where(first, own, far_len))
    half_len = (length + 1) // 2
    join_len = mine(jnp.where(first, far_len, own)[picks])
    meta1 = jnp.concatenate([length, half_len, flag])
    meta2 = jnp.concatenate([half_len, join_len, flag, picks[MB - 1 :]])
    both = jnp.concatenate([length, half_len, flag, half_len, join_len, flag, picks[MB - 1 :]])

    def small(block):
        t = jnp.where(first == (block == 0), taps, far_taps)
        return t[: 5 * TAPS].reshape(5, TAPS, C), t[5 * TAPS : 5 * TAPS + 6], t[5 * TAPS + 6 :]

    excitations = split_squeeze(meta1, squeeze, far_squeeze)

    def prepared(block, start, stop):
        array = prepare(meta1, (pw[0], res_w[0]), (far_pw, far_res), block, start, stop)
        return array, {i: (array, i - start) for i in range(start, stop)}

    parts0 = [prepared(0, 1, 3), prepared(0, 3, 6)]
    parts1 = [prepared(1, 0, 1), prepared(1, 1, 4), prepared(1, 4, 6)]

    stages, deep = radices(size, 16), radices(size, 4)
    c14 = Block(False, meta1, small(0), {**parts0[0][1], **parts0[1][1]}, stages)
    c14.x, c14.x_far, c14.first_matrix = inputs, far_rows, (pw[0], far_w0)
    c14.excitation = excitations[0]
    c14.forward({2: (parts0[1][0],)})
    late_picks, _ = lax.optimization_barrier((picks, c14.z[3]))
    far_joining = to_lower(pick_joining(late_picks, features.reshape(MB, 2, HALF, C)))
    c15 = Block(True, meta2, small(1), {**parts1[0][1], **parts1[1][1], **parts1[2][1]}, stages)
    c15.excitation = excitations[1]
    c15.arrived, c15.joined_far, c15.joined = Linked(0, HALF), far_joining, features.reshape(MB, 2, HALF, C)
    c15.start()
    out0, _ = run_joined(c14.tail_steps(), c15.forward_steps(0), (both, 0, meta1.shape[0]))
    c15.arrived = out0
    c15.forward({1: (parts1[1][0],), 2: (parts1[2][0],)}, joined=True)
    out1 = c15.tail(cotangent, far_cot)
    c15.stop = 2
    c15.backward((4, 3))
    begin = c15.back_got
    c15.backward((2,))
    always = own[0] > 0

    half0 = c15.half(0, first, begin, c15.du)
    sum0 = lax.psum(half0, "dp")

    def middle(half0):
        upper, lower = c15.fork(), c14.fork()
        upper.resume(2)
        upper.done += (half0,)
        upper.backward((1,))
        (_, dx1), _ = run_joined(
            upper.backward_steps(0), lower.tail_backward_steps(cotangent, far_cot, Linked(2, HALF)), (both, meta1.shape[0], 0)
        )
        lower.done = upper.done
        lower.backward((4,))
        begin1 = lower.back_got
        lower.backward((3,))
        half1 = upper.half(1, first, begin1, lower.du)
        begin2 = lower.back_got
        lower.stop = 2
        lower.backward((2,))
        half2 = lower.half(0, first, begin2, lower.du)
        return dx1, jnp.concatenate([half1, half2], axis=0), lower.state()

    dx1, half12, state = fenced(always, middle, half0)
    sum0, half12 = lax.optimization_barrier((sum0, half12))
    sum12 = lax.psum(half12, "dp")

    def ending(half12):
        last = c14.fork(state)
        last.resume(2)
        last.done += (half12,)
        came0 = to_upper(sum0)
        dx0, = last.backward((1, 0))
        half3 = last.half(1, first)
        half3, dx0, *kept = lax.optimization_barrier((half3, dx0, out0, out1, dx1))
        reduction = Reduction(half3, deep)
        reduction.step()
        pad = jnp.zeros((1, HALF, C), F32)
        lower = jnp.concatenate([kept[0], jnp.concatenate([to_lower(kept[0][0:1, :HALF]), pad], axis=1)], axis=0)
        upper = jnp.concatenate([to_upper(kept[1]), kept[1][0:1]], axis=0)
        block_out = jnp.where(first, lower, upper)
        lower = jnp.concatenate([dx0, to_lower(dx0[0:1])], axis=0)
        joins = jnp.concatenate([to_upper(kept[2]), kept[2][0:1]], axis=0)
        joins = jnp.stack([lax.dynamic_index_in_dim(joins, jnp.argmax(picks == s), 0, False) for s in range(MB)])
        upper = jnp.concatenate([jnp.zeros_like(joins), joins], axis=1)
        dx = jnp.where(first, lower, upper)
        reduction.x, block_out, dx, came0 = lax.optimization_barrier((reduction.x, block_out, dx, came0))
        return block_out, dx, came0, reduction.finish()

    block_out, dx, came0, sum3 = fenced(always, ending, half12)
    came3 = to_lower(sum3)
    sum12, _ = lax.optimization_barrier((sum12, sum3))
    spare = sum12.shape[0] - PIECE_ROWS[1]
    came12 = swap(lax.dynamic_slice_in_dim(sum12, jnp.where(first, 0, spare), PIECE_ROWS[1]))
    split, lead = PIECE_ROWS[1], 3 * C // 2

    def assembled(rest_top, rest_bottom, lead_top, lead_bottom):
        halves_of = lambda x: x.reshape(-1, 1, C // 2, C)
        both = lambda top, bottom: jnp.concatenate([halves_of(top), halves_of(bottom)], axis=1).reshape(-1, C, C)
        rest, top = both(rest_top[:lead], rest_bottom[:lead]), both(lead_top[:C], lead_bottom[:C])
        res = both(lead_top[C:], lead_bottom[C:])
        return jnp.concatenate([rest, top], axis=0)[None], res, jnp.concatenate([rest_top[lead:], rest_bottom[lead:]], axis=0)

    pw_grad, res_grad, rows = lax.cond(
        first,
        lambda s3, c3, s12, c12, s0, c0: assembled(s3, c3, s12[split:], c12[split - spare :]),
        lambda s3, c3, s12, c12, s0, c0: assembled(c12, s12[:split], c0, s0),
        sum3, came3, sum12, came12, sum0, came0,
    )
    dw_grad = rows[TAIL_ROWS : TAIL_ROWS + 40].reshape(1, 5, 8, C)
    norms = jnp.concatenate([dw_grad[0, 1:, TAPS : TAPS + 2], rows[None, 2 * SE + 2 : 2 * SE + 4], rows[None, 2 * SE + 4 : 2 * SE + 6]], axis=0)
    return (
        block_out.reshape(features.shape), dx.reshape(features.shape), dw_grad[:, :, :TAPS], pw_grad,
        norms[None, :, 1], norms[None, :, 0], res_grad, rows[SE : 2 * SE].T[None], rows[2 * SE + 1 : 2 * SE + 2, :SE],
        rows[:SE][None], rows[2 * SE : 2 * SE + 1],
    )


def solution(mesh):
    rows = P("section", "dp", None)
    own = lambda dims: P("section", *([None] * dims))
    weights = (own(3), own(3), own(2), own(2), own(2), own(2), own(1), own(2), own(1))
    in_specs = (rows, rows, rows, P("dp", None), *weights)
    out_specs = (rows, rows, *weights)
    return jax.shard_map(per_device, mesh=mesh, in_specs=in_specs, out_specs=out_specs, check_vma=False)
```
